32 devices in a mesh: dp: 2 (over y), expert: 16 (over z, x, core).
Axes of the slice: x: 2, y: 2, z: 4, core: 2. Of those that a mesh axis runs over, the one named last changes fastest.
Arguments:
- attn: bfloat16 [16, 64, 4096], P('expert', None, 'dp'), may hold values from -6 to 6
- resid: bfloat16 [16, 64, 2048], P('expert', 'dp'), may hold values from -6 to 6
- w_out: bfloat16 [4096, 2048], P('dp', 'expert'), may hold values from -0.09375 to 0.09375
- gain_post: float32 [2048], replicated, may hold values from 0.1 to 1.9
- route_ids: int32 [16, 64, 8], P('expert', 'dp'), may hold values from 0 to 15, all different within a row; in each aligned block of 32 rows (0 to 31, 32 to 63, ..., all dimensions but the last counted through in order) at most 32 rows name the same one
- route_logits: float32 [16, 64, 8], P('expert', 'dp'), may hold values from -2 to 260
- live_count: int32 [16, 2], P('expert', 'dp'), may hold values from 1 to 32, as said below
- w_gate_up: bfloat16 [16, 2048, 1536], P('expert', 'dp'), may hold values from -0.125 to 0.125
- w_down: bfloat16 [16, 768, 2048], P('expert', None, 'dp'), may hold values from -0.21875 to 0.21875
- gain_final: float32 [2048], replicated, may hold values from 0.1 to 1.9
Outputs:
- stream_out: bfloat16 [16, 64, 2048], P('expert', 'dp')
- normed_out: bfloat16 [16, 64, 2048], P('expert', 'dp')
The draws below stay inside these ranges and needn't reach their ends.
Inputs may be any that keep to these rules, and one draw needn't show every extreme that they name: `route_ids`: each row names 8 different experts; among the rows of one device no expert is named more than 32 times. `live_count`: the devices whose dp index is a multiple of 3 hold prefill rows, all live; the others hold decode rows with a varying count.
All inputs are finite; a program needn't handle non-finite values.
Results may differ from the reference program's by a relative error of at most 0.018.
Values may be sent and summed in bfloat16 or wider, within the bound.
No kernel may reach another device: no remote copies, remote signals or barrier semaphores. Data moves between devices by JAX's collectives and lax.ppermute only.
A program may use at most 64 MiB of HBM per device.

```python
import math
import jax
import jax.numpy as jnp
import numpy as np
from jax import lax

D = 2048
F = 4096
FF = 768
TOP = 8
ROWS_DEV = 32
EXPERTS = 16
GROUPS = 16
ROWS_GRP = 64
CAP = 32
N_DP = 2


def draw_route_logits(key, part):
    first = jax.random.fold_in(key, 0)
    return jnp.clip(0.6 * jax.random.normal(first, (GROUPS, ROWS_GRP, TOP), jnp.float32), -1.8, 1.8)


def draw_live_count(key, part):
    counted = jax.random.randint(key, (GROUPS, N_DP), 1, ROWS_DEV + 1)
    dp_place = jnp.arange(N_DP)[None, :]
    return jnp.where(dp_place % 3 == 0, ROWS_DEV, counted).astype(jnp.int32)


def block_scale(key, extent, cuts, smallest, largest):
    factor_of, own = 1.0, jax.random.fold_in(key, 6)
    for axis_at, parts in cuts:
        draws = jnp.exp(jax.random.uniform(jax.random.fold_in(own, axis_at), (parts,), jnp.float32, smallest / len(cuts), largest / len(cuts)))
        factor_of = factor_of * jnp.repeat(draws, extent[axis_at] // parts).reshape([-1 if axis == axis_at else 1 for axis in range(len(extent))])
    return factor_of


def routed_block(key, own, number, rows, amount, top, reach, lean):
    order = jax.random.permutation(key, amount)
    crowded, common = load_shares(amount, rows * top, reach, lean, True), load_shares(amount, rows * top, reach, lean, False)
    places = jnp.arange(amount)

    def named(sizes, offset_by):
        used = int((sizes > 0).sum())
        fixed = max(1, used // 4)
        passed = fixed + (places - fixed + offset_by * (used - fixed)) % max(1, amount - fixed)
        return jnp.zeros((amount,), jnp.int32).at[order[jnp.where(places < fixed, places, passed)]].set(jnp.asarray(sizes, jnp.int32))

    sizes = jnp.where(number % 4 == 0, named(crowded, number // 4), named(common, number - number // 4 - 1))
    mixed = jax.random.permutation(jax.random.fold_in(own, 3), amount)
    donor, taker = mixed[0:amount // 2 * 2:2], mixed[1:amount // 2 * 2:2]
    margin = jnp.minimum(sizes[donor] - 1, reach - sizes[taker]) // 2
    margin = jnp.where((donor == order[0]) | (taker == order[0]) | (sizes[taker] == 0), 0, jnp.maximum(margin, 0))
    passed = jax.random.randint(jax.random.fold_in(own, 4), (amount // 2,), 0, 1 << 20) % (margin + 1)
    sizes = sizes.at[donor].add(-passed).at[taker].add(passed)
    members = jnp.searchsorted(jnp.cumsum(sizes), jnp.arange(rows * top), side="right").astype(jnp.int32)
    listing = members.reshape(top, rows).T
    listing = listing[jax.random.permutation(jax.random.fold_in(own, 1), rows)]
    offset_by = jax.random.randint(jax.random.fold_in(own, 2), (rows, 1), 0, top)
    return jnp.take_along_axis(listing, (jnp.arange(top)[None, :] + offset_by) % top, axis=1)


def load_shares(number_of, total, reach, slope, full):
    loads = [(1 << 20) // math.isqrt(standing ** slope) + 1 for standing in range(1, number_of + 1)]
    largest = reach if full else min(reach, max(-(-total // number_of), total * loads[0] // sum(loads)))
    least = 1 if total - largest >= number_of - 1 else 0
    given, spare = [largest] + [least] * (number_of - 1), total - largest - least * (number_of - 1)
    while spare > 0:
        candidates = [i for i in range(1, number_of) if given[i] < largest] or [i for i in range(1, number_of) if given[i] < reach]
        whole, remaining = sum([loads[i] for i in candidates]), spare
        for i in candidates:
            extra = min(reach - given[i], max(1, remaining * loads[i] // whole), spare)
            given[i] = given[i] + extra
            spare = spare - extra
    return np.array(given)


def scatter_about(stream_key, extent, deviation, limit, cuts=(), kind=jnp.bfloat16):
    level = block_scale(stream_key, extent, cuts, -0.22, 0.18) if cuts else 1.0
    entries = jax.random.normal(stream_key, extent, jnp.float32) * deviation * level
    return jnp.minimum(jnp.maximum(entries, -limit), limit).astype(kind)


def setup_inputs(seed: int = 0) -> dict:
    keys = jax.random.split(jax.random.key(seed), 11)
    attn = scatter_about(keys[0], (GROUPS, ROWS_GRP, F), 1.0, 6.0, ((0, 16), (2, 2)))
    resid = scatter_about(keys[1], (GROUPS, ROWS_GRP, D), 1.0, 6.0, ((0, 16), (1, 2)))
    w_out = scatter_about(keys[2], (F, D), F ** -0.5, 0.09375, ((0, 2), (1, 16)))
    gain_post = jnp.clip(1.0 + 0.18 * jax.random.normal(keys[3], (D,), jnp.float32), 0.1, 1.9)
    route_ids_keys = jax.random.split(jax.random.fold_in(keys[4], 1), GROUPS * ROWS_GRP // ROWS_DEV)
    route_ids_turns = jax.random.permutation(jax.random.fold_in(keys[4], 3), GROUPS * ROWS_GRP // ROWS_DEV)
    route_ids = jax.vmap(lambda own, number: routed_block(jax.random.fold_in(keys[4], 2), own, number, ROWS_DEV, EXPERTS, TOP, CAP, 2))(route_ids_keys, route_ids_turns).reshape((GROUPS, ROWS_GRP, TOP))
    route_logits = draw_route_logits(jax.random.fold_in(keys[10], 71), 0)
    live_count = draw_live_count(jax.random.fold_in(keys[10], 71), 0)
    w_gate_up = scatter_about(keys[7], (EXPERTS, D, 2 * FF), D ** -0.5, 0.125, ((0, 16), (1, 2)))
    w_down = scatter_about(keys[8], (EXPERTS, FF, D), FF ** -0.5, 0.21875, ((0, 16), (2, 2)))
    gain_final = jnp.clip(1.0 + 0.18 * jax.random.normal(keys[9], (D,), jnp.float32), 0.1, 1.9)
    return {"attn": attn, "resid": resid, "w_out": w_out, "gain_post": gain_post, "route_ids": route_ids, "route_logits": route_logits, "live_count": live_count, "w_gate_up": w_gate_up, "w_down": w_down, "gain_final": gain_final}


def rms_scale(values, gain):
    return values * lax.rsqrt(lax.optimization_barrier(jnp.mean(values * values, axis=-1, keepdims=True)) + 1e-06) * gain

def reference(attn, resid, w_out, gain_post, route_ids, route_logits, live_count, w_gate_up, w_down, gain_final):
    row_total = GROUPS * ROWS_GRP
    feat_block = F // N_DP
    proj = jnp.zeros((row_total, D), jnp.float32)
    for blk in range(N_DP):
        part = attn[:, :, blk * feat_block:(blk + 1) * feat_block].reshape(row_total, feat_block)
        term = jnp.dot(part, w_out[blk * feat_block:(blk + 1) * feat_block], preferred_element_type=jnp.float32)
        term = lax.optimization_barrier(term.astype(jnp.bfloat16))
        proj = proj + term.astype(jnp.float32)
    stream_in = (resid.reshape(row_total, D).astype(jnp.float32) + proj).astype(jnp.bfloat16)
    stream_float = stream_in.astype(jnp.float32)
    normed_in = rms_scale(stream_float, gain_post).astype(jnp.bfloat16)
    probs = jax.nn.softmax(route_logits.reshape(row_total, TOP).astype(jnp.float32), axis=-1).astype(jnp.bfloat16)
    position = jnp.arange(ROWS_GRP, dtype=jnp.int32)
    device_row = position // ROWS_DEV
    within = position % ROWS_DEV
    alive = (within[None, :] < live_count[:, device_row]).reshape(row_total)
    weights = (probs.astype(jnp.float32) * alive[:, None].astype(jnp.float32)).reshape(-1)
    block_len = 256
    route_total = row_total * TOP
    chosen = route_ids.reshape(route_total).astype(jnp.int32)
    order = jnp.argsort(chosen, stable=True).astype(jnp.int32)
    sorted_ids = chosen[order]
    counts = lax.optimization_barrier(jnp.sum((chosen[:, None] == jnp.arange(EXPERTS, dtype=jnp.int32)[None, :]).astype(jnp.int32), axis=0))
    starts = jnp.cumsum(counts) - counts
    padded = (counts + block_len - 1) // block_len * block_len
    pad_start = jnp.cumsum(padded) - padded
    pad_end = pad_start + padded
    slot_pos = (pad_start[sorted_ids] + jnp.arange(route_total, dtype=jnp.int32) - starts[sorted_ids]).astype(jnp.int32)
    block_count = (route_total + block_len - 1) // block_len + EXPERTS
    slot_route = jnp.full((block_count * block_len,), -1, jnp.int32).at[slot_pos].set(order)
    block_first = jnp.arange(block_count, dtype=jnp.int32) * block_len
    block_expert = jnp.minimum(lax.optimization_barrier(jnp.sum((block_first[:, None] >= pad_end[None, :]).astype(jnp.int32), axis=1)), EXPERTS - 1).astype(jnp.int32)

    def one_block(mixture, block):
        routes = lax.dynamic_slice_in_dim(slot_route, block * block_len, block_len)
        valid = routes >= 0
        route = jnp.where(valid, routes, 0)
        row = route // TOP
        rows_in = normed_in[row]
        expert = block_expert[block]
        gate_up = lax.dynamic_index_in_dim(w_gate_up, expert, 0, keepdims=False)
        down = lax.dynamic_index_in_dim(w_down, expert, 0, keepdims=False)
        both = jnp.dot(rows_in, gate_up, preferred_element_type=jnp.float32)
        inner = (jax.nn.silu(both[:, :FF]) * both[:, FF:]).astype(jnp.bfloat16)
        expert_out = jnp.dot(inner, down, preferred_element_type=jnp.float32).astype(jnp.bfloat16)
        scale = jnp.where(valid, weights[route], jnp.float32(0.0))
        mixture = mixture.at[row].add(scale[:, None] * expert_out.astype(jnp.float32))
        return (mixture, None)
    mixture, unused = lax.scan(one_block, jnp.zeros((row_total, D), jnp.float32), jnp.arange(block_count, dtype=jnp.int32))
    stream_out = (stream_float + mixture).astype(jnp.bfloat16)
    normed_out = rms_scale(stream_out.astype(jnp.float32), gain_final).astype(jnp.bfloat16)
    return (stream_out.reshape(GROUPS, ROWS_GRP, D), normed_out.reshape(GROUPS, ROWS_GRP, D))
```

```python
import math

import jax
import jax.numpy as jnp
from jax import lax
from jax.experimental import pallas as pl
from jax.experimental.pallas import tpu as pltpu
from jax.sharding import PartitionSpec as P


def rms_scale(values, gain):
    return values * lax.rsqrt(jnp.mean(values * values, axis=-1, keepdims=True) + 1e-06) * gain


def swiglu_rows(rows_in, gate_up, down, hidden_units):
    both = jnp.dot(rows_in, gate_up, preferred_element_type=jnp.float32)
    inner = (jax.nn.silu(both[:, :hidden_units]) * both[:, hidden_units:]).astype(jnp.bfloat16)
    return jnp.dot(inner, down, preferred_element_type=jnp.float32).astype(jnp.bfloat16)


def body_general(
    attn,
    resid,
    w_out,
    gain_post,
    route_ids,
    route_logits,
    live_count,
    w_gate_up,
    w_down,
    gain_final,
):
    rows_here = resid.shape[1]
    model_width = resid.shape[2]
    top_count = route_ids.shape[2]
    dp_count = lax.axis_size("dp")
    expert_count = lax.axis_size("expert")
    hidden_units = w_down.shape[1]
    capacity = dp_count * max(1, 2 * rows_here * top_count // (expert_count * dp_count))
    slot_count = expert_count * capacity
    flat_attn = attn[0]
    partial_out = jnp.dot(
        flat_attn,
        lax.all_gather(w_out, "expert", axis=1, tiled=True),
        preferred_element_type=jnp.float32,
    )
    projected = lax.psum_scatter(
        partial_out.astype(jnp.bfloat16), "dp", scatter_dimension=0, tiled=True
    ).astype(jnp.float32)
    stream_in = (resid[0].astype(jnp.float32) + projected).astype(jnp.bfloat16)
    stream_float = stream_in.astype(jnp.float32)
    normed_in = rms_scale(stream_float, gain_post).astype(jnp.bfloat16)
    probs = jax.nn.softmax(route_logits[0], axis=-1).astype(jnp.bfloat16)
    alive = jnp.arange(rows_here, dtype=jnp.int32) < live_count[0, 0]
    expert_of = route_ids[0].reshape(-1)
    route_alive = jnp.repeat(alive, top_count)
    onehot = (
        (expert_of[:, None] == jnp.arange(expert_count, dtype=jnp.int32)[None, :])
        & route_alive[:, None]
    ).astype(jnp.int32)
    earlier = jnp.sum((jnp.cumsum(onehot, axis=0) - onehot) * onehot, axis=1)
    target = expert_of * capacity + earlier
    match = (target[:, None] == jnp.arange(slot_count, dtype=jnp.int32)[None, :]) & route_alive[
        :, None
    ]
    placed = match.reshape(rows_here, top_count, slot_count)
    gather_matrix = jnp.any(placed, axis=1).astype(jnp.bfloat16)
    send_rows = lax.dot_general(
        gather_matrix, normed_in, (((0,), (0,)), ((), ())), preferred_element_type=jnp.float32
    ).astype(jnp.bfloat16)
    send_flags = jnp.sum(gather_matrix.astype(jnp.float32), axis=0).astype(jnp.bfloat16)
    combine_matrix = jnp.sum(
        jnp.where(placed, probs.astype(jnp.float32)[:, :, None], jnp.float32(0.0)), axis=1
    ).astype(jnp.bfloat16)
    arrived_rows, arrived_flags = (
        lax.all_to_all(
            send_rows.reshape(expert_count, capacity, model_width),
            "expert",
            split_axis=0,
            concat_axis=0,
            tiled=True,
        ),
        lax.all_to_all(
            send_flags.reshape(expert_count, capacity),
            "expert",
            split_axis=0,
            concat_axis=0,
            tiled=True,
        ),
    )
    arrived = arrived_rows.reshape(slot_count, model_width)
    flags = arrived_flags.reshape(slot_count)
    gate_up_full, down_full = (
        lax.all_gather(w_gate_up, "dp", axis=1, tiled=True),
        lax.all_gather(w_down, "dp", axis=2, tiled=True),
    )
    live_slot = (flags > 0.5).astype(jnp.int32)
    order = jnp.argsort(1 - live_slot, stable=True)
    live_total = jnp.sum(live_slot)
    packed = arrived[order]
    block_len = math.gcd(slot_count, 128)
    block_total = (live_total + block_len - 1) // block_len

    def run_block(index, outputs):
        begin = index * block_len
        rows_in = lax.dynamic_slice_in_dim(packed, begin, block_len, 0)
        block_out = swiglu_rows(rows_in, gate_up_full[0], down_full[0], hidden_units)
        return lax.dynamic_update_slice_in_dim(outputs, block_out, begin, 0)

    packed_out = lax.fori_loop(
        0, block_total, run_block, jnp.zeros((slot_count, model_width), jnp.bfloat16)
    )
    position = (
        jnp.zeros((slot_count,), jnp.int32).at[order].set(jnp.arange(slot_count, dtype=jnp.int32))
    )
    results = packed_out[position]
    returned = lax.all_to_all(
        results.reshape(expert_count, capacity, model_width),
        "expert",
        split_axis=0,
        concat_axis=0,
        tiled=True,
    )
    returned = returned.reshape(slot_count, model_width)
    mixture = jnp.dot(combine_matrix, returned, preferred_element_type=jnp.float32)
    stream_out = (stream_float + mixture).astype(jnp.bfloat16)
    normed_out = rms_scale(stream_out.astype(jnp.float32), gain_final).astype(jnp.bfloat16)
    return (stream_out[None], normed_out[None])


VMEM_BYTES = 56 * 1024 * 1024


def whole_vmem():
    return pl.BlockSpec(memory_space=pltpu.VMEM)


def whole_smem():
    return pl.BlockSpec(memory_space=pltpu.SMEM)


def proj_kernel(place, a0, a1, a2, a3, w0, w1, w2, w3, r0, r1, r2, r3, base_ref, send_ref, rows, part):
    outer, inner, dp = place[0], place[1], place[2]
    full, width = a0.shape
    half = full // 2
    block = w0.shape[1]
    for s, a in enumerate((a0, a1, a2, a3)):
        spot = lax.rem(outer + 4 - s, 4)
        rows[pl.ds(pl.multiple_of(spot * full, full), full), :] = a[...]
    for j, w in enumerate((w0, w1, w2, w3)):
        spot = pl.multiple_of((inner ^ j) * block, block)
        part[:, pl.ds(spot, block)] = jnp.dot(
            rows[...], w[...], preferred_element_type=jnp.float32
        ).astype(jnp.bfloat16)
    for s, r in enumerate((r0, r1, r2, r3)):
        spot = lax.rem(outer + 4 - s, 4)
        mine = pl.multiple_of(spot * full + dp * half, half)
        other = pl.multiple_of(spot * full + (1 - dp) * half, half)
        out = pl.ds(pl.multiple_of(spot * half, half), half)
        base_ref[out, :] = r[...].astype(jnp.float32) + part[pl.ds(mine, half), :].astype(jnp.float32)
        send_ref[out, :] = part[pl.ds(other, half), :]


def gate_kernel(place, blocks, blocks_x, blocks_c, gain, ga, ua, gb, ub, inner_ref, own_ref, normed):
    outer, dp = place[0], place[2]
    step = pl.program_id(0)
    count, width = blocks.shape[1], blocks.shape[2]
    half = normed.shape[1] // 2
    small = own_ref.shape[0]

    @pl.when(step == 0)
    def _():
        for j in range(4):
            square = jnp.zeros((count, 1), jnp.float32)
            for s in range(4):
                block = (blocks, blocks_c.at[0], blocks_x, blocks_c.at[1])[j][s]
                spot = lax.rem(outer + 4 - s, 4)
                cols = pl.ds(pl.multiple_of(spot * width, width), width)
                normed[j * count : (j + 1) * count, cols] = block
                value = block.astype(jnp.float32)
                square = square + jnp.sum(value * value, axis=1, keepdims=True)
            if j == 0:
                own_ref[...] = normed[pl.ds(pl.multiple_of(outer * small, small), small), :]
            scale = lax.rsqrt(square / (4 * width) + 1e-06)
            for s in range(4):
                cols = slice(s * width, (s + 1) * width)
                value = normed[j * count : (j + 1) * count, cols].astype(jnp.float32)
                normed[j * count : (j + 1) * count, cols] = (value * scale * gain[:, cols]).astype(jnp.bfloat16)

    mine = normed[:, pl.ds(pl.multiple_of(dp * half, half), half)]
    other = normed[:, pl.ds(pl.multiple_of((1 - dp) * half, half), half)]
    dot = lambda a, b: jnp.dot(a, b, preferred_element_type=jnp.float32)
    gate = dot(mine, ga[...]) + dot(other, gb[...])
    up = dot(mine, ua[...]) + dot(other, ub[...])
    inner_ref[...] = (gate / (1.0 + jnp.exp(-gate)) * up).astype(jnp.bfloat16)


def down_kernel(inner, weight, wd, out_ref):
    value = jnp.dot(inner[...], wd[...], preferred_element_type=jnp.float32).astype(jnp.bfloat16)
    out_ref[...] = (value.astype(jnp.float32) * weight[...]).astype(jnp.bfloat16)


def body_paired(
    attn,
    resid,
    w_out,
    gain_post,
    route_ids,
    route_logits,
    live_count,
    w_gate_up,
    w_down,
    gain_final,
):
    rows_here = resid.shape[1]
    model_width = resid.shape[2]
    expert_count = lax.axis_size("expert")
    hidden = w_down.shape[1]
    half_width = w_down.shape[2]
    quarter = model_width // 4
    dp = lax.axis_index("dp")
    expert = lax.axis_index("expert")
    outer, inner_at = expert // 4, expert % 4
    place = jnp.stack([outer, inner_at, dp]).astype(jnp.int32)
    bf16, f32 = jnp.bfloat16, jnp.float32
    vmem, smem = whole_vmem(), whole_smem()
    params = pltpu.CompilerParams(vmem_limit_bytes=VMEM_BYTES)

    def swap_dp(x):
        return lax.ppermute(x, "dp", [(0, 1), (1, 0)])

    def shift_outer(x, s):
        return lax.ppermute(
            x, "expert", [(i, (i + 4 * s) % expert_count) for i in range(expert_count)]
        )

    def swap_inner(x, j):
        return lax.ppermute(x, "expert", [(i, i ^ j) for i in range(expert_count)])

    a = [attn[0]] + [shift_outer(attn[0], s) for s in (1, 2, 3)]
    w_x = swap_inner(w_out, 2)
    w_c = swap_inner(w_out, 1)
    w_cx = swap_inner(w_x, 1)

    def resid_piece(s):
        return lax.dynamic_slice_in_dim(resid[0], ((outer + s) % 4) * quarter, quarter, 1)

    r = [resid_piece(0)] + [shift_outer(resid_piece(s), s) for s in (1, 2, 3)]
    gate_up_other = swap_dp(w_gate_up)
    down_other = swap_dp(w_down)

    probs = jax.nn.softmax(route_logits[0], axis=-1).astype(bf16)
    alive = jnp.arange(rows_here, dtype=jnp.int32) < live_count[0, 0]
    chosen = (
        route_ids[0][:, :, None] == jnp.arange(expert_count, dtype=jnp.int32)[None, None, :]
    ) & alive[:, None, None]
    share = jnp.sum(jnp.where(chosen, probs.astype(f32)[:, :, None], 0.0), axis=1).astype(bf16)
    shares = lax.all_gather(share, "expert", axis=0, tiled=False)
    shares = shares.reshape(4, 4, rows_here, expert_count)
    seat = jnp.arange(4, dtype=jnp.int32)
    seated = seat[None, :] == (inner_at ^ seat[:, None])
    pick = seated[:, None, :, None, None] & (
        jnp.arange(expert_count, dtype=jnp.int32) == expert
    )[None, None, None, None, :]
    weight = jnp.sum(jnp.where(pick, shares.astype(f32)[None], 0.0), axis=(2, 4))
    weight = weight.reshape(16 * rows_here, 1)

    base, send = pl.pallas_call(
        proj_kernel,
        out_shape=(
            jax.ShapeDtypeStruct((4 * rows_here, quarter), f32),
            jax.ShapeDtypeStruct((4 * rows_here, quarter), bf16),
        ),
        in_specs=[smem] + [vmem] * 12,
        out_specs=(vmem, vmem),
        scratch_shapes=[
            pltpu.VMEM((8 * rows_here, attn.shape[2]), bf16),
            pltpu.VMEM((8 * rows_here, quarter), bf16),
        ],
        compiler_params=params,
        name="projection",
    )(place, *a, w_out, w_c, w_x, w_cx, *r)
    stream_block = (base + swap_dp(send).astype(f32)).astype(bf16)

    blocks = jnp.stack([stream_block] + [shift_outer(stream_block, s) for s in (1, 2, 3)])
    blocks_x = swap_inner(blocks, 2)
    blocks_c = swap_inner(jnp.stack([blocks, blocks_x]), 1)

    unit = 256
    hidden_steps = hidden // unit
    row_total = 16 * rows_here
    fixed = lambda *shape: pl.BlockSpec(shape, lambda i: (0,) * len(shape))
    gate_spec = pl.BlockSpec((half_width, unit), lambda i: (0, i))
    up_spec = pl.BlockSpec((half_width, unit), lambda i: (0, i + hidden_steps))
    inner, stream_own = pl.pallas_call(
        gate_kernel,
        grid=(hidden_steps,),
        out_shape=(
            jax.ShapeDtypeStruct((row_total, hidden), bf16),
            jax.ShapeDtypeStruct((rows_here, model_width), bf16),
        ),
        in_specs=[
            smem,
            fixed(*blocks.shape),
            fixed(*blocks_x.shape),
            fixed(*blocks_c.shape),
            fixed(1, model_width),
            gate_spec,
            up_spec,
            gate_spec,
            up_spec,
        ],
        out_specs=(
            pl.BlockSpec((row_total, unit), lambda i: (0, i)),
            fixed(rows_here, model_width),
        ),
        scratch_shapes=[pltpu.VMEM((row_total, model_width), bf16)],
        compiler_params=params,
        name="gate_up",
    )(
        place,
        blocks,
        blocks_x,
        blocks_c,
        gain_post[None],
        w_gate_up[0],
        w_gate_up[0],
        gate_up_other[0],
        gate_up_other[0],
    )

    def down_half(wd):
        return pl.pallas_call(
            down_kernel,
            grid=(half_width // 256,),
            out_shape=jax.ShapeDtypeStruct((row_total, half_width), bf16),
            in_specs=[
                fixed(row_total, hidden),
                fixed(row_total, 1),
                pl.BlockSpec((hidden, 256), lambda i: (0, i)),
            ],
            out_specs=pl.BlockSpec((row_total, 256), lambda i: (0, i)),
            compiler_params=params,
            name="down",
        )(inner, weight, wd)

    mine, other = down_half(w_down[0]), down_half(down_other[0])
    swapped = dp > 0
    partial = jnp.concatenate(
        [jnp.where(swapped, other, mine), jnp.where(swapped, mine, other)], axis=1
    ).reshape(4, 4 * rows_here, model_width)

    def add(x, y):
        return (x.astype(f32) + y.astype(f32)).astype(bf16)

    arrived = swap_inner(jnp.stack([partial[1], partial[3]]), 1)
    far = add(partial[2], arrived[1])
    near = add(partial[0], arrived[0])
    near = add(near, swap_inner(far, 2)).reshape(4, rows_here, model_width)

    def outer_piece(s):
        return lax.dynamic_index_in_dim(near, (outer + s) % 4, 0, keepdims=False)

    mixture = outer_piece(0).astype(f32)
    for s in (1, 2, 3):
        mixture = mixture + shift_outer(outer_piece(s), s).astype(f32)
    stream_out = (stream_own.astype(f32) + mixture).astype(bf16)
    normed_out = rms_scale(stream_out.astype(f32), gain_final).astype(bf16)
    return (stream_out[None], normed_out[None])


def solution(mesh):
    placed = (
        P("expert", None, "dp"),
        P("expert", "dp", None),
        P("dp", "expert"),
        P(),
        P("expert", "dp", None),
        P("expert", "dp", None),
        P("expert", "dp"),
        P("expert", "dp", None),
        P("expert", None, "dp"),
        P(),
    )
    paired = mesh.shape["dp"] == 2 and mesh.shape["expert"] == 16
    return jax.shard_map(
        body_paired if paired else body_general,
        mesh=mesh,
        in_specs=placed,
        out_specs=(P("expert", "dp", None), P("expert", "dp", None)),
        check_vma=False,
    )
```

```python
import math

import jax
import jax.numpy as jnp
from jax import lax
from jax.experimental import pallas as pl
from jax.experimental.pallas import tpu as pltpu
from jax.sharding import PartitionSpec as P


def rms_scale(values, gain):
    return values * lax.rsqrt(jnp.mean(values * values, axis=-1, keepdims=True) + 1e-06) * gain


def swiglu_rows(rows_in, gate_up, down, hidden_units):
    both = jnp.dot(rows_in, gate_up, preferred_element_type=jnp.float32)
    inner = (jax.nn.silu(both[:, :hidden_units]) * both[:, hidden_units:]).astype(jnp.bfloat16)
    return jnp.dot(inner, down, preferred_element_type=jnp.float32).astype(jnp.bfloat16)


def body_general(
    attn,
    resid,
    w_out,
    gain_post,
    route_ids,
    route_logits,
    live_count,
    w_gate_up,
    w_down,
    gain_final,
):
    rows_here = resid.shape[1]
    model_width = resid.shape[2]
    top_count = route_ids.shape[2]
    dp_count = lax.axis_size("dp")
    expert_count = lax.axis_size("expert")
    hidden_units = w_down.shape[1]
    capacity = dp_count * max(1, 2 * rows_here * top_count // (expert_count * dp_count))
    slot_count = expert_count * capacity
    flat_attn = attn[0]
    partial_out = jnp.dot(
        flat_attn,
        lax.all_gather(w_out, "expert", axis=1, tiled=True),
        preferred_element_type=jnp.float32,
    )
    projected = lax.psum_scatter(
        partial_out.astype(jnp.bfloat16), "dp", scatter_dimension=0, tiled=True
    ).astype(jnp.float32)
    stream_in = (resid[0].astype(jnp.float32) + projected).astype(jnp.bfloat16)
    stream_float = stream_in.astype(jnp.float32)
    normed_in = rms_scale(stream_float, gain_post).astype(jnp.bfloat16)
    probs = jax.nn.softmax(route_logits[0], axis=-1).astype(jnp.bfloat16)
    alive = jnp.arange(rows_here, dtype=jnp.int32) < live_count[0, 0]
    expert_of = route_ids[0].reshape(-1)
    route_alive = jnp.repeat(alive, top_count)
    onehot = (
        (expert_of[:, None] == jnp.arange(expert_count, dtype=jnp.int32)[None, :])
        & route_alive[:, None]
    ).astype(jnp.int32)
    earlier = jnp.sum((jnp.cumsum(onehot, axis=0) - onehot) * onehot, axis=1)
    target = expert_of * capacity + earlier
    match = (target[:, None] == jnp.arange(slot_count, dtype=jnp.int32)[None, :]) & route_alive[
        :, None
    ]
    placed = match.reshape(rows_here, top_count, slot_count)
    gather_matrix = jnp.any(placed, axis=1).astype(jnp.bfloat16)
    send_rows = lax.dot_general(
        gather_matrix, normed_in, (((0,), (0,)), ((), ())), preferred_element_type=jnp.float32
    ).astype(jnp.bfloat16)
    send_flags = jnp.sum(gather_matrix.astype(jnp.float32), axis=0).astype(jnp.bfloat16)
    combine_matrix = jnp.sum(
        jnp.where(placed, probs.astype(jnp.float32)[:, :, None], jnp.float32(0.0)), axis=1
    ).astype(jnp.bfloat16)
    arrived_rows, arrived_flags = (
        lax.all_to_all(
            send_rows.reshape(expert_count, capacity, model_width),
            "expert",
            split_axis=0,
            concat_axis=0,
            tiled=True,
        ),
        lax.all_to_all(
            send_flags.reshape(expert_count, capacity),
            "expert",
            split_axis=0,
            concat_axis=0,
            tiled=True,
        ),
    )
    arrived = arrived_rows.reshape(slot_count, model_width)
    flags = arrived_flags.reshape(slot_count)
    gate_up_full, down_full = (
        lax.all_gather(w_gate_up, "dp", axis=1, tiled=True),
        lax.all_gather(w_down, "dp", axis=2, tiled=True),
    )
    live_slot = (flags > 0.5).astype(jnp.int32)
    order = jnp.argsort(1 - live_slot, stable=True)
    live_total = jnp.sum(live_slot)
    packed = arrived[order]
    block_len = math.gcd(slot_count, 128)
    block_total = (live_total + block_len - 1) // block_len

    def run_block(index, outputs):
        begin = index * block_len
        rows_in = lax.dynamic_slice_in_dim(packed, begin, block_len, 0)
        block_out = swiglu_rows(rows_in, gate_up_full[0], down_full[0], hidden_units)
        return lax.dynamic_update_slice_in_dim(outputs, block_out, begin, 0)

    packed_out = lax.fori_loop(
        0, block_total, run_block, jnp.zeros((slot_count, model_width), jnp.bfloat16)
    )
    position = (
        jnp.zeros((slot_count,), jnp.int32).at[order].set(jnp.arange(slot_count, dtype=jnp.int32))
    )
    results = packed_out[position]
    returned = lax.all_to_all(
        results.reshape(expert_count, capacity, model_width),
        "expert",
        split_axis=0,
        concat_axis=0,
        tiled=True,
    )
    returned = returned.reshape(slot_count, model_width)
    mixture = jnp.dot(combine_matrix, returned, preferred_element_type=jnp.float32)
    stream_out = (stream_float + mixture).astype(jnp.bfloat16)
    normed_out = rms_scale(stream_out.astype(jnp.float32), gain_final).astype(jnp.bfloat16)
    return (stream_out[None], normed_out[None])


VMEM_BYTES = 56 * 1024 * 1024
BF16, F32 = jnp.bfloat16, jnp.float32


def whole_vmem():
    return pl.BlockSpec(memory_space=pltpu.VMEM)


def whole_smem():
    return pl.BlockSpec(memory_space=pltpu.SMEM)


def fixed(*shape):
    return pl.BlockSpec(shape, lambda i: (0,) * len(shape))


def dot(a, b):
    return jnp.dot(a, b, preferred_element_type=F32)


def kernel_params():
    return pltpu.CompilerParams(vmem_limit_bytes=VMEM_BYTES)


def proj_kernel(place, a0, a1, a2, a3, w0, w1, w2, w3, r0, r1, r2, r3, base_ref, send_ref, rows, part):
    outer, inner, dp = place[0], place[1], place[2]
    full = a0.shape[0]
    half = full // 2
    block = w0.shape[1]
    for s, a in enumerate((a0, a1, a2, a3)):
        spot = lax.rem(outer + 4 - s, 4)
        rows[pl.ds(pl.multiple_of(spot * full, full), full), :] = a[...]
    for j, w in enumerate((w0, w1, w2, w3)):
        spot = pl.multiple_of((inner ^ j) * block, block)
        part[:, pl.ds(spot, block)] = dot(rows[...], w[...]).astype(BF16)
    for s, r in enumerate((r0, r1, r2, r3)):
        spot = lax.rem(outer + 4 - s, 4)
        mine = pl.multiple_of(spot * full + dp * half, half)
        other = pl.multiple_of(spot * full + (1 - dp) * half, half)
        out = pl.ds(pl.multiple_of(spot * half, half), half)
        base_ref[out, :] = r[...].astype(F32) + part[pl.ds(mine, half), :].astype(F32)
        send_ref[out, :] = part[pl.ds(other, half), :]


def first_gate_kernel(
    place, blocks, blocks_x, blocks_c, blocks_cx, gain, ga, ua, gb, ub,
    gate_ref, up_ref, last_ref, share_ref, own_ref, normed,
):
    outer, inner, dp = place[0], place[1], place[2]
    step = pl.program_id(0)
    width = blocks.shape[2]
    count = share_ref.shape[0] // 4
    experts = blocks.shape[1] - count
    half = normed.shape[1] // 2
    small = own_ref.shape[0]
    depth = gb.shape[0]
    rest = half - depth

    @pl.when(step == 0)
    def _():
        expert = outer * 4 + inner
        picked = lax.broadcasted_iota(jnp.int32, (experts, count), 0) == expert
        diagonal = lax.broadcasted_iota(jnp.int32, (count, count), 0) == lax.broadcasted_iota(
            jnp.int32, (count, count), 1
        )
        for j, group in enumerate((blocks, blocks_c, blocks_x, blocks_cx)):
            rows = slice(j * count, (j + 1) * count)
            square = jnp.zeros((count, 1), F32)
            share = jnp.zeros((experts, count), F32)
            for s in range(4):
                spot = lax.rem(outer + 4 - s, 4)
                value = group[s, 0:count, :]
                normed[rows, pl.ds(pl.multiple_of(spot * width, width), width)] = value
                value = value.astype(F32)
                square = square + jnp.sum(value * value, axis=1, keepdims=True)
                share = share + group[s, count : count + experts, 0:count].astype(F32)
            line = jnp.sum(jnp.where(picked, share, 0.0), axis=0, keepdims=True)
            column = jnp.sum(jnp.where(diagonal, line, 0.0), axis=1, keepdims=True)
            share_ref[rows, :] = jnp.broadcast_to(column, (count, share_ref.shape[1]))
            if j == 0:
                own_ref[...] = normed[pl.ds(pl.multiple_of(outer * small, small), small), :]
            scale = lax.rsqrt(square / (4 * width) + 1e-06)
            for s in range(4):
                cols = slice(s * width, (s + 1) * width)
                value = normed[rows, cols].astype(F32)
                normed[rows, cols] = (value * scale * gain[:, cols]).astype(BF16)
        last_ref[...] = normed[:, pl.ds(pl.multiple_of((1 - dp) * half + depth, 128), rest)]

    mine = normed[:, pl.ds(pl.multiple_of(dp * half, half), half)]
    early = normed[:, pl.ds(pl.multiple_of((1 - dp) * half, half), depth)]
    gate_ref[...] = dot(mine, ga[...]) + dot(early, gb[...])
    up_ref[...] = dot(mine, ua[...]) + dot(early, ub[...])


def last_gate_kernel(gate, up, rows, share, gw, uw, inner_ref):
    g = gate[...] + dot(rows[...], gw[...])
    u = up[...] + dot(rows[...], uw[...])
    inner_ref[...] = (g / (1.0 + jnp.exp(-g)) * u * share[:, 0:1]).astype(BF16)


def down_kernel(inner, wd, keep_ref, send_ref):
    count = inner.shape[0] // 4
    value = dot(inner[...], wd[...]).astype(BF16)
    for i in range(2):
        keep_ref[i * count : (i + 1) * count, :] = value[2 * i * count : (2 * i + 1) * count]
        send_ref[i * count : (i + 1) * count, :] = value[(2 * i + 1) * count : (2 * i + 2) * count]


def tail_kernel(place, own, m0, m1, m2, m3, o0, o1, o2, o3, gain, stream_ref, normed_ref):
    dp = place[2]
    half = m0.shape[1]
    for at, pieces in ((dp, (m0, m1, m2, m3)), (1 - dp, (o0, o1, o2, o3))):
        cols = pl.ds(pl.multiple_of(at * half, half), half)
        total = own[:, cols].astype(F32)
        mixture = pieces[0][...].astype(F32)
        for piece in pieces[1:]:
            mixture = mixture + piece[...].astype(F32)
        stream_ref[:, cols] = (total + mixture).astype(BF16)
    normed_ref[...] = rms_scale(stream_ref[...].astype(F32), gain[...]).astype(BF16)


def body_paired(
    attn,
    resid,
    w_out,
    gain_post,
    route_ids,
    route_logits,
    live_count,
    w_gate_up,
    w_down,
    gain_final,
):
    rows_here = resid.shape[1]
    model_width = resid.shape[2]
    expert_count = lax.axis_size("expert")
    hidden = w_down.shape[1]
    half_width = w_down.shape[2]
    quarter = model_width // 4
    dp = lax.axis_index("dp")
    expert = lax.axis_index("expert")
    outer, inner_at = expert // 4, expert % 4
    place = jnp.stack([outer, inner_at, dp]).astype(jnp.int32)
    vmem, smem = whole_vmem(), whole_smem()

    def swap_dp(x):
        return lax.ppermute(x, "dp", [(0, 1), (1, 0)])

    def shift_outer(x, s):
        return lax.ppermute(
            x, "expert", [(i, (i + 4 * s) % expert_count) for i in range(expert_count)]
        )

    def cross_outer(x, s):
        return lax.ppermute(
            x,
            ("dp", "expert"),
            [
                (d * expert_count + i, (1 - d) * expert_count + (i + 4 * s) % expert_count)
                for d in range(2)
                for i in range(expert_count)
            ],
        )

    def swap_inner(x, j):
        return lax.ppermute(x, "expert", [(i, i ^ j) for i in range(expert_count)])

    def after(x, *results):
        return lax.optimization_barrier((x, *results))[0]

    depth = half_width * 3 // 8
    a = [attn[0]] + [shift_outer(attn[0], s) for s in (1, 2, 3)]
    w_x = swap_inner(w_out, 2)
    gate_up_early = swap_dp(w_gate_up[0, :depth])
    w_c = swap_inner(after(w_out, w_x), 1)
    w_cx = swap_inner(w_x, 1)

    def resid_piece(s):
        return lax.dynamic_slice_in_dim(resid[0], ((outer + s) % 4) * quarter, quarter, 1)

    r = [resid_piece(0)] + [shift_outer(after(resid_piece(s), w_cx), s) for s in (1, 2, 3)]

    probs = jax.nn.softmax(route_logits[0], axis=-1).astype(BF16)
    alive = jnp.arange(rows_here, dtype=jnp.int32) < live_count[0, 0]
    chosen = (
        route_ids[0][None] == jnp.arange(expert_count, dtype=jnp.int32)[:, None, None]
    ) & alive[None, :, None]
    share = jnp.sum(jnp.where(chosen, probs.astype(F32)[None], 0.0), axis=2)
    spots = jnp.arange(quarter // rows_here, dtype=jnp.int32) == outer
    share = jnp.where(spots[None, :, None], share[:, None, :], 0.0)
    share = share.reshape(expert_count, quarter).astype(BF16)

    base, send = pl.pallas_call(
        proj_kernel,
        out_shape=(
            jax.ShapeDtypeStruct((4 * rows_here, quarter), F32),
            jax.ShapeDtypeStruct((4 * rows_here, quarter), BF16),
        ),
        in_specs=[smem] + [vmem] * 12,
        out_specs=(vmem, vmem),
        scratch_shapes=[
            pltpu.VMEM((8 * rows_here, attn.shape[2]), BF16),
            pltpu.VMEM((8 * rows_here, quarter), BF16),
        ],
        compiler_params=kernel_params(),
        name="projection",
    )(place, *a, w_out, w_c, w_x, w_cx, *r)
    arrived = swap_dp(send)
    gate_up_late = swap_dp(after(w_gate_up[0, depth:], arrived))
    block = (base + arrived.astype(F32)).astype(BF16)
    block = jnp.concatenate([block, share], axis=0)

    blocks = jnp.stack([block] + [shift_outer(block, s) for s in (1, 2, 3)])
    blocks_x = swap_inner(blocks, 2)
    blocks_c = swap_inner(blocks, 1)
    blocks_cx = swap_inner(blocks_x, 1)

    unit = 256
    steps = hidden // unit
    row_total = 16 * rows_here
    block_spec = fixed(*blocks.shape)
    gate_cols = lambda k: pl.BlockSpec((k, unit), lambda i: (0, i))
    up_cols = lambda k: pl.BlockSpec((k, unit), lambda i: (0, i + steps))
    out_cols = pl.BlockSpec((row_total, unit), lambda i: (0, i))
    gate, up, last_rows, share_rows, stream_own = pl.pallas_call(
        first_gate_kernel,
        grid=(steps,),
        out_shape=(
            jax.ShapeDtypeStruct((row_total, hidden), F32),
            jax.ShapeDtypeStruct((row_total, hidden), F32),
            jax.ShapeDtypeStruct((row_total, half_width - depth), BF16),
            jax.ShapeDtypeStruct((row_total, 128), F32),
            jax.ShapeDtypeStruct((rows_here, model_width), BF16),
        ),
        in_specs=[smem]
        + [block_spec] * 4
        + [
            fixed(1, model_width),
            gate_cols(half_width),
            up_cols(half_width),
            gate_cols(depth),
            up_cols(depth),
        ],
        out_specs=(
            out_cols,
            out_cols,
            fixed(row_total, half_width - depth),
            fixed(row_total, 128),
            fixed(rows_here, model_width),
        ),
        scratch_shapes=[pltpu.VMEM((row_total, model_width), BF16)],
        compiler_params=kernel_params(),
        name="first_gate_up",
    )(
        place,
        blocks,
        blocks_x,
        blocks_c,
        blocks_cx,
        gain_post[None],
        w_gate_up[0],
        w_gate_up[0],
        gate_up_early,
        gate_up_early,
    )
    inner = pl.pallas_call(
        last_gate_kernel,
        grid=(steps,),
        out_shape=jax.ShapeDtypeStruct((row_total, hidden), BF16),
        in_specs=[
            out_cols,
            out_cols,
            fixed(row_total, half_width - depth),
            fixed(row_total, 128),
            gate_cols(half_width - depth),
            up_cols(half_width - depth),
        ],
        out_specs=out_cols,
        compiler_params=kernel_params(),
        name="last_gate_up",
    )(gate, up, last_rows, share_rows, gate_up_late, gate_up_late)
    inner_other = swap_dp(inner)

    def down(rows):
        out = jax.ShapeDtypeStruct((row_total // 2, half_width), BF16)
        spec = pl.BlockSpec((row_total // 2, 256), lambda i: (0, i))
        return pl.pallas_call(
            down_kernel,
            grid=(half_width // 256,),
            out_shape=(out, out),
            in_specs=[
                fixed(row_total, hidden),
                pl.BlockSpec((hidden, 256), lambda i: (0, i)),
            ],
            out_specs=(spec, spec),
            compiler_params=kernel_params(),
            name="down",
        )(rows, w_down[0])

    def add(x, y):
        return (x.astype(F32) + y.astype(F32)).astype(BF16)

    def sum_inner(rows):
        keep, send = down(rows)
        near = add(keep, swap_inner(send, 1))
        count = near.shape[0] // 2
        near = add(near[:count], swap_inner(near[count:], 2))
        return near.reshape(4, rows_here, half_width)

    def outer_piece(near, s):
        return lax.dynamic_index_in_dim(near, (outer + s) % 4, 0, keepdims=False)

    near = sum_inner(inner)
    mine = [outer_piece(near, 0)] + [shift_outer(outer_piece(near, s), s) for s in (1, 2, 3)]
    near = sum_inner(inner_other)
    others = [cross_outer(outer_piece(near, s), s) for s in range(4)]

    out = jax.ShapeDtypeStruct((rows_here, model_width), BF16)
    stream_out, normed_out = pl.pallas_call(
        tail_kernel,
        out_shape=(out, out),
        in_specs=[smem] + [vmem] * 10,
        out_specs=(vmem, vmem),
        compiler_params=kernel_params(),
        name="closing",
    )(place, stream_own, *mine, *others, gain_final[None])
    return (stream_out[None], normed_out[None])


def solution(mesh):
    placed = (
        P("expert", None, "dp"),
        P("expert", "dp", None),
        P("dp", "expert"),
        P(),
        P("expert", "dp", None),
        P("expert", "dp", None),
        P("expert", "dp"),
        P("expert", "dp", None),
        P("expert", None, "dp"),
        P(),
    )
    paired = mesh.shape["dp"] == 2 and mesh.shape["expert"] == 16
    return jax.shard_map(
        body_paired if paired else body_general,
        mesh=mesh,
        in_specs=placed,
        out_specs=(P("expert", "dp", None), P("expert", "dp", None)),
        check_vma=False,
    )
```

```python
import math

import jax
import jax.numpy as jnp
from jax import lax
from jax.experimental import pallas as pl
from jax.experimental.pallas import tpu as pltpu
from jax.sharding import PartitionSpec as P


def rms_scale(values, gain):
    return values * lax.rsqrt(jnp.mean(values * values, axis=-1, keepdims=True) + 1e-06) * gain


def swiglu_rows(rows_in, gate_up, down, hidden_units):
    both = jnp.dot(rows_in, gate_up, preferred_element_type=jnp.float32)
    inner = (jax.nn.silu(both[:, :hidden_units]) * both[:, hidden_units:]).astype(jnp.bfloat16)
    return jnp.dot(inner, down, preferred_element_type=jnp.float32).astype(jnp.bfloat16)


def body_general(
    attn,
    resid,
    w_out,
    gain_post,
    route_ids,
    route_logits,
    live_count,
    w_gate_up,
    w_down,
    gain_final,
):
    rows_here = resid.shape[1]
    model_width = resid.shape[2]
    top_count = route_ids.shape[2]
    dp_count = lax.axis_size("dp")
    expert_count = lax.axis_size("expert")
    hidden_units = w_down.shape[1]
    capacity = dp_count * max(1, 2 * rows_here * top_count // (expert_count * dp_count))
    slot_count = expert_count * capacity
    flat_attn = attn[0]
    partial_out = jnp.dot(
        flat_attn,
        lax.all_gather(w_out, "expert", axis=1, tiled=True),
        preferred_element_type=jnp.float32,
    )
    projected = lax.psum_scatter(
        partial_out.astype(jnp.bfloat16), "dp", scatter_dimension=0, tiled=True
    ).astype(jnp.float32)
    stream_in = (resid[0].astype(jnp.float32) + projected).astype(jnp.bfloat16)
    stream_float = stream_in.astype(jnp.float32)
    normed_in = rms_scale(stream_float, gain_post).astype(jnp.bfloat16)
    probs = jax.nn.softmax(route_logits[0], axis=-1).astype(jnp.bfloat16)
    alive = jnp.arange(rows_here, dtype=jnp.int32) < live_count[0, 0]
    expert_of = route_ids[0].reshape(-1)
    route_alive = jnp.repeat(alive, top_count)
    onehot = (
        (expert_of[:, None] == jnp.arange(expert_count, dtype=jnp.int32)[None, :])
        & route_alive[:, None]
    ).astype(jnp.int32)
    earlier = jnp.sum((jnp.cumsum(onehot, axis=0) - onehot) * onehot, axis=1)
    target = expert_of * capacity + earlier
    match = (target[:, None] == jnp.arange(slot_count, dtype=jnp.int32)[None, :]) & route_alive[
        :, None
    ]
    placed = match.reshape(rows_here, top_count, slot_count)
    gather_matrix = jnp.any(placed, axis=1).astype(jnp.bfloat16)
    send_rows = lax.dot_general(
        gather_matrix, normed_in, (((0,), (0,)), ((), ())), preferred_element_type=jnp.float32
    ).astype(jnp.bfloat16)
    send_flags = jnp.sum(gather_matrix.astype(jnp.float32), axis=0).astype(jnp.bfloat16)
    combine_matrix = jnp.sum(
        jnp.where(placed, probs.astype(jnp.float32)[:, :, None], jnp.float32(0.0)), axis=1
    ).astype(jnp.bfloat16)
    arrived_rows, arrived_flags = (
        lax.all_to_all(
            send_rows.reshape(expert_count, capacity, model_width),
            "expert",
            split_axis=0,
            concat_axis=0,
            tiled=True,
        ),
        lax.all_to_all(
            send_flags.reshape(expert_count, capacity),
            "expert",
            split_axis=0,
            concat_axis=0,
            tiled=True,
        ),
    )
    arrived = arrived_rows.reshape(slot_count, model_width)
    flags = arrived_flags.reshape(slot_count)
    gate_up_full, down_full = (
        lax.all_gather(w_gate_up, "dp", axis=1, tiled=True),
        lax.all_gather(w_down, "dp", axis=2, tiled=True),
    )
    live_slot = (flags > 0.5).astype(jnp.int32)
    order = jnp.argsort(1 - live_slot, stable=True)
    live_total = jnp.sum(live_slot)
    packed = arrived[order]
    block_len = math.gcd(slot_count, 128)
    block_total = (live_total + block_len - 1) // block_len

    def run_block(index, outputs):
        begin = index * block_len
        rows_in = lax.dynamic_slice_in_dim(packed, begin, block_len, 0)
        block_out = swiglu_rows(rows_in, gate_up_full[0], down_full[0], hidden_units)
        return lax.dynamic_update_slice_in_dim(outputs, block_out, begin, 0)

    packed_out = lax.fori_loop(
        0, block_total, run_block, jnp.zeros((slot_count, model_width), jnp.bfloat16)
    )
    position = (
        jnp.zeros((slot_count,), jnp.int32).at[order].set(jnp.arange(slot_count, dtype=jnp.int32))
    )
    results = packed_out[position]
    returned = lax.all_to_all(
        results.reshape(expert_count, capacity, model_width),
        "expert",
        split_axis=0,
        concat_axis=0,
        tiled=True,
    )
    returned = returned.reshape(slot_count, model_width)
    mixture = jnp.dot(combine_matrix, returned, preferred_element_type=jnp.float32)
    stream_out = (stream_float + mixture).astype(jnp.bfloat16)
    normed_out = rms_scale(stream_out.astype(jnp.float32), gain_final).astype(jnp.bfloat16)
    return (stream_out[None], normed_out[None])


MIB = 1024 * 1024
BF16, F32 = jnp.bfloat16, jnp.float32


def whole_vmem():
    return pl.BlockSpec(memory_space=pltpu.VMEM)


def whole_smem():
    return pl.BlockSpec(memory_space=pltpu.SMEM)


def fixed(*shape):
    return pl.BlockSpec(shape, lambda i: (0,) * len(shape))


def dot(a, b):
    return jnp.dot(a, b, preferred_element_type=F32)


def kernel_params(mib):
    return pltpu.CompilerParams(vmem_limit_bytes=mib * MIB)


def proj_kernel(place, a0, a1, a2, a3, w0, w1, w2, w3, keep_ref, send_ref, rows, part):
    outer, inner, dp = place[0], place[1], place[2]
    full = a0.shape[0]
    half = full // 2
    block = w0.shape[1]
    for s, a in enumerate((a0, a1, a2, a3)):
        spot = lax.rem(outer + 4 - s, 4)
        rows[pl.ds(pl.multiple_of(spot * full, full), full), :] = a[...]
    for j, w in enumerate((w0, w1, w2, w3)):
        spot = pl.multiple_of((inner ^ j) * block, block)
        part[:, pl.ds(spot, block)] = dot(rows[...], w[...]).astype(BF16)
    for spot in range(4):
        mine = pl.multiple_of(spot * full + dp * half, half)
        other = pl.multiple_of(spot * full + (1 - dp) * half, half)
        keep_ref[spot * half : (spot + 1) * half, :] = part[pl.ds(mine, half), :]
        send_ref[spot * half : (spot + 1) * half, :] = part[pl.ds(other, half), :]


def stream_kernel(place, keep, arrived, r0, r1, r2, r3, share, block_ref):
    outer = place[0]
    count = keep.shape[0]
    small = r0.shape[0]
    for s, r in enumerate((r0, r1, r2, r3)):
        rows = pl.ds(pl.multiple_of(lax.rem(outer + 4 - s, 4) * small, small), small)
        product = keep[rows, :].astype(F32) + arrived[rows, :].astype(F32)
        block_ref[rows, :] = (r[...].astype(F32) + product).astype(BF16)
    block_ref[count:, :] = share[...]


def first_gate_kernel(
    place, blocks, blocks_x, blocks_c, blocks_cx, gain, ga, ua, gb, ub,
    gate_ref, up_ref, last_ref, share_ref, own_ref, normed,
):
    outer, inner, dp = place[0], place[1], place[2]
    step = pl.program_id(0)
    width = blocks.shape[2]
    count = share_ref.shape[0] // 4
    experts = blocks.shape[1] - count
    half = normed.shape[1] // 2
    small = own_ref.shape[0]
    depth = gb.shape[0]
    rest = half - depth

    @pl.when(step == 0)
    def _():
        expert = outer * 4 + inner
        picked = lax.broadcasted_iota(jnp.int32, (experts, count), 0) == expert
        diagonal = lax.broadcasted_iota(jnp.int32, (count, count), 0) == lax.broadcasted_iota(
            jnp.int32, (count, count), 1
        )
        for j, group in enumerate((blocks, blocks_c, blocks_x, blocks_cx)):
            rows = slice(j * count, (j + 1) * count)
            square = jnp.zeros((count, 1), F32)
            share = jnp.zeros((experts, count), F32)
            for s in range(4):
                spot = lax.rem(outer + 4 - s, 4)
                value = group[s, 0:count, :]
                normed[rows, pl.ds(pl.multiple_of(spot * width, width), width)] = value
                value = value.astype(F32)
                square = square + jnp.sum(value * value, axis=1, keepdims=True)
                share = share + group[s, count : count + experts, 0:count].astype(F32)
            line = jnp.sum(jnp.where(picked, share, 0.0), axis=0, keepdims=True)
            column = jnp.sum(jnp.where(diagonal, line, 0.0), axis=1, keepdims=True)
            share_ref[rows, :] = jnp.broadcast_to(column, (count, share_ref.shape[1]))
            if j == 0:
                own_ref[...] = normed[pl.ds(pl.multiple_of(outer * small, small), small), :]
            scale = lax.rsqrt(square / (4 * width) + 1e-06)
            for s in range(4):
                cols = slice(s * width, (s + 1) * width)
                value = normed[rows, cols].astype(F32)
                normed[rows, cols] = (value * scale * gain[:, cols]).astype(BF16)
        last_ref[...] = normed[:, pl.ds(pl.multiple_of((1 - dp) * half + depth, 128), rest)]

    mine = normed[:, pl.ds(pl.multiple_of(dp * half, half), half)]
    early = normed[:, pl.ds(pl.multiple_of((1 - dp) * half, half), depth)]
    gate_ref[...] = dot(mine, ga[...]) + dot(early, gb[...])
    up_ref[...] = dot(mine, ua[...]) + dot(early, ub[...])


def last_gate_kernel(gate, up, rows, share, gw, uw, inner_ref):
    g = gate[...] + dot(rows[...], gw[...])
    u = up[...] + dot(rows[...], uw[...])
    inner_ref[...] = (g / (1.0 + jnp.exp(-g)) * u * share[:, 0:1]).astype(BF16)


def down_kernel(inner, wd, keep_ref, send_ref):
    count = inner.shape[0] // 4
    value = dot(inner[...], wd[...]).astype(BF16)
    for i in range(2):
        keep_ref[i * count : (i + 1) * count, :] = value[2 * i * count : (2 * i + 1) * count]
        send_ref[i * count : (i + 1) * count, :] = value[(2 * i + 1) * count : (2 * i + 2) * count]


def tail_kernel(place, own, m0, m1, m2, m3, o0, o1, o2, o3, gain, stream_ref, normed_ref):
    dp = place[2]
    half = m0.shape[1]
    for at, pieces in ((dp, (m0, m1, m2, m3)), (1 - dp, (o0, o1, o2, o3))):
        cols = pl.ds(pl.multiple_of(at * half, half), half)
        total = own[:, cols].astype(F32)
        mixture = pieces[0][...].astype(F32)
        for piece in pieces[1:]:
            mixture = mixture + piece[...].astype(F32)
        stream_ref[:, cols] = (total + mixture).astype(BF16)
    normed_ref[...] = rms_scale(stream_ref[...].astype(F32), gain[...]).astype(BF16)


def body_paired(
    attn,
    resid,
    w_out,
    gain_post,
    route_ids,
    route_logits,
    live_count,
    w_gate_up,
    w_down,
    gain_final,
):
    rows_here = resid.shape[1]
    model_width = resid.shape[2]
    expert_count = lax.axis_size("expert")
    hidden = w_down.shape[1]
    half_width = w_down.shape[2]
    quarter = model_width // 4
    dp = lax.axis_index("dp")
    expert = lax.axis_index("expert")
    outer, inner_at = expert // 4, expert % 4
    place = jnp.stack([outer, inner_at, dp]).astype(jnp.int32)
    vmem, smem = whole_vmem(), whole_smem()

    def swap_dp(x):
        return lax.ppermute(x, "dp", [(0, 1), (1, 0)])

    def shift_outer(x, s):
        return lax.ppermute(
            x, "expert", [(i, (i + 4 * s) % expert_count) for i in range(expert_count)]
        )

    def cross_outer(x, s):
        return lax.ppermute(
            x,
            ("dp", "expert"),
            [
                (d * expert_count + i, (1 - d) * expert_count + (i + 4 * s) % expert_count)
                for d in range(2)
                for i in range(expert_count)
            ],
        )

    def swap_inner(x, j):
        return lax.ppermute(x, "expert", [(i, i ^ j) for i in range(expert_count)])

    def after(x, *results):
        return lax.optimization_barrier((x, *results))[0]

    depth = half_width * 3 // 8
    early_piece = w_gate_up[0, :depth]
    sent = after(attn[0], early_piece)
    a = [attn[0]] + [shift_outer(sent, s) for s in (1, 2, 3)]
    w_x = swap_inner(w_out, 2)
    gate_up_early = swap_dp(early_piece)
    w_c = swap_inner(after(w_out, w_x), 1)
    w_cx = swap_inner(w_x, 1)

    def resid_piece(s):
        return lax.dynamic_slice_in_dim(resid[0], ((outer + s) % 4) * quarter, quarter, 1)

    r = [resid_piece(0)] + [shift_outer(after(resid_piece(s), w_cx), s) for s in (1, 2, 3)]

    probs = jax.nn.softmax(route_logits[0], axis=-1).astype(BF16)
    alive = jnp.arange(rows_here, dtype=jnp.int32) < live_count[0, 0]
    chosen = (
        route_ids[0][None] == jnp.arange(expert_count, dtype=jnp.int32)[:, None, None]
    ) & alive[None, :, None]
    share = jnp.sum(jnp.where(chosen, probs.astype(F32)[None], 0.0), axis=2)
    spots = jnp.arange(quarter // rows_here, dtype=jnp.int32) == outer
    share = jnp.where(spots[None, :, None], share[:, None, :], 0.0)
    share = share.reshape(expert_count, quarter).astype(BF16)

    product = jax.ShapeDtypeStruct((4 * rows_here, quarter), BF16)
    keep, send = pl.pallas_call(
        proj_kernel,
        out_shape=(product, product),
        in_specs=[smem] + [vmem] * 8,
        out_specs=(vmem, vmem),
        scratch_shapes=[
            pltpu.VMEM((8 * rows_here, attn.shape[2]), BF16),
            pltpu.VMEM((8 * rows_here, quarter), BF16),
        ],
        compiler_params=kernel_params(16),
        name="projection",
    )(place, *a, w_out, w_c, w_x, w_cx)
    arrived = swap_dp(after(send, gate_up_early, *r[1:]))
    gate_up_late = swap_dp(after(w_gate_up[0, depth:], arrived))
    block = pl.pallas_call(
        stream_kernel,
        out_shape=jax.ShapeDtypeStruct((4 * rows_here + expert_count, quarter), BF16),
        in_specs=[smem] + [vmem] * 7,
        out_specs=vmem,
        compiler_params=kernel_params(8),
        name="stream",
    )(place, keep, arrived, *r, share)

    blocks = jnp.stack([block] + [shift_outer(block, s) for s in (1, 2, 3)])
    blocks_x = swap_inner(blocks, 2)
    blocks_c = swap_inner(blocks, 1)
    blocks_cx = swap_inner(blocks_x, 1)

    unit = 256
    steps = hidden // unit
    row_total = 16 * rows_here
    block_spec = fixed(*blocks.shape)
    gate_cols = lambda k: pl.BlockSpec((k, unit), lambda i: (0, i))
    up_cols = lambda k: pl.BlockSpec((k, unit), lambda i: (0, i + steps))
    out_cols = pl.BlockSpec((row_total, unit), lambda i: (0, i))
    gate, up, last_rows, share_rows, stream_own = pl.pallas_call(
        first_gate_kernel,
        grid=(steps,),
        out_shape=(
            jax.ShapeDtypeStruct((row_total, hidden), F32),
            jax.ShapeDtypeStruct((row_total, hidden), F32),
            jax.ShapeDtypeStruct((row_total, half_width - depth), BF16),
            jax.ShapeDtypeStruct((row_total, 128), F32),
            jax.ShapeDtypeStruct((rows_here, model_width), BF16),
        ),
        in_specs=[smem]
        + [block_spec] * 4
        + [
            fixed(1, model_width),
            gate_cols(half_width),
            up_cols(half_width),
            gate_cols(depth),
            up_cols(depth),
        ],
        out_specs=(
            out_cols,
            out_cols,
            fixed(row_total, half_width - depth),
            fixed(row_total, 128),
            fixed(rows_here, model_width),
        ),
        scratch_shapes=[pltpu.VMEM((row_total, model_width), BF16)],
        compiler_params=kernel_params(24),
        name="first_gate_up",
    )(
        place,
        blocks,
        blocks_x,
        blocks_c,
        blocks_cx,
        gain_post[None],
        w_gate_up[0],
        w_gate_up[0],
        gate_up_early,
        gate_up_early,
    )
    inner = pl.pallas_call(
        last_gate_kernel,
        grid=(steps,),
        out_shape=jax.ShapeDtypeStruct((row_total, hidden), BF16),
        in_specs=[
            out_cols,
            out_cols,
            fixed(row_total, half_width - depth),
            fixed(row_total, 128),
            gate_cols(half_width - depth),
            up_cols(half_width - depth),
        ],
        out_specs=out_cols,
        compiler_params=kernel_params(16),
        name="last_gate_up",
    )(gate, up, last_rows, share_rows, gate_up_late, gate_up_late)
    inner_other = swap_dp(inner)

    def down(rows):
        out = jax.ShapeDtypeStruct((row_total // 2, half_width), BF16)
        spec = pl.BlockSpec((row_total // 2, 256), lambda i: (0, i))
        return pl.pallas_call(
            down_kernel,
            grid=(half_width // 256,),
            out_shape=(out, out),
            in_specs=[
                fixed(row_total, hidden),
                pl.BlockSpec((hidden, 256), lambda i: (0, i)),
            ],
            out_specs=(spec, spec),
            compiler_params=kernel_params(12),
            name="down",
        )(rows, w_down[0])

    def add(x, y):
        return (x.astype(F32) + y.astype(F32)).astype(BF16)

    def sum_inner(rows, *earlier):
        keep, send = down(rows)
        near = add(keep, swap_inner(send, 1))
        count = near.shape[0] // 2
        far = near[count:] if not earlier else after(near[count:], *earlier)
        near = add(near[:count], swap_inner(far, 2))
        return near.reshape(4, rows_here, half_width)

    def outer_piece(near, s):
        return lax.dynamic_index_in_dim(near, (outer + s) % 4, 0, keepdims=False)

    near = sum_inner(inner)
    mine = [outer_piece(near, 0)] + [shift_outer(outer_piece(near, s), s) for s in (1, 2, 3)]
    near = sum_inner(after(inner_other, near), *mine[1:])
    others = [cross_outer(outer_piece(near, s), s) for s in range(4)]

    out = jax.ShapeDtypeStruct((rows_here, model_width), BF16)
    stream_out, normed_out = pl.pallas_call(
        tail_kernel,
        out_shape=(out, out),
        in_specs=[smem] + [vmem] * 10,
        out_specs=(vmem, vmem),
        compiler_params=kernel_params(8),
        name="closing",
    )(place, stream_own, *mine, *others, gain_final[None])
    return (stream_out[None], normed_out[None])


def solution(mesh):
    placed = (
        P("expert", None, "dp"),
        P("expert", "dp", None),
        P("dp", "expert"),
        P(),
        P("expert", "dp", None),
        P("expert", "dp", None),
        P("expert", "dp"),
        P("expert", "dp", None),
        P("expert", None, "dp"),
        P(),
    )
    paired = mesh.shape["dp"] == 2 and mesh.shape["expert"] == 16
    return jax.shard_map(
        body_paired if paired else body_general,
        mesh=mesh,
        in_specs=placed,
        out_specs=(P("expert", "dp", None), P("expert", "dp", None)),
        check_vma=False,
    )
```

```python
import math

import jax
import jax.numpy as jnp
from jax import lax
from jax.experimental import pallas as pl
from jax.experimental.pallas import tpu as pltpu
from jax.sharding import PartitionSpec as P


def rms_scale(values, gain):
    return values * lax.rsqrt(jnp.mean(values * values, axis=-1, keepdims=True) + 1e-06) * gain


def swiglu_rows(rows_in, gate_up, down, hidden_units):
    both = jnp.dot(rows_in, gate_up, preferred_element_type=jnp.float32)
    inner = (jax.nn.silu(both[:, :hidden_units]) * both[:, hidden_units:]).astype(jnp.bfloat16)
    return jnp.dot(inner, down, preferred_element_type=jnp.float32).astype(jnp.bfloat16)


def body_general(
    attn,
    resid,
    w_out,
    gain_post,
    route_ids,
    route_logits,
    live_count,
    w_gate_up,
    w_down,
    gain_final,
):
    rows_here = resid.shape[1]
    model_width = resid.shape[2]
    top_count = route_ids.shape[2]
    dp_count = lax.axis_size("dp")
    expert_count = lax.axis_size("expert")
    hidden_units = w_down.shape[1]
    capacity = dp_count * max(1, 2 * rows_here * top_count // (expert_count * dp_count))
    slot_count = expert_count * capacity
    flat_attn = attn[0]
    partial_out = jnp.dot(
        flat_attn,
        lax.all_gather(w_out, "expert", axis=1, tiled=True),
        preferred_element_type=jnp.float32,
    )
    projected = lax.psum_scatter(
        partial_out.astype(jnp.bfloat16), "dp", scatter_dimension=0, tiled=True
    ).astype(jnp.float32)
    stream_in = (resid[0].astype(jnp.float32) + projected).astype(jnp.bfloat16)
    stream_float = stream_in.astype(jnp.float32)
    normed_in = rms_scale(stream_float, gain_post).astype(jnp.bfloat16)
    probs = jax.nn.softmax(route_logits[0], axis=-1).astype(jnp.bfloat16)
    alive = jnp.arange(rows_here, dtype=jnp.int32) < live_count[0, 0]
    expert_of = route_ids[0].reshape(-1)
    route_alive = jnp.repeat(alive, top_count)
    onehot = (
        (expert_of[:, None] == jnp.arange(expert_count, dtype=jnp.int32)[None, :])
        & route_alive[:, None]
    ).astype(jnp.int32)
    earlier = jnp.sum((jnp.cumsum(onehot, axis=0) - onehot) * onehot, axis=1)
    target = expert_of * capacity + earlier
    match = (target[:, None] == jnp.arange(slot_count, dtype=jnp.int32)[None, :]) & route_alive[
        :, None
    ]
    placed = match.reshape(rows_here, top_count, slot_count)
    gather_matrix = jnp.any(placed, axis=1).astype(jnp.bfloat16)
    send_rows = lax.dot_general(
        gather_matrix, normed_in, (((0,), (0,)), ((), ())), preferred_element_type=jnp.float32
    ).astype(jnp.bfloat16)
    send_flags = jnp.sum(gather_matrix.astype(jnp.float32), axis=0).astype(jnp.bfloat16)
    combine_matrix = jnp.sum(
        jnp.where(placed, probs.astype(jnp.float32)[:, :, None], jnp.float32(0.0)), axis=1
    ).astype(jnp.bfloat16)
    arrived_rows, arrived_flags = (
        lax.all_to_all(
            send_rows.reshape(expert_count, capacity, model_width),
            "expert",
            split_axis=0,
            concat_axis=0,
            tiled=True,
        ),
        lax.all_to_all(
            send_flags.reshape(expert_count, capacity),
            "expert",
            split_axis=0,
            concat_axis=0,
            tiled=True,
        ),
    )
    arrived = arrived_rows.reshape(slot_count, model_width)
    flags = arrived_flags.reshape(slot_count)
    gate_up_full, down_full = (
        lax.all_gather(w_gate_up, "dp", axis=1, tiled=True),
        lax.all_gather(w_down, "dp", axis=2, tiled=True),
    )
    live_slot = (flags > 0.5).astype(jnp.int32)
    order = jnp.argsort(1 - live_slot, stable=True)
    live_total = jnp.sum(live_slot)
    packed = arrived[order]
    block_len = math.gcd(slot_count, 128)
    block_total = (live_total + block_len - 1) // block_len

    def run_block(index, outputs):
        begin = index * block_len
        rows_in = lax.dynamic_slice_in_dim(packed, begin, block_len, 0)
        block_out = swiglu_rows(rows_in, gate_up_full[0], down_full[0], hidden_units)
        return lax.dynamic_update_slice_in_dim(outputs, block_out, begin, 0)

    packed_out = lax.fori_loop(
        0, block_total, run_block, jnp.zeros((slot_count, model_width), jnp.bfloat16)
    )
    position = (
        jnp.zeros((slot_count,), jnp.int32).at[order].set(jnp.arange(slot_count, dtype=jnp.int32))
    )
    results = packed_out[position]
    returned = lax.all_to_all(
        results.reshape(expert_count, capacity, model_width),
        "expert",
        split_axis=0,
        concat_axis=0,
        tiled=True,
    )
    returned = returned.reshape(slot_count, model_width)
    mixture = jnp.dot(combine_matrix, returned, preferred_element_type=jnp.float32)
    stream_out = (stream_float + mixture).astype(jnp.bfloat16)
    normed_out = rms_scale(stream_out.astype(jnp.float32), gain_final).astype(jnp.bfloat16)
    return (stream_out[None], normed_out[None])


MIB = 1024 * 1024
BF16, F32 = jnp.bfloat16, jnp.float32


def whole_vmem():
    return pl.BlockSpec(memory_space=pltpu.VMEM)


def whole_smem():
    return pl.BlockSpec(memory_space=pltpu.SMEM)


def fixed(*shape):
    return pl.BlockSpec(shape, lambda i: (0,) * len(shape))


def dot(a, b):
    return jnp.dot(a, b, preferred_element_type=F32)


def cost(flops, moved):
    return pl.CostEstimate(flops=flops, bytes_accessed=moved, transcendentals=0)


def kernel_params(mib):
    return pltpu.CompilerParams(vmem_limit_bytes=mib * MIB)


def seat():
    expert = lax.axis_index("expert")
    return expert, lax.shift_right_logical(expert, 2), expert & 3, lax.axis_index("dp")


def aligned(index, step):
    return pl.ds(pl.multiple_of(index * step, step), step)


def prepare_kernel(live, ids, logits, resid, share_ref, r0, r1, r2, r3):
    expert, outer, inner, dp = seat()
    rows, top = ids.shape
    experts, lanes = share_ref.shape
    value = logits[...]
    value = jnp.exp(value - jnp.max(value, axis=1, keepdims=True))
    probs = (value / jnp.sum(value, axis=1, keepdims=True)).astype(BF16).astype(F32)
    probs = jnp.where(lax.broadcasted_iota(jnp.int32, (rows, top), 0) < live[0, 0], probs, 0.0)
    names = lax.broadcasted_iota(jnp.int32, (rows, experts), 1)
    table = jnp.zeros((rows, experts), F32)
    for k in range(top):
        table = table + jnp.where(ids[:, k : k + 1] == names, probs[:, k : k + 1], 0.0)
    spots = lax.broadcasted_iota(jnp.int32, (rows, lanes), 1) - outer * rows
    spots = (spots == lax.broadcasted_iota(jnp.int32, (rows, lanes), 0)).astype(F32).astype(BF16)
    share_ref[...] = lax.dot_general(
        table.astype(BF16), spots, (((0,), (0,)), ((), ())), preferred_element_type=F32
    ).astype(BF16)
    for s, r in enumerate((r0, r1, r2, r3)):
        r[...] = resid[:, aligned((outer + s) & 3, lanes)]


def proj_kernel(a0, a1, a2, a3, w0, w1, w2, w3, keep_ref, send_ref, rows, part):
    expert, outer, inner, dp = seat()
    full = a0.shape[0]
    half = full // 2
    block = w0.shape[1]
    for s, a in enumerate((a0, a1, a2, a3)):
        rows[aligned(outer ^ s, full), :] = a[...]
    for j, w in enumerate((w0, w1, w2, w3)):
        part[:, aligned(inner ^ j, block)] = dot(rows[...], w[...]).astype(BF16)
    for spot in range(4):
        keep_ref[spot * half : (spot + 1) * half, :] = part[aligned(2 * spot + dp, half), :]
        send_ref[spot * half : (spot + 1) * half, :] = part[aligned(2 * spot + 1 - dp, half), :]


def stream_kernel(keep, arrived, r0, r1, r2, r3, share, block_ref):
    expert, outer, inner, dp = seat()
    count = keep.shape[0]
    small = r0.shape[0]
    for s, r in enumerate((r0, r1, r2, r3)):
        rows = aligned((outer + 4 - s) & 3, small)
        product = keep[rows, :].astype(F32) + arrived[rows, :].astype(F32)
        block_ref[rows, :] = (r[...].astype(F32) + product).astype(BF16)
    block_ref[count:, :] = share[...]


def first_gate_kernel(
    blocks, blocks_x, blocks_c, blocks_cx, gain, ga, ua, gb, ub,
    gate_ref, up_ref, last_ref, share_ref, own_ref, normed,
):
    expert, outer, inner, dp = seat()
    step = pl.program_id(0)
    width = blocks.shape[2]
    count = share_ref.shape[0] // 4
    experts = blocks.shape[1] - count
    half = normed.shape[1] // 2
    small = own_ref.shape[0]
    depth = gb.shape[0]
    rest = half - depth

    @pl.when(step == 0)
    def _():
        picked = lax.broadcasted_iota(jnp.int32, (experts, count), 0) == expert
        diagonal = lax.broadcasted_iota(jnp.int32, (count, count), 0) == lax.broadcasted_iota(
            jnp.int32, (count, count), 1
        )
        for j, group in enumerate((blocks_x, blocks_cx, blocks, blocks_c)):
            rows = slice(j * count, (j + 1) * count)
            square = jnp.zeros((count, 1), F32)
            share = jnp.zeros((experts, count), F32)
            for s in range(4):
                value = group[s, 0:count, :]
                normed[rows, aligned((outer + 4 - s) & 3, width)] = value
                value = value.astype(F32)
                square = square + jnp.sum(value * value, axis=1, keepdims=True)
                share = share + group[s, count : count + experts, 0:count].astype(F32)
            line = jnp.sum(jnp.where(picked, share, 0.0), axis=0, keepdims=True)
            column = jnp.sum(jnp.where(diagonal, line, 0.0), axis=1, keepdims=True)
            share_ref[rows, :] = jnp.broadcast_to(column, (count, share_ref.shape[1]))
            if j == 2:
                own_ref[...] = normed[aligned(outer + 2 * (count // small), small), :]
            scale = lax.rsqrt(square / (4 * width) + 1e-06)
            for s in range(4):
                cols = slice(s * width, (s + 1) * width)
                value = normed[rows, cols].astype(F32)
                normed[rows, cols] = (value * scale * gain[:, cols]).astype(BF16)
        last_ref[...] = normed[:, pl.ds(pl.multiple_of((1 - dp) * half + depth, 128), rest)]

    mine = normed[:, aligned(dp, half)]
    early = normed[:, pl.ds(pl.multiple_of((1 - dp) * half, half), depth)]
    gate_ref[...] = dot(mine, ga[...]) + dot(early, gb[...])
    up_ref[...] = dot(mine, ua[...]) + dot(early, ub[...])


def last_gate_kernel(gate, up, rows, share, gw, uw, far_ref, near_ref):
    g = gate[...] + dot(rows[...], gw[...])
    u = up[...] + dot(rows[...], uw[...])
    inner = (g / (1.0 + jnp.exp(-g)) * u * share[:, 0:1]).astype(BF16)
    half = far_ref.shape[0]
    far_ref[...] = inner[:half]
    near_ref[...] = inner[half:]


def down_both_kernel(far, near, wd, keep_far, keep_near, send_ref):
    count = keep_far.shape[0]
    value = dot(far[...], wd[...]).astype(BF16)
    keep_far[...] = value[:count]
    send_ref[0:count, :] = value[count:]
    value = dot(near[...], wd[...]).astype(BF16)
    keep_near[...] = value[:count]
    send_ref[count : 2 * count, :] = value[count:]


def down_kernel(rows, wd, keep_ref, send_ref):
    count = keep_ref.shape[0]
    value = dot(rows[...], wd[...]).astype(BF16)
    keep_ref[...] = value[:count]
    send_ref[...] = value[count:]


def pieces_kernel(keep, core, far, p0, p1, p2, p3):
    expert, outer, inner, dp = seat()
    small = p0.shape[0]
    for s, p in enumerate((p0, p1, p2, p3)):
        rows = aligned((outer + s) & 3, small)
        total = keep[rows, :].astype(F32) + core[rows, :].astype(F32)
        p[...] = (total + far[rows, :].astype(F32)).astype(BF16)


def tail_kernel(own, m0, m1, m2, m3, o0, o1, o2, o3, gain, stream_ref, normed_ref):
    expert, outer, inner, dp = seat()
    half = m0.shape[1]
    for at, pieces in ((dp, (m0, m1, m2, m3)), (1 - dp, (o0, o1, o2, o3))):
        cols = aligned(at, half)
        mixture = pieces[0][...].astype(F32)
        for piece in pieces[1:]:
            mixture = mixture + piece[...].astype(F32)
        stream_ref[:, cols] = (own[:, cols].astype(F32) + mixture).astype(BF16)
    normed_ref[...] = rms_scale(stream_ref[...].astype(F32), gain[...]).astype(BF16)


def body_paired(
    attn,
    resid,
    w_out,
    gain_post,
    route_ids,
    route_logits,
    live_count,
    w_gate_up,
    w_down,
    gain_final,
):
    rows_here = resid.shape[1]
    model_width = resid.shape[2]
    expert_count = lax.axis_size("expert")
    hidden = w_down.shape[1]
    half_width = w_down.shape[2]
    quarter = model_width // 4
    vmem, smem = whole_vmem(), whole_smem()

    def shape_of(*shape, dtype=BF16):
        return jax.ShapeDtypeStruct(shape, dtype)

    def call(kernel, name, mib, outs, *args, scratch=(), first=vmem, flops=1_000_000):
        moved = sum(math.prod(x.shape) * x.dtype.itemsize for x in (*args, *outs))
        return pl.pallas_call(
            kernel,
            out_shape=outs,
            in_specs=[first] + [vmem] * (len(args) - 1),
            out_specs=tuple(vmem for _ in outs),
            scratch_shapes=list(scratch),
            compiler_params=kernel_params(mib),
            cost_estimate=cost(flops, moved),
            name=name,
        )(*args)

    def swap_dp(x):
        return lax.ppermute(x, "dp", [(0, 1), (1, 0)])

    def shift_outer(x, s):
        return lax.ppermute(
            x, "expert", [(i, (i + 4 * s) % expert_count) for i in range(expert_count)]
        )

    def cross_outer(x, s):
        return lax.ppermute(
            x,
            ("dp", "expert"),
            [
                (d * expert_count + i, (1 - d) * expert_count + (i + 4 * s) % expert_count)
                for d in range(2)
                for i in range(expert_count)
            ],
        )

    def swap_inner(x, j):
        return lax.ppermute(x, "expert", [(i, i ^ j) for i in range(expert_count)])

    def swap_outer(x, s):
        return lax.ppermute(x, "expert", [(i, i ^ (4 * s)) for i in range(expert_count)])

    def after(x, *results):
        return lax.optimization_barrier((x, *results))[0]

    depth = half_width * 3 // 8
    a = [attn[0], swap_outer(attn[0], 1), swap_outer(attn[0], 2)]
    a.append(swap_outer(a[2], 1))
    w_x = swap_inner(w_out, 2)
    gate_up_early = swap_dp(w_gate_up[0, :depth])
    w_c = swap_inner(after(w_out, w_x), 1)
    w_cx = swap_inner(w_x, 1)

    piece = shape_of(rows_here, quarter)
    share, *r = call(
        prepare_kernel,
        "prepare",
        4,
        (shape_of(expert_count, quarter), piece, piece, piece, piece),
        live_count,
        route_ids[0],
        route_logits[0],
        resid[0],
        first=smem,
    )
    r = [r[0]] + [shift_outer(after(r[s], a[1]), s) for s in (1, 2, 3)]

    product = shape_of(4 * rows_here, quarter)
    keep, send = call(
        proj_kernel,
        "projection",
        8,
        (product, product),
        *a,
        w_out,
        w_c,
        w_x,
        w_cx,
        flops=16 * rows_here * attn.shape[2] * quarter,
        scratch=(
            pltpu.VMEM((8 * rows_here, attn.shape[2]), BF16),
            pltpu.VMEM((8 * rows_here, quarter), BF16),
        ),
    )
    arrived = swap_dp(after(send, gate_up_early, *r[1:]))
    gate_up_late = swap_dp(after(w_gate_up[0, depth:], arrived))
    (block,) = call(
        stream_kernel,
        "stream",
        4,
        (shape_of(4 * rows_here + expert_count, quarter),),
        keep,
        arrived,
        *r,
        share,
    )

    blocks = jnp.stack([block] + [shift_outer(block, s) for s in (1, 2, 3)])
    blocks_x = swap_inner(blocks, 2)
    blocks_c = swap_inner(blocks, 1)
    blocks_cx = swap_inner(blocks_x, 1)

    unit = 256
    steps = hidden // unit
    row_total = 16 * rows_here
    block_spec = fixed(*blocks.shape)
    gate_cols = lambda k: pl.BlockSpec((k, unit), lambda i: (0, i))
    up_cols = lambda k: pl.BlockSpec((k, unit), lambda i: (0, i + steps))
    out_cols = lambda k: pl.BlockSpec((k, unit), lambda i: (0, i))
    gate, up, last_rows, share_rows, stream_own = pl.pallas_call(
        first_gate_kernel,
        grid=(steps,),
        out_shape=(
            shape_of(row_total, hidden, dtype=F32),
            shape_of(row_total, hidden, dtype=F32),
            shape_of(row_total, half_width - depth),
            shape_of(row_total, 128, dtype=F32),
            shape_of(rows_here, model_width),
        ),
        in_specs=[block_spec] * 4
        + [
            fixed(1, model_width),
            gate_cols(half_width),
            up_cols(half_width),
            gate_cols(depth),
            up_cols(depth),
        ],
        out_specs=(
            out_cols(row_total),
            out_cols(row_total),
            fixed(row_total, half_width - depth),
            fixed(row_total, 128),
            fixed(rows_here, model_width),
        ),
        scratch_shapes=[pltpu.VMEM((row_total, model_width), BF16)],
        compiler_params=kernel_params(24),
        name="first_gate_up",
        cost_estimate=cost(4 * row_total * (half_width + depth) * hidden, 12 * row_total * hidden),
    )(
        blocks,
        blocks_x,
        blocks_c,
        blocks_cx,
        gain_post[None],
        w_gate_up[0],
        w_gate_up[0],
        gate_up_early,
        gate_up_early,
    )
    inner_half = shape_of(row_total // 2, hidden)
    inner_far, inner_near = pl.pallas_call(
        last_gate_kernel,
        grid=(steps,),
        out_shape=(inner_half, inner_half),
        in_specs=[
            out_cols(row_total),
            out_cols(row_total),
            fixed(row_total, half_width - depth),
            fixed(row_total, 128),
            gate_cols(half_width - depth),
            up_cols(half_width - depth),
        ],
        out_specs=(out_cols(row_total // 2), out_cols(row_total // 2)),
        compiler_params=kernel_params(16),
        name="last_gate_up",
        cost_estimate=cost(4 * row_total * (half_width - depth) * hidden, 14 * row_total * hidden),
    )(gate, up, last_rows, share_rows, gate_up_late, gate_up_late)
    far_other = swap_dp(inner_far)
    near_other = swap_dp(inner_near)

    count = row_total // 4
    quarter_out = shape_of(count, half_width)
    half_spec = fixed(row_total // 2, hidden)
    wd_spec = pl.BlockSpec((hidden, unit), lambda i: (0, i))

    def down(rows):
        return pl.pallas_call(
            down_kernel,
            grid=(half_width // unit,),
            out_shape=(quarter_out, quarter_out),
            in_specs=[half_spec, wd_spec],
            out_specs=(out_cols(count), out_cols(count)),
            compiler_params=kernel_params(8),
            name="down",
            cost_estimate=cost(row_total * hidden * half_width, 3 * row_total * half_width),
        )(rows, w_down[0])

    def add(x, y):
        return (x.astype(F32) + y.astype(F32)).astype(BF16)

    def pieces(keep, core, far):
        out = shape_of(rows_here, half_width)
        return call(pieces_kernel, "pieces", 4, (out, out, out, out), keep, core, far)

    keep_far, keep_near, core_send = pl.pallas_call(
        down_both_kernel,
        grid=(half_width // unit,),
        out_shape=(quarter_out, quarter_out, shape_of(2 * count, half_width)),
        in_specs=[half_spec, half_spec, wd_spec],
        out_specs=(out_cols(count), out_cols(count), out_cols(2 * count)),
        compiler_params=kernel_params(12),
        name="down_both",
        cost_estimate=cost(2 * row_total * hidden * half_width, 4 * row_total * half_width),
    )(inner_far, inner_near, w_down[0])
    core = swap_inner(core_send, 1)
    far = swap_inner(add(keep_far, core[:count]), 2)
    ready = far
    cut = pieces(keep_near, core[count:], far)
    mine = [cut[0]] + [shift_outer(cut[s], s) for s in (1, 2, 3)]

    keep_far, core_send = down(after(far_other, ready))
    far = swap_inner(add(keep_far, swap_inner(core_send, 1)), 2)
    keep_near, core_send = down(after(near_other, far, *mine[1:]))
    cut = pieces(keep_near, swap_inner(core_send, 1), far)
    others = [cross_outer(cut[s], s) for s in range(4)]

    out = shape_of(rows_here, model_width)
    stream_out, normed_out = call(
        tail_kernel, "closing", 8, (out, out), stream_own, *mine, *others, gain_final[None]
    )
    return (stream_out[None], normed_out[None])


def solution(mesh):
    placed = (
        P("expert", None, "dp"),
        P("expert", "dp", None),
        P("dp", "expert"),
        P(),
        P("expert", "dp", None),
        P("expert", "dp", None),
        P("expert", "dp"),
        P("expert", "dp", None),
        P("expert", None, "dp"),
        P(),
    )
    paired = mesh.shape["dp"] == 2 and mesh.shape["expert"] == 16
    return jax.shard_map(
        body_paired if paired else body_general,
        mesh=mesh,
        in_specs=placed,
        out_specs=(P("expert", "dp", None), P("expert", "dp", None)),
        check_vma=False,
    )
```

```python
import functools
import math

import jax
import jax.numpy as jnp
from jax import lax
from jax.experimental import pallas as pl
from jax.experimental.pallas import tpu as pltpu
from jax.sharding import PartitionSpec as P


def rms_scale(values, gain):
    return values * lax.rsqrt(jnp.mean(values * values, axis=-1, keepdims=True) + 1e-06) * gain


def swiglu_rows(rows_in, gate_up, down, hidden_units):
    both = jnp.dot(rows_in, gate_up, preferred_element_type=jnp.float32)
    inner = (jax.nn.silu(both[:, :hidden_units]) * both[:, hidden_units:]).astype(jnp.bfloat16)
    return jnp.dot(inner, down, preferred_element_type=jnp.float32).astype(jnp.bfloat16)


def body_general(
    attn,
    resid,
    w_out,
    gain_post,
    route_ids,
    route_logits,
    live_count,
    w_gate_up,
    w_down,
    gain_final,
):
    rows_here = resid.shape[1]
    model_width = resid.shape[2]
    top_count = route_ids.shape[2]
    dp_count = lax.axis_size("dp")
    expert_count = lax.axis_size("expert")
    hidden_units = w_down.shape[1]
    capacity = dp_count * max(1, 2 * rows_here * top_count // (expert_count * dp_count))
    slot_count = expert_count * capacity
    flat_attn = attn[0]
    partial_out = jnp.dot(
        flat_attn,
        lax.all_gather(w_out, "expert", axis=1, tiled=True),
        preferred_element_type=jnp.float32,
    )
    projected = lax.psum_scatter(
        partial_out.astype(jnp.bfloat16), "dp", scatter_dimension=0, tiled=True
    ).astype(jnp.float32)
    stream_in = (resid[0].astype(jnp.float32) + projected).astype(jnp.bfloat16)
    stream_float = stream_in.astype(jnp.float32)
    normed_in = rms_scale(stream_float, gain_post).astype(jnp.bfloat16)
    probs = jax.nn.softmax(route_logits[0], axis=-1).astype(jnp.bfloat16)
    alive = jnp.arange(rows_here, dtype=jnp.int32) < live_count[0, 0]
    expert_of = route_ids[0].reshape(-1)
    route_alive = jnp.repeat(alive, top_count)
    onehot = (
        (expert_of[:, None] == jnp.arange(expert_count, dtype=jnp.int32)[None, :])
        & route_alive[:, None]
    ).astype(jnp.int32)
    earlier = jnp.sum((jnp.cumsum(onehot, axis=0) - onehot) * onehot, axis=1)
    target = expert_of * capacity + earlier
    match = (target[:, None] == jnp.arange(slot_count, dtype=jnp.int32)[None, :]) & route_alive[
        :, None
    ]
    placed = match.reshape(rows_here, top_count, slot_count)
    gather_matrix = jnp.any(placed, axis=1).astype(jnp.bfloat16)
    send_rows = lax.dot_general(
        gather_matrix, normed_in, (((0,), (0,)), ((), ())), preferred_element_type=jnp.float32
    ).astype(jnp.bfloat16)
    send_flags = jnp.sum(gather_matrix.astype(jnp.float32), axis=0).astype(jnp.bfloat16)
    combine_matrix = jnp.sum(
        jnp.where(placed, probs.astype(jnp.float32)[:, :, None], jnp.float32(0.0)), axis=1
    ).astype(jnp.bfloat16)
    arrived_rows, arrived_flags = (
        lax.all_to_all(
            send_rows.reshape(expert_count, capacity, model_width),
            "expert",
            split_axis=0,
            concat_axis=0,
            tiled=True,
        ),
        lax.all_to_all(
            send_flags.reshape(expert_count, capacity),
            "expert",
            split_axis=0,
            concat_axis=0,
            tiled=True,
        ),
    )
    arrived = arrived_rows.reshape(slot_count, model_width)
    flags = arrived_flags.reshape(slot_count)
    gate_up_full, down_full = (
        lax.all_gather(w_gate_up, "dp", axis=1, tiled=True),
        lax.all_gather(w_down, "dp", axis=2, tiled=True),
    )
    live_slot = (flags > 0.5).astype(jnp.int32)
    order = jnp.argsort(1 - live_slot, stable=True)
    live_total = jnp.sum(live_slot)
    packed = arrived[order]
    block_len = math.gcd(slot_count, 128)
    block_total = (live_total + block_len - 1) // block_len

    def run_block(index, outputs):
        begin = index * block_len
        rows_in = lax.dynamic_slice_in_dim(packed, begin, block_len, 0)
        block_out = swiglu_rows(rows_in, gate_up_full[0], down_full[0], hidden_units)
        return lax.dynamic_update_slice_in_dim(outputs, block_out, begin, 0)

    packed_out = lax.fori_loop(
        0, block_total, run_block, jnp.zeros((slot_count, model_width), jnp.bfloat16)
    )
    position = (
        jnp.zeros((slot_count,), jnp.int32).at[order].set(jnp.arange(slot_count, dtype=jnp.int32))
    )
    results = packed_out[position]
    returned = lax.all_to_all(
        results.reshape(expert_count, capacity, model_width),
        "expert",
        split_axis=0,
        concat_axis=0,
        tiled=True,
    )
    returned = returned.reshape(slot_count, model_width)
    mixture = jnp.dot(combine_matrix, returned, preferred_element_type=jnp.float32)
    stream_out = (stream_float + mixture).astype(jnp.bfloat16)
    normed_out = rms_scale(stream_out.astype(jnp.float32), gain_final).astype(jnp.bfloat16)
    return (stream_out[None], normed_out[None])


MIB = 1024 * 1024
BF16, F32 = jnp.bfloat16, jnp.float32


def whole_vmem():
    return pl.BlockSpec(memory_space=pltpu.VMEM)


def whole_smem():
    return pl.BlockSpec(memory_space=pltpu.SMEM)


def fixed(*shape):
    return pl.BlockSpec(shape, lambda i: (0,) * len(shape))


def dot(a, b):
    return jnp.dot(a, b, preferred_element_type=F32)


def cost(flops, moved):
    return pl.CostEstimate(flops=flops, bytes_accessed=moved, transcendentals=0)


def kernel_params(mib):
    return pltpu.CompilerParams(vmem_limit_bytes=mib * MIB)


def seat():
    expert = lax.axis_index("expert")
    return expert, lax.shift_right_logical(expert, 2), expert & 3, lax.axis_index("dp")


def aligned(index, step):
    return pl.ds(pl.multiple_of(index * step, step), step)


def prepare_kernel(live, ids, logits, resid, share_ref, r0, r1, r2, r3):
    expert, outer, inner, dp = seat()
    rows, top = ids.shape
    experts, lanes = share_ref.shape
    value = logits[...]
    value = jnp.exp(value - jnp.max(value, axis=1, keepdims=True))
    probs = (value / jnp.sum(value, axis=1, keepdims=True)).astype(BF16).astype(F32)
    probs = jnp.where(lax.broadcasted_iota(jnp.int32, (rows, top), 0) < live[0, 0], probs, 0.0)
    names = lax.broadcasted_iota(jnp.int32, (rows, experts), 1)
    table = jnp.zeros((rows, experts), F32)
    for k in range(top):
        table = table + jnp.where(ids[:, k : k + 1] == names, probs[:, k : k + 1], 0.0)
    spots = lax.broadcasted_iota(jnp.int32, (rows, lanes), 1) - outer * rows
    spots = (spots == lax.broadcasted_iota(jnp.int32, (rows, lanes), 0)).astype(F32).astype(BF16)
    share_ref[...] = lax.dot_general(
        table.astype(BF16), spots, (((0,), (0,)), ((), ())), preferred_element_type=F32
    ).astype(BF16)
    for s, r in enumerate((r0, r1, r2, r3)):
        r[...] = resid[:, aligned((outer + s) & 3, lanes)]


def proj_kernel(a0, a1, a2, a3, w0, w1, w2, w3, keep_ref, send_ref, rows, part):
    expert, outer, inner, dp = seat()
    full = a0.shape[0]
    half = full // 2
    block = w0.shape[1]
    for s, a in enumerate((a0, a1, a2, a3)):
        rows[aligned(outer ^ s, full), :] = a[...]
    for j, w in enumerate((w0, w1, w2, w3)):
        part[:, aligned(inner ^ j, block)] = dot(rows[...], w[...]).astype(BF16)
    for spot in range(4):
        keep_ref[spot * half : (spot + 1) * half, :] = part[aligned(2 * spot + dp, half), :]
        send_ref[spot * half : (spot + 1) * half, :] = part[aligned(2 * spot + 1 - dp, half), :]


def stream_kernel(keep, arrived, r0, r1, r2, r3, share, block_ref):
    expert, outer, inner, dp = seat()
    count = keep.shape[0]
    small = r0.shape[0]
    for s, r in enumerate((r0, r1, r2, r3)):
        rows = aligned((outer + 4 - s) & 3, small)
        product = keep[rows, :].astype(F32) + arrived[rows, :].astype(F32)
        block_ref[rows, :] = (r[...].astype(F32) + product).astype(BF16)
    block_ref[count:, :] = share[...]


def piece_kernel(at, weights, out, semaphores):
    width = out.shape[1] // 2
    copies = [
        pltpu.make_async_copy(
            weights.at[:, pl.ds((2 * i + at) * width, width)],
            out.at[:, pl.ds(i * width, width)],
            semaphores.at[i],
        )
        for i in range(2)
    ]
    for copy in copies:
        copy.start()
    for copy in copies:
        copy.wait()


def swiglu(gate, up, share):
    return (gate / (1.0 + jnp.exp(-gate)) * up * share).astype(BF16)


def first_gate_kernel(
    blocks, blocks_x, blocks_c, blocks_cx, gain, own, early,
    inner_ref, part_ref, other_ref, share_ref, own_ref, normed,
):
    expert, outer, inner, dp = seat()
    width = blocks.shape[2]
    count = share_ref.shape[0] // 4
    experts = blocks.shape[1] - count
    half = normed.shape[1] // 2
    small = own_ref.shape[0]
    cut = inner_ref.shape[1]
    picked = lax.broadcasted_iota(jnp.int32, (experts, count), 0) == expert
    diagonal = lax.broadcasted_iota(jnp.int32, (count, count), 0) == lax.broadcasted_iota(
        jnp.int32, (count, count), 1
    )
    for j, group in enumerate((blocks_x, blocks_cx, blocks, blocks_c)):
        rows = slice(j * count, (j + 1) * count)
        square = jnp.zeros((count, 1), F32)
        share = jnp.zeros((experts, count), F32)
        for s in range(4):
            value = group[s, 0:count, :]
            normed[rows, aligned((outer + 4 - s) & 3, width)] = value
            value = value.astype(F32)
            square = square + jnp.sum(value * value, axis=1, keepdims=True)
            share = share + group[s, count : count + experts, 0:count].astype(F32)
        line = jnp.sum(jnp.where(picked, share, 0.0), axis=0, keepdims=True)
        column = jnp.sum(jnp.where(diagonal, line, 0.0), axis=1, keepdims=True)
        share_ref[rows, :] = jnp.broadcast_to(column, (count, share_ref.shape[1]))
        if j == 2:
            own_ref[...] = normed[aligned(outer + 2 * (count // small), small), :]
        scale = lax.rsqrt(square / (4 * width) + 1e-06)
        for s in range(4):
            cols = slice(s * width, (s + 1) * width)
            value = normed[rows, cols].astype(F32)
            normed[rows, cols] = (value * scale * gain[:, cols]).astype(BF16)
    other_ref[...] = normed[:, aligned(1 - dp, half)]

    mine = normed[:, aligned(dp, half)]
    other = other_ref[...]
    gate = dot(mine, own[:, 0:cut]) + dot(other, early[:, 0:cut])
    up = dot(mine, own[:, 2 * cut : 3 * cut]) + dot(other, early[:, cut : 2 * cut])
    inner_ref[...] = swiglu(gate, up, share_ref[:, 0:1])
    part_ref[:, 0:cut] = dot(mine, own[:, cut : 2 * cut])
    part_ref[:, cut : 2 * cut] = dot(mine, own[:, 3 * cut : 4 * cut])


def last_gate_kernel(first, part, other, share, late, far_ref, near_ref):
    cut = first.shape[1]
    gate = part[:, 0:cut] + dot(other[...], late[:, 0:cut])
    up = part[:, cut : 2 * cut] + dot(other[...], late[:, cut : 2 * cut])
    value = swiglu(gate, up, share[:, 0:1])
    half = far_ref.shape[0]
    far_ref[:, 0:cut] = first[0:half, :]
    near_ref[:, 0:cut] = first[half:, :]
    far_ref[:, cut : 2 * cut] = value[:half]
    near_ref[:, cut : 2 * cut] = value[half:]


def column_chunks(wd):
    return [slice(at, at + 256) for at in range(0, wd.shape[1], 256)]


def down_both_kernel(far, near, wd, keep_far, keep_near, send_ref):
    count = keep_far.shape[0]
    for cols in column_chunks(wd):
        value = dot(far[...], wd[:, cols]).astype(BF16)
        keep_far[:, cols] = value[:count]
        send_ref[0:count, cols] = value[count:]
        value = dot(near[...], wd[:, cols]).astype(BF16)
        keep_near[:, cols] = value[:count]
        send_ref[count : 2 * count, cols] = value[count:]


def down_kernel(rows, wd, keep_ref, send_ref):
    count = keep_ref.shape[0]
    for cols in column_chunks(wd):
        value = dot(rows[...], wd[:, cols]).astype(BF16)
        keep_ref[:, cols] = value[:count]
        send_ref[:, cols] = value[count:]


def pieces_kernel(keep, core, far, p0, p1, p2, p3):
    expert, outer, inner, dp = seat()
    small = p0.shape[0]
    for s, p in enumerate((p0, p1, p2, p3)):
        rows = aligned((outer + s) & 3, small)
        total = keep[rows, :].astype(F32) + core[rows, :].astype(F32)
        p[...] = (total + far[rows, :].astype(F32)).astype(BF16)


def tail_kernel(own, m0, m1, m2, m3, o0, o1, o2, o3, gain, stream_ref, normed_ref):
    expert, outer, inner, dp = seat()
    half = m0.shape[1]
    for at, pieces in ((dp, (m0, m1, m2, m3)), (1 - dp, (o0, o1, o2, o3))):
        cols = aligned(at, half)
        mixture = pieces[0][...].astype(F32)
        for piece in pieces[1:]:
            mixture = mixture + piece[...].astype(F32)
        stream_ref[:, cols] = (own[:, cols].astype(F32) + mixture).astype(BF16)
    normed_ref[...] = rms_scale(stream_ref[...].astype(F32), gain[...]).astype(BF16)


def body_paired(
    attn,
    resid,
    w_out,
    gain_post,
    route_ids,
    route_logits,
    live_count,
    w_gate_up,
    w_down,
    gain_final,
):
    rows_here = resid.shape[1]
    model_width = resid.shape[2]
    expert_count = lax.axis_size("expert")
    hidden = w_down.shape[1]
    half_width = w_down.shape[2]
    quarter = model_width // 4
    vmem, smem = whole_vmem(), whole_smem()

    def shape_of(*shape, dtype=BF16):
        return jax.ShapeDtypeStruct(shape, dtype)

    def call(kernel, name, mib, outs, *args, scratch=(), first=vmem, flops=1_000_000):
        moved = sum(math.prod(x.shape) * x.dtype.itemsize for x in (*args, *outs))
        return pl.pallas_call(
            kernel,
            out_shape=outs,
            in_specs=[first] + [vmem] * (len(args) - 1),
            out_specs=tuple(vmem for _ in outs),
            scratch_shapes=list(scratch),
            compiler_params=kernel_params(mib),
            cost_estimate=cost(flops, moved),
            name=name,
        )(*args)

    def swap_dp(x):
        return lax.ppermute(x, "dp", [(0, 1), (1, 0)])

    def shift_outer(x, s):
        return lax.ppermute(
            x, "expert", [(i, (i + 4 * s) % expert_count) for i in range(expert_count)]
        )

    def cross_outer(x, s):
        return lax.ppermute(
            x,
            ("dp", "expert"),
            [
                (d * expert_count + i, (1 - d) * expert_count + (i + 4 * s) % expert_count)
                for d in range(2)
                for i in range(expert_count)
            ],
        )

    def swap_inner(x, j):
        return lax.ppermute(x, "expert", [(i, i ^ j) for i in range(expert_count)])

    def swap_outer(x, s):
        return lax.ppermute(x, "expert", [(i, i ^ (4 * s)) for i in range(expert_count)])

    def after(x, *results):
        return lax.optimization_barrier((x, *results))[0]

    def weight_piece(i):
        return pl.pallas_call(
            functools.partial(piece_kernel, i),
            out_shape=shape_of(half_width, hidden),
            in_specs=[pl.BlockSpec(memory_space=pl.ANY)],
            out_specs=vmem,
            scratch_shapes=[pltpu.SemaphoreType.DMA((2,))],
            compiler_params=kernel_params(8),
            cost_estimate=cost(1000, 4 * half_width * hidden),
            name="weight_piece",
        )(w_gate_up[0])

    cut_width = hidden // 2
    early_piece, late_piece = (weight_piece(i) for i in range(2))
    a = [attn[0], swap_outer(attn[0], 1), swap_outer(attn[0], 2)]
    a.append(swap_outer(after(a[2], a[1]), 1))
    w_x = swap_inner(w_out, 2)
    gate_up_early = swap_dp(early_piece)
    w_c = swap_inner(after(w_out, w_x), 1)
    w_cx = swap_inner(w_x, 1)

    piece = shape_of(rows_here, quarter)
    share, *r = call(
        prepare_kernel,
        "prepare",
        4,
        (shape_of(expert_count, quarter), piece, piece, piece, piece),
        live_count,
        route_ids[0],
        route_logits[0],
        resid[0],
        first=smem,
    )
    r = [r[0]] + [shift_outer(after(r[s], a[1]), s) for s in (1, 2, 3)]

    product = shape_of(4 * rows_here, quarter)
    keep, send = call(
        proj_kernel,
        "projection",
        8,
        (product, product),
        *a,
        w_out,
        w_c,
        w_x,
        w_cx,
        flops=16 * rows_here * attn.shape[2] * quarter,
        scratch=(
            pltpu.VMEM((8 * rows_here, attn.shape[2]), BF16),
            pltpu.VMEM((8 * rows_here, quarter), BF16),
        ),
    )
    arrived = swap_dp(after(send, gate_up_early, late_piece, *r[1:]))
    gate_up_late = swap_dp(after(late_piece, arrived))
    (block,) = call(
        stream_kernel,
        "stream",
        4,
        (shape_of(4 * rows_here + expert_count, quarter),),
        keep,
        arrived,
        *r,
        share,
    )

    blocks = jnp.stack([block] + [shift_outer(block, s) for s in (1, 2, 3)])
    blocks_x = swap_inner(blocks, 2)
    blocks_c = swap_inner(blocks, 1)
    blocks_cx = swap_inner(blocks_x, 1)

    row_total = 16 * rows_here
    half_rows = row_total // 2
    product_flops = 2 * row_total * half_width * hidden
    inner_first, part, other_rows, share_rows, stream_own = call(
        first_gate_kernel,
        "first_gate_up",
        24,
        (
            shape_of(row_total, cut_width),
            shape_of(row_total, hidden, dtype=F32),
            shape_of(row_total, half_width),
            shape_of(row_total, 128, dtype=F32),
            shape_of(rows_here, model_width),
        ),
        blocks,
        blocks_x,
        blocks_c,
        blocks_cx,
        gain_post[None],
        w_gate_up[0],
        gate_up_early,
        flops=3 * product_flops,
        scratch=(pltpu.VMEM((row_total, model_width), BF16),),
    )
    inner_half = shape_of(half_rows, hidden)
    inner_far, inner_near = call(
        last_gate_kernel,
        "last_gate_up",
        16,
        (inner_half, inner_half),
        inner_first,
        part,
        other_rows,
        share_rows,
        gate_up_late,
        flops=product_flops,
    )
    far_other = swap_dp(inner_far)
    near_other = swap_dp(after(inner_near, far_other))

    count = row_total // 4
    quarter_out = shape_of(count, half_width)

    def down(rows):
        return call(
            down_kernel,
            "down",
            12,
            (quarter_out, quarter_out),
            rows,
            w_down[0],
            flops=product_flops // 2,
        )

    def add(x, y):
        return (x.astype(F32) + y.astype(F32)).astype(BF16)

    def pieces(keep, core, far):
        out = shape_of(rows_here, half_width)
        return call(pieces_kernel, "pieces", 4, (out, out, out, out), keep, core, far)

    keep_far, keep_near, core_send = call(
        down_both_kernel,
        "down_both",
        16,
        (quarter_out, quarter_out, shape_of(2 * count, half_width)),
        inner_far,
        inner_near,
        w_down[0],
        flops=product_flops,
    )
    core = swap_inner(core_send, 1)
    far = swap_inner(add(keep_far, core[:count]), 2)
    ready = far
    cut = pieces(keep_near, core[count:], far)
    mine = [cut[0]] + [shift_outer(cut[s], s) for s in (1, 2, 3)]

    keep_far, core_send = down(after(far_other, ready))
    far = swap_inner(add(keep_far, swap_inner(core_send, 1)), 2)
    keep_near, core_send = down(after(near_other, far, *mine[1:]))
    cut = pieces(keep_near, swap_inner(core_send, 1), far)
    others = [cross_outer(cut[s], s) for s in range(4)]

    out = shape_of(rows_here, model_width)
    stream_out, normed_out = call(
        tail_kernel, "closing", 8, (out, out), stream_own, *mine, *others, gain_final[None]
    )
    return (stream_out[None], normed_out[None])


def solution(mesh):
    placed = (
        P("expert", None, "dp"),
        P("expert", "dp", None),
        P("dp", "expert"),
        P(),
        P("expert", "dp", None),
        P("expert", "dp", None),
        P("expert", "dp"),
        P("expert", "dp", None),
        P("expert", None, "dp"),
        P(),
    )
    paired = mesh.shape["dp"] == 2 and mesh.shape["expert"] == 16
    return jax.shard_map(
        body_paired if paired else body_general,
        mesh=mesh,
        in_specs=placed,
        out_specs=(P("expert", "dp", None), P("expert", "dp", None)),
        check_vma=False,
    )
```

```python
import functools
import math

import jax
import jax.numpy as jnp
from jax import lax
from jax.experimental import pallas as pl
from jax.experimental.pallas import tpu as pltpu
from jax.sharding import PartitionSpec as P


def rms_scale(values, gain):
    return values * lax.rsqrt(jnp.mean(values * values, axis=-1, keepdims=True) + 1e-06) * gain


def swiglu_rows(rows_in, gate_up, down, hidden_units):
    both = jnp.dot(rows_in, gate_up, preferred_element_type=jnp.float32)
    inner = (jax.nn.silu(both[:, :hidden_units]) * both[:, hidden_units:]).astype(jnp.bfloat16)
    return jnp.dot(inner, down, preferred_element_type=jnp.float32).astype(jnp.bfloat16)


def body_general(
    attn,
    resid,
    w_out,
    gain_post,
    route_ids,
    route_logits,
    live_count,
    w_gate_up,
    w_down,
    gain_final,
):
    rows_here = resid.shape[1]
    model_width = resid.shape[2]
    top_count = route_ids.shape[2]
    dp_count = lax.axis_size("dp")
    expert_count = lax.axis_size("expert")
    hidden_units = w_down.shape[1]
    capacity = dp_count * max(1, 2 * rows_here * top_count // (expert_count * dp_count))
    slot_count = expert_count * capacity
    flat_attn = attn[0]
    partial_out = jnp.dot(
        flat_attn,
        lax.all_gather(w_out, "expert", axis=1, tiled=True),
        preferred_element_type=jnp.float32,
    )
    projected = lax.psum_scatter(
        partial_out.astype(jnp.bfloat16), "dp", scatter_dimension=0, tiled=True
    ).astype(jnp.float32)
    stream_in = (resid[0].astype(jnp.float32) + projected).astype(jnp.bfloat16)
    stream_float = stream_in.astype(jnp.float32)
    normed_in = rms_scale(stream_float, gain_post).astype(jnp.bfloat16)
    probs = jax.nn.softmax(route_logits[0], axis=-1).astype(jnp.bfloat16)
    alive = jnp.arange(rows_here, dtype=jnp.int32) < live_count[0, 0]
    expert_of = route_ids[0].reshape(-1)
    route_alive = jnp.repeat(alive, top_count)
    onehot = (
        (expert_of[:, None] == jnp.arange(expert_count, dtype=jnp.int32)[None, :])
        & route_alive[:, None]
    ).astype(jnp.int32)
    earlier = jnp.sum((jnp.cumsum(onehot, axis=0) - onehot) * onehot, axis=1)
    target = expert_of * capacity + earlier
    match = (target[:, None] == jnp.arange(slot_count, dtype=jnp.int32)[None, :]) & route_alive[
        :, None
    ]
    placed = match.reshape(rows_here, top_count, slot_count)
    gather_matrix = jnp.any(placed, axis=1).astype(jnp.bfloat16)
    send_rows = lax.dot_general(
        gather_matrix, normed_in, (((0,), (0,)), ((), ())), preferred_element_type=jnp.float32
    ).astype(jnp.bfloat16)
    send_flags = jnp.sum(gather_matrix.astype(jnp.float32), axis=0).astype(jnp.bfloat16)
    combine_matrix = jnp.sum(
        jnp.where(placed, probs.astype(jnp.float32)[:, :, None], jnp.float32(0.0)), axis=1
    ).astype(jnp.bfloat16)
    arrived_rows, arrived_flags = (
        lax.all_to_all(
            send_rows.reshape(expert_count, capacity, model_width),
            "expert",
            split_axis=0,
            concat_axis=0,
            tiled=True,
        ),
        lax.all_to_all(
            send_flags.reshape(expert_count, capacity),
            "expert",
            split_axis=0,
            concat_axis=0,
            tiled=True,
        ),
    )
    arrived = arrived_rows.reshape(slot_count, model_width)
    flags = arrived_flags.reshape(slot_count)
    gate_up_full, down_full = (
        lax.all_gather(w_gate_up, "dp", axis=1, tiled=True),
        lax.all_gather(w_down, "dp", axis=2, tiled=True),
    )
    live_slot = (flags > 0.5).astype(jnp.int32)
    order = jnp.argsort(1 - live_slot, stable=True)
    live_total = jnp.sum(live_slot)
    packed = arrived[order]
    block_len = math.gcd(slot_count, 128)
    block_total = (live_total + block_len - 1) // block_len

    def run_block(index, outputs):
        begin = index * block_len
        rows_in = lax.dynamic_slice_in_dim(packed, begin, block_len, 0)
        block_out = swiglu_rows(rows_in, gate_up_full[0], down_full[0], hidden_units)
        return lax.dynamic_update_slice_in_dim(outputs, block_out, begin, 0)

    packed_out = lax.fori_loop(
        0, block_total, run_block, jnp.zeros((slot_count, model_width), jnp.bfloat16)
    )
    position = (
        jnp.zeros((slot_count,), jnp.int32).at[order].set(jnp.arange(slot_count, dtype=jnp.int32))
    )
    results = packed_out[position]
    returned = lax.all_to_all(
        results.reshape(expert_count, capacity, model_width),
        "expert",
        split_axis=0,
        concat_axis=0,
        tiled=True,
    )
    returned = returned.reshape(slot_count, model_width)
    mixture = jnp.dot(combine_matrix, returned, preferred_element_type=jnp.float32)
    stream_out = (stream_float + mixture).astype(jnp.bfloat16)
    normed_out = rms_scale(stream_out.astype(jnp.float32), gain_final).astype(jnp.bfloat16)
    return (stream_out[None], normed_out[None])


MIB = 1024 * 1024
BF16, F32 = jnp.bfloat16, jnp.float32


def whole_vmem():
    return pl.BlockSpec(memory_space=pltpu.VMEM)


def whole_smem():
    return pl.BlockSpec(memory_space=pltpu.SMEM)


def fixed(*shape):
    return pl.BlockSpec(shape, lambda i: (0,) * len(shape))


def dot(a, b):
    return jnp.dot(a, b, preferred_element_type=F32)


def small_cost():
    return pl.CostEstimate(flops=1, bytes_accessed=1, transcendentals=0)


def kernel_params(mib):
    return pltpu.CompilerParams(vmem_limit_bytes=mib * MIB)


def seat():
    expert = lax.axis_index("expert")
    return expert, lax.shift_right_logical(expert, 2), expert & 3, lax.axis_index("dp")


def aligned(index, step):
    return pl.ds(pl.multiple_of(index * step, step), step)


def cut_kernel(resid, r0, r1, r23):
    expert, outer, inner, dp = seat()
    rows, lanes = r0.shape
    r0[...] = resid[:, aligned(outer, lanes)]
    r1[...] = resid[:, aligned(outer ^ 1, lanes)]
    for i in range(2):
        r23[i * rows : (i + 1) * rows, :] = resid[:, aligned(outer ^ (2 + i), lanes)]


def share_kernel(live, ids, logits, share_ref):
    expert, outer, inner, dp = seat()
    rows, top = ids.shape
    experts, lanes = share_ref.shape
    value = logits[...]
    value = jnp.exp(value - jnp.max(value, axis=1, keepdims=True))
    probs = (value / jnp.sum(value, axis=1, keepdims=True)).astype(BF16).astype(F32)
    probs = jnp.where(lax.broadcasted_iota(jnp.int32, (rows, top), 0) < live[0, 0], probs, 0.0)
    names = lax.broadcasted_iota(jnp.int32, (rows, experts), 1)
    table = jnp.zeros((rows, experts), F32)
    for k in range(top):
        table = table + jnp.where(ids[:, k : k + 1] == names, probs[:, k : k + 1], 0.0)
    spots = lax.broadcasted_iota(jnp.int32, (rows, lanes), 1) - outer * rows
    spots = (spots == lax.broadcasted_iota(jnp.int32, (rows, lanes), 0)).astype(F32).astype(BF16)
    share_ref[...] = lax.dot_general(
        table.astype(BF16), spots, (((0,), (0,)), ((), ())), preferred_element_type=F32
    ).astype(BF16)


def proj_kernel(a0, a1, a2, a3, w0, w1, w2, w3, keep_ref, send_ref, rows, part):
    expert, outer, inner, dp = seat()
    full = a0.shape[0]
    half = full // 2
    block = w0.shape[1]
    for s, a in enumerate((a0, a1, a2, a3)):
        rows[aligned(outer ^ s, full), :] = a[...]
    for j, w in enumerate((w0, w1, w2, w3)):
        part[:, aligned(inner ^ j, block)] = dot(rows[...], w[...]).astype(BF16)
    for spot in range(4):
        keep_ref[spot * half : (spot + 1) * half, :] = part[aligned(2 * spot + dp, half), :]
        send_ref[spot * half : (spot + 1) * half, :] = part[aligned(2 * spot + 1 - dp, half), :]


def stream_kernel(keep, arrived, r0, r13, r2, share, block_ref):
    expert, outer, inner, dp = seat()
    count = keep.shape[0]
    small = r0.shape[0]
    for s, r in enumerate((r0[...], r13[0:small, :], r2[0:small, :], r13[small:, :])):
        rows = aligned(outer ^ s, small)
        product = keep[rows, :].astype(F32) + arrived[rows, :].astype(F32)
        block_ref[rows, :] = (r.astype(F32) + product).astype(BF16)
    block_ref[count:, :] = share[...]


def piece_kernel(at, weights, out, semaphores):
    width = out.shape[1] // 2
    copies = [
        pltpu.make_async_copy(
            weights.at[:, pl.ds((2 * i + at) * width, width)],
            out.at[:, pl.ds(i * width, width)],
            semaphores.at[i],
        )
        for i in range(2)
    ]
    for copy in copies:
        copy.start()
    for copy in copies:
        copy.wait()


def swiglu(gate, up, share):
    return (gate / (1.0 + jnp.exp(-gate)) * up * share).astype(BF16)


def norm_kernel(b0, b1, b2, b3, gain, group_ref, own_ref):
    expert, outer, inner, dp = seat()
    count = group_ref.shape[0]
    width = b0.shape[1]
    experts = b0.shape[0] - count
    small = own_ref.shape[0]
    square = jnp.zeros((count, 1), F32)
    share = jnp.zeros((experts, count), F32)
    for s, b in enumerate((b0, b1, b2, b3)):
        value = b[0:count, :]
        group_ref[:, aligned((outer + 4 - s) & 3, width)] = value
        value = value.astype(F32)
        square = square + jnp.sum(value * value, axis=1, keepdims=True)
        share = share + b[count : count + experts, 0:count].astype(F32)
    own_ref[...] = group_ref[aligned(outer, small), 0 : 4 * width]
    scale = lax.rsqrt(square / (4 * width) + 1e-06)
    for s in range(4):
        cols = slice(s * width, (s + 1) * width)
        value = group_ref[:, cols].astype(F32)
        group_ref[:, cols] = (value * scale * gain[:, cols]).astype(BF16)
    lanes = (experts, 128)
    spread = lax.broadcasted_iota(jnp.int32, lanes, 0) == lax.broadcasted_iota(jnp.int32, lanes, 1)
    group_ref[:, 4 * width :] = lax.dot_general(
        share.astype(BF16),
        spread.astype(F32).astype(BF16),
        (((0,), (0,)), ((), ())),
        preferred_element_type=F32,
    ).astype(BF16)


def first_gate_kernel(
    group_x, group_cx, group, group_c, own, early, inner_ref, part_ref, other_ref, share_ref, mine_ref
):
    expert, outer, inner, dp = seat()
    count = group.shape[0]
    half = other_ref.shape[1]
    cut = inner_ref.shape[1]
    for j, g in enumerate((group_x, group_cx, group, group_c)):
        rows = slice(j * count, (j + 1) * count)
        mine_ref[rows, :] = g[:, aligned(dp, half)]
        other_ref[rows, :] = g[:, aligned(1 - dp, half)]
        share = g[:, 2 * half : 2 * half + 128].astype(F32)
        picked = lax.broadcasted_iota(jnp.int32, share.shape, 1) == expert
        share = jnp.sum(jnp.where(picked, share, 0.0), axis=1, keepdims=True)
        share_ref[rows, :] = jnp.broadcast_to(share, (count, 128))
    mine, other = mine_ref[...], other_ref[...]
    gate = dot(mine, own[:, 0:cut]) + dot(other, early[:, 0:cut])
    up = dot(mine, own[:, 2 * cut : 3 * cut]) + dot(other, early[:, cut : 2 * cut])
    inner_ref[...] = swiglu(gate, up, share_ref[:, 0:1])
    part_ref[:, 0:cut] = dot(mine, own[:, cut : 2 * cut])
    part_ref[:, cut : 2 * cut] = dot(mine, own[:, 3 * cut : 4 * cut])


def last_gate_kernel(first, part, other, share, late, far_ref, near_ref):
    cut = first.shape[1]
    gate = part[:, 0:cut] + dot(other[...], late[:, 0:cut])
    up = part[:, cut : 2 * cut] + dot(other[...], late[:, cut : 2 * cut])
    value = swiglu(gate, up, share[:, 0:1])
    half = far_ref.shape[0]
    far_ref[:, 0:cut] = first[0:half, :]
    near_ref[:, 0:cut] = first[half:, :]
    far_ref[:, cut : 2 * cut] = value[:half]
    near_ref[:, cut : 2 * cut] = value[half:]


def column_chunks(wd):
    return [slice(at, at + 256) for at in range(0, wd.shape[1], 256)]


def down_both_kernel(far, near, wd, keep_far, keep_near, send_far, send_near):
    down_kernel(far, wd, keep_far, send_far)
    down_kernel(near, wd, keep_near, send_near)


def down_kernel(rows, wd, keep_ref, send_ref):
    count = keep_ref.shape[0]
    for cols in column_chunks(wd):
        value = dot(rows[...], wd[:, cols]).astype(BF16)
        keep_ref[:, cols] = value[:count]
        send_ref[:, cols] = value[count:]


def pieces_kernel(keep, core, far, p0, p1, p2, p3):
    expert, outer, inner, dp = seat()
    small = p0.shape[0]
    for s, p in enumerate((p0, p1, p2, p3)):
        rows = aligned((outer + s) & 3, small)
        total = keep[rows, :].astype(F32) + core[rows, :].astype(F32)
        p[...] = (total + far[rows, :].astype(F32)).astype(BF16)


def tail_kernel(own, m0, o0, o1, o2, o3, gain, stream_ref, normed_ref):
    expert, outer, inner, dp = seat()
    half = m0.shape[1]
    for at, pieces in ((dp, (m0,)), (1 - dp, (o0, o1, o2, o3))):
        cols = aligned(at, half)
        mixture = pieces[0][...].astype(F32)
        for piece in pieces[1:]:
            mixture = mixture + piece[...].astype(F32)
        stream_ref[:, cols] = (own[:, cols].astype(F32) + mixture).astype(BF16)
    normed_ref[...] = rms_scale(stream_ref[...].astype(F32), gain[...]).astype(BF16)


def body_paired(
    attn,
    resid,
    w_out,
    gain_post,
    route_ids,
    route_logits,
    live_count,
    w_gate_up,
    w_down,
    gain_final,
):
    rows_here = resid.shape[1]
    model_width = resid.shape[2]
    expert_count = lax.axis_size("expert")
    hidden = w_down.shape[1]
    half_width = w_down.shape[2]
    quarter = model_width // 4
    vmem, smem = whole_vmem(), whole_smem()

    def shape_of(*shape, dtype=BF16):
        return jax.ShapeDtypeStruct(shape, dtype)

    def call(kernel, name, mib, outs, *args, scratch=(), first=vmem):
        return pl.pallas_call(
            kernel,
            out_shape=outs,
            in_specs=[first] + [vmem] * (len(args) - 1),
            out_specs=tuple(vmem for _ in outs),
            scratch_shapes=list(scratch),
            compiler_params=kernel_params(mib),
            cost_estimate=small_cost(),
            name=name,
        )(*args)

    def swap_dp(x):
        return lax.ppermute(x, "dp", [(0, 1), (1, 0)])

    def shift_outer(x, s):
        return lax.ppermute(
            x, "expert", [(i, (i + 4 * s) % expert_count) for i in range(expert_count)]
        )

    def cross_outer(x, s):
        return lax.ppermute(
            x,
            ("dp", "expert"),
            [
                (d * expert_count + i, (1 - d) * expert_count + (i + 4 * s) % expert_count)
                for d in range(2)
                for i in range(expert_count)
            ],
        )

    def swap_inner(x, j):
        return lax.ppermute(x, "expert", [(i, i ^ j) for i in range(expert_count)])

    def swap_outer(x, s):
        return lax.ppermute(x, "expert", [(i, i ^ (4 * s)) for i in range(expert_count)])

    def after(x, *results):
        return lax.optimization_barrier((x, *results))[0]

    def weight_piece(i):
        return pl.pallas_call(
            functools.partial(piece_kernel, i),
            out_shape=shape_of(half_width, hidden),
            in_specs=[pl.BlockSpec(memory_space=pl.ANY)],
            out_specs=vmem,
            scratch_shapes=[pltpu.SemaphoreType.DMA((2,))],
            compiler_params=kernel_params(8),
            cost_estimate=small_cost(),
            name="weight_piece",
        )(w_gate_up[0])

    piece = shape_of(rows_here, quarter)
    r_own, r_1, r_23 = call(
        cut_kernel, "cut_resid", 4, (piece, piece, shape_of(2 * rows_here, quarter)), resid[0]
    )
    (share,) = call(
        share_kernel,
        "share",
        4,
        (shape_of(expert_count, quarter),),
        live_count,
        route_ids[0],
        route_logits[0],
        first=smem,
    )
    cut_width = hidden // 2
    early_piece, late_piece = (weight_piece(i) for i in range(2))
    gate_up_early = swap_dp(early_piece)
    a = [attn[0], swap_outer(attn[0], 1), swap_outer(attn[0], 2)]
    w_x = swap_inner(w_out, 2)
    r_2 = swap_outer(r_23, 2)
    a.append(swap_outer(after(a[2], a[1], r_2), 1))
    w_c = swap_inner(after(w_out, w_x), 1)
    w_cx = swap_inner(w_x, 1)
    r_13 = swap_outer(jnp.concatenate([r_1, r_2[rows_here:]], axis=0), 1)

    product = shape_of(4 * rows_here, quarter)
    keep, send = call(
        proj_kernel,
        "projection",
        8,
        (product, product),
        *a,
        w_out,
        w_c,
        w_x,
        w_cx,
        scratch=(
            pltpu.VMEM((8 * rows_here, attn.shape[2]), BF16),
            pltpu.VMEM((8 * rows_here, quarter), BF16),
        ),
    )
    arrived = swap_dp(after(send, gate_up_early, late_piece, r_13, share))
    gate_up_late = swap_dp(after(late_piece, arrived))
    (block,) = call(
        stream_kernel,
        "stream",
        4,
        (shape_of(4 * rows_here + expert_count, quarter),),
        keep,
        arrived,
        r_own,
        r_13,
        r_2,
        share,
    )

    group, stream_own = call(
        norm_kernel,
        "norm",
        8,
        (
            shape_of(4 * rows_here, model_width + 128),
            shape_of(rows_here, model_width),
        ),
        block,
        *(shift_outer(block, s) for s in (1, 2, 3)),
        gain_post[None],
    )
    group_x = swap_inner(group, 2)
    group_c = swap_inner(group, 1)
    group_cx = swap_inner(group_x, 1)

    row_total = 16 * rows_here
    half_rows = row_total // 2
    inner_first, part, other_rows, share_rows = call(
        first_gate_kernel,
        "first_gate_up",
        24,
        (
            shape_of(row_total, cut_width),
            shape_of(row_total, hidden, dtype=F32),
            shape_of(row_total, half_width),
            shape_of(row_total, 128, dtype=F32),
        ),
        group_x,
        group_cx,
        group,
        group_c,
        w_gate_up[0],
        gate_up_early,
        scratch=(pltpu.VMEM((row_total, half_width), BF16),),
    )
    inner_half = shape_of(half_rows, hidden)
    inner_far, inner_near = call(
        last_gate_kernel,
        "last_gate_up",
        16,
        (inner_half, inner_half),
        inner_first,
        part,
        other_rows,
        share_rows,
        gate_up_late,
    )
    far_other = swap_dp(inner_far)
    near_other = swap_dp(inner_near)

    count = row_total // 4
    quarter_out = shape_of(count, half_width)

    def down(rows):
        return call(
            down_kernel,
            "down",
            12,
            (quarter_out, quarter_out),
            rows,
            w_down[0],
        )

    def add(x, y):
        return (x.astype(F32) + y.astype(F32)).astype(BF16)

    def pieces(keep, core, far):
        out = shape_of(rows_here, half_width)
        return call(pieces_kernel, "pieces", 4, (out, out, out, out), keep, core, far)

    keep_far, keep_near, send_far, send_near = call(
        down_both_kernel,
        "down_both",
        16,
        (quarter_out, quarter_out, quarter_out, quarter_out),
        inner_far,
        inner_near,
        w_down[0],
    )
    far = swap_inner(add(keep_far, swap_inner(send_far, 1)), 2)
    ready = far
    outer_groups = [[i + 4 * z for z in range(4)] for i in range(4)]
    total = add(add(keep_near, swap_inner(send_near, 1)), far).reshape(4, rows_here, half_width)
    mine = [lax.psum_scatter(total, "expert", scatter_dimension=0, axis_index_groups=outer_groups)]

    keep_far, send_far = down(after(far_other, ready))
    far = swap_inner(add(keep_far, swap_inner(send_far, 1)), 2)
    keep_near, send_near = down(after(near_other, far))
    cut = pieces(keep_near, swap_inner(send_near, 1), far)
    others = [cross_outer(cut[s], s) for s in range(4)]

    out = shape_of(rows_here, model_width)
    stream_out, normed_out = call(
        tail_kernel, "closing", 8, (out, out), stream_own, *mine, *others, gain_final[None]
    )
    return (stream_out[None], normed_out[None])


def solution(mesh):
    placed = (
        P("expert", None, "dp"),
        P("expert", "dp", None),
        P("dp", "expert"),
        P(),
        P("expert", "dp", None),
        P("expert", "dp", None),
        P("expert", "dp"),
        P("expert", "dp", None),
        P("expert", None, "dp"),
        P(),
    )
    paired = mesh.shape["dp"] == 2 and mesh.shape["expert"] == 16
    return jax.shard_map(
        body_paired if paired else body_general,
        mesh=mesh,
        in_specs=placed,
        out_specs=(P("expert", "dp", None), P("expert", "dp", None)),
        check_vma=False,
    )
```

```python
import functools
import math

import jax
import jax.numpy as jnp
from jax import lax
from jax.experimental import pallas as pl
from jax.experimental.pallas import tpu as pltpu
from jax.sharding import PartitionSpec as P


def rms_scale(values, gain):
    return values * lax.rsqrt(jnp.mean(values * values, axis=-1, keepdims=True) + 1e-06) * gain


def swiglu_rows(rows_in, gate_up, down, hidden_units):
    both = jnp.dot(rows_in, gate_up, preferred_element_type=jnp.float32)
    inner = (jax.nn.silu(both[:, :hidden_units]) * both[:, hidden_units:]).astype(jnp.bfloat16)
    return jnp.dot(inner, down, preferred_element_type=jnp.float32).astype(jnp.bfloat16)


def body_general(
    attn,
    resid,
    w_out,
    gain_post,
    route_ids,
    route_logits,
    live_count,
    w_gate_up,
    w_down,
    gain_final,
):
    rows_here = resid.shape[1]
    model_width = resid.shape[2]
    top_count = route_ids.shape[2]
    dp_count = lax.axis_size("dp")
    expert_count = lax.axis_size("expert")
    hidden_units = w_down.shape[1]
    capacity = dp_count * max(1, 2 * rows_here * top_count // (expert_count * dp_count))
    slot_count = expert_count * capacity
    flat_attn = attn[0]
    partial_out = jnp.dot(
        flat_attn,
        lax.all_gather(w_out, "expert", axis=1, tiled=True),
        preferred_element_type=jnp.float32,
    )
    projected = lax.psum_scatter(
        partial_out.astype(jnp.bfloat16), "dp", scatter_dimension=0, tiled=True
    ).astype(jnp.float32)
    stream_in = (resid[0].astype(jnp.float32) + projected).astype(jnp.bfloat16)
    stream_float = stream_in.astype(jnp.float32)
    normed_in = rms_scale(stream_float, gain_post).astype(jnp.bfloat16)
    probs = jax.nn.softmax(route_logits[0], axis=-1).astype(jnp.bfloat16)
    alive = jnp.arange(rows_here, dtype=jnp.int32) < live_count[0, 0]
    expert_of = route_ids[0].reshape(-1)
    route_alive = jnp.repeat(alive, top_count)
    onehot = (
        (expert_of[:, None] == jnp.arange(expert_count, dtype=jnp.int32)[None, :])
        & route_alive[:, None]
    ).astype(jnp.int32)
    earlier = jnp.sum((jnp.cumsum(onehot, axis=0) - onehot) * onehot, axis=1)
    target = expert_of * capacity + earlier
    match = (target[:, None] == jnp.arange(slot_count, dtype=jnp.int32)[None, :]) & route_alive[
        :, None
    ]
    placed = match.reshape(rows_here, top_count, slot_count)
    gather_matrix = jnp.any(placed, axis=1).astype(jnp.bfloat16)
    send_rows = lax.dot_general(
        gather_matrix, normed_in, (((0,), (0,)), ((), ())), preferred_element_type=jnp.float32
    ).astype(jnp.bfloat16)
    send_flags = jnp.sum(gather_matrix.astype(jnp.float32), axis=0).astype(jnp.bfloat16)
    combine_matrix = jnp.sum(
        jnp.where(placed, probs.astype(jnp.float32)[:, :, None], jnp.float32(0.0)), axis=1
    ).astype(jnp.bfloat16)
    arrived_rows, arrived_flags = (
        lax.all_to_all(
            send_rows.reshape(expert_count, capacity, model_width),
            "expert",
            split_axis=0,
            concat_axis=0,
            tiled=True,
        ),
        lax.all_to_all(
            send_flags.reshape(expert_count, capacity),
            "expert",
            split_axis=0,
            concat_axis=0,
            tiled=True,
        ),
    )
    arrived = arrived_rows.reshape(slot_count, model_width)
    flags = arrived_flags.reshape(slot_count)
    gate_up_full, down_full = (
        lax.all_gather(w_gate_up, "dp", axis=1, tiled=True),
        lax.all_gather(w_down, "dp", axis=2, tiled=True),
    )
    live_slot = (flags > 0.5).astype(jnp.int32)
    order = jnp.argsort(1 - live_slot, stable=True)
    live_total = jnp.sum(live_slot)
    packed = arrived[order]
    block_len = math.gcd(slot_count, 128)
    block_total = (live_total + block_len - 1) // block_len

    def run_block(index, outputs):
        begin = index * block_len
        rows_in = lax.dynamic_slice_in_dim(packed, begin, block_len, 0)
        block_out = swiglu_rows(rows_in, gate_up_full[0], down_full[0], hidden_units)
        return lax.dynamic_update_slice_in_dim(outputs, block_out, begin, 0)

    packed_out = lax.fori_loop(
        0, block_total, run_block, jnp.zeros((slot_count, model_width), jnp.bfloat16)
    )
    position = (
        jnp.zeros((slot_count,), jnp.int32).at[order].set(jnp.arange(slot_count, dtype=jnp.int32))
    )
    results = packed_out[position]
    returned = lax.all_to_all(
        results.reshape(expert_count, capacity, model_width),
        "expert",
        split_axis=0,
        concat_axis=0,
        tiled=True,
    )
    returned = returned.reshape(slot_count, model_width)
    mixture = jnp.dot(combine_matrix, returned, preferred_element_type=jnp.float32)
    stream_out = (stream_float + mixture).astype(jnp.bfloat16)
    normed_out = rms_scale(stream_out.astype(jnp.float32), gain_final).astype(jnp.bfloat16)
    return (stream_out[None], normed_out[None])


MIB = 1024 * 1024
BF16, F32 = jnp.bfloat16, jnp.float32


def whole_vmem():
    return pl.BlockSpec(memory_space=pltpu.VMEM)


def whole_smem():
    return pl.BlockSpec(memory_space=pltpu.SMEM)


def fixed(*shape):
    return pl.BlockSpec(shape, lambda i: (0,) * len(shape))


def dot(a, b):
    return jnp.dot(a, b, preferred_element_type=F32)


def small_cost():
    return pl.CostEstimate(flops=1, bytes_accessed=1, transcendentals=0)


def kernel_params(mib):
    return pltpu.CompilerParams(vmem_limit_bytes=mib * MIB)


def seat():
    expert = lax.axis_index("expert")
    return expert, lax.shift_right_logical(expert, 2), expert & 3, lax.axis_index("dp")


def aligned(index, step):
    return pl.ds(pl.multiple_of(index * step, step), step)


def cut_kernel(resid, r0, r1, r23):
    expert, outer, inner, dp = seat()
    rows, lanes = r0.shape
    r0[...] = resid[:, aligned(outer, lanes)]
    r1[...] = resid[:, aligned(outer ^ 1, lanes)]
    for i in range(2):
        r23[i * rows : (i + 1) * rows, :] = resid[:, aligned(outer ^ (2 + i), lanes)]


def share_kernel(live, ids, logits, share_ref):
    expert, outer, inner, dp = seat()
    rows, top = ids.shape
    experts, lanes = share_ref.shape
    value = logits[...]
    value = jnp.exp(value - jnp.max(value, axis=1, keepdims=True))
    probs = (value / jnp.sum(value, axis=1, keepdims=True)).astype(BF16).astype(F32)
    probs = jnp.where(lax.broadcasted_iota(jnp.int32, (rows, top), 0) < live[0, 0], probs, 0.0)
    names = lax.broadcasted_iota(jnp.int32, (rows, experts), 1)
    table = jnp.zeros((rows, experts), F32)
    for k in range(top):
        table = table + jnp.where(ids[:, k : k + 1] == names, probs[:, k : k + 1], 0.0)
    spots = lax.broadcasted_iota(jnp.int32, (rows, lanes), 1) - outer * rows
    spots = (spots == lax.broadcasted_iota(jnp.int32, (rows, lanes), 0)).astype(F32).astype(BF16)
    share_ref[...] = lax.dot_general(
        table.astype(BF16), spots, (((0,), (0,)), ((), ())), preferred_element_type=F32
    ).astype(BF16)


def proj_kernel(a0, a1, a2, a3, w0, w1, w2, w3, keep_ref, send_ref, rows, part):
    expert, outer, inner, dp = seat()
    full = a0.shape[0]
    half = full // 2
    block = w0.shape[1]
    for s, a in enumerate((a0, a1, a2, a3)):
        rows[aligned(outer ^ s, full), :] = a[...]
    for j, w in enumerate((w0, w1, w2, w3)):
        part[:, aligned(inner ^ j, block)] = dot(rows[...], w[...]).astype(BF16)
    for spot in range(4):
        keep_ref[spot * half : (spot + 1) * half, :] = part[aligned(2 * spot + dp, half), :]
        send_ref[spot * half : (spot + 1) * half, :] = part[aligned(2 * spot + 1 - dp, half), :]


def stream_kernel(keep, arrived, r0, r13, r2, share, block_ref):
    expert, outer, inner, dp = seat()
    count = keep.shape[0]
    small = r0.shape[0]
    for s, r in enumerate((r0[...], r13[0:small, :], r2[0:small, :], r13[small:, :])):
        rows = aligned(outer ^ s, small)
        product = keep[rows, :].astype(F32) + arrived[rows, :].astype(F32)
        block_ref[rows, :] = (r.astype(F32) + product).astype(BF16)
    block_ref[count:, :] = share[...]


def piece_kernel(starts, weights, out, semaphores):
    width = out.shape[1] // 2
    copies = [
        pltpu.make_async_copy(
            weights.at[:, pl.ds(starts[i], width)],
            out.at[:, pl.ds(i * width, width)],
            semaphores.at[i],
        )
        for i in range(2)
    ]
    for copy in copies:
        copy.start()
    for copy in copies:
        copy.wait()


def swiglu(gate, up, share):
    return (gate / (1.0 + jnp.exp(-gate)) * up * share).astype(BF16)


def norm_kernel(b0, b1, b2, b3, gain, group_ref, own_ref):
    expert, outer, inner, dp = seat()
    count = group_ref.shape[0]
    width = b0.shape[1]
    experts = b0.shape[0] - count
    small = own_ref.shape[0]
    square = jnp.zeros((count, 1), F32)
    share = jnp.zeros((experts, count), F32)
    for s, b in enumerate((b0, b1, b2, b3)):
        value = b[0:count, :]
        group_ref[:, aligned((outer + 4 - s) & 3, width)] = value
        value = value.astype(F32)
        square = square + jnp.sum(value * value, axis=1, keepdims=True)
        share = share + b[count : count + experts, 0:count].astype(F32)
    own_ref[...] = group_ref[aligned(outer, small), 0 : 4 * width]
    scale = lax.rsqrt(square / (4 * width) + 1e-06)
    for s in range(4):
        cols = slice(s * width, (s + 1) * width)
        value = group_ref[:, cols].astype(F32)
        group_ref[:, cols] = (value * scale * gain[:, cols]).astype(BF16)
    lanes = (experts, 128)
    spread = lax.broadcasted_iota(jnp.int32, lanes, 0) == lax.broadcasted_iota(jnp.int32, lanes, 1)
    group_ref[:, 4 * width :] = lax.dot_general(
        share.astype(BF16),
        spread.astype(F32).astype(BF16),
        (((0,), (0,)), ((), ())),
        preferred_element_type=F32,
    ).astype(BF16)


def first_gate_kernel(
    group_x, group_cx, group, group_c, own, early, inner_ref, part_ref, other_ref, share_ref, mine_ref
):
    expert, outer, inner, dp = seat()
    count = group.shape[0]
    half = other_ref.shape[1]
    cut = inner_ref.shape[1]
    for j, g in enumerate((group_x, group_cx, group, group_c)):
        rows = slice(j * count, (j + 1) * count)
        mine_ref[rows, :] = g[:, aligned(dp, half)]
        other_ref[rows, :] = g[:, aligned(1 - dp, half)]
        share = g[:, 2 * half : 2 * half + 128].astype(F32)
        picked = lax.broadcasted_iota(jnp.int32, share.shape, 1) == expert
        share = jnp.sum(jnp.where(picked, share, 0.0), axis=1, keepdims=True)
        share_ref[rows, :] = jnp.broadcast_to(share, (count, 128))
    mine, other = mine_ref[...], other_ref[...]
    gate = dot(mine, own[:, 0:cut]) + dot(other, early[:, 0:cut])
    up = dot(mine, own[:, 2 * cut : 3 * cut]) + dot(other, early[:, cut : 2 * cut])
    inner_ref[...] = swiglu(gate, up, share_ref[:, 0:1])
    part_ref[:, 0:cut] = dot(mine, own[:, cut : 2 * cut])
    part_ref[:, cut : 2 * cut] = dot(mine, own[:, 3 * cut : 4 * cut])


def last_gate_kernel(first, part, other, share, *refs):
    *late, far_ref, near_ref = refs
    cut = first.shape[1]
    half = far_ref.shape[0]
    far_ref[:, 0:cut] = first[0:half, :]
    near_ref[:, 0:cut] = first[half:, :]
    at = 0
    for piece in late:
        size = piece.shape[1] // 2
        gate = part[:, at : at + size] + dot(other[...], piece[:, 0:size])
        up = part[:, cut + at : cut + at + size] + dot(other[...], piece[:, size : 2 * size])
        value = swiglu(gate, up, share[:, 0:1])
        cols = slice(cut + at, cut + at + size)
        far_ref[:, cols] = value[:half]
        near_ref[:, cols] = value[half:]
        at += size


def column_chunks(wd):
    return [slice(at, at + 256) for at in range(0, wd.shape[1], 256)]


def down_both_kernel(far, near, wd, keep_far, keep_near, far_a, far_b, near_a, near_b):
    down_kernel(far, wd, keep_far, far_a, far_b)
    down_kernel(near, wd, keep_near, near_a, near_b)


def down_kernel(rows, wd, keep_ref, send_a, send_b):
    count, side = send_a.shape
    for at in range(0, wd.shape[1], 256):
        value = dot(rows[...], wd[:, at : at + 256]).astype(BF16)
        keep_ref[:, at : at + 256] = value[:count]
        send = send_a if at < side else send_b
        send[:, at % side : at % side + 256] = value[count:]


def fold_kernel(keep, core_a, core_b, out):
    side = core_a.shape[1]
    for i, core in enumerate((core_a, core_b)):
        cols = slice(i * side, (i + 1) * side)
        out[:, cols] = (keep[:, cols].astype(F32) + core[...].astype(F32)).astype(BF16)


def pieces_kernel(keep, core_a, core_b, far, p0, p1, p2, p3):
    expert, outer, inner, dp = seat()
    small = p0.shape[0]
    for s, p in enumerate((p0, p1, p2, p3)):
        rows = aligned((outer + s) & 3, small)
        side = core_a.shape[1]
        for i, core in enumerate((core_a, core_b)):
            cols = slice(i * side, (i + 1) * side)
            total = keep[rows, cols].astype(F32) + core[rows, :].astype(F32)
            p[:, cols] = (total + far[rows, cols].astype(F32)).astype(BF16)


def tail_kernel(own, m0, m1, m2, m3, o0, o1, o2, o3, gain, stream_ref, normed_ref):
    expert, outer, inner, dp = seat()
    half = m0.shape[1]
    for at, pieces in ((dp, (m0, m1, m2, m3)), (1 - dp, (o0, o1, o2, o3))):
        cols = aligned(at, half)
        mixture = pieces[0][...].astype(F32)
        for piece in pieces[1:]:
            mixture = mixture + piece[...].astype(F32)
        stream_ref[:, cols] = (own[:, cols].astype(F32) + mixture).astype(BF16)
    normed_ref[...] = rms_scale(stream_ref[...].astype(F32), gain[...]).astype(BF16)


def body_paired(
    attn,
    resid,
    w_out,
    gain_post,
    route_ids,
    route_logits,
    live_count,
    w_gate_up,
    w_down,
    gain_final,
):
    rows_here = resid.shape[1]
    model_width = resid.shape[2]
    expert_count = lax.axis_size("expert")
    hidden = w_down.shape[1]
    half_width = w_down.shape[2]
    quarter = model_width // 4
    vmem, smem = whole_vmem(), whole_smem()

    def shape_of(*shape, dtype=BF16):
        return jax.ShapeDtypeStruct(shape, dtype)

    def call(kernel, name, mib, outs, *args, scratch=(), first=vmem):
        return pl.pallas_call(
            kernel,
            out_shape=outs,
            in_specs=[first] + [vmem] * (len(args) - 1),
            out_specs=tuple(vmem for _ in outs),
            scratch_shapes=list(scratch),
            compiler_params=kernel_params(mib),
            cost_estimate=small_cost(),
            name=name,
        )(*args)

    def swap_dp(x):
        return lax.ppermute(x, "dp", [(0, 1), (1, 0)])

    def shift_outer(x, s):
        return lax.ppermute(
            x, "expert", [(i, (i + 4 * s) % expert_count) for i in range(expert_count)]
        )

    def cross_outer(x, s):
        return lax.ppermute(
            x,
            ("dp", "expert"),
            [
                (d * expert_count + i, (1 - d) * expert_count + (i + 4 * s) % expert_count)
                for d in range(2)
                for i in range(expert_count)
            ],
        )

    def swap_inner(x, j):
        return lax.ppermute(x, "expert", [(i, i ^ j) for i in range(expert_count)])

    def swap_outer(x, s):
        return lax.ppermute(x, "expert", [(i, i ^ (4 * s)) for i in range(expert_count)])

    def after(x, *results):
        return lax.optimization_barrier((x, *results))[0]

    def weight_piece(first, size):
        return pl.pallas_call(
            functools.partial(piece_kernel, (first, hidden + first)),
            out_shape=shape_of(half_width, 2 * size),
            in_specs=[pl.BlockSpec(memory_space=pltpu.HBM)],
            out_specs=vmem,
            scratch_shapes=[pltpu.SemaphoreType.DMA((2,))],
            compiler_params=kernel_params(8),
            cost_estimate=small_cost(),
            name="weight_piece",
        )(w_gate_up[0])

    piece = shape_of(rows_here, quarter)
    r_own, r_1, r_23 = call(
        cut_kernel, "cut_resid", 4, (piece, piece, shape_of(2 * rows_here, quarter)), resid[0]
    )
    (share,) = call(
        share_kernel,
        "share",
        4,
        (shape_of(expert_count, quarter),),
        live_count,
        route_ids[0],
        route_logits[0],
        first=smem,
    )
    cut_width = hidden // 2
    early_piece = weight_piece(0, cut_width)
    late_sizes = (cut_width * 384 // 384,)
    late_pieces = [
        weight_piece(cut_width + sum(late_sizes[:i]), size) for i, size in enumerate(late_sizes)
    ]
    gate_up_early = swap_dp(early_piece)
    a = [attn[0], swap_outer(attn[0], 1), swap_outer(attn[0], 2)]
    w_x = swap_inner(w_out, 2)
    r_2 = swap_outer(r_23, 2)
    a.append(swap_outer(after(a[2], a[1]), 1))
    w_c = swap_inner(after(w_out, w_x), 1)
    w_cx = swap_inner(w_x, 1)
    r_13 = swap_outer(jnp.concatenate([r_1, r_2[rows_here:]], axis=0), 1)

    product = shape_of(4 * rows_here, quarter)
    keep, send = call(
        proj_kernel,
        "projection",
        8,
        (product, product),
        *a,
        w_out,
        w_c,
        w_x,
        w_cx,
        scratch=(
            pltpu.VMEM((8 * rows_here, attn.shape[2]), BF16),
            pltpu.VMEM((8 * rows_here, quarter), BF16),
        ),
    )
    arrived = swap_dp(after(send, gate_up_early, r_13, share, *late_pieces))
    gate_up_late = [swap_dp(after(piece, arrived)) for piece in late_pieces]
    (block,) = call(
        stream_kernel,
        "stream",
        4,
        (shape_of(4 * rows_here + expert_count, quarter),),
        keep,
        arrived,
        r_own,
        r_13,
        r_2,
        share,
    )

    def norm(b0, b1, b2, b3):
        outs = (shape_of(4 * rows_here, model_width + 128), shape_of(rows_here, model_width))
        return call(norm_kernel, "norm", 8, outs, b0, b1, b2, b3, gain_post[None])

    blocks = [block] + [shift_outer(block, s) for s in (1, 2, 3)]
    group, stream_own = norm(*blocks)
    blocks_x = [swap_inner(b, 2) for b in blocks]
    group_x, unused = norm(*blocks_x)
    group_c = swap_inner(group, 1)
    group_cx = swap_inner(group_x, 1)

    row_total = 16 * rows_here
    half_rows = row_total // 2
    inner_first, part, other_rows, share_rows = call(
        first_gate_kernel,
        "first_gate_up",
        24,
        (
            shape_of(row_total, cut_width),
            shape_of(row_total, hidden, dtype=F32),
            shape_of(row_total, half_width),
            shape_of(row_total, 128, dtype=F32),
        ),
        group_x,
        group_cx,
        group,
        group_c,
        w_gate_up[0],
        gate_up_early,
        scratch=(pltpu.VMEM((row_total, half_width), BF16),),
    )
    inner_half = shape_of(half_rows, hidden)
    inner_far, inner_near = call(
        last_gate_kernel,
        "last_gate_up",
        16,
        (inner_half, inner_half),
        inner_first,
        part,
        other_rows,
        share_rows,
        *gate_up_late,
    )
    far_other = swap_dp(inner_far)
    near_other = swap_dp(inner_near)

    count = row_total // 4
    quarter_out = shape_of(count, half_width)
    half_out = shape_of(count, half_width // 2)

    def down(rows):
        return call(
            down_kernel,
            "down",
            12,
            (quarter_out, half_out, half_out),
            rows,
            w_down[0],
        )

    def add(x, y):
        return (x.astype(F32) + y.astype(F32)).astype(BF16)

    def swap_cores(halves):
        return [swap_inner(half, 1) for half in halves]

    def fold(keep, halves):
        return call(fold_kernel, "fold", 4, (quarter_out,), keep, *halves)[0]

    def pieces(*args):
        out = shape_of(rows_here, half_width)
        return call(pieces_kernel, "pieces", 4, (out, out, out, out), *args)

    keep_far, keep_near, *send = call(
        down_both_kernel,
        "down_both",
        16,
        (quarter_out, quarter_out, half_out, half_out, half_out, half_out),
        inner_far,
        inner_near,
        w_down[0],
    )
    far = swap_inner(fold(keep_far, swap_cores(send[:2])), 2)
    ready = far
    cut = pieces(keep_near, *swap_cores(send[2:]), far)
    mine = [cut[0]] + [shift_outer(cut[s], s) for s in (1, 2, 3)]

    keep_far, *send = down(after(far_other, ready))
    far = swap_inner(fold(keep_far, swap_cores(send)), 2)
    keep_near, *send = down(after(near_other, *mine[1:]))
    cut = pieces(keep_near, *swap_cores(send), far)
    others = [cross_outer(cut[s], s) for s in range(4)]

    out = shape_of(rows_here, model_width)
    stream_out, normed_out = call(
        tail_kernel, "closing", 8, (out, out), stream_own, *mine, *others, gain_final[None]
    )
    return (stream_out[None], normed_out[None])


def solution(mesh):
    placed = (
        P("expert", None, "dp"),
        P("expert", "dp", None),
        P("dp", "expert"),
        P(),
        P("expert", "dp", None),
        P("expert", "dp", None),
        P("expert", "dp"),
        P("expert", "dp", None),
        P("expert", None, "dp"),
        P(),
    )
    paired = mesh.shape["dp"] == 2 and mesh.shape["expert"] == 16
    return jax.shard_map(
        body_paired if paired else body_general,
        mesh=mesh,
        in_specs=placed,
        out_specs=(P("expert", "dp", None), P("expert", "dp", None)),
        check_vma=False,
    )
```

```python
import functools
import math

import jax
import jax.numpy as jnp
from jax import lax
from jax.experimental import pallas as pl
from jax.experimental.pallas import tpu as pltpu
from jax.sharding import PartitionSpec as P


def rms_scale(values, gain):
    return values * lax.rsqrt(jnp.mean(values * values, axis=-1, keepdims=True) + 1e-06) * gain


def swiglu_rows(rows_in, gate_up, down, hidden_units):
    both = jnp.dot(rows_in, gate_up, preferred_element_type=jnp.float32)
    inner = (jax.nn.silu(both[:, :hidden_units]) * both[:, hidden_units:]).astype(jnp.bfloat16)
    return jnp.dot(inner, down, preferred_element_type=jnp.float32).astype(jnp.bfloat16)


def body_general(
    attn,
    resid,
    w_out,
    gain_post,
    route_ids,
    route_logits,
    live_count,
    w_gate_up,
    w_down,
    gain_final,
):
    rows_here = resid.shape[1]
    model_width = resid.shape[2]
    top_count = route_ids.shape[2]
    dp_count = lax.axis_size("dp")
    expert_count = lax.axis_size("expert")
    hidden_units = w_down.shape[1]
    capacity = dp_count * max(1, 2 * rows_here * top_count // (expert_count * dp_count))
    slot_count = expert_count * capacity
    flat_attn = attn[0]
    partial_out = jnp.dot(
        flat_attn,
        lax.all_gather(w_out, "expert", axis=1, tiled=True),
        preferred_element_type=jnp.float32,
    )
    projected = lax.psum_scatter(
        partial_out.astype(jnp.bfloat16), "dp", scatter_dimension=0, tiled=True
    ).astype(jnp.float32)
    stream_in = (resid[0].astype(jnp.float32) + projected).astype(jnp.bfloat16)
    stream_float = stream_in.astype(jnp.float32)
    normed_in = rms_scale(stream_float, gain_post).astype(jnp.bfloat16)
    probs = jax.nn.softmax(route_logits[0], axis=-1).astype(jnp.bfloat16)
    alive = jnp.arange(rows_here, dtype=jnp.int32) < live_count[0, 0]
    expert_of = route_ids[0].reshape(-1)
    route_alive = jnp.repeat(alive, top_count)
    onehot = (
        (expert_of[:, None] == jnp.arange(expert_count, dtype=jnp.int32)[None, :])
        & route_alive[:, None]
    ).astype(jnp.int32)
    earlier = jnp.sum((jnp.cumsum(onehot, axis=0) - onehot) * onehot, axis=1)
    target = expert_of * capacity + earlier
    match = (target[:, None] == jnp.arange(slot_count, dtype=jnp.int32)[None, :]) & route_alive[
        :, None
    ]
    placed = match.reshape(rows_here, top_count, slot_count)
    gather_matrix = jnp.any(placed, axis=1).astype(jnp.bfloat16)
    send_rows = lax.dot_general(
        gather_matrix, normed_in, (((0,), (0,)), ((), ())), preferred_element_type=jnp.float32
    ).astype(jnp.bfloat16)
    send_flags = jnp.sum(gather_matrix.astype(jnp.float32), axis=0).astype(jnp.bfloat16)
    combine_matrix = jnp.sum(
        jnp.where(placed, probs.astype(jnp.float32)[:, :, None], jnp.float32(0.0)), axis=1
    ).astype(jnp.bfloat16)
    arrived_rows, arrived_flags = (
        lax.all_to_all(
            send_rows.reshape(expert_count, capacity, model_width),
            "expert",
            split_axis=0,
            concat_axis=0,
            tiled=True,
        ),
        lax.all_to_all(
            send_flags.reshape(expert_count, capacity),
            "expert",
            split_axis=0,
            concat_axis=0,
            tiled=True,
        ),
    )
    arrived = arrived_rows.reshape(slot_count, model_width)
    flags = arrived_flags.reshape(slot_count)
    gate_up_full, down_full = (
        lax.all_gather(w_gate_up, "dp", axis=1, tiled=True),
        lax.all_gather(w_down, "dp", axis=2, tiled=True),
    )
    live_slot = (flags > 0.5).astype(jnp.int32)
    order = jnp.argsort(1 - live_slot, stable=True)
    live_total = jnp.sum(live_slot)
    packed = arrived[order]
    block_len = math.gcd(slot_count, 128)
    block_total = (live_total + block_len - 1) // block_len

    def run_block(index, outputs):
        begin = index * block_len
        rows_in = lax.dynamic_slice_in_dim(packed, begin, block_len, 0)
        block_out = swiglu_rows(rows_in, gate_up_full[0], down_full[0], hidden_units)
        return lax.dynamic_update_slice_in_dim(outputs, block_out, begin, 0)

    packed_out = lax.fori_loop(
        0, block_total, run_block, jnp.zeros((slot_count, model_width), jnp.bfloat16)
    )
    position = (
        jnp.zeros((slot_count,), jnp.int32).at[order].set(jnp.arange(slot_count, dtype=jnp.int32))
    )
    results = packed_out[position]
    returned = lax.all_to_all(
        results.reshape(expert_count, capacity, model_width),
        "expert",
        split_axis=0,
        concat_axis=0,
        tiled=True,
    )
    returned = returned.reshape(slot_count, model_width)
    mixture = jnp.dot(combine_matrix, returned, preferred_element_type=jnp.float32)
    stream_out = (stream_float + mixture).astype(jnp.bfloat16)
    normed_out = rms_scale(stream_out.astype(jnp.float32), gain_final).astype(jnp.bfloat16)
    return (stream_out[None], normed_out[None])


MIB = 1024 * 1024
BF16, F32 = jnp.bfloat16, jnp.float32


def whole_vmem():
    return pl.BlockSpec(memory_space=pltpu.VMEM)


def whole_smem():
    return pl.BlockSpec(memory_space=pltpu.SMEM)


def fixed(*shape):
    return pl.BlockSpec(shape, lambda i: (0,) * len(shape))


def dot(a, b):
    return jnp.dot(a, b, preferred_element_type=F32)


def small_cost():
    return pl.CostEstimate(flops=1, bytes_accessed=1, transcendentals=0)


def kernel_params(mib):
    return pltpu.CompilerParams(vmem_limit_bytes=mib * MIB)


def seat():
    expert = lax.axis_index("expert")
    return expert, lax.shift_right_logical(expert, 2), expert & 3, lax.axis_index("dp")


def aligned(index, step):
    return pl.ds(pl.multiple_of(index * step, step), step)


def cut_kernel(resid, r0, r1, r23):
    expert, outer, inner, dp = seat()
    rows, lanes = r0.shape
    r0[...] = resid[:, aligned(outer, lanes)]
    r1[...] = resid[:, aligned(outer ^ 1, lanes)]
    for i in range(2):
        r23[i * rows : (i + 1) * rows, :] = resid[:, aligned(outer ^ (2 + i), lanes)]


def share_kernel(live, ids, logits, share_ref):
    expert, outer, inner, dp = seat()
    rows, top = ids.shape
    experts, lanes = share_ref.shape
    value = logits[...]
    value = jnp.exp(value - jnp.max(value, axis=1, keepdims=True))
    probs = (value / jnp.sum(value, axis=1, keepdims=True)).astype(BF16).astype(F32)
    probs = jnp.where(lax.broadcasted_iota(jnp.int32, (rows, top), 0) < live[0, 0], probs, 0.0)
    names = lax.broadcasted_iota(jnp.int32, (rows, experts), 1)
    table = jnp.zeros((rows, experts), F32)
    for k in range(top):
        table = table + jnp.where(ids[:, k : k + 1] == names, probs[:, k : k + 1], 0.0)
    spots = lax.broadcasted_iota(jnp.int32, (rows, lanes), 1) - outer * rows
    spots = (spots == lax.broadcasted_iota(jnp.int32, (rows, lanes), 0)).astype(F32).astype(BF16)
    share_ref[...] = lax.dot_general(
        table.astype(BF16), spots, (((0,), (0,)), ((), ())), preferred_element_type=F32
    ).astype(BF16)


def proj_kernel(a0, a1, a2, a3, w0, w1, w2, w3, keep_ref, send_ref, rows, part):
    expert, outer, inner, dp = seat()
    full = a0.shape[0]
    half = full // 2
    block = w0.shape[1]
    for s, a in enumerate((a0, a1, a2, a3)):
        rows[aligned(outer ^ s, full), :] = a[...]
    for j, w in enumerate((w0, w1, w2, w3)):
        part[:, aligned(inner ^ j, block)] = dot(rows[...], w[...]).astype(BF16)
    for spot in range(4):
        keep_ref[spot * half : (spot + 1) * half, :] = part[aligned(2 * spot + dp, half), :]
        send_ref[spot * half : (spot + 1) * half, :] = part[aligned(2 * spot + 1 - dp, half), :]


def stream_kernel(keep, arrived, r0, r13, r2, share, block_ref):
    expert, outer, inner, dp = seat()
    count = keep.shape[0]
    small = r0.shape[0]
    for s, r in enumerate((r0[...], r13[0:small, :], r2[0:small, :], r13[small:, :])):
        rows = aligned(outer ^ s, small)
        product = keep[rows, :].astype(F32) + arrived[rows, :].astype(F32)
        block_ref[rows, :] = (r.astype(F32) + product).astype(BF16)
    block_ref[count:, :] = share[...]


def piece_kernel(starts, weights, out, semaphores):
    depth, width = out.shape[0] // 4, out.shape[1] // 2
    copies = [
        pltpu.make_async_copy(
            weights.at[pl.ds(k * depth, depth), pl.ds(starts[i], width)],
            out.at[pl.ds(k * depth, depth), pl.ds(i * width, width)],
            semaphores.at[i, k],
        )
        for i in range(2)
        for k in range(4)
    ]
    for copy in copies:
        copy.start()
    for copy in copies:
        copy.wait()


def swiglu(gate, up, share):
    return (gate / (1.0 + jnp.exp(-gate)) * up * share).astype(BF16)


def norm_kernel(b0, b1, b2, b3, gain, group_ref, own_ref):
    expert, outer, inner, dp = seat()
    count = group_ref.shape[0]
    width = b0.shape[1]
    experts = b0.shape[0] - count
    small = own_ref.shape[0]
    square = jnp.zeros((count, 1), F32)
    share = jnp.zeros((experts, count), F32)
    for s, b in enumerate((b0, b1, b2, b3)):
        value = b[0:count, :]
        group_ref[:, aligned((outer + 4 - s) & 3, width)] = value
        value = value.astype(F32)
        square = square + jnp.sum(value * value, axis=1, keepdims=True)
        share = share + b[count : count + experts, 0:count].astype(F32)
    own_ref[...] = group_ref[aligned(outer, small), 0 : 4 * width]
    scale = lax.rsqrt(square / (4 * width) + 1e-06)
    for s in range(4):
        cols = slice(s * width, (s + 1) * width)
        value = group_ref[:, cols].astype(F32)
        group_ref[:, cols] = (value * scale * gain[:, cols]).astype(BF16)
    lanes = (experts, 128)
    spread = lax.broadcasted_iota(jnp.int32, lanes, 0) == lax.broadcasted_iota(jnp.int32, lanes, 1)
    group_ref[:, 4 * width :] = lax.dot_general(
        share.astype(BF16),
        spread.astype(F32).astype(BF16),
        (((0,), (0,)), ((), ())),
        preferred_element_type=F32,
    ).astype(BF16)


def first_gate_kernel(
    group_x, group_cx, group, group_c, own, early, inner_ref, part_ref, other_ref, share_ref, mine_ref
):
    expert, outer, inner, dp = seat()
    count = group.shape[0]
    half = other_ref.shape[1]
    cut = inner_ref.shape[1]
    for j, g in enumerate((group_x, group_cx, group, group_c)):
        rows = slice(j * count, (j + 1) * count)
        mine_ref[rows, :] = g[:, aligned(dp, half)]
        other_ref[rows, :] = g[:, aligned(1 - dp, half)]
        share = g[:, 2 * half : 2 * half + 128].astype(F32)
        picked = lax.broadcasted_iota(jnp.int32, share.shape, 1) == expert
        share = jnp.sum(jnp.where(picked, share, 0.0), axis=1, keepdims=True)
        share_ref[rows, :] = jnp.broadcast_to(share, (count, 128))
    mine, other = mine_ref[...], other_ref[...]
    gate = dot(mine, own[:, 0:cut]) + dot(other, early[:, 0:cut])
    up = dot(mine, own[:, 2 * cut : 3 * cut]) + dot(other, early[:, cut : 2 * cut])
    inner_ref[...] = swiglu(gate, up, share_ref[:, 0:1])
    part_ref[:, 0:cut] = dot(mine, own[:, cut : 2 * cut])
    part_ref[:, cut : 2 * cut] = dot(mine, own[:, 3 * cut : 4 * cut])


def last_gate_kernel(first, part, other, share, *refs):
    *late, far_ref, near_ref = refs
    cut = first.shape[1]
    half = far_ref.shape[0]
    far_ref[:, 0:cut] = first[0:half, :]
    near_ref[:, 0:cut] = first[half:, :]
    at = 0
    for piece in late:
        size = piece.shape[1] // 2
        gate = part[:, at : at + size] + dot(other[...], piece[:, 0:size])
        up = part[:, cut + at : cut + at + size] + dot(other[...], piece[:, size : 2 * size])
        value = swiglu(gate, up, share[:, 0:1])
        cols = slice(cut + at, cut + at + size)
        far_ref[:, cols] = value[:half]
        near_ref[:, cols] = value[half:]
        at += size


def column_chunks(wd):
    return [slice(at, at + 256) for at in range(0, wd.shape[1], 256)]


def down_both_kernel(far, near, wd, keep_far, keep_near, far_a, far_b, near_a, near_b):
    down_kernel(far, wd, keep_far, far_a, far_b)
    down_kernel(near, wd, keep_near, near_a, near_b)


def down_kernel(rows, wd, keep_ref, send_a, send_b):
    count, side = send_a.shape
    for at in range(0, wd.shape[1], 256):
        value = dot(rows[...], wd[:, at : at + 256]).astype(BF16)
        keep_ref[:, at : at + 256] = value[:count]
        send = send_a if at < side else send_b
        send[:, at % side : at % side + 256] = value[count:]


def fold_kernel(keep, core_a, core_b, out):
    side = core_a.shape[1]
    for i, core in enumerate((core_a, core_b)):
        cols = slice(i * side, (i + 1) * side)
        out[:, cols] = (keep[:, cols].astype(F32) + core[...].astype(F32)).astype(BF16)


def pieces_kernel(keep, core_a, core_b, far, p0, p1, p2, p3):
    expert, outer, inner, dp = seat()
    small = p0.shape[0]
    for s, p in enumerate((p0, p1, p2, p3)):
        rows = aligned((outer + s) & 3, small)
        side = core_a.shape[1]
        for i, core in enumerate((core_a, core_b)):
            cols = slice(i * side, (i + 1) * side)
            total = keep[rows, cols].astype(F32) + core[rows, :].astype(F32)
            p[:, cols] = (total + far[rows, cols].astype(F32)).astype(BF16)


def tail_kernel(own, m0, m1, m2, m3, o0, o1, o2, o3, gain, stream_ref, normed_ref):
    expert, outer, inner, dp = seat()
    half = m0.shape[1]
    for at, pieces in ((dp, (m0, m1, m2, m3)), (1 - dp, (o0, o1, o2, o3))):
        cols = aligned(at, half)
        mixture = pieces[0][...].astype(F32)
        for piece in pieces[1:]:
            mixture = mixture + piece[...].astype(F32)
        stream_ref[:, cols] = (own[:, cols].astype(F32) + mixture).astype(BF16)
    normed_ref[...] = rms_scale(stream_ref[...].astype(F32), gain[...]).astype(BF16)


def body_paired(
    attn,
    resid,
    w_out,
    gain_post,
    route_ids,
    route_logits,
    live_count,
    w_gate_up,
    w_down,
    gain_final,
):
    rows_here = resid.shape[1]
    model_width = resid.shape[2]
    expert_count = lax.axis_size("expert")
    hidden = w_down.shape[1]
    half_width = w_down.shape[2]
    quarter = model_width // 4
    vmem, smem = whole_vmem(), whole_smem()

    def shape_of(*shape, dtype=BF16):
        return jax.ShapeDtypeStruct(shape, dtype)

    def call(kernel, name, mib, outs, *args, scratch=(), first=vmem):
        return pl.pallas_call(
            kernel,
            out_shape=outs,
            in_specs=[first] + [vmem] * (len(args) - 1),
            out_specs=tuple(vmem for _ in outs),
            scratch_shapes=list(scratch),
            compiler_params=kernel_params(mib),
            cost_estimate=small_cost(),
            name=name,
        )(*args)

    def swap_dp(x):
        return lax.ppermute(x, "dp", [(0, 1), (1, 0)])

    def shift_outer(x, s):
        return lax.ppermute(
            x, "expert", [(i, (i + 4 * s) % expert_count) for i in range(expert_count)]
        )

    def cross_outer(x, s):
        return lax.ppermute(
            x,
            ("dp", "expert"),
            [
                (d * expert_count + i, (1 - d) * expert_count + (i + 4 * s) % expert_count)
                for d in range(2)
                for i in range(expert_count)
            ],
        )

    def swap_inner(x, j):
        return lax.ppermute(x, "expert", [(i, i ^ j) for i in range(expert_count)])

    def swap_outer(x, s):
        return lax.ppermute(x, "expert", [(i, i ^ (4 * s)) for i in range(expert_count)])

    def after(x, *results):
        return lax.optimization_barrier((x, *results))[0]

    def weight_piece(first, size, mib=8):
        return pl.pallas_call(
            functools.partial(piece_kernel, (first, hidden + first)),
            out_shape=shape_of(half_width, 2 * size),
            in_specs=[pl.BlockSpec(memory_space=pl.ANY)],
            out_specs=pl.BlockSpec(memory_space=pl.ANY),
            scratch_shapes=[pltpu.SemaphoreType.DMA((2, 4))],
            compiler_params=kernel_params(mib),
            cost_estimate=small_cost(),
            name="weight_piece",
        )(w_gate_up[0])

    piece = shape_of(rows_here, quarter)
    r_own, r_1, r_23 = call(
        cut_kernel, "cut_resid", 4, (piece, piece, shape_of(2 * rows_here, quarter)), resid[0]
    )
    (share,) = call(
        share_kernel,
        "share",
        4,
        (shape_of(expert_count, quarter),),
        live_count,
        route_ids[0],
        route_logits[0],
        first=smem,
    )
    cut_width = hidden // 2
    early_piece = weight_piece(0, cut_width, 60)
    late_sizes = (cut_width * 384 // 384,)
    late_pieces = [
        weight_piece(cut_width + sum(late_sizes[:i]), size) for i, size in enumerate(late_sizes)
    ]
    gate_up_early = swap_dp(early_piece)
    a = [attn[0], swap_outer(attn[0], 1), swap_outer(attn[0], 2)]
    w_x = swap_inner(w_out, 2)
    r_2 = swap_outer(r_23, 2)
    a.append(swap_outer(after(a[2], a[1], r_2), 1))
    w_c = swap_inner(after(w_out, w_x, share, *late_pieces), 1)
    w_cx = swap_inner(w_x, 1)
    r_13 = swap_outer(jnp.concatenate([r_1, r_2[rows_here:]], axis=0), 1)

    product = shape_of(4 * rows_here, quarter)
    keep, send = call(
        proj_kernel,
        "projection",
        8,
        (product, product),
        *a,
        w_out,
        w_c,
        w_x,
        w_cx,
        scratch=(
            pltpu.VMEM((8 * rows_here, attn.shape[2]), BF16),
            pltpu.VMEM((8 * rows_here, quarter), BF16),
        ),
    )
    arrived = swap_dp(after(send, gate_up_early, r_13))
    gate_up_late = [swap_dp(after(piece, arrived)) for piece in late_pieces]
    (block,) = call(
        stream_kernel,
        "stream",
        4,
        (shape_of(4 * rows_here + expert_count, quarter),),
        keep,
        arrived,
        r_own,
        r_13,
        r_2,
        share,
    )

    def norm(b0, b1, b2, b3):
        outs = (shape_of(4 * rows_here, model_width + 128), shape_of(rows_here, model_width))
        return call(norm_kernel, "norm", 8, outs, b0, b1, b2, b3, gain_post[None])

    blocks = [block] + [shift_outer(block, s) for s in (1, 2, 3)]
    group, stream_own = norm(*blocks)
    blocks_x = [swap_inner(b, 2) for b in blocks]
    group_x, unused = norm(*blocks_x)
    group_c = swap_inner(group, 1)
    group_cx = swap_inner(group_x, 1)

    row_total = 16 * rows_here
    half_rows = row_total // 2
    inner_first, part, other_rows, share_rows = call(
        first_gate_kernel,
        "first_gate_up",
        24,
        (
            shape_of(row_total, cut_width),
            shape_of(row_total, hidden, dtype=F32),
            shape_of(row_total, half_width),
            shape_of(row_total, 128, dtype=F32),
        ),
        group_x,
        group_cx,
        group,
        group_c,
        w_gate_up[0],
        gate_up_early,
        scratch=(pltpu.VMEM((row_total, half_width), BF16),),
    )
    inner_half = shape_of(half_rows, hidden)
    inner_far, inner_near = call(
        last_gate_kernel,
        "last_gate_up",
        16,
        (inner_half, inner_half),
        inner_first,
        part,
        other_rows,
        share_rows,
        *gate_up_late,
    )
    far_other = swap_dp(inner_far)
    near_other = swap_dp(inner_near)

    count = row_total // 4
    quarter_out = shape_of(count, half_width)
    half_out = shape_of(count, half_width // 2)

    def down(rows):
        return call(
            down_kernel,
            "down",
            12,
            (quarter_out, half_out, half_out),
            rows,
            w_down[0],
        )

    def add(x, y):
        return (x.astype(F32) + y.astype(F32)).astype(BF16)

    def swap_cores(halves):
        return [swap_inner(half, 1) for half in halves]

    def fold(keep, halves):
        return call(fold_kernel, "fold", 4, (quarter_out,), keep, *halves)[0]

    def pieces(*args):
        out = shape_of(rows_here, half_width)
        return call(pieces_kernel, "pieces", 4, (out, out, out, out), *args)

    keep_far, keep_near, *send = call(
        down_both_kernel,
        "down_both",
        16,
        (quarter_out, quarter_out, half_out, half_out, half_out, half_out),
        inner_far,
        inner_near,
        w_down[0],
    )
    far = swap_inner(fold(keep_far, swap_cores(send[:2])), 2)
    ready = far
    cut = pieces(keep_near, *swap_cores(send[2:]), far)
    mine = [cut[0]] + [shift_outer(cut[s], s) for s in (1, 2, 3)]

    keep_far, *send = down(after(far_other, ready))
    far = swap_inner(fold(keep_far, swap_cores(send)), 2)
    keep_near, *send = down(after(near_other, *mine[1:]))
    cut = pieces(keep_near, *swap_cores(send), far)
    others = [cross_outer(cut[s], s) for s in range(4)]

    out = shape_of(rows_here, model_width)
    stream_out, normed_out = call(
        tail_kernel, "closing", 8, (out, out), stream_own, *mine, *others, gain_final[None]
    )
    return (stream_out[None], normed_out[None])


def solution(mesh):
    placed = (
        P("expert", None, "dp"),
        P("expert", "dp", None),
        P("dp", "expert"),
        P(),
        P("expert", "dp", None),
        P("expert", "dp", None),
        P("expert", "dp"),
        P("expert", "dp", None),
        P("expert", None, "dp"),
        P(),
    )
    paired = mesh.shape["dp"] == 2 and mesh.shape["expert"] == 16
    return jax.shard_map(
        body_paired if paired else body_general,
        mesh=mesh,
        in_specs=placed,
        out_specs=(P("expert", "dp", None), P("expert", "dp", None)),
        check_vma=False,
    )
```

```python
import functools
import math

import jax
import jax.numpy as jnp
from jax import lax
from jax.experimental import pallas as pl
from jax.experimental.pallas import tpu as pltpu
from jax.sharding import PartitionSpec as P


def rms_scale(values, gain):
    return values * lax.rsqrt(jnp.mean(values * values, axis=-1, keepdims=True) + 1e-06) * gain


def swiglu_rows(rows_in, gate_up, down, hidden_units):
    both = jnp.dot(rows_in, gate_up, preferred_element_type=jnp.float32)
    inner = (jax.nn.silu(both[:, :hidden_units]) * both[:, hidden_units:]).astype(jnp.bfloat16)
    return jnp.dot(inner, down, preferred_element_type=jnp.float32).astype(jnp.bfloat16)


def body_general(
    attn,
    resid,
    w_out,
    gain_post,
    route_ids,
    route_logits,
    live_count,
    w_gate_up,
    w_down,
    gain_final,
):
    rows_here = resid.shape[1]
    model_width = resid.shape[2]
    top_count = route_ids.shape[2]
    dp_count = lax.axis_size("dp")
    expert_count = lax.axis_size("expert")
    hidden_units = w_down.shape[1]
    capacity = dp_count * max(1, 2 * rows_here * top_count // (expert_count * dp_count))
    slot_count = expert_count * capacity
    flat_attn = attn[0]
    partial_out = jnp.dot(
        flat_attn,
        lax.all_gather(w_out, "expert", axis=1, tiled=True),
        preferred_element_type=jnp.float32,
    )
    projected = lax.psum_scatter(
        partial_out.astype(jnp.bfloat16), "dp", scatter_dimension=0, tiled=True
    ).astype(jnp.float32)
    stream_in = (resid[0].astype(jnp.float32) + projected).astype(jnp.bfloat16)
    stream_float = stream_in.astype(jnp.float32)
    normed_in = rms_scale(stream_float, gain_post).astype(jnp.bfloat16)
    probs = jax.nn.softmax(route_logits[0], axis=-1).astype(jnp.bfloat16)
    alive = jnp.arange(rows_here, dtype=jnp.int32) < live_count[0, 0]
    expert_of = route_ids[0].reshape(-1)
    route_alive = jnp.repeat(alive, top_count)
    onehot = (
        (expert_of[:, None] == jnp.arange(expert_count, dtype=jnp.int32)[None, :])
        & route_alive[:, None]
    ).astype(jnp.int32)
    earlier = jnp.sum((jnp.cumsum(onehot, axis=0) - onehot) * onehot, axis=1)
    target = expert_of * capacity + earlier
    match = (target[:, None] == jnp.arange(slot_count, dtype=jnp.int32)[None, :]) & route_alive[
        :, None
    ]
    placed = match.reshape(rows_here, top_count, slot_count)
    gather_matrix = jnp.any(placed, axis=1).astype(jnp.bfloat16)
    send_rows = lax.dot_general(
        gather_matrix, normed_in, (((0,), (0,)), ((), ())), preferred_element_type=jnp.float32
    ).astype(jnp.bfloat16)
    send_flags = jnp.sum(gather_matrix.astype(jnp.float32), axis=0).astype(jnp.bfloat16)
    combine_matrix = jnp.sum(
        jnp.where(placed, probs.astype(jnp.float32)[:, :, None], jnp.float32(0.0)), axis=1
    ).astype(jnp.bfloat16)
    arrived_rows, arrived_flags = (
        lax.all_to_all(
            send_rows.reshape(expert_count, capacity, model_width),
            "expert",
            split_axis=0,
            concat_axis=0,
            tiled=True,
        ),
        lax.all_to_all(
            send_flags.reshape(expert_count, capacity),
            "expert",
            split_axis=0,
            concat_axis=0,
            tiled=True,
        ),
    )
    arrived = arrived_rows.reshape(slot_count, model_width)
    flags = arrived_flags.reshape(slot_count)
    gate_up_full, down_full = (
        lax.all_gather(w_gate_up, "dp", axis=1, tiled=True),
        lax.all_gather(w_down, "dp", axis=2, tiled=True),
    )
    live_slot = (flags > 0.5).astype(jnp.int32)
    order = jnp.argsort(1 - live_slot, stable=True)
    live_total = jnp.sum(live_slot)
    packed = arrived[order]
    block_len = math.gcd(slot_count, 128)
    block_total = (live_total + block_len - 1) // block_len

    def run_block(index, outputs):
        begin = index * block_len
        rows_in = lax.dynamic_slice_in_dim(packed, begin, block_len, 0)
        block_out = swiglu_rows(rows_in, gate_up_full[0], down_full[0], hidden_units)
        return lax.dynamic_update_slice_in_dim(outputs, block_out, begin, 0)

    packed_out = lax.fori_loop(
        0, block_total, run_block, jnp.zeros((slot_count, model_width), jnp.bfloat16)
    )
    position = (
        jnp.zeros((slot_count,), jnp.int32).at[order].set(jnp.arange(slot_count, dtype=jnp.int32))
    )
    results = packed_out[position]
    returned = lax.all_to_all(
        results.reshape(expert_count, capacity, model_width),
        "expert",
        split_axis=0,
        concat_axis=0,
        tiled=True,
    )
    returned = returned.reshape(slot_count, model_width)
    mixture = jnp.dot(combine_matrix, returned, preferred_element_type=jnp.float32)
    stream_out = (stream_float + mixture).astype(jnp.bfloat16)
    normed_out = rms_scale(stream_out.astype(jnp.float32), gain_final).astype(jnp.bfloat16)
    return (stream_out[None], normed_out[None])


MIB = 1024 * 1024
BF16, F32 = jnp.bfloat16, jnp.float32


def whole_vmem():
    return pl.BlockSpec(memory_space=pltpu.VMEM)


def whole_smem():
    return pl.BlockSpec(memory_space=pltpu.SMEM)


def fixed(*shape):
    return pl.BlockSpec(shape, lambda i: (0,) * len(shape))


def dot(a, b):
    return jnp.dot(a, b, preferred_element_type=F32)


def small_cost():
    return pl.CostEstimate(flops=1, bytes_accessed=1, transcendentals=0)


def kernel_params(mib):
    return pltpu.CompilerParams(vmem_limit_bytes=mib * MIB)


def seat():
    expert = lax.axis_index("expert")
    return expert, lax.shift_right_logical(expert, 2), expert & 3, lax.axis_index("dp")


def aligned(index, step):
    return pl.ds(pl.multiple_of(index * step, step), step)


def cut_kernel(resid, r0, r1, r23):
    expert, outer, inner, dp = seat()
    rows, lanes = r0.shape
    r0[...] = resid[:, aligned(outer, lanes)]
    r1[...] = resid[:, aligned(outer ^ 1, lanes)]
    for i in range(2):
        r23[i * rows : (i + 1) * rows, :] = resid[:, aligned(outer ^ (2 + i), lanes)]


def share_kernel(live, ids, logits, share_ref):
    expert, outer, inner, dp = seat()
    rows, top = ids.shape
    experts, lanes = share_ref.shape
    value = logits[...]
    value = jnp.exp(value - jnp.max(value, axis=1, keepdims=True))
    probs = (value / jnp.sum(value, axis=1, keepdims=True)).astype(BF16).astype(F32)
    probs = jnp.where(lax.broadcasted_iota(jnp.int32, (rows, top), 0) < live[0, 0], probs, 0.0)
    names = lax.broadcasted_iota(jnp.int32, (rows, experts), 1)
    table = jnp.zeros((rows, experts), F32)
    for k in range(top):
        table = table + jnp.where(ids[:, k : k + 1] == names, probs[:, k : k + 1], 0.0)
    spots = lax.broadcasted_iota(jnp.int32, (rows, lanes), 1) - outer * rows
    spots = (spots == lax.broadcasted_iota(jnp.int32, (rows, lanes), 0)).astype(F32).astype(BF16)
    share_ref[...] = lax.dot_general(
        table.astype(BF16), spots, (((0,), (0,)), ((), ())), preferred_element_type=F32
    ).astype(BF16)


def proj_kernel(a0, a1, a2, a3, w0, w1, w2, w3, keep_ref, send_ref, rows, part):
    expert, outer, inner, dp = seat()
    full = a0.shape[0]
    half = full // 2
    block = w0.shape[1]
    for s, a in enumerate((a0, a1, a2, a3)):
        rows[aligned(outer ^ s, full), :] = a[...]
    for j, w in enumerate((w0, w1, w2, w3)):
        part[:, aligned(inner ^ j, block)] = dot(rows[...], w[...]).astype(BF16)
    for spot in range(4):
        keep_ref[spot * half : (spot + 1) * half, :] = part[aligned(2 * spot + dp, half), :]
        send_ref[spot * half : (spot + 1) * half, :] = part[aligned(2 * spot + 1 - dp, half), :]


def stream_kernel(keep, arrived, r0, r13, r2, share, block_ref):
    expert, outer, inner, dp = seat()
    count = keep.shape[0]
    small = r0.shape[0]
    for s, r in enumerate((r0[...], r13[0:small, :], r2[0:small, :], r13[small:, :])):
        rows = aligned(outer ^ s, small)
        product = keep[rows, :].astype(F32) + arrived[rows, :].astype(F32)
        block_ref[rows, :] = (r.astype(F32) + product).astype(BF16)
    block_ref[count:, :] = share[...]


def piece_kernel(starts, weights, out, semaphores):
    depth, width = out.shape[0] // 4, out.shape[1] // 2
    copies = [
        pltpu.make_async_copy(
            weights.at[pl.ds(k * depth, depth), pl.ds(starts[i], width)],
            out.at[pl.ds(k * depth, depth), pl.ds(i * width, width)],
            semaphores.at[i, k],
        )
        for i in range(2)
        for k in range(4)
    ]
    for copy in copies:
        copy.start()
    for copy in copies:
        copy.wait()


def swiglu(gate, up, share):
    return (gate / (1.0 + jnp.exp(-gate)) * up * share).astype(BF16)


def norm_kernel(b0, b1, b2, b3, gain, group_ref, own_ref):
    expert, outer, inner, dp = seat()
    count = group_ref.shape[0]
    width = b0.shape[1]
    experts = b0.shape[0] - count
    small = own_ref.shape[0]
    square = jnp.zeros((count, 1), F32)
    share = jnp.zeros((experts, count), F32)
    for s, b in enumerate((b0, b1, b2, b3)):
        value = b[0:count, :]
        group_ref[:, aligned((outer + 4 - s) & 3, width)] = value
        value = value.astype(F32)
        square = square + jnp.sum(value * value, axis=1, keepdims=True)
        share = share + b[count : count + experts, 0:count].astype(F32)
    own_ref[...] = group_ref[aligned(outer, small), 0 : 4 * width]
    scale = lax.rsqrt(square / (4 * width) + 1e-06)
    for s in range(4):
        cols = slice(s * width, (s + 1) * width)
        value = group_ref[:, cols].astype(F32)
        group_ref[:, cols] = (value * scale * gain[:, cols]).astype(BF16)
    lanes = (experts, 128)
    spread = lax.broadcasted_iota(jnp.int32, lanes, 0) == lax.broadcasted_iota(jnp.int32, lanes, 1)
    group_ref[:, 4 * width :] = lax.dot_general(
        share.astype(BF16),
        spread.astype(F32).astype(BF16),
        (((0,), (0,)), ((), ())),
        preferred_element_type=F32,
    ).astype(BF16)


def first_gate_kernel(group_x, group_cx, group, group_c, own, *refs):
    *early, inner_ref, part_ref, other_ref, share_ref, mine_ref = refs
    expert, outer, inner, dp = seat()
    count = group.shape[0]
    half = other_ref.shape[1]
    cut = inner_ref.shape[1]
    for j, g in enumerate((group_x, group_cx, group, group_c)):
        rows = slice(j * count, (j + 1) * count)
        mine_ref[rows, :] = g[:, aligned(dp, half)]
        other_ref[rows, :] = g[:, aligned(1 - dp, half)]
        share = g[:, 2 * half : 2 * half + 128].astype(F32)
        picked = lax.broadcasted_iota(jnp.int32, share.shape, 1) == expert
        share = jnp.sum(jnp.where(picked, share, 0.0), axis=1, keepdims=True)
        share_ref[rows, :] = jnp.broadcast_to(share, (count, 128))
    mine, other = mine_ref[...], other_ref[...]
    at = 0
    for piece in early:
        size = piece.shape[1] // 2
        gate = dot(mine, own[:, at : at + size]) + dot(other, piece[:, 0:size])
        up = dot(mine, own[:, 2 * cut + at : 2 * cut + at + size]) + dot(other, piece[:, size:])
        inner_ref[:, at : at + size] = swiglu(gate, up, share_ref[:, 0:1])
        at += size
    part_ref[:, 0:cut] = dot(mine, own[:, cut : 2 * cut])
    part_ref[:, cut : 2 * cut] = dot(mine, own[:, 3 * cut : 4 * cut])


def last_gate_kernel(first, part, other, share, *refs):
    *late, far_ref, near_ref = refs
    cut = first.shape[1]
    half = far_ref.shape[0]
    far_ref[:, 0:cut] = first[0:half, :]
    near_ref[:, 0:cut] = first[half:, :]
    at = 0
    for piece in late:
        size = piece.shape[1] // 2
        gate = part[:, at : at + size] + dot(other[...], piece[:, 0:size])
        up = part[:, cut + at : cut + at + size] + dot(other[...], piece[:, size : 2 * size])
        value = swiglu(gate, up, share[:, 0:1])
        cols = slice(cut + at, cut + at + size)
        far_ref[:, cols] = value[:half]
        near_ref[:, cols] = value[half:]
        at += size


def column_chunks(wd):
    return [slice(at, at + 256) for at in range(0, wd.shape[1], 256)]


def down_both_kernel(far, near, wd, keep_far, keep_near, far_a, far_b, near_a, near_b):
    down_kernel(far, wd, keep_far, far_a, far_b)
    down_kernel(near, wd, keep_near, near_a, near_b)


def down_kernel(rows, wd, keep_ref, send_a, send_b):
    count, side = send_a.shape
    for at in range(0, wd.shape[1], 256):
        value = dot(rows[...], wd[:, at : at + 256]).astype(BF16)
        keep_ref[:, at : at + 256] = value[:count]
        send = send_a if at < side else send_b
        send[:, at % side : at % side + 256] = value[count:]


def fold_kernel(keep, core_a, core_b, out):
    side = core_a.shape[1]
    for i, core in enumerate((core_a, core_b)):
        cols = slice(i * side, (i + 1) * side)
        out[:, cols] = (keep[:, cols].astype(F32) + core[...].astype(F32)).astype(BF16)


def pieces_kernel(keep, core_a, core_b, far, p0, p1, p2, p3):
    expert, outer, inner, dp = seat()
    small = p0.shape[0]
    for s, p in enumerate((p0, p1, p2, p3)):
        rows = aligned((outer + s) & 3, small)
        side = core_a.shape[1]
        for i, core in enumerate((core_a, core_b)):
            cols = slice(i * side, (i + 1) * side)
            total = keep[rows, cols].astype(F32) + core[rows, :].astype(F32)
            p[:, cols] = (total + far[rows, cols].astype(F32)).astype(BF16)


def tail_kernel(own, m0, m1, m2, m3, o0, o1, o2, o3, gain, stream_ref, normed_ref):
    expert, outer, inner, dp = seat()
    half = m0.shape[1]
    for at, pieces in ((dp, (m0, m1, m2, m3)), (1 - dp, (o0, o1, o2, o3))):
        cols = aligned(at, half)
        mixture = pieces[0][...].astype(F32)
        for piece in pieces[1:]:
            mixture = mixture + piece[...].astype(F32)
        stream_ref[:, cols] = (own[:, cols].astype(F32) + mixture).astype(BF16)
    normed_ref[...] = rms_scale(stream_ref[...].astype(F32), gain[...]).astype(BF16)


def body_paired(
    attn,
    resid,
    w_out,
    gain_post,
    route_ids,
    route_logits,
    live_count,
    w_gate_up,
    w_down,
    gain_final,
):
    rows_here = resid.shape[1]
    model_width = resid.shape[2]
    expert_count = lax.axis_size("expert")
    hidden = w_down.shape[1]
    half_width = w_down.shape[2]
    quarter = model_width // 4
    vmem, smem = whole_vmem(), whole_smem()

    def shape_of(*shape, dtype=BF16):
        return jax.ShapeDtypeStruct(shape, dtype)

    def call(kernel, name, mib, outs, *args, scratch=(), first=vmem):
        return pl.pallas_call(
            kernel,
            out_shape=outs,
            in_specs=[first] + [vmem] * (len(args) - 1),
            out_specs=tuple(vmem for _ in outs),
            scratch_shapes=list(scratch),
            compiler_params=kernel_params(mib),
            cost_estimate=small_cost(),
            name=name,
        )(*args)

    def swap_dp(x):
        return lax.ppermute(x, "dp", [(0, 1), (1, 0)])

    def shift_outer(x, s):
        return lax.ppermute(
            x, "expert", [(i, (i + 4 * s) % expert_count) for i in range(expert_count)]
        )

    def cross_outer(x, s):
        return lax.ppermute(
            x,
            ("dp", "expert"),
            [
                (d * expert_count + i, (1 - d) * expert_count + (i + 4 * s) % expert_count)
                for d in range(2)
                for i in range(expert_count)
            ],
        )

    def swap_inner(x, j):
        return lax.ppermute(x, "expert", [(i, i ^ j) for i in range(expert_count)])

    def swap_outer(x, s):
        return lax.ppermute(x, "expert", [(i, i ^ (4 * s)) for i in range(expert_count)])

    def after(x, *results):
        return lax.optimization_barrier((x, *results))[0]

    def weight_piece(first, size):
        return pl.pallas_call(
            functools.partial(piece_kernel, (first, hidden + first)),
            out_shape=shape_of(half_width, 2 * size),
            in_specs=[pl.BlockSpec(memory_space=pl.ANY)],
            out_specs=vmem,
            scratch_shapes=[pltpu.SemaphoreType.DMA((2, 4))],
            compiler_params=kernel_params(8),
            cost_estimate=small_cost(),
            name="weight_piece",
        )(w_gate_up[0])

    def weight_pieces(first, sizes):
        return [weight_piece(first + sum(sizes[:i]), size) for i, size in enumerate(sizes)]

    piece = shape_of(rows_here, quarter)
    r_own, r_1, r_23 = call(
        cut_kernel, "cut_resid", 4, (piece, piece, shape_of(2 * rows_here, quarter)), resid[0]
    )
    (share,) = call(
        share_kernel,
        "share",
        4,
        (shape_of(expert_count, quarter),),
        live_count,
        route_ids[0],
        route_logits[0],
        first=smem,
    )
    cut_width = hidden // 2
    early_pieces = weight_pieces(0, (cut_width * 384 // 384,))
    late_pieces = weight_pieces(cut_width, (cut_width * 384 // 384,))
    gate_up_early = [swap_dp(piece) for piece in early_pieces]
    a = [attn[0], swap_outer(attn[0], 1), swap_outer(attn[0], 2)]
    w_x = swap_inner(w_out, 2)
    r_2 = swap_outer(r_23, 2)
    a.append(swap_outer(after(a[2], a[1], r_2), 1))
    w_c = swap_inner(after(w_out, w_x, share, *late_pieces), 1)
    w_cx = swap_inner(w_x, 1)
    r_13 = swap_outer(jnp.concatenate([r_1, r_2[rows_here:]], axis=0), 1)

    product = shape_of(4 * rows_here, quarter)
    keep, send = call(
        proj_kernel,
        "projection",
        8,
        (product, product),
        *a,
        w_out,
        w_c,
        w_x,
        w_cx,
        scratch=(
            pltpu.VMEM((8 * rows_here, attn.shape[2]), BF16),
            pltpu.VMEM((8 * rows_here, quarter), BF16),
        ),
    )
    arrived = swap_dp(after(send, gate_up_early[0], r_13))
    gate_up_late = [swap_dp(after(piece, arrived)) for piece in late_pieces]
    (block,) = call(
        stream_kernel,
        "stream",
        4,
        (shape_of(4 * rows_here + expert_count, quarter),),
        keep,
        arrived,
        r_own,
        r_13,
        r_2,
        share,
    )

    def norm(b0, b1, b2, b3):
        outs = (shape_of(4 * rows_here, model_width + 128), shape_of(rows_here, model_width))
        return call(norm_kernel, "norm", 8, outs, b0, b1, b2, b3, gain_post[None])

    blocks = [block] + [shift_outer(block, s) for s in (1, 2, 3)]
    group, stream_own = norm(*blocks)
    blocks_x = [swap_inner(b, 2) for b in blocks]
    group_x, unused = norm(*blocks_x)
    group_c = swap_inner(group, 1)
    group_cx = swap_inner(group_x, 1)

    row_total = 16 * rows_here
    half_rows = row_total // 2
    inner_first, part, other_rows, share_rows = call(
        first_gate_kernel,
        "first_gate_up",
        24,
        (
            shape_of(row_total, cut_width),
            shape_of(row_total, hidden, dtype=F32),
            shape_of(row_total, half_width),
            shape_of(row_total, 128, dtype=F32),
        ),
        group_x,
        group_cx,
        group,
        group_c,
        w_gate_up[0],
        *gate_up_early,
        scratch=(pltpu.VMEM((row_total, half_width), BF16),),
    )
    inner_half = shape_of(half_rows, hidden)
    inner_far, inner_near = call(
        last_gate_kernel,
        "last_gate_up",
        16,
        (inner_half, inner_half),
        inner_first,
        part,
        other_rows,
        share_rows,
        *gate_up_late,
    )
    far_other = swap_dp(inner_far)
    near_other = swap_dp(inner_near)

    count = row_total // 4
    quarter_out = shape_of(count, half_width)
    half_out = shape_of(count, half_width // 2)

    def down(rows):
        return call(
            down_kernel,
            "down",
            12,
            (quarter_out, half_out, half_out),
            rows,
            w_down[0],
        )

    def add(x, y):
        return (x.astype(F32) + y.astype(F32)).astype(BF16)

    def swap_cores(halves):
        return [swap_inner(half, 1) for half in halves]

    def fold(keep, halves):
        return call(fold_kernel, "fold", 4, (quarter_out,), keep, *halves)[0]

    def pieces(*args):
        out = shape_of(rows_here, half_width)
        return call(pieces_kernel, "pieces", 4, (out, out, out, out), *args)

    keep_far, keep_near, *send = call(
        down_both_kernel,
        "down_both",
        16,
        (quarter_out, quarter_out, half_out, half_out, half_out, half_out),
        inner_far,
        inner_near,
        w_down[0],
    )
    far = swap_inner(fold(keep_far, swap_cores(send[:2])), 2)
    ready = far
    cut = pieces(keep_near, *swap_cores(send[2:]), far)
    mine = [cut[0]] + [shift_outer(cut[s], s) for s in (1, 2, 3)]

    keep_far, *send = down(after(far_other, ready))
    far = swap_inner(fold(keep_far, swap_cores(send)), 2)
    keep_near, *send = down(after(near_other, *mine[1:]))
    cut = pieces(keep_near, *swap_cores(send), far)
    others = [cross_outer(cut[s], s) for s in range(4)]

    out = shape_of(rows_here, model_width)
    stream_out, normed_out = call(
        tail_kernel, "closing", 8, (out, out), stream_own, *mine, *others, gain_final[None]
    )
    return (stream_out[None], normed_out[None])


def solution(mesh):
    placed = (
        P("expert", None, "dp"),
        P("expert", "dp", None),
        P("dp", "expert"),
        P(),
        P("expert", "dp", None),
        P("expert", "dp", None),
        P("expert", "dp"),
        P("expert", "dp", None),
        P("expert", None, "dp"),
        P(),
    )
    paired = mesh.shape["dp"] == 2 and mesh.shape["expert"] == 16
    return jax.shard_map(
        body_paired if paired else body_general,
        mesh=mesh,
        in_specs=placed,
        out_specs=(P("expert", "dp", None), P("expert", "dp", None)),
        check_vma=False,
    )
```

```python
import functools
import math

import jax
import jax.numpy as jnp
from jax import lax
from jax.experimental import pallas as pl
from jax.experimental.pallas import tpu as pltpu
from jax.sharding import PartitionSpec as P


def rms_scale(values, gain):
    return values * lax.rsqrt(jnp.mean(values * values, axis=-1, keepdims=True) + 1e-06) * gain


def swiglu_rows(rows_in, gate_up, down, hidden_units):
    both = jnp.dot(rows_in, gate_up, preferred_element_type=jnp.float32)
    inner = (jax.nn.silu(both[:, :hidden_units]) * both[:, hidden_units:]).astype(jnp.bfloat16)
    return jnp.dot(inner, down, preferred_element_type=jnp.float32).astype(jnp.bfloat16)


def body_general(
    attn,
    resid,
    w_out,
    gain_post,
    route_ids,
    route_logits,
    live_count,
    w_gate_up,
    w_down,
    gain_final,
):
    rows_here = resid.shape[1]
    model_width = resid.shape[2]
    top_count = route_ids.shape[2]
    dp_count = lax.axis_size("dp")
    expert_count = lax.axis_size("expert")
    hidden_units = w_down.shape[1]
    capacity = dp_count * max(1, 2 * rows_here * top_count // (expert_count * dp_count))
    slot_count = expert_count * capacity
    flat_attn = attn[0]
    partial_out = jnp.dot(
        flat_attn,
        lax.all_gather(w_out, "expert", axis=1, tiled=True),
        preferred_element_type=jnp.float32,
    )
    projected = lax.psum_scatter(
        partial_out.astype(jnp.bfloat16), "dp", scatter_dimension=0, tiled=True
    ).astype(jnp.float32)
    stream_in = (resid[0].astype(jnp.float32) + projected).astype(jnp.bfloat16)
    stream_float = stream_in.astype(jnp.float32)
    normed_in = rms_scale(stream_float, gain_post).astype(jnp.bfloat16)
    probs = jax.nn.softmax(route_logits[0], axis=-1).astype(jnp.bfloat16)
    alive = jnp.arange(rows_here, dtype=jnp.int32) < live_count[0, 0]
    expert_of = route_ids[0].reshape(-1)
    route_alive = jnp.repeat(alive, top_count)
    onehot = (
        (expert_of[:, None] == jnp.arange(expert_count, dtype=jnp.int32)[None, :])
        & route_alive[:, None]
    ).astype(jnp.int32)
    earlier = jnp.sum((jnp.cumsum(onehot, axis=0) - onehot) * onehot, axis=1)
    target = expert_of * capacity + earlier
    match = (target[:, None] == jnp.arange(slot_count, dtype=jnp.int32)[None, :]) & route_alive[
        :, None
    ]
    placed = match.reshape(rows_here, top_count, slot_count)
    gather_matrix = jnp.any(placed, axis=1).astype(jnp.bfloat16)
    send_rows = lax.dot_general(
        gather_matrix, normed_in, (((0,), (0,)), ((), ())), preferred_element_type=jnp.float32
    ).astype(jnp.bfloat16)
    send_flags = jnp.sum(gather_matrix.astype(jnp.float32), axis=0).astype(jnp.bfloat16)
    combine_matrix = jnp.sum(
        jnp.where(placed, probs.astype(jnp.float32)[:, :, None], jnp.float32(0.0)), axis=1
    ).astype(jnp.bfloat16)
    arrived_rows, arrived_flags = (
        lax.all_to_all(
            send_rows.reshape(expert_count, capacity, model_width),
            "expert",
            split_axis=0,
            concat_axis=0,
            tiled=True,
        ),
        lax.all_to_all(
            send_flags.reshape(expert_count, capacity),
            "expert",
            split_axis=0,
            concat_axis=0,
            tiled=True,
        ),
    )
    arrived = arrived_rows.reshape(slot_count, model_width)
    flags = arrived_flags.reshape(slot_count)
    gate_up_full, down_full = (
        lax.all_gather(w_gate_up, "dp", axis=1, tiled=True),
        lax.all_gather(w_down, "dp", axis=2, tiled=True),
    )
    live_slot = (flags > 0.5).astype(jnp.int32)
    order = jnp.argsort(1 - live_slot, stable=True)
    live_total = jnp.sum(live_slot)
    packed = arrived[order]
    block_len = math.gcd(slot_count, 128)
    block_total = (live_total + block_len - 1) // block_len

    def run_block(index, outputs):
        begin = index * block_len
        rows_in = lax.dynamic_slice_in_dim(packed, begin, block_len, 0)
        block_out = swiglu_rows(rows_in, gate_up_full[0], down_full[0], hidden_units)
        return lax.dynamic_update_slice_in_dim(outputs, block_out, begin, 0)

    packed_out = lax.fori_loop(
        0, block_total, run_block, jnp.zeros((slot_count, model_width), jnp.bfloat16)
    )
    position = (
        jnp.zeros((slot_count,), jnp.int32).at[order].set(jnp.arange(slot_count, dtype=jnp.int32))
    )
    results = packed_out[position]
    returned = lax.all_to_all(
        results.reshape(expert_count, capacity, model_width),
        "expert",
        split_axis=0,
        concat_axis=0,
        tiled=True,
    )
    returned = returned.reshape(slot_count, model_width)
    mixture = jnp.dot(combine_matrix, returned, preferred_element_type=jnp.float32)
    stream_out = (stream_float + mixture).astype(jnp.bfloat16)
    normed_out = rms_scale(stream_out.astype(jnp.float32), gain_final).astype(jnp.bfloat16)
    return (stream_out[None], normed_out[None])


MIB = 1024 * 1024
BF16, F32 = jnp.bfloat16, jnp.float32


def whole_vmem():
    return pl.BlockSpec(memory_space=pltpu.VMEM)


def whole_smem():
    return pl.BlockSpec(memory_space=pltpu.SMEM)


def fixed(*shape):
    return pl.BlockSpec(shape, lambda i: (0,) * len(shape))


def dot(a, b):
    return jnp.dot(a, b, preferred_element_type=F32)


def small_cost():
    return pl.CostEstimate(flops=1, bytes_accessed=1, transcendentals=0)


def kernel_params(mib):
    return pltpu.CompilerParams(vmem_limit_bytes=mib * MIB)


def seat():
    expert = lax.axis_index("expert")
    return expert, lax.shift_right_logical(expert, 2), expert & 3, lax.axis_index("dp")


def aligned(index, step):
    return pl.ds(pl.multiple_of(index * step, step), step)


def cut_kernel(resid, r0, r1, r23):
    expert, outer, inner, dp = seat()
    rows, lanes = r0.shape
    r0[...] = resid[:, aligned(outer, lanes)]
    r1[...] = resid[:, aligned(outer ^ 1, lanes)]
    for i in range(2):
        r23[i * rows : (i + 1) * rows, :] = resid[:, aligned(outer ^ (2 + i), lanes)]


def share_kernel(live, ids, logits, share_ref):
    expert, outer, inner, dp = seat()
    rows, top = ids.shape
    experts, lanes = share_ref.shape
    value = logits[...]
    value = jnp.exp(value - jnp.max(value, axis=1, keepdims=True))
    probs = (value / jnp.sum(value, axis=1, keepdims=True)).astype(BF16).astype(F32)
    probs = jnp.where(lax.broadcasted_iota(jnp.int32, (rows, top), 0) < live[0, 0], probs, 0.0)
    names = lax.broadcasted_iota(jnp.int32, (rows, experts), 1)
    table = jnp.zeros((rows, experts), F32)
    for k in range(top):
        table = table + jnp.where(ids[:, k : k + 1] == names, probs[:, k : k + 1], 0.0)
    spots = lax.broadcasted_iota(jnp.int32, (rows, lanes), 1) - outer * rows
    spots = (spots == lax.broadcasted_iota(jnp.int32, (rows, lanes), 0)).astype(F32).astype(BF16)
    share_ref[...] = lax.dot_general(
        table.astype(BF16), spots, (((0,), (0,)), ((), ())), preferred_element_type=F32
    ).astype(BF16)


def proj_kernel(a0, a1, a2, a3, w0, w1, w2, w3, keep_ref, send_ref, rows, part):
    expert, outer, inner, dp = seat()
    full = a0.shape[0]
    half = full // 2
    block = w0.shape[1]
    for s, a in enumerate((a0, a1, a2, a3)):
        rows[aligned(outer ^ s, full), :] = a[...]
    for j, w in enumerate((w0, w1, w2, w3)):
        part[:, aligned(inner ^ j, block)] = dot(rows[...], w[...]).astype(BF16)
    for spot in range(4):
        keep_ref[spot * half : (spot + 1) * half, :] = part[aligned(2 * spot + dp, half), :]
        send_ref[spot * half : (spot + 1) * half, :] = part[aligned(2 * spot + 1 - dp, half), :]


def stream_kernel(keep, arrived, r0, r13, r2, share, block_ref):
    expert, outer, inner, dp = seat()
    count = keep.shape[0]
    small = r0.shape[0]
    for s, r in enumerate((r0[...], r13[0:small, :], r2[0:small, :], r13[small:, :])):
        rows = aligned(outer ^ s, small)
        product = keep[rows, :].astype(F32) + arrived[rows, :].astype(F32)
        block_ref[rows, :] = (r.astype(F32) + product).astype(BF16)
    block_ref[count:, :] = share[...]


def piece_kernel(starts, weights, out, semaphores):
    depth, width = out.shape[0] // 4, out.shape[1] // 2
    copies = [
        pltpu.make_async_copy(
            weights.at[pl.ds(k * depth, depth), pl.ds(starts[i], width)],
            out.at[pl.ds(k * depth, depth), pl.ds(i * width, width)],
            semaphores.at[i, k],
        )
        for i in range(2)
        for k in range(4)
    ]
    for copy in copies:
        copy.start()
    for copy in copies:
        copy.wait()


def swiglu(gate, up, share):
    return (gate / (1.0 + jnp.exp(-gate)) * up * share).astype(BF16)


def norm_kernel(b0, b1, b2, b3, gain, group_ref, own_ref):
    expert, outer, inner, dp = seat()
    count = group_ref.shape[0]
    width = b0.shape[1]
    experts = b0.shape[0] - count
    small = own_ref.shape[0]
    square = jnp.zeros((count, 1), F32)
    share = jnp.zeros((experts, count), F32)
    for s, b in enumerate((b0, b1, b2, b3)):
        value = b[0:count, :]
        group_ref[:, aligned((outer + 4 - s) & 3, width)] = value
        value = value.astype(F32)
        square = square + jnp.sum(value * value, axis=1, keepdims=True)
        share = share + b[count : count + experts, 0:count].astype(F32)
    own_ref[...] = group_ref[aligned(outer, small), 0 : 4 * width]
    scale = lax.rsqrt(square / (4 * width) + 1e-06)
    for s in range(4):
        cols = slice(s * width, (s + 1) * width)
        value = group_ref[:, cols].astype(F32)
        group_ref[:, cols] = (value * scale * gain[:, cols]).astype(BF16)
    lanes = (experts, 128)
    spread = lax.broadcasted_iota(jnp.int32, lanes, 0) == lax.broadcasted_iota(jnp.int32, lanes, 1)
    group_ref[:, 4 * width :] = lax.dot_general(
        share.astype(BF16),
        spread.astype(F32).astype(BF16),
        (((0,), (0,)), ((), ())),
        preferred_element_type=F32,
    ).astype(BF16)


def first_gate_kernel(group_x, group_cx, group, group_c, own, *refs):
    *early, inner_ref, part_ref, other_ref, share_ref, mine_ref = refs
    expert, outer, inner, dp = seat()
    count = group.shape[0]
    half = other_ref.shape[1]
    cut = inner_ref.shape[1]
    for j, g in enumerate((group_x, group_cx, group, group_c)):
        rows = slice(j * count, (j + 1) * count)
        mine_ref[rows, :] = g[:, aligned(dp, half)]
        other_ref[rows, :] = g[:, aligned(1 - dp, half)]
        share = g[:, 2 * half : 2 * half + 128].astype(F32)
        picked = lax.broadcasted_iota(jnp.int32, share.shape, 1) == expert
        share = jnp.sum(jnp.where(picked, share, 0.0), axis=1, keepdims=True)
        share_ref[rows, :] = jnp.broadcast_to(share, (count, 128))
    mine, other = mine_ref[...], other_ref[...]
    at = 0
    for piece in early:
        size = piece.shape[1] // 2
        gate = dot(mine, own[:, at : at + size]) + dot(other, piece[:, 0:size])
        up = dot(mine, own[:, 2 * cut + at : 2 * cut + at + size]) + dot(other, piece[:, size:])
        inner_ref[:, at : at + size] = swiglu(gate, up, share_ref[:, 0:1])
        at += size
    part_ref[:, 0:cut] = dot(mine, own[:, cut : 2 * cut])
    part_ref[:, cut : 2 * cut] = dot(mine, own[:, 3 * cut : 4 * cut])


def last_gate_kernel(first, part, other, share, *refs):
    *late, far_ref, near_ref = refs
    cut = first.shape[1]
    half = far_ref.shape[0]
    far_ref[:, 0:cut] = first[0:half, :]
    near_ref[:, 0:cut] = first[half:, :]
    at = 0
    for piece in late:
        size = piece.shape[1] // 2
        gate = part[:, at : at + size] + dot(other[...], piece[:, 0:size])
        up = part[:, cut + at : cut + at + size] + dot(other[...], piece[:, size : 2 * size])
        value = swiglu(gate, up, share[:, 0:1])
        cols = slice(cut + at, cut + at + size)
        far_ref[:, cols] = value[:half]
        near_ref[:, cols] = value[half:]
        at += size


def column_chunks(wd):
    return [slice(at, at + 256) for at in range(0, wd.shape[1], 256)]


def down_both_kernel(far, near, wd, keep_far, *refs):
    *sends, keep_near, rows = refs
    half = len(sends) // 2
    down_kernel(far, wd, keep_far, *sends[:half], rows)
    down_kernel(near, wd, keep_near, *sends[half:], rows)


def down_kernel(block, wd, keep_ref, *refs):
    *sends, rows = refs
    expert, outer, inner, dp = seat()
    core = inner & 1
    count, side = sends[0].shape
    small = count // 4
    for i in range(2):
        for j in range(2):
            kept = aligned(4 * j + ((outer + 2 * core + i) & 3), small)
            sent = aligned(4 * (1 - j) + ((outer + 2 - 2 * core + i) & 3), small)
            at = (2 * i + j) * small
            rows[at : at + small, :] = block[kept, :]
            rows[count + at : count + at + small, :] = block[sent, :]
    for at in range(0, wd.shape[1], 256):
        value = dot(rows[...], wd[:, at : at + 256]).astype(BF16)
        keep_ref[:, at : at + 256] = value[:count]
        sends[at // side][:, at % side : at % side + 256] = value[count:]


def added(keep, cores, cols):
    side = cores[0].shape[1]
    return keep[:, cols].astype(F32) + cores[cols.start // side][:, cols.start % side : cols.start % side + 256].astype(F32)


def fold_kernel(keep, *refs):
    *cores, out = refs
    for at in range(0, keep.shape[1], 256):
        cols = slice(at, at + 256)
        out[:, cols] = added(keep, cores, cols).astype(BF16)


def pieces_kernel(far, keep, *refs):
    *cores, first, second = refs
    half = first.shape[0]
    for at in range(0, keep.shape[1], 256):
        cols = slice(at, at + 256)
        total = (added(keep, cores, cols) + far[:, cols].astype(F32)).astype(BF16)
        first[:, cols] = total[:half]
        second[:, cols] = total[half:]


def gather_kernel(own, a0, a1, b0, b1, keep_ref, send_ref):
    expert, outer, inner, dp = seat()
    small = own.shape[0] // 2
    start = jnp.where((inner & 1) == 0, own[...].astype(F32), a0[...].astype(F32))
    for i, total in enumerate((start + a1[...].astype(F32), b0[...].astype(F32) + b1[...].astype(F32))):
        rows = slice(i * small, (i + 1) * small)
        keep_ref[rows, :] = total[:small]
        send_ref[rows, :] = total[small:].astype(BF16)


def tail_kernel(own, keep, core, gain, stream_ref, normed_ref):
    expert, outer, inner, dp = seat()
    small, half = own.shape[0], keep.shape[1]
    for i, at in enumerate((dp, 1 - dp)):
        rows = slice(i * small, (i + 1) * small)
        cols = aligned(at, half)
        mixture = keep[rows, :] + core[rows, :].astype(F32)
        stream_ref[:, cols] = (own[:, cols].astype(F32) + mixture).astype(BF16)
    normed_ref[...] = rms_scale(stream_ref[...].astype(F32), gain[...]).astype(BF16)


def body_paired(
    attn,
    resid,
    w_out,
    gain_post,
    route_ids,
    route_logits,
    live_count,
    w_gate_up,
    w_down,
    gain_final,
):
    rows_here = resid.shape[1]
    model_width = resid.shape[2]
    expert_count = lax.axis_size("expert")
    hidden = w_down.shape[1]
    half_width = w_down.shape[2]
    quarter = model_width // 4
    vmem, smem = whole_vmem(), whole_smem()

    def shape_of(*shape, dtype=BF16):
        return jax.ShapeDtypeStruct(shape, dtype)

    def call(kernel, name, mib, outs, *args, scratch=(), first=vmem):
        return pl.pallas_call(
            kernel,
            out_shape=outs,
            in_specs=[first] + [vmem] * (len(args) - 1),
            out_specs=tuple(vmem for _ in outs),
            scratch_shapes=list(scratch),
            compiler_params=kernel_params(mib),
            cost_estimate=small_cost(),
            name=name,
        )(*args)

    def swap_dp(x):
        return lax.ppermute(x, "dp", [(0, 1), (1, 0)])

    def shift_outer(x, s):
        return lax.ppermute(
            x, "expert", [(i, (i + 4 * s) % expert_count) for i in range(expert_count)]
        )

    def send_outer(x, i, cross):
        pairs = []
        for at in range(2 * expert_count):
            d, e = divmod(at, expert_count)
            step = 2 * (e % 2) + i
            if step or cross:
                pairs.append((at, (d ^ cross) * expert_count + (e + 4 * step) % expert_count))
        return lax.ppermute(x, ("dp", "expert"), pairs)

    def swap_inner(x, j):
        return lax.ppermute(x, "expert", [(i, i ^ j) for i in range(expert_count)])

    def swap_outer(x, s):
        return lax.ppermute(x, "expert", [(i, i ^ (4 * s)) for i in range(expert_count)])

    def after(x, *results):
        return lax.optimization_barrier((x, *results))[0]

    def weight_piece(first, size, mib=8):
        return pl.pallas_call(
            functools.partial(piece_kernel, (first, hidden + first)),
            out_shape=shape_of(half_width, 2 * size),
            in_specs=[pl.BlockSpec(memory_space=pl.ANY)],
            out_specs=vmem,
            scratch_shapes=[pltpu.SemaphoreType.DMA((2, 4))],
            compiler_params=kernel_params(mib),
            cost_estimate=small_cost(),
            name="weight_piece",
        )(w_gate_up[0])

    piece = shape_of(rows_here, quarter)
    r_own, r_1, r_23 = call(
        cut_kernel, "cut_resid", 4, (piece, piece, shape_of(2 * rows_here, quarter)), resid[0]
    )
    (share,) = call(
        share_kernel,
        "share",
        4,
        (shape_of(expert_count, quarter),),
        live_count,
        route_ids[0],
        route_logits[0],
        first=smem,
    )
    cut_width = hidden // 2
    early_pieces = [weight_piece(0, cut_width, 58)]
    late_pieces = [weight_piece(cut_width, hidden - cut_width)]
    gate_up_early = [swap_dp(piece) for piece in early_pieces]
    a = [attn[0], swap_outer(attn[0], 1), swap_outer(attn[0], 2)]
    w_x = swap_inner(w_out, 2)
    r_2 = swap_outer(r_23, 2)
    a.append(swap_outer(after(a[2], a[1], r_2), 1))
    w_c = swap_inner(after(w_out, w_x, share, *late_pieces), 1)
    w_cx = swap_inner(w_x, 1)
    r_13 = swap_outer(jnp.concatenate([r_1, r_2[rows_here:]], axis=0), 1)

    product = shape_of(4 * rows_here, quarter)
    keep, send = call(
        proj_kernel,
        "projection",
        8,
        (product, product),
        *a,
        w_out,
        w_c,
        w_x,
        w_cx,
        scratch=(
            pltpu.VMEM((8 * rows_here, attn.shape[2]), BF16),
            pltpu.VMEM((8 * rows_here, quarter), BF16),
        ),
    )
    arrived = swap_dp(after(send, gate_up_early[0], r_13))
    gate_up_late = [swap_dp(after(piece, arrived)) for piece in late_pieces]
    (block,) = call(
        stream_kernel,
        "stream",
        4,
        (shape_of(4 * rows_here + expert_count, quarter),),
        keep,
        arrived,
        r_own,
        r_13,
        r_2,
        share,
    )

    def norm(b0, b1, b2, b3):
        outs = (shape_of(4 * rows_here, model_width + 128), shape_of(rows_here, model_width))
        return call(norm_kernel, "norm", 8, outs, b0, b1, b2, b3, gain_post[None])

    blocks = [block] + [shift_outer(block, s) for s in (1, 2, 3)]
    group, stream_own = norm(*blocks)
    blocks_x = [swap_inner(b, 2) for b in blocks]
    group_x, unused = norm(*blocks_x)
    group_c = swap_inner(group, 1)
    group_cx = swap_inner(group_x, 1)

    row_total = 16 * rows_here
    half_rows = row_total // 2
    inner_first, part, other_rows, share_rows = call(
        first_gate_kernel,
        "first_gate_up",
        24,
        (
            shape_of(row_total, cut_width),
            shape_of(row_total, hidden, dtype=F32),
            shape_of(row_total, half_width),
            shape_of(row_total, 128, dtype=F32),
        ),
        group_x,
        group_cx,
        group,
        group_c,
        w_gate_up[0],
        *gate_up_early,
        scratch=(pltpu.VMEM((row_total, half_width), BF16),),
    )
    inner_half = shape_of(half_rows, hidden)
    inner_far, inner_near = call(
        last_gate_kernel,
        "last_gate_up",
        16,
        (inner_half, inner_half),
        inner_first,
        part,
        other_rows,
        share_rows,
        *gate_up_late,
    )
    far_other = swap_dp(inner_far)
    near_other = swap_dp(inner_near)

    count = row_total // 4
    quarter_out = shape_of(count, half_width)

    def parts_of(many):
        return (shape_of(count, half_width // many),) * many

    scratch = (pltpu.VMEM((half_rows, hidden), BF16),)

    def down(rows, many):
        keep, *send = call(
            down_kernel, "down", 12, (quarter_out, *parts_of(many)), rows, w_down[0], scratch=scratch
        )
        return keep, send

    def swap_cores(halves):
        return [swap_inner(half, 1) for half in halves]

    def fold(keep, halves):
        return call(fold_kernel, "fold", 4, (quarter_out,), keep, *halves)[0]

    def pieces(far, keep, send):
        outs = (shape_of(2 * rows_here, half_width),) * 2
        return call(pieces_kernel, "pieces", 4, outs, far, keep, *swap_cores(send))

    outs = (quarter_out, *parts_of(2), *parts_of(2), quarter_out)
    keep_far, *send, keep_near = call(
        down_both_kernel, "down_both", 16, outs, inner_far, inner_near, w_down[0], scratch=scratch
    )
    far = swap_inner(fold(keep_far, swap_cores(send[:2])), 2)
    ready = far
    own, second = pieces(far, keep_near, send[2:])
    mine = [send_outer(own, 0, False), send_outer(second, 1, False)]

    keep_far, send = down(after(far_other, ready), 2)
    far = swap_inner(fold(keep_far, swap_cores(send)), 2)
    keep_near, send = down(near_other, 2)
    cut = pieces(far, after(keep_near, *mine), send)
    others = [send_outer(cut[i], i, True) for i in range(2)]

    sums = shape_of(2 * rows_here, half_width)
    keep, send = call(
        gather_kernel,
        "gather",
        4,
        (shape_of(2 * rows_here, half_width, dtype=F32), sums),
        own,
        *mine,
        *others,
    )
    out = shape_of(rows_here, model_width)
    stream_out, normed_out = call(
        tail_kernel, "closing", 8, (out, out), stream_own, keep, swap_inner(send, 1), gain_final[None]
    )
    return (stream_out[None], normed_out[None])


def solution(mesh):
    placed = (
        P("expert", None, "dp"),
        P("expert", "dp", None),
        P("dp", "expert"),
        P(),
        P("expert", "dp", None),
        P("expert", "dp", None),
        P("expert", "dp"),
        P("expert", "dp", None),
        P("expert", None, "dp"),
        P(),
    )
    paired = mesh.shape["dp"] == 2 and mesh.shape["expert"] == 16
    return jax.shard_map(
        body_paired if paired else body_general,
        mesh=mesh,
        in_specs=placed,
        out_specs=(P("expert", "dp", None), P("expert", "dp", None)),
        check_vma=False,
    )
```

```python
import functools
import math

import jax
import jax.numpy as jnp
from jax import lax
from jax.experimental import pallas as pl
from jax.experimental.pallas import tpu as pltpu
from jax.sharding import PartitionSpec as P


def rms_scale(values, gain):
    return values * lax.rsqrt(jnp.mean(values * values, axis=-1, keepdims=True) + 1e-06) * gain


def swiglu_rows(rows_in, gate_up, down, hidden_units):
    both = jnp.dot(rows_in, gate_up, preferred_element_type=jnp.float32)
    inner = (jax.nn.silu(both[:, :hidden_units]) * both[:, hidden_units:]).astype(jnp.bfloat16)
    return jnp.dot(inner, down, preferred_element_type=jnp.float32).astype(jnp.bfloat16)


def body_general(
    attn,
    resid,
    w_out,
    gain_post,
    route_ids,
    route_logits,
    live_count,
    w_gate_up,
    w_down,
    gain_final,
):
    rows_here = resid.shape[1]
    model_width = resid.shape[2]
    top_count = route_ids.shape[2]
    dp_count = lax.axis_size("dp")
    expert_count = lax.axis_size("expert")
    hidden_units = w_down.shape[1]
    capacity = dp_count * max(1, 2 * rows_here * top_count // (expert_count * dp_count))
    slot_count = expert_count * capacity
    flat_attn = attn[0]
    partial_out = jnp.dot(
        flat_attn,
        lax.all_gather(w_out, "expert", axis=1, tiled=True),
        preferred_element_type=jnp.float32,
    )
    projected = lax.psum_scatter(
        partial_out.astype(jnp.bfloat16), "dp", scatter_dimension=0, tiled=True
    ).astype(jnp.float32)
    stream_in = (resid[0].astype(jnp.float32) + projected).astype(jnp.bfloat16)
    stream_float = stream_in.astype(jnp.float32)
    normed_in = rms_scale(stream_float, gain_post).astype(jnp.bfloat16)
    probs = jax.nn.softmax(route_logits[0], axis=-1).astype(jnp.bfloat16)
    alive = jnp.arange(rows_here, dtype=jnp.int32) < live_count[0, 0]
    expert_of = route_ids[0].reshape(-1)
    route_alive = jnp.repeat(alive, top_count)
    onehot = (
        (expert_of[:, None] == jnp.arange(expert_count, dtype=jnp.int32)[None, :])
        & route_alive[:, None]
    ).astype(jnp.int32)
    earlier = jnp.sum((jnp.cumsum(onehot, axis=0) - onehot) * onehot, axis=1)
    target = expert_of * capacity + earlier
    match = (target[:, None] == jnp.arange(slot_count, dtype=jnp.int32)[None, :]) & route_alive[
        :, None
    ]
    placed = match.reshape(rows_here, top_count, slot_count)
    gather_matrix = jnp.any(placed, axis=1).astype(jnp.bfloat16)
    send_rows = lax.dot_general(
        gather_matrix, normed_in, (((0,), (0,)), ((), ())), preferred_element_type=jnp.float32
    ).astype(jnp.bfloat16)
    send_flags = jnp.sum(gather_matrix.astype(jnp.float32), axis=0).astype(jnp.bfloat16)
    combine_matrix = jnp.sum(
        jnp.where(placed, probs.astype(jnp.float32)[:, :, None], jnp.float32(0.0)), axis=1
    ).astype(jnp.bfloat16)
    arrived_rows, arrived_flags = (
        lax.all_to_all(
            send_rows.reshape(expert_count, capacity, model_width),
            "expert",
            split_axis=0,
            concat_axis=0,
            tiled=True,
        ),
        lax.all_to_all(
            send_flags.reshape(expert_count, capacity),
            "expert",
            split_axis=0,
            concat_axis=0,
            tiled=True,
        ),
    )
    arrived = arrived_rows.reshape(slot_count, model_width)
    flags = arrived_flags.reshape(slot_count)
    gate_up_full, down_full = (
        lax.all_gather(w_gate_up, "dp", axis=1, tiled=True),
        lax.all_gather(w_down, "dp", axis=2, tiled=True),
    )
    live_slot = (flags > 0.5).astype(jnp.int32)
    order = jnp.argsort(1 - live_slot, stable=True)
    live_total = jnp.sum(live_slot)
    packed = arrived[order]
    block_len = math.gcd(slot_count, 128)
    block_total = (live_total + block_len - 1) // block_len

    def run_block(index, outputs):
        begin = index * block_len
        rows_in = lax.dynamic_slice_in_dim(packed, begin, block_len, 0)
        block_out = swiglu_rows(rows_in, gate_up_full[0], down_full[0], hidden_units)
        return lax.dynamic_update_slice_in_dim(outputs, block_out, begin, 0)

    packed_out = lax.fori_loop(
        0, block_total, run_block, jnp.zeros((slot_count, model_width), jnp.bfloat16)
    )
    position = (
        jnp.zeros((slot_count,), jnp.int32).at[order].set(jnp.arange(slot_count, dtype=jnp.int32))
    )
    results = packed_out[position]
    returned = lax.all_to_all(
        results.reshape(expert_count, capacity, model_width),
        "expert",
        split_axis=0,
        concat_axis=0,
        tiled=True,
    )
    returned = returned.reshape(slot_count, model_width)
    mixture = jnp.dot(combine_matrix, returned, preferred_element_type=jnp.float32)
    stream_out = (stream_float + mixture).astype(jnp.bfloat16)
    normed_out = rms_scale(stream_out.astype(jnp.float32), gain_final).astype(jnp.bfloat16)
    return (stream_out[None], normed_out[None])


MIB = 1024 * 1024
BF16, F32 = jnp.bfloat16, jnp.float32


def whole_vmem():
    return pl.BlockSpec(memory_space=pltpu.VMEM)


def whole_smem():
    return pl.BlockSpec(memory_space=pltpu.SMEM)


def fixed(*shape):
    return pl.BlockSpec(shape, lambda i: (0,) * len(shape))


def dot(a, b):
    return jnp.dot(a, b, preferred_element_type=F32)


def small_cost():
    return pl.CostEstimate(flops=1, bytes_accessed=1, transcendentals=0)


def kernel_params(mib):
    return pltpu.CompilerParams(vmem_limit_bytes=mib * MIB)


def seat():
    expert = lax.axis_index("expert")
    return expert, lax.shift_right_logical(expert, 2), expert & 3, lax.axis_index("dp")


def aligned(index, step):
    return pl.ds(pl.multiple_of(index * step, step), step)


def cut_kernel(resid, r0, r1, r23):
    expert, outer, inner, dp = seat()
    rows, lanes = r0.shape
    r0[...] = resid[:, aligned(outer, lanes)]
    r1[...] = resid[:, aligned(outer ^ 1, lanes)]
    for i in range(2):
        r23[i * rows : (i + 1) * rows, :] = resid[:, aligned(outer ^ (2 + i), lanes)]


def share_kernel(live, ids, logits, share_ref):
    expert, outer, inner, dp = seat()
    rows, top = ids.shape
    experts, lanes = share_ref.shape
    value = logits[...]
    value = jnp.exp(value - jnp.max(value, axis=1, keepdims=True))
    probs = (value / jnp.sum(value, axis=1, keepdims=True)).astype(BF16).astype(F32)
    probs = jnp.where(lax.broadcasted_iota(jnp.int32, (rows, top), 0) < live[0, 0], probs, 0.0)
    names = lax.broadcasted_iota(jnp.int32, (rows, experts), 1)
    table = jnp.zeros((rows, experts), F32)
    for k in range(top):
        table = table + jnp.where(ids[:, k : k + 1] == names, probs[:, k : k + 1], 0.0)
    spots = lax.broadcasted_iota(jnp.int32, (rows, lanes), 1) - outer * rows
    spots = (spots == lax.broadcasted_iota(jnp.int32, (rows, lanes), 0)).astype(F32).astype(BF16)
    share_ref[...] = lax.dot_general(
        table.astype(BF16), spots, (((0,), (0,)), ((), ())), preferred_element_type=F32
    ).astype(BF16)


def proj_kernel(a0, a1, a2, a3, w0, w1, w2, w3, keep_ref, send_ref, rows, part):
    expert, outer, inner, dp = seat()
    full = a0.shape[0]
    half = full // 2
    block = w0.shape[1]
    for s, a in enumerate((a0, a1, a2, a3)):
        rows[aligned(outer ^ s, full), :] = a[...]
    for j, w in enumerate((w0, w1, w2, w3)):
        part[:, aligned(inner ^ j, block)] = dot(rows[...], w[...]).astype(BF16)
    for spot in range(4):
        keep_ref[spot * half : (spot + 1) * half, :] = part[aligned(2 * spot + dp, half), :]
        send_ref[spot * half : (spot + 1) * half, :] = part[aligned(2 * spot + 1 - dp, half), :]


def stream_kernel(keep, arrived, r0, r13, r2, share, block_ref):
    expert, outer, inner, dp = seat()
    count = keep.shape[0]
    small = r0.shape[0]
    for s, r in enumerate((r0[...], r13[0:small, :], r2[0:small, :], r13[small:, :])):
        rows = aligned(outer ^ s, small)
        product = keep[rows, :].astype(F32) + arrived[rows, :].astype(F32)
        block_ref[rows, :] = (r.astype(F32) + product).astype(BF16)
    block_ref[count:, :] = share[...]


def piece_kernel(starts, weights, out, semaphores):
    parts = semaphores.shape[1]
    depth, width = out.shape[0] // parts, out.shape[1] // 2
    copies = [
        pltpu.make_async_copy(
            weights.at[pl.ds(k * depth, depth), pl.ds(starts[i], width)],
            out.at[pl.ds(k * depth, depth), pl.ds(i * width, width)],
            semaphores.at[i, k],
        )
        for i in range(2)
        for k in range(parts)
    ]
    for copy in copies:
        copy.start()
    for copy in copies:
        copy.wait()


def swiglu(gate, up, share):
    return (gate / (1.0 + jnp.exp(-gate)) * up * share).astype(BF16)


def norm_kernel(b0, b1, b2, b3, gain, group_ref, own_ref):
    expert, outer, inner, dp = seat()
    count = group_ref.shape[0]
    width = b0.shape[1]
    experts = b0.shape[0] - count
    small = own_ref.shape[0]
    square = jnp.zeros((count, 1), F32)
    share = jnp.zeros((experts, count), F32)
    for s, b in enumerate((b0, b1, b2, b3)):
        value = b[0:count, :]
        group_ref[:, aligned((outer + 4 - s) & 3, width)] = value
        value = value.astype(F32)
        square = square + jnp.sum(value * value, axis=1, keepdims=True)
        share = share + b[count : count + experts, 0:count].astype(F32)
    own_ref[...] = group_ref[aligned(outer, small), 0 : 4 * width]
    scale = lax.rsqrt(square / (4 * width) + 1e-06)
    for s in range(4):
        cols = slice(s * width, (s + 1) * width)
        value = group_ref[:, cols].astype(F32)
        group_ref[:, cols] = (value * scale * gain[:, cols]).astype(BF16)
    lanes = (experts, 128)
    spread = lax.broadcasted_iota(jnp.int32, lanes, 0) == lax.broadcasted_iota(jnp.int32, lanes, 1)
    group_ref[:, 4 * width :] = lax.dot_general(
        share.astype(BF16),
        spread.astype(F32).astype(BF16),
        (((0,), (0,)), ((), ())),
        preferred_element_type=F32,
    ).astype(BF16)


def first_gate_kernel(group_x, group_cx, group, group_c, own, *refs):
    *early, inner_ref, part_ref, other_ref, share_ref, mine_ref = refs
    expert, outer, inner, dp = seat()
    count = group.shape[0]
    half = other_ref.shape[1]
    cut = inner_ref.shape[1]
    for j, g in enumerate((group_x, group_cx, group, group_c)):
        rows = slice(j * count, (j + 1) * count)
        mine_ref[rows, :] = g[:, aligned(dp, half)]
        other_ref[rows, :] = g[:, aligned(1 - dp, half)]
        share = g[:, 2 * half : 2 * half + 128].astype(F32)
        picked = lax.broadcasted_iota(jnp.int32, share.shape, 1) == expert
        share = jnp.sum(jnp.where(picked, share, 0.0), axis=1, keepdims=True)
        share_ref[rows, :] = jnp.broadcast_to(share, (count, 128))
    mine, other = mine_ref[...], other_ref[...]
    at = 0
    for piece in early:
        size = piece.shape[1] // 2
        gate = dot(mine, own[:, at : at + size]) + dot(other, piece[:, 0:size])
        up = dot(mine, own[:, 2 * cut + at : 2 * cut + at + size]) + dot(other, piece[:, size:])
        inner_ref[:, at : at + size] = swiglu(gate, up, share_ref[:, 0:1])
        at += size
    part_ref[:, 0:cut] = dot(mine, own[:, cut : 2 * cut])
    part_ref[:, cut : 2 * cut] = dot(mine, own[:, 3 * cut : 4 * cut])


def last_gate_kernel(first, part, other, share, *refs):
    *late, far_ref, near_ref = refs
    cut = first.shape[1]
    half = far_ref.shape[0]
    far_ref[:, 0:cut] = first[0:half, :]
    near_ref[:, 0:cut] = first[half:, :]
    at = 0
    for piece in late:
        size = piece.shape[1] // 2
        gate = part[:, at : at + size] + dot(other[...], piece[:, 0:size])
        up = part[:, cut + at : cut + at + size] + dot(other[...], piece[:, size : 2 * size])
        value = swiglu(gate, up, share[:, 0:1])
        cols = slice(cut + at, cut + at + size)
        far_ref[:, cols] = value[:half]
        near_ref[:, cols] = value[half:]
        at += size


def column_chunks(wd):
    return [slice(at, at + 256) for at in range(0, wd.shape[1], 256)]


def down_both_kernel(far, near, wd, keep_far, *refs):
    *sends, keep_near, rows = refs
    half = len(sends) // 2
    down_kernel(far, wd, keep_far, *sends[:half], rows)
    down_kernel(near, wd, keep_near, *sends[half:], rows)


def down_kernel(block, wd, keep_ref, *refs):
    *sends, rows = refs
    expert, outer, inner, dp = seat()
    core = inner & 1
    count, side = sends[0].shape
    small = count // 4
    for i in range(2):
        for j in range(2):
            kept = aligned(4 * j + ((outer + 2 * core + i) & 3), small)
            sent = aligned(4 * (1 - j) + ((outer + 2 - 2 * core + i) & 3), small)
            at = (2 * i + j) * small
            rows[at : at + small, :] = block[kept, :]
            rows[count + at : count + at + small, :] = block[sent, :]
    for at in range(0, wd.shape[1], 256):
        value = dot(rows[...], wd[:, at : at + 256]).astype(BF16)
        keep_ref[:, at : at + 256] = value[:count]
        sends[at // side][:, at % side : at % side + 256] = value[count:]


def added(keep, cores, cols):
    side = cores[0].shape[1]
    return keep[:, cols].astype(F32) + cores[cols.start // side][:, cols.start % side : cols.start % side + 256].astype(F32)


def fold_kernel(keep, *refs):
    *cores, out = refs
    for at in range(0, keep.shape[1], 256):
        cols = slice(at, at + 256)
        out[:, cols] = added(keep, cores, cols).astype(BF16)


def pieces_kernel(far, keep, *refs):
    *cores, first, second = refs
    half = first.shape[0]
    for at in range(0, keep.shape[1], 256):
        cols = slice(at, at + 256)
        total = (added(keep, cores, cols) + far[:, cols].astype(F32)).astype(BF16)
        first[:, cols] = total[:half]
        second[:, cols] = total[half:]


def gather_kernel(own, a0, a1, b0, b1, keep_ref, send_ref):
    expert, outer, inner, dp = seat()
    small = own.shape[0] // 2
    start = jnp.where((inner & 1) == 0, own[...].astype(F32), a0[...].astype(F32))
    for i, total in enumerate((start + a1[...].astype(F32), b0[...].astype(F32) + b1[...].astype(F32))):
        rows = slice(i * small, (i + 1) * small)
        keep_ref[rows, :] = total[:small]
        send_ref[rows, :] = total[small:].astype(BF16)


def tail_kernel(own, keep, core, gain, stream_ref, normed_ref):
    expert, outer, inner, dp = seat()
    small, half = own.shape[0], keep.shape[1]
    for i, at in enumerate((dp, 1 - dp)):
        rows = slice(i * small, (i + 1) * small)
        cols = aligned(at, half)
        mixture = keep[rows, :] + core[rows, :].astype(F32)
        stream_ref[:, cols] = (own[:, cols].astype(F32) + mixture).astype(BF16)
    normed_ref[...] = rms_scale(stream_ref[...].astype(F32), gain[...]).astype(BF16)


def body_paired(
    attn,
    resid,
    w_out,
    gain_post,
    route_ids,
    route_logits,
    live_count,
    w_gate_up,
    w_down,
    gain_final,
):
    rows_here = resid.shape[1]
    model_width = resid.shape[2]
    expert_count = lax.axis_size("expert")
    hidden = w_down.shape[1]
    half_width = w_down.shape[2]
    quarter = model_width // 4
    vmem, smem = whole_vmem(), whole_smem()

    def shape_of(*shape, dtype=BF16):
        return jax.ShapeDtypeStruct(shape, dtype)

    def call(kernel, name, mib, outs, *args, scratch=(), first=vmem):
        return pl.pallas_call(
            kernel,
            out_shape=outs,
            in_specs=[first] + [vmem] * (len(args) - 1),
            out_specs=tuple(vmem for _ in outs),
            scratch_shapes=list(scratch),
            compiler_params=kernel_params(mib),
            cost_estimate=small_cost(),
            name=name,
        )(*args)

    def swap_dp(x):
        return lax.ppermute(x, "dp", [(0, 1), (1, 0)])

    def shift_outer(x, s):
        return lax.ppermute(
            x, "expert", [(i, (i + 4 * s) % expert_count) for i in range(expert_count)]
        )

    def send_outer(x, i, cross):
        pairs = []
        for at in range(2 * expert_count):
            d, e = divmod(at, expert_count)
            step = 2 * (e % 2) + i
            if step or cross:
                pairs.append((at, (d ^ cross) * expert_count + (e + 4 * step) % expert_count))
        return lax.ppermute(x, ("dp", "expert"), pairs)

    def swap_inner(x, j):
        return lax.ppermute(x, "expert", [(i, i ^ j) for i in range(expert_count)])

    def swap_outer(x, s):
        return lax.ppermute(x, "expert", [(i, i ^ (4 * s)) for i in range(expert_count)])

    def after(x, *results):
        return lax.optimization_barrier((x, *results))[0]

    def weight_piece(first, size, mib=8):
        return pl.pallas_call(
            functools.partial(piece_kernel, (first, hidden + first)),
            out_shape=shape_of(half_width, 2 * size),
            in_specs=[pl.BlockSpec(memory_space=pl.ANY)],
            out_specs=vmem,
            scratch_shapes=[pltpu.SemaphoreType.DMA((2, 16))],
            compiler_params=kernel_params(mib),
            cost_estimate=small_cost(),
            name="weight_piece",
        )(w_gate_up[0])

    piece = shape_of(rows_here, quarter)
    r_own, r_1, r_23 = call(
        cut_kernel, "cut_resid", 4, (piece, piece, shape_of(2 * rows_here, quarter)), resid[0]
    )
    (share,) = call(
        share_kernel,
        "share",
        4,
        (shape_of(expert_count, quarter),),
        live_count,
        route_ids[0],
        route_logits[0],
        first=smem,
    )
    cut_width = hidden // 2
    early_pieces = [weight_piece(0, cut_width, 58)]
    late_pieces = [weight_piece(cut_width, hidden - cut_width)]
    gate_up_early = [swap_dp(piece) for piece in early_pieces]
    a = [attn[0], swap_outer(attn[0], 1), swap_outer(attn[0], 2)]
    w_x = swap_inner(w_out, 2)
    r_2 = swap_outer(r_23, 2)
    a.append(swap_outer(after(a[2], a[1], r_2), 1))
    w_c = swap_inner(after(w_out, w_x, share, *late_pieces), 1)
    w_cx = swap_inner(w_x, 1)
    r_13 = swap_outer(jnp.concatenate([r_1, r_2[rows_here:]], axis=0), 1)

    product = shape_of(4 * rows_here, quarter)
    keep, send = call(
        proj_kernel,
        "projection",
        8,
        (product, product),
        *a,
        w_out,
        w_c,
        w_x,
        w_cx,
        scratch=(
            pltpu.VMEM((8 * rows_here, attn.shape[2]), BF16),
            pltpu.VMEM((8 * rows_here, quarter), BF16),
        ),
    )
    arrived = swap_dp(after(send, r_13))
    gate_up_late = [swap_dp(after(piece, arrived)) for piece in late_pieces]
    (block,) = call(
        stream_kernel,
        "stream",
        4,
        (shape_of(4 * rows_here + expert_count, quarter),),
        after(keep, *gate_up_early),
        arrived,
        r_own,
        r_13,
        r_2,
        share,
    )

    def norm(b0, b1, b2, b3):
        outs = (shape_of(4 * rows_here, model_width + 128), shape_of(rows_here, model_width))
        return call(norm_kernel, "norm", 8, outs, b0, b1, b2, b3, gain_post[None])

    blocks = [block] + [shift_outer(block, s) for s in (1, 2, 3)]
    group, stream_own = norm(*blocks)
    blocks_x = [swap_inner(b, 2) for b in blocks]
    group_x, unused = norm(*blocks_x)
    group_c = swap_inner(group, 1)
    group_cx = swap_inner(group_x, 1)

    row_total = 16 * rows_here
    half_rows = row_total // 2
    inner_first, part, other_rows, share_rows = call(
        first_gate_kernel,
        "first_gate_up",
        24,
        (
            shape_of(row_total, cut_width),
            shape_of(row_total, hidden, dtype=F32),
            shape_of(row_total, half_width),
            shape_of(row_total, 128, dtype=F32),
        ),
        group_x,
        group_cx,
        group,
        group_c,
        w_gate_up[0],
        *gate_up_early,
        scratch=(pltpu.VMEM((row_total, half_width), BF16),),
    )
    inner_half = shape_of(half_rows, hidden)
    inner_far, inner_near = call(
        last_gate_kernel,
        "last_gate_up",
        16,
        (inner_half, inner_half),
        inner_first,
        part,
        other_rows,
        share_rows,
        *gate_up_late,
    )
    far_other = swap_dp(inner_far)
    near_other = swap_dp(inner_near)

    count = row_total // 4
    quarter_out = shape_of(count, half_width)

    def parts_of(many):
        return (shape_of(count, half_width // many),) * many

    scratch = (pltpu.VMEM((half_rows, hidden), BF16),)

    def down(rows, many):
        keep, *send = call(
            down_kernel, "down", 12, (quarter_out, *parts_of(many)), rows, w_down[0], scratch=scratch
        )
        return keep, send

    def swap_cores(halves):
        return [swap_inner(half, 1) for half in halves]

    def fold(keep, halves):
        return call(fold_kernel, "fold", 4, (quarter_out,), keep, *halves)[0]

    def pieces(far, keep, send):
        outs = (shape_of(2 * rows_here, half_width),) * 2
        return call(pieces_kernel, "pieces", 4, outs, far, keep, *swap_cores(send))

    outs = (quarter_out, *parts_of(2), *parts_of(2), quarter_out)
    keep_far, *send, keep_near = call(
        down_both_kernel, "down_both", 16, outs, inner_far, inner_near, w_down[0], scratch=scratch
    )
    far = swap_inner(fold(keep_far, swap_cores(send[:2])), 2)
    ready = far
    own, second = pieces(far, keep_near, send[2:])
    mine = [send_outer(own, 0, False), send_outer(second, 1, False)]

    keep_far, send = down(after(far_other, ready), 2)
    far = swap_inner(fold(keep_far, swap_cores(send)), 2)
    keep_near, send = down(near_other, 2)
    cut = pieces(far, after(keep_near, *mine), send)
    others = [send_outer(cut[i], i, True) for i in range(2)]

    sums = shape_of(2 * rows_here, half_width)
    keep, send = call(
        gather_kernel,
        "gather",
        4,
        (shape_of(2 * rows_here, half_width, dtype=F32), sums),
        own,
        *mine,
        *others,
    )
    out = shape_of(rows_here, model_width)
    stream_out, normed_out = call(
        tail_kernel, "closing", 8, (out, out), stream_own, keep, swap_inner(send, 1), gain_final[None]
    )
    return (stream_out[None], normed_out[None])


def solution(mesh):
    placed = (
        P("expert", None, "dp"),
        P("expert", "dp", None),
        P("dp", "expert"),
        P(),
        P("expert", "dp", None),
        P("expert", "dp", None),
        P("expert", "dp"),
        P("expert", "dp", None),
        P("expert", None, "dp"),
        P(),
    )
    paired = mesh.shape["dp"] == 2 and mesh.shape["expert"] == 16
    return jax.shard_map(
        body_paired if paired else body_general,
        mesh=mesh,
        in_specs=placed,
        out_specs=(P("expert", "dp", None), P("expert", "dp", None)),
        check_vma=False,
    )
```

```python
import functools
import math

import jax
import jax.numpy as jnp
from jax import lax
from jax.experimental import pallas as pl
from jax.experimental.pallas import tpu as pltpu
from jax.sharding import PartitionSpec as P


def rms_scale(values, gain):
    return values * lax.rsqrt(jnp.mean(values * values, axis=-1, keepdims=True) + 1e-06) * gain


def swiglu_rows(rows_in, gate_up, down, hidden_units):
    both = jnp.dot(rows_in, gate_up, preferred_element_type=jnp.float32)
    inner = (jax.nn.silu(both[:, :hidden_units]) * both[:, hidden_units:]).astype(jnp.bfloat16)
    return jnp.dot(inner, down, preferred_element_type=jnp.float32).astype(jnp.bfloat16)


def body_general(
    attn,
    resid,
    w_out,
    gain_post,
    route_ids,
    route_logits,
    live_count,
    w_gate_up,
    w_down,
    gain_final,
):
    rows_here = resid.shape[1]
    model_width = resid.shape[2]
    top_count = route_ids.shape[2]
    dp_count = lax.axis_size("dp")
    expert_count = lax.axis_size("expert")
    hidden_units = w_down.shape[1]
    capacity = dp_count * max(1, 2 * rows_here * top_count // (expert_count * dp_count))
    slot_count = expert_count * capacity
    flat_attn = attn[0]
    partial_out = jnp.dot(
        flat_attn,
        lax.all_gather(w_out, "expert", axis=1, tiled=True),
        preferred_element_type=jnp.float32,
    )
    projected = lax.psum_scatter(
        partial_out.astype(jnp.bfloat16), "dp", scatter_dimension=0, tiled=True
    ).astype(jnp.float32)
    stream_in = (resid[0].astype(jnp.float32) + projected).astype(jnp.bfloat16)
    stream_float = stream_in.astype(jnp.float32)
    normed_in = rms_scale(stream_float, gain_post).astype(jnp.bfloat16)
    probs = jax.nn.softmax(route_logits[0], axis=-1).astype(jnp.bfloat16)
    alive = jnp.arange(rows_here, dtype=jnp.int32) < live_count[0, 0]
    expert_of = route_ids[0].reshape(-1)
    route_alive = jnp.repeat(alive, top_count)
    onehot = (
        (expert_of[:, None] == jnp.arange(expert_count, dtype=jnp.int32)[None, :])
        & route_alive[:, None]
    ).astype(jnp.int32)
    earlier = jnp.sum((jnp.cumsum(onehot, axis=0) - onehot) * onehot, axis=1)
    target = expert_of * capacity + earlier
    match = (target[:, None] == jnp.arange(slot_count, dtype=jnp.int32)[None, :]) & route_alive[
        :, None
    ]
    placed = match.reshape(rows_here, top_count, slot_count)
    gather_matrix = jnp.any(placed, axis=1).astype(jnp.bfloat16)
    send_rows = lax.dot_general(
        gather_matrix, normed_in, (((0,), (0,)), ((), ())), preferred_element_type=jnp.float32
    ).astype(jnp.bfloat16)
    send_flags = jnp.sum(gather_matrix.astype(jnp.float32), axis=0).astype(jnp.bfloat16)
    combine_matrix = jnp.sum(
        jnp.where(placed, probs.astype(jnp.float32)[:, :, None], jnp.float32(0.0)), axis=1
    ).astype(jnp.bfloat16)
    arrived_rows, arrived_flags = (
        lax.all_to_all(
            send_rows.reshape(expert_count, capacity, model_width),
            "expert",
            split_axis=0,
            concat_axis=0,
            tiled=True,
        ),
        lax.all_to_all(
            send_flags.reshape(expert_count, capacity),
            "expert",
            split_axis=0,
            concat_axis=0,
            tiled=True,
        ),
    )
    arrived = arrived_rows.reshape(slot_count, model_width)
    flags = arrived_flags.reshape(slot_count)
    gate_up_full, down_full = (
        lax.all_gather(w_gate_up, "dp", axis=1, tiled=True),
        lax.all_gather(w_down, "dp", axis=2, tiled=True),
    )
    live_slot = (flags > 0.5).astype(jnp.int32)
    order = jnp.argsort(1 - live_slot, stable=True)
    live_total = jnp.sum(live_slot)
    packed = arrived[order]
    block_len = math.gcd(slot_count, 128)
    block_total = (live_total + block_len - 1) // block_len

    def run_block(index, outputs):
        begin = index * block_len
        rows_in = lax.dynamic_slice_in_dim(packed, begin, block_len, 0)
        block_out = swiglu_rows(rows_in, gate_up_full[0], down_full[0], hidden_units)
        return lax.dynamic_update_slice_in_dim(outputs, block_out, begin, 0)

    packed_out = lax.fori_loop(
        0, block_total, run_block, jnp.zeros((slot_count, model_width), jnp.bfloat16)
    )
    position = (
        jnp.zeros((slot_count,), jnp.int32).at[order].set(jnp.arange(slot_count, dtype=jnp.int32))
    )
    results = packed_out[position]
    returned = lax.all_to_all(
        results.reshape(expert_count, capacity, model_width),
        "expert",
        split_axis=0,
        concat_axis=0,
        tiled=True,
    )
    returned = returned.reshape(slot_count, model_width)
    mixture = jnp.dot(combine_matrix, returned, preferred_element_type=jnp.float32)
    stream_out = (stream_float + mixture).astype(jnp.bfloat16)
    normed_out = rms_scale(stream_out.astype(jnp.float32), gain_final).astype(jnp.bfloat16)
    return (stream_out[None], normed_out[None])


MIB = 1024 * 1024
BF16, F32 = jnp.bfloat16, jnp.float32


def whole_vmem():
    return pl.BlockSpec(memory_space=pltpu.VMEM)


def whole_smem():
    return pl.BlockSpec(memory_space=pltpu.SMEM)


def fixed(*shape):
    return pl.BlockSpec(shape, lambda i: (0,) * len(shape))


def dot(a, b):
    return jnp.dot(a, b, preferred_element_type=F32)


def small_cost():
    return pl.CostEstimate(flops=1, bytes_accessed=1, transcendentals=0)


def kernel_params(mib):
    return pltpu.CompilerParams(vmem_limit_bytes=mib * MIB)


def seat():
    expert = lax.axis_index("expert")
    return expert, lax.shift_right_logical(expert, 2), expert & 3, lax.axis_index("dp")


def aligned(index, step):
    return pl.ds(pl.multiple_of(index * step, step), step)


def cut_kernel(resid, r0, r1, r23):
    expert, outer, inner, dp = seat()
    rows, lanes = r0.shape
    r0[...] = resid[:, aligned(outer, lanes)]
    r1[...] = resid[:, aligned(outer ^ 1, lanes)]
    for i in range(2):
        r23[i * rows : (i + 1) * rows, :] = resid[:, aligned(outer ^ (2 + i), lanes)]


def share_kernel(live, ids, logits, share_ref):
    expert, outer, inner, dp = seat()
    rows, top = ids.shape
    experts, lanes = share_ref.shape
    value = logits[...]
    value = jnp.exp(value - jnp.max(value, axis=1, keepdims=True))
    probs = (value / jnp.sum(value, axis=1, keepdims=True)).astype(BF16).astype(F32)
    probs = jnp.where(lax.broadcasted_iota(jnp.int32, (rows, top), 0) < live[0, 0], probs, 0.0)
    names = lax.broadcasted_iota(jnp.int32, (rows, experts), 1)
    table = jnp.zeros((rows, experts), F32)
    for k in range(top):
        table = table + jnp.where(ids[:, k : k + 1] == names, probs[:, k : k + 1], 0.0)
    spots = lax.broadcasted_iota(jnp.int32, (rows, lanes), 1) - outer * rows
    spots = (spots == lax.broadcasted_iota(jnp.int32, (rows, lanes), 0)).astype(F32).astype(BF16)
    share_ref[...] = lax.dot_general(
        table.astype(BF16), spots, (((0,), (0,)), ((), ())), preferred_element_type=F32
    ).astype(BF16)


def proj_kernel(a0, a1, a2, a3, w0, w1, w2, w3, keep_ref, send_ref, rows, part):
    expert, outer, inner, dp = seat()
    full = a0.shape[0]
    half = full // 2
    block = w0.shape[1]
    for s, a in enumerate((a0, a1, a2, a3)):
        rows[aligned(outer ^ s, full), :] = a[...]
    for j, w in enumerate((w0, w1, w2, w3)):
        part[:, aligned(inner ^ j, block)] = dot(rows[...], w[...]).astype(BF16)
    for spot in range(4):
        keep_ref[spot * half : (spot + 1) * half, :] = part[aligned(2 * spot + dp, half), :]
        send_ref[spot * half : (spot + 1) * half, :] = part[aligned(2 * spot + 1 - dp, half), :]


def stream_kernel(keep, arrived, r0, r13, r2, share, block_ref):
    expert, outer, inner, dp = seat()
    count = keep.shape[0]
    small = r0.shape[0]
    for s, r in enumerate((r0[...], r13[0:small, :], r2[0:small, :], r13[small:, :])):
        rows = aligned(outer ^ s, small)
        product = keep[rows, :].astype(F32) + arrived[rows, :].astype(F32)
        block_ref[rows, :] = (r.astype(F32) + product).astype(BF16)
    block_ref[count:, :] = share[...]


def piece_kernel(starts, weights, *refs):
    *outs, semaphores = refs
    copies = []
    at = 0
    for k, out in enumerate(outs):
        depth, width = out.shape[0], out.shape[1] // 2
        for i in range(2):
            copies.append(
                pltpu.make_async_copy(
                    weights.at[pl.ds(at, depth), pl.ds(starts[i], width)],
                    out.at[:, pl.ds(i * width, width)],
                    semaphores.at[i, k],
                )
            )
        at += depth
    for copy in copies:
        copy.start()
    for copy in copies:
        copy.wait()


def swiglu(gate, up, share):
    return (gate / (1.0 + jnp.exp(-gate)) * up * share).astype(BF16)


def norm_kernel(b0, b1, b2, b3, gain, group_ref, own_ref):
    expert, outer, inner, dp = seat()
    count = group_ref.shape[0]
    width = b0.shape[1]
    experts = b0.shape[0] - count
    small = own_ref.shape[0]
    square = jnp.zeros((count, 1), F32)
    share = jnp.zeros((experts, count), F32)
    for s, b in enumerate((b0, b1, b2, b3)):
        value = b[0:count, :]
        group_ref[:, aligned((outer + 4 - s) & 3, width)] = value
        value = value.astype(F32)
        square = square + jnp.sum(value * value, axis=1, keepdims=True)
        share = share + b[count : count + experts, 0:count].astype(F32)
    own_ref[...] = group_ref[aligned(outer, small), 0 : 4 * width]
    scale = lax.rsqrt(square / (4 * width) + 1e-06)
    for s in range(4):
        cols = slice(s * width, (s + 1) * width)
        value = group_ref[:, cols].astype(F32)
        group_ref[:, cols] = (value * scale * gain[:, cols]).astype(BF16)
    lanes = (experts, 128)
    spread = lax.broadcasted_iota(jnp.int32, lanes, 0) == lax.broadcasted_iota(jnp.int32, lanes, 1)
    group_ref[:, 4 * width :] = lax.dot_general(
        share.astype(BF16),
        spread.astype(F32).astype(BF16),
        (((0,), (0,)), ((), ())),
        preferred_element_type=F32,
    ).astype(BF16)


def first_gate_kernel(
    group_x, group_cx, group, group_c, own, early, inner_ref, part_ref, other_ref, share_ref, mine_ref
):
    expert, outer, inner, dp = seat()
    count = group.shape[0]
    half = other_ref.shape[1]
    cut = inner_ref.shape[1]
    for j, g in enumerate((group_x, group_cx, group, group_c)):
        rows = slice(j * count, (j + 1) * count)
        mine_ref[rows, :] = g[:, aligned(dp, half)]
        other_ref[rows, :] = g[:, aligned(1 - dp, half)]
        share = g[:, 2 * half : 2 * half + 128].astype(F32)
        picked = lax.broadcasted_iota(jnp.int32, share.shape, 1) == expert
        share = jnp.sum(jnp.where(picked, share, 0.0), axis=1, keepdims=True)
        share_ref[rows, :] = jnp.broadcast_to(share, (count, 128))
    mine, other = mine_ref[...], other_ref[...]
    gate = dot(mine, own[:, 0:cut]) + dot(other, early[:, 0:cut])
    up = dot(mine, own[:, 2 * cut : 3 * cut]) + dot(other, early[:, cut : 2 * cut])
    inner_ref[...] = swiglu(gate, up, share_ref[:, 0:1])
    part_ref[:, 0:cut] = dot(mine, own[:, cut : 2 * cut])
    part_ref[:, cut : 2 * cut] = dot(mine, own[:, 3 * cut : 4 * cut])


def last_gate_kernel(first, part, other, share, *refs):
    *late, far_ref, near_ref = refs
    cut = first.shape[1]
    half = far_ref.shape[0]
    gate, up = part[:, 0:cut], part[:, cut : 2 * cut]
    at = 0
    for piece in late:
        rows = other[:, at : at + piece.shape[0]]
        gate = gate + dot(rows, piece[:, 0:cut])
        up = up + dot(rows, piece[:, cut : 2 * cut])
        at += piece.shape[0]
    value = swiglu(gate, up, share[:, 0:1])
    far_ref[:, 0:cut] = first[0:half, :]
    near_ref[:, 0:cut] = first[half:, :]
    far_ref[:, cut : 2 * cut] = value[:half]
    near_ref[:, cut : 2 * cut] = value[half:]


def down_both_kernel(far, near, wd, keep_far, *refs):
    *sends, keep_near, rows = refs
    half = len(sends) // 2
    down_kernel(far, wd, keep_far, *sends[:half], rows)
    down_kernel(near, wd, keep_near, *sends[half:], rows)


def down_kernel(block, wd, keep_ref, *refs):
    *sends, rows = refs
    expert, outer, inner, dp = seat()
    core = inner & 1
    count, side = sends[0].shape
    small = count // 4
    for i in range(2):
        for j in range(2):
            kept = aligned(4 * j + ((outer + 2 * core + i) & 3), small)
            sent = aligned(4 * (1 - j) + ((outer + 2 - 2 * core + i) & 3), small)
            at = (2 * i + j) * small
            rows[at : at + small, :] = block[kept, :]
            rows[count + at : count + at + small, :] = block[sent, :]
    for at in range(0, wd.shape[1], 256):
        value = dot(rows[...], wd[:, at : at + 256]).astype(BF16)
        keep_ref[:, at : at + 256] = value[:count]
        sends[at // side][:, at % side : at % side + 256] = value[count:]


def added(keep, cores, cols):
    side = cores[0].shape[1]
    return keep[:, cols].astype(F32) + cores[cols.start // side][:, cols.start % side : cols.start % side + 256].astype(F32)


def fold_kernel(keep, *refs):
    *cores, out = refs
    for at in range(0, keep.shape[1], 256):
        cols = slice(at, at + 256)
        out[:, cols] = added(keep, cores, cols).astype(BF16)


def pieces_kernel(far, keep, *refs):
    *cores, first, second = refs
    half = first.shape[0]
    for at in range(0, keep.shape[1], 256):
        cols = slice(at, at + 256)
        total = (added(keep, cores, cols) + far[:, cols].astype(F32)).astype(BF16)
        first[:, cols] = total[:half]
        second[:, cols] = total[half:]


def gather_kernel(own, a0, a1, b0, b1, keep_ref, send_ref):
    expert, outer, inner, dp = seat()
    small = own.shape[0] // 2
    start = jnp.where((inner & 1) == 0, own[...].astype(F32), a0[...].astype(F32))
    for i, total in enumerate((start + a1[...].astype(F32), b0[...].astype(F32) + b1[...].astype(F32))):
        rows = slice(i * small, (i + 1) * small)
        keep_ref[rows, :] = total[:small]
        send_ref[rows, :] = total[small:].astype(BF16)


def tail_kernel(own, keep, core, gain, stream_ref, normed_ref):
    expert, outer, inner, dp = seat()
    small, half = own.shape[0], keep.shape[1]
    for i, at in enumerate((dp, 1 - dp)):
        rows = slice(i * small, (i + 1) * small)
        cols = aligned(at, half)
        mixture = keep[rows, :] + core[rows, :].astype(F32)
        stream_ref[:, cols] = (own[:, cols].astype(F32) + mixture).astype(BF16)
    normed_ref[...] = rms_scale(stream_ref[...].astype(F32), gain[...]).astype(BF16)


def body_paired(
    attn,
    resid,
    w_out,
    gain_post,
    route_ids,
    route_logits,
    live_count,
    w_gate_up,
    w_down,
    gain_final,
):
    rows_here = resid.shape[1]
    model_width = resid.shape[2]
    expert_count = lax.axis_size("expert")
    hidden = w_down.shape[1]
    half_width = w_down.shape[2]
    quarter = model_width // 4
    vmem, smem = whole_vmem(), whole_smem()

    def shape_of(*shape, dtype=BF16):
        return jax.ShapeDtypeStruct(shape, dtype)

    def call(kernel, name, mib, outs, *args, scratch=(), first=vmem):
        return pl.pallas_call(
            kernel,
            out_shape=outs,
            in_specs=[first] + [vmem] * (len(args) - 1),
            out_specs=tuple(vmem for _ in outs),
            scratch_shapes=list(scratch),
            compiler_params=kernel_params(mib),
            cost_estimate=small_cost(),
            name=name,
        )(*args)

    def swap_dp(x):
        return lax.ppermute(x, "dp", [(0, 1), (1, 0)])

    def shift_outer(x, s):
        return lax.ppermute(
            x, "expert", [(i, (i + 4 * s) % expert_count) for i in range(expert_count)]
        )

    def send_outer(x, i, cross):
        pairs = []
        for at in range(2 * expert_count):
            d, e = divmod(at, expert_count)
            step = 2 * (e % 2) + i
            if step or cross:
                pairs.append((at, (d ^ cross) * expert_count + (e + 4 * step) % expert_count))
        return lax.ppermute(x, ("dp", "expert"), pairs)

    def swap_inner(x, j):
        return lax.ppermute(x, "expert", [(i, i ^ j) for i in range(expert_count)])

    def swap_outer(x, s):
        return lax.ppermute(x, "expert", [(i, i ^ (4 * s)) for i in range(expert_count)])

    def after(x, *results):
        return lax.optimization_barrier((x, *results))[0]

    def weight_piece(first, size, depths):
        return pl.pallas_call(
            functools.partial(piece_kernel, (first, hidden + first)),
            out_shape=tuple(shape_of(depth, 2 * size) for depth in depths),
            in_specs=[pl.BlockSpec(memory_space=pl.ANY)],
            out_specs=tuple(vmem for _ in depths),
            scratch_shapes=[pltpu.SemaphoreType.DMA((2, len(depths)))],
            compiler_params=kernel_params(8),
            cost_estimate=small_cost(),
            name="weight_piece",
        )(w_gate_up[0])

    piece = shape_of(rows_here, quarter)
    r_own, r_1, r_23 = call(
        cut_kernel, "cut_resid", 4, (piece, piece, shape_of(2 * rows_here, quarter)), resid[0]
    )
    (share,) = call(
        share_kernel,
        "share",
        4,
        (shape_of(expert_count, quarter),),
        live_count,
        route_ids[0],
        route_logits[0],
        first=smem,
    )
    cut_width = hidden // 2
    early_piece = weight_piece(0, cut_width, (half_width,))[0]
    late_pieces = weight_piece(cut_width, cut_width, (half_width * 640 // 1024, half_width * 384 // 1024))
    gate_up_early = swap_dp(early_piece)
    a = [attn[0], swap_outer(attn[0], 1), swap_outer(attn[0], 2)]
    w_x = swap_inner(w_out, 2)
    r_2 = swap_outer(r_23, 2)
    a.append(swap_outer(after(a[2], a[1], r_2), 1))
    w_c = swap_inner(after(w_out, w_x, share, *late_pieces), 1)
    w_cx = swap_inner(w_x, 1)
    r_13 = swap_outer(jnp.concatenate([r_1, r_2[rows_here:]], axis=0), 1)

    product = shape_of(4 * rows_here, quarter)
    keep, send = call(
        proj_kernel,
        "projection",
        8,
        (product, product),
        *a[:3],
        after(a[3], r_13),
        w_out,
        w_c,
        w_x,
        w_cx,
        scratch=(
            pltpu.VMEM((8 * rows_here, attn.shape[2]), BF16),
            pltpu.VMEM((8 * rows_here, quarter), BF16),
        ),
    )
    arrived = swap_dp(send)
    gate_up_late = [swap_dp(after(piece, send)) for piece in late_pieces]
    (block,) = call(
        stream_kernel,
        "stream",
        4,
        (shape_of(4 * rows_here + expert_count, quarter),),
        after(keep, gate_up_early),
        arrived,
        r_own,
        r_13,
        r_2,
        share,
    )

    def norm(b0, b1, b2, b3):
        outs = (shape_of(4 * rows_here, model_width + 128), shape_of(rows_here, model_width))
        return call(norm_kernel, "norm", 8, outs, b0, b1, b2, b3, gain_post[None])

    blocks = [block] + [shift_outer(block, s) for s in (1, 2, 3)]
    group, stream_own = norm(*blocks)
    blocks_x = [swap_inner(b, 2) for b in blocks]
    group_x, unused = norm(*blocks_x)
    group_c = swap_inner(group, 1)
    group_cx = swap_inner(group_x, 1)

    row_total = 16 * rows_here
    half_rows = row_total // 2
    inner_first, part, other_rows, share_rows = call(
        first_gate_kernel,
        "first_gate_up",
        24,
        (
            shape_of(row_total, cut_width),
            shape_of(row_total, hidden, dtype=F32),
            shape_of(row_total, half_width),
            shape_of(row_total, 128, dtype=F32),
        ),
        group_x,
        group_cx,
        group,
        group_c,
        w_gate_up[0],
        gate_up_early,
        scratch=(pltpu.VMEM((row_total, half_width), BF16),),
    )
    inner_half = shape_of(half_rows, hidden)
    inner_far, inner_near = call(
        last_gate_kernel,
        "last_gate_up",
        16,
        (inner_half, inner_half),
        inner_first,
        part,
        other_rows,
        share_rows,
        *gate_up_late,
    )
    far_other = swap_dp(inner_far)
    near_other = swap_dp(inner_near)

    count = row_total // 4
    quarter_out = shape_of(count, half_width)

    def parts_of(many):
        return (shape_of(count, half_width // many),) * many

    scratch = (pltpu.VMEM((half_rows, hidden), BF16),)

    def down(rows, many):
        keep, *send = call(
            down_kernel, "down", 12, (quarter_out, *parts_of(many)), rows, w_down[0], scratch=scratch
        )
        return keep, send

    def swap_cores(halves):
        return [swap_inner(half, 1) for half in halves]

    def fold(keep, halves):
        return call(fold_kernel, "fold", 4, (quarter_out,), keep, *halves)[0]

    def pieces(far, keep, send):
        outs = (shape_of(2 * rows_here, half_width),) * 2
        return call(pieces_kernel, "pieces", 4, outs, far, keep, *swap_cores(send))

    outs = (quarter_out, *parts_of(2), *parts_of(2), quarter_out)
    keep_far, *send, keep_near = call(
        down_both_kernel, "down_both", 16, outs, inner_far, inner_near, w_down[0], scratch=scratch
    )
    far = swap_inner(fold(keep_far, swap_cores(send[:2])), 2)
    ready = far
    own, second = pieces(far, keep_near, send[2:])
    mine = [send_outer(own, 0, False), send_outer(second, 1, False)]

    keep_far, send = down(after(far_other, ready), 2)
    far = swap_inner(fold(keep_far, swap_cores(send)), 2)
    keep_near, send = down(near_other, 2)
    cut = pieces(far, after(keep_near, *mine), send)
    others = [send_outer(cut[i], i, True) for i in range(2)]

    sums = shape_of(2 * rows_here, half_width)
    keep, send = call(
        gather_kernel,
        "gather",
        4,
        (shape_of(2 * rows_here, half_width, dtype=F32), sums),
        own,
        *mine,
        *others,
    )
    out = shape_of(rows_here, model_width)
    stream_out, normed_out = call(
        tail_kernel, "closing", 8, (out, out), stream_own, keep, swap_inner(send, 1), gain_final[None]
    )
    return (stream_out[None], normed_out[None])


def solution(mesh):
    placed = (
        P("expert", None, "dp"),
        P("expert", "dp", None),
        P("dp", "expert"),
        P(),
        P("expert", "dp", None),
        P("expert", "dp", None),
        P("expert", "dp"),
        P("expert", "dp", None),
        P("expert", None, "dp"),
        P(),
    )
    paired = mesh.shape["dp"] == 2 and mesh.shape["expert"] == 16
    return jax.shard_map(
        body_paired if paired else body_general,
        mesh=mesh,
        in_specs=placed,
        out_specs=(P("expert", "dp", None), P("expert", "dp", None)),
        check_vma=False,
    )
```

```python
import functools
import math

import jax
import jax.numpy as jnp
from jax import lax
from jax.experimental import pallas as pl
from jax.experimental.pallas import tpu as pltpu
from jax.sharding import PartitionSpec as P


def rms_scale(values, gain):
    return values * lax.rsqrt(jnp.mean(values * values, axis=-1, keepdims=True) + 1e-06) * gain


def swiglu_rows(rows_in, gate_up, down, hidden_units):
    both = jnp.dot(rows_in, gate_up, preferred_element_type=jnp.float32)
    inner = (jax.nn.silu(both[:, :hidden_units]) * both[:, hidden_units:]).astype(jnp.bfloat16)
    return jnp.dot(inner, down, preferred_element_type=jnp.float32).astype(jnp.bfloat16)


def body_general(
    attn,
    resid,
    w_out,
    gain_post,
    route_ids,
    route_logits,
    live_count,
    w_gate_up,
    w_down,
    gain_final,
):
    rows_here = resid.shape[1]
    model_width = resid.shape[2]
    top_count = route_ids.shape[2]
    dp_count = lax.axis_size("dp")
    expert_count = lax.axis_size("expert")
    hidden_units = w_down.shape[1]
    capacity = dp_count * max(1, 2 * rows_here * top_count // (expert_count * dp_count))
    slot_count = expert_count * capacity
    flat_attn = attn[0]
    partial_out = jnp.dot(
        flat_attn,
        lax.all_gather(w_out, "expert", axis=1, tiled=True),
        preferred_element_type=jnp.float32,
    )
    projected = lax.psum_scatter(
        partial_out.astype(jnp.bfloat16), "dp", scatter_dimension=0, tiled=True
    ).astype(jnp.float32)
    stream_in = (resid[0].astype(jnp.float32) + projected).astype(jnp.bfloat16)
    stream_float = stream_in.astype(jnp.float32)
    normed_in = rms_scale(stream_float, gain_post).astype(jnp.bfloat16)
    probs = jax.nn.softmax(route_logits[0], axis=-1).astype(jnp.bfloat16)
    alive = jnp.arange(rows_here, dtype=jnp.int32) < live_count[0, 0]
    expert_of = route_ids[0].reshape(-1)
    route_alive = jnp.repeat(alive, top_count)
    onehot = (
        (expert_of[:, None] == jnp.arange(expert_count, dtype=jnp.int32)[None, :])
        & route_alive[:, None]
    ).astype(jnp.int32)
    earlier = jnp.sum((jnp.cumsum(onehot, axis=0) - onehot) * onehot, axis=1)
    target = expert_of * capacity + earlier
    match = (target[:, None] == jnp.arange(slot_count, dtype=jnp.int32)[None, :]) & route_alive[
        :, None
    ]
    placed = match.reshape(rows_here, top_count, slot_count)
    gather_matrix = jnp.any(placed, axis=1).astype(jnp.bfloat16)
    send_rows = lax.dot_general(
        gather_matrix, normed_in, (((0,), (0,)), ((), ())), preferred_element_type=jnp.float32
    ).astype(jnp.bfloat16)
    send_flags = jnp.sum(gather_matrix.astype(jnp.float32), axis=0).astype(jnp.bfloat16)
    combine_matrix = jnp.sum(
        jnp.where(placed, probs.astype(jnp.float32)[:, :, None], jnp.float32(0.0)), axis=1
    ).astype(jnp.bfloat16)
    arrived_rows, arrived_flags = (
        lax.all_to_all(
            send_rows.reshape(expert_count, capacity, model_width),
            "expert",
            split_axis=0,
            concat_axis=0,
            tiled=True,
        ),
        lax.all_to_all(
            send_flags.reshape(expert_count, capacity),
            "expert",
            split_axis=0,
            concat_axis=0,
            tiled=True,
        ),
    )
    arrived = arrived_rows.reshape(slot_count, model_width)
    flags = arrived_flags.reshape(slot_count)
    gate_up_full, down_full = (
        lax.all_gather(w_gate_up, "dp", axis=1, tiled=True),
        lax.all_gather(w_down, "dp", axis=2, tiled=True),
    )
    live_slot = (flags > 0.5).astype(jnp.int32)
    order = jnp.argsort(1 - live_slot, stable=True)
    live_total = jnp.sum(live_slot)
    packed = arrived[order]
    block_len = math.gcd(slot_count, 128)
    block_total = (live_total + block_len - 1) // block_len

    def run_block(index, outputs):
        begin = index * block_len
        rows_in = lax.dynamic_slice_in_dim(packed, begin, block_len, 0)
        block_out = swiglu_rows(rows_in, gate_up_full[0], down_full[0], hidden_units)
        return lax.dynamic_update_slice_in_dim(outputs, block_out, begin, 0)

    packed_out = lax.fori_loop(
        0, block_total, run_block, jnp.zeros((slot_count, model_width), jnp.bfloat16)
    )
    position = (
        jnp.zeros((slot_count,), jnp.int32).at[order].set(jnp.arange(slot_count, dtype=jnp.int32))
    )
    results = packed_out[position]
    returned = lax.all_to_all(
        results.reshape(expert_count, capacity, model_width),
        "expert",
        split_axis=0,
        concat_axis=0,
        tiled=True,
    )
    returned = returned.reshape(slot_count, model_width)
    mixture = jnp.dot(combine_matrix, returned, preferred_element_type=jnp.float32)
    stream_out = (stream_float + mixture).astype(jnp.bfloat16)
    normed_out = rms_scale(stream_out.astype(jnp.float32), gain_final).astype(jnp.bfloat16)
    return (stream_out[None], normed_out[None])


MIB = 1024 * 1024
BF16, F32 = jnp.bfloat16, jnp.float32


def whole_vmem():
    return pl.BlockSpec(memory_space=pltpu.VMEM)


def whole_smem():
    return pl.BlockSpec(memory_space=pltpu.SMEM)


def fixed(*shape):
    return pl.BlockSpec(shape, lambda i: (0,) * len(shape))


def dot(a, b):
    return jnp.dot(a, b, preferred_element_type=F32)


def small_cost():
    return pl.CostEstimate(flops=1, bytes_accessed=1, transcendentals=0)


def kernel_params(mib):
    return pltpu.CompilerParams(vmem_limit_bytes=mib * MIB)


def seat():
    expert = lax.axis_index("expert")
    return expert, lax.shift_right_logical(expert, 2), expert & 3, lax.axis_index("dp")


def aligned(index, step):
    return pl.ds(pl.multiple_of(index * step, step), step)


def cut_kernel(resid, r0, r1, r23):
    expert, outer, inner, dp = seat()
    rows, lanes = r0.shape
    r0[...] = resid[:, aligned(outer, lanes)]
    r1[...] = resid[:, aligned(outer ^ 1, lanes)]
    for i in range(2):
        r23[i * rows : (i + 1) * rows, :] = resid[:, aligned(outer ^ (2 + i), lanes)]


def share_kernel(live, ids, logits, share_ref):
    expert, outer, inner, dp = seat()
    rows, top = ids.shape
    experts, lanes = share_ref.shape
    value = logits[...]
    value = jnp.exp(value - jnp.max(value, axis=1, keepdims=True))
    probs = (value / jnp.sum(value, axis=1, keepdims=True)).astype(BF16).astype(F32)
    probs = jnp.where(lax.broadcasted_iota(jnp.int32, (rows, top), 0) < live[0, 0], probs, 0.0)
    names = lax.broadcasted_iota(jnp.int32, (rows, experts), 1)
    table = jnp.zeros((rows, experts), F32)
    for k in range(top):
        table = table + jnp.where(ids[:, k : k + 1] == names, probs[:, k : k + 1], 0.0)
    spots = lax.broadcasted_iota(jnp.int32, (rows, lanes), 1) - outer * rows
    spots = (spots == lax.broadcasted_iota(jnp.int32, (rows, lanes), 0)).astype(F32).astype(BF16)
    share_ref[...] = lax.dot_general(
        table.astype(BF16), spots, (((0,), (0,)), ((), ())), preferred_element_type=F32
    ).astype(BF16)


def proj_kernel(a0, a1, a2, a3, w0, w1, w2, w3, keep_ref, send_ref, rows, part):
    expert, outer, inner, dp = seat()
    full = a0.shape[0]
    half = full // 2
    block = w0.shape[1]
    for s, a in enumerate((a0, a1, a2, a3)):
        rows[aligned(outer ^ s, full), :] = a[...]
    for j, w in enumerate((w0, w1, w2, w3)):
        part[:, aligned(inner ^ j, block)] = dot(rows[...], w[...]).astype(BF16)
    for spot in range(4):
        keep_ref[spot * half : (spot + 1) * half, :] = part[aligned(2 * spot + dp, half), :]
        send_ref[spot * half : (spot + 1) * half, :] = part[aligned(2 * spot + 1 - dp, half), :]


def stream_kernel(keep, arrived, r0, r13, r2, share, block_ref):
    expert, outer, inner, dp = seat()
    count = keep.shape[0]
    small = r0.shape[0]
    for s, r in enumerate((r0[...], r13[0:small, :], r2[0:small, :], r13[small:, :])):
        rows = aligned(outer ^ s, small)
        product = keep[rows, :].astype(F32) + arrived[rows, :].astype(F32)
        block_ref[rows, :] = (r.astype(F32) + product).astype(BF16)
    block_ref[count:, :] = share[...]


def piece_kernel(starts, weights, *refs):
    *outs, semaphores = refs
    copies = []
    at = 0
    for k, out in enumerate(outs):
        depth, width = out.shape[0], out.shape[1] // 2
        for i in range(2):
            copies.append(
                pltpu.make_async_copy(
                    weights.at[pl.ds(at, depth), pl.ds(starts[i], width)],
                    out.at[:, pl.ds(i * width, width)],
                    semaphores.at[i, k],
                )
            )
        at += depth
    for copy in copies:
        copy.start()
    for copy in copies:
        copy.wait()


def swiglu(gate, up, share):
    return (gate / (1.0 + jnp.exp(-gate)) * up * share).astype(BF16)


def norm_kernel(b0, b1, b2, b3, gain, group_ref, own_ref):
    expert, outer, inner, dp = seat()
    count = group_ref.shape[0]
    width = b0.shape[1]
    experts = b0.shape[0] - count
    small = own_ref.shape[0]
    square = jnp.zeros((count, 1), F32)
    share = jnp.zeros((experts, count), F32)
    for s, b in enumerate((b0, b1, b2, b3)):
        value = b[0:count, :]
        group_ref[:, aligned((outer + 4 - s) & 3, width)] = value
        value = value.astype(F32)
        square = square + jnp.sum(value * value, axis=1, keepdims=True)
        share = share + b[count : count + experts, 0:count].astype(F32)
    own_ref[...] = group_ref[aligned(outer, small), 0 : 4 * width]
    scale = lax.rsqrt(square / (4 * width) + 1e-06)
    for s in range(4):
        cols = slice(s * width, (s + 1) * width)
        value = group_ref[:, cols].astype(F32)
        group_ref[:, cols] = (value * scale * gain[:, cols]).astype(BF16)
    lanes = (experts, 128)
    spread = lax.broadcasted_iota(jnp.int32, lanes, 0) == lax.broadcasted_iota(jnp.int32, lanes, 1)
    group_ref[:, 4 * width :] = lax.dot_general(
        share.astype(BF16),
        spread.astype(F32).astype(BF16),
        (((0,), (0,)), ((), ())),
        preferred_element_type=F32,
    ).astype(BF16)


def first_gate_kernel(
    group_x, group_cx, group, group_c, own, early, inner_ref, part_ref, other_ref, share_ref, mine_ref
):
    expert, outer, inner, dp = seat()
    count = group.shape[0]
    half = other_ref.shape[1]
    cut = inner_ref.shape[1]
    for j, g in enumerate((group_x, group_cx, group, group_c)):
        rows = slice(j * count, (j + 1) * count)
        mine_ref[rows, :] = g[:, aligned(dp, half)]
        other_ref[rows, :] = g[:, aligned(1 - dp, half)]
        share = g[:, 2 * half : 2 * half + 128].astype(F32)
        picked = lax.broadcasted_iota(jnp.int32, share.shape, 1) == expert
        share = jnp.sum(jnp.where(picked, share, 0.0), axis=1, keepdims=True)
        share_ref[rows, :] = jnp.broadcast_to(share, (count, 128))
    mine, other = mine_ref[...], other_ref[...]
    gate = dot(mine, own[:, 0:cut]) + dot(other, early[:, 0:cut])
    up = dot(mine, own[:, 2 * cut : 3 * cut]) + dot(other, early[:, cut : 2 * cut])
    inner_ref[...] = swiglu(gate, up, share_ref[:, 0:1])
    part_ref[:, 0:cut] = dot(mine, own[:, cut : 2 * cut])
    part_ref[:, cut : 2 * cut] = dot(mine, own[:, 3 * cut : 4 * cut])


def last_gate_kernel(first, part, other, share, *refs):
    *late, far_ref, near_ref = refs
    cut = first.shape[1]
    half = far_ref.shape[0]
    gate, up = part[:, 0:cut], part[:, cut : 2 * cut]
    at = 0
    for piece in late:
        rows = other[:, at : at + piece.shape[0]]
        gate = gate + dot(rows, piece[:, 0:cut])
        up = up + dot(rows, piece[:, cut : 2 * cut])
        at += piece.shape[0]
    value = swiglu(gate, up, share[:, 0:1])
    far_ref[:, 0:cut] = first[0:half, :]
    near_ref[:, 0:cut] = first[half:, :]
    far_ref[:, cut : 2 * cut] = value[:half]
    near_ref[:, cut : 2 * cut] = value[half:]


def down_both_kernel(far, near, wd, keep_far, *refs):
    *sends, keep_near, rows = refs
    half = len(sends) // 2
    down_kernel(far, wd, keep_far, *sends[:half], rows)
    down_kernel(near, wd, keep_near, *sends[half:], rows)


def down_kernel(block, wd, keep_ref, *refs):
    *sends, rows = refs
    expert, outer, inner, dp = seat()
    core = inner & 1
    count, side = sends[0].shape
    small = count // 4
    for i in range(2):
        for j in range(2):
            kept = aligned(4 * j + ((outer + 2 * core + i) & 3), small)
            sent = aligned(4 * (1 - j) + ((outer + 2 - 2 * core + i) & 3), small)
            at = (2 * i + j) * small
            rows[at : at + small, :] = block[kept, :]
            rows[count + at : count + at + small, :] = block[sent, :]
    for at in range(0, wd.shape[1], 256):
        value = dot(rows[...], wd[:, at : at + 256]).astype(BF16)
        keep_ref[:, at : at + 256] = value[:count]
        sends[at // side][:, at % side : at % side + 256] = value[count:]


def added(keep, cores, cols):
    side = cores[0].shape[1]
    return keep[:, cols].astype(F32) + cores[cols.start // side][:, cols.start % side : cols.start % side + 256].astype(F32)


def fold_kernel(keep, *refs):
    *cores, out = refs
    for at in range(0, keep.shape[1], 256):
        cols = slice(at, at + 256)
        out[:, cols] = added(keep, cores, cols).astype(BF16)


def pieces_kernel(far, keep, *refs):
    *cores, first, second = refs
    half = first.shape[0]
    for at in range(0, keep.shape[1], 256):
        cols = slice(at, at + 256)
        total = (added(keep, cores, cols) + far[:, cols].astype(F32)).astype(BF16)
        first[:, cols] = total[:half]
        second[:, cols] = total[half:]


def gather_kernel(own, a0, a1, b0, b1, keep_ref, send_ref):
    expert, outer, inner, dp = seat()
    small = own.shape[0] // 2
    start = jnp.where((inner & 1) == 0, own[...].astype(F32), a0[...].astype(F32))
    for i, total in enumerate((start + a1[...].astype(F32), b0[...].astype(F32) + b1[...].astype(F32))):
        rows = slice(i * small, (i + 1) * small)
        keep_ref[rows, :] = total[:small]
        send_ref[rows, :] = total[small:].astype(BF16)


def tail_kernel(own, keep, core, gain, stream_ref, normed_ref):
    expert, outer, inner, dp = seat()
    small, half = own.shape[0], keep.shape[1]
    for i, at in enumerate((dp, 1 - dp)):
        rows = slice(i * small, (i + 1) * small)
        cols = aligned(at, half)
        mixture = keep[rows, :] + core[rows, :].astype(F32)
        stream_ref[:, cols] = (own[:, cols].astype(F32) + mixture).astype(BF16)
    normed_ref[...] = rms_scale(stream_ref[...].astype(F32), gain[...]).astype(BF16)


def body_paired(
    attn,
    resid,
    w_out,
    gain_post,
    route_ids,
    route_logits,
    live_count,
    w_gate_up,
    w_down,
    gain_final,
):
    rows_here = resid.shape[1]
    model_width = resid.shape[2]
    expert_count = lax.axis_size("expert")
    hidden = w_down.shape[1]
    half_width = w_down.shape[2]
    quarter = model_width // 4
    vmem, smem = whole_vmem(), whole_smem()

    def shape_of(*shape, dtype=BF16):
        return jax.ShapeDtypeStruct(shape, dtype)

    def call(kernel, name, mib, outs, *args, scratch=(), first=vmem):
        return pl.pallas_call(
            kernel,
            out_shape=outs,
            in_specs=[first] + [vmem] * (len(args) - 1),
            out_specs=tuple(vmem for _ in outs),
            scratch_shapes=list(scratch),
            compiler_params=kernel_params(mib),
            cost_estimate=small_cost(),
            name=name,
        )(*args)

    def swap_dp(x):
        return lax.ppermute(x, "dp", [(0, 1), (1, 0)])

    def shift_outer(x, s):
        return lax.ppermute(
            x, "expert", [(i, (i + 4 * s) % expert_count) for i in range(expert_count)]
        )

    def send_outer(x, i, cross):
        pairs = []
        for at in range(2 * expert_count):
            d, e = divmod(at, expert_count)
            step = 2 * (e % 2) + i
            if step or cross:
                pairs.append((at, (d ^ cross) * expert_count + (e + 4 * step) % expert_count))
        return lax.ppermute(x, ("dp", "expert"), pairs)

    def swap_inner(x, j):
        return lax.ppermute(x, "expert", [(i, i ^ j) for i in range(expert_count)])

    def swap_outer(x, s):
        return lax.ppermute(x, "expert", [(i, i ^ (4 * s)) for i in range(expert_count)])

    def after(x, *results):
        return lax.optimization_barrier((x, *results))[0]

    def weight_piece(first, size, depths):
        return pl.pallas_call(
            functools.partial(piece_kernel, (first, hidden + first)),
            out_shape=tuple(shape_of(depth, 2 * size) for depth in depths),
            in_specs=[pl.BlockSpec(memory_space=pl.ANY)],
            out_specs=tuple(vmem for _ in depths),
            scratch_shapes=[pltpu.SemaphoreType.DMA((2, len(depths)))],
            compiler_params=kernel_params(8),
            cost_estimate=small_cost(),
            name="weight_piece",
        )(w_gate_up[0])

    piece = shape_of(rows_here, quarter)
    r_own, r_1, r_23 = call(
        cut_kernel, "cut_resid", 4, (piece, piece, shape_of(2 * rows_here, quarter)), resid[0]
    )
    (share,) = call(
        share_kernel,
        "share",
        4,
        (shape_of(expert_count, quarter),),
        live_count,
        route_ids[0],
        route_logits[0],
        first=smem,
    )
    cut_width = hidden // 2
    early_piece = weight_piece(0, cut_width, (half_width,))[0]
    late_pieces = weight_piece(cut_width, cut_width, (half_width * 640 // 1024, half_width * 384 // 1024))
    gate_up_early = swap_dp(early_piece)
    a = [attn[0], swap_outer(attn[0], 1), swap_outer(attn[0], 2)]
    w_x = swap_inner(w_out, 2)
    r_2 = swap_outer(r_23, 2)
    a.append(swap_outer(after(a[2], a[1], r_2), 1))
    w_c = swap_inner(after(w_out, w_x, share, *late_pieces), 1)
    w_cx = swap_inner(w_x, 1)
    r_13 = swap_outer(jnp.concatenate([r_1, r_2[rows_here:]], axis=0), 1)

    product = shape_of(4 * rows_here, quarter)
    keep, send = call(
        proj_kernel,
        "projection",
        8,
        (product, product),
        *a[:3],
        after(a[3], r_13),
        w_out,
        w_c,
        w_x,
        w_cx,
        scratch=(
            pltpu.VMEM((8 * rows_here, attn.shape[2]), BF16),
            pltpu.VMEM((8 * rows_here, quarter), BF16),
        ),
    )
    arrived = swap_dp(send)
    gate_up_late = [swap_dp(after(piece, send)) for piece in late_pieces]
    (block,) = call(
        stream_kernel,
        "stream",
        4,
        (shape_of(4 * rows_here + expert_count, quarter),),
        after(keep, gate_up_early),
        arrived,
        r_own,
        r_13,
        r_2,
        share,
    )

    def norm(b0, b1, b2, b3):
        outs = (shape_of(4 * rows_here, model_width + 128), shape_of(rows_here, model_width))
        return call(norm_kernel, "norm", 8, outs, b0, b1, b2, b3, gain_post[None])

    blocks = [block] + [shift_outer(block, s) for s in (1, 2, 3)]
    group, stream_own = norm(*blocks)
    blocks_x = [swap_inner(b, 2) for b in blocks]
    group_x, unused = norm(*blocks_x)
    group_c = swap_inner(group, 1)
    group_cx = swap_inner(group_x, 1)

    row_total = 16 * rows_here
    half_rows = row_total // 2
    inner_first, part, other_rows, share_rows = call(
        first_gate_kernel,
        "first_gate_up",
        24,
        (
            shape_of(row_total, cut_width),
            shape_of(row_total, hidden, dtype=F32),
            shape_of(row_total, half_width),
            shape_of(row_total, 128, dtype=F32),
        ),
        group_x,
        group_cx,
        group,
        group_c,
        w_gate_up[0],
        gate_up_early,
        scratch=(pltpu.VMEM((row_total, half_width), BF16),),
    )
    inner_half = shape_of(half_rows, hidden)
    inner_far, inner_near = call(
        last_gate_kernel,
        "last_gate_up",
        16,
        (inner_half, inner_half),
        inner_first,
        part,
        other_rows,
        share_rows,
        *gate_up_late,
    )
    far_other = swap_dp(inner_far)
    near_other = swap_dp(inner_near)

    count = row_total // 4
    quarter_out = shape_of(count, half_width)

    def parts_of(many):
        return (shape_of(count, half_width // many),) * many

    scratch = (pltpu.VMEM((half_rows, hidden), BF16),)

    def down(rows, many):
        keep, *send = call(
            down_kernel, "down", 12, (quarter_out, *parts_of(many)), rows, w_down[0], scratch=scratch
        )
        return keep, send

    def swap_cores(halves):
        return [swap_inner(half, 1) for half in halves]

    def fold(keep, halves):
        return call(fold_kernel, "fold", 4, (quarter_out,), keep, *halves)[0]

    def pieces(far, keep, send):
        outs = (shape_of(2 * rows_here, half_width),) * 2
        return call(pieces_kernel, "pieces", 4, outs, far, keep, *swap_cores(send))

    outs = (quarter_out, *parts_of(2), *parts_of(2), quarter_out)
    keep_far, *send, keep_near = call(
        down_both_kernel, "down_both", 16, outs, inner_far, inner_near, w_down[0], scratch=scratch
    )
    far = swap_inner(fold(keep_far, swap_cores(send[:2])), 2)
    first_far = far
    own, second = pieces(far, keep_near, send[2:])
    mine = [send_outer(own, 0, False), send_outer(second, 1, False)]

    keep_far, send = down(far_other, 2)
    far = swap_inner(fold(after(keep_far, own), swap_cores(send)), 2)
    keep_near, send = down(near_other, 2)
    cut = pieces(far, after(keep_near, *mine), send)
    others = [send_outer(cut[i], i, True) for i in range(2)]

    sums = shape_of(2 * rows_here, half_width)
    keep, send = call(
        gather_kernel,
        "gather",
        4,
        (shape_of(2 * rows_here, half_width, dtype=F32), sums),
        own,
        *mine,
        *others,
    )
    out = shape_of(rows_here, model_width)
    stream_out, normed_out = call(
        tail_kernel, "closing", 8, (out, out), stream_own, keep, swap_inner(send, 1), gain_final[None]
    )
    return (stream_out[None], normed_out[None])


def solution(mesh):
    placed = (
        P("expert", None, "dp"),
        P("expert", "dp", None),
        P("dp", "expert"),
        P(),
        P("expert", "dp", None),
        P("expert", "dp", None),
        P("expert", "dp"),
        P("expert", "dp", None),
        P("expert", None, "dp"),
        P(),
    )
    paired = mesh.shape["dp"] == 2 and mesh.shape["expert"] == 16
    return jax.shard_map(
        body_paired if paired else body_general,
        mesh=mesh,
        in_specs=placed,
        out_specs=(P("expert", "dp", None), P("expert", "dp", None)),
        check_vma=False,
    )
```

```python
import functools
import math

import jax
import jax.numpy as jnp
from jax import lax
from jax.experimental import pallas as pl
from jax.experimental.pallas import tpu as pltpu
from jax.sharding import PartitionSpec as P


def rms_scale(values, gain):
    return values * lax.rsqrt(jnp.mean(values * values, axis=-1, keepdims=True) + 1e-06) * gain


def swiglu_rows(rows_in, gate_up, down, hidden_units):
    both = jnp.dot(rows_in, gate_up, preferred_element_type=jnp.float32)
    inner = (jax.nn.silu(both[:, :hidden_units]) * both[:, hidden_units:]).astype(jnp.bfloat16)
    return jnp.dot(inner, down, preferred_element_type=jnp.float32).astype(jnp.bfloat16)


def body_general(
    attn,
    resid,
    w_out,
    gain_post,
    route_ids,
    route_logits,
    live_count,
    w_gate_up,
    w_down,
    gain_final,
):
    rows_here = resid.shape[1]
    model_width = resid.shape[2]
    top_count = route_ids.shape[2]
    dp_count = lax.axis_size("dp")
    expert_count = lax.axis_size("expert")
    hidden_units = w_down.shape[1]
    capacity = dp_count * max(1, 2 * rows_here * top_count // (expert_count * dp_count))
    slot_count = expert_count * capacity
    flat_attn = attn[0]
    partial_out = jnp.dot(
        flat_attn,
        lax.all_gather(w_out, "expert", axis=1, tiled=True),
        preferred_element_type=jnp.float32,
    )
    projected = lax.psum_scatter(
        partial_out.astype(jnp.bfloat16), "dp", scatter_dimension=0, tiled=True
    ).astype(jnp.float32)
    stream_in = (resid[0].astype(jnp.float32) + projected).astype(jnp.bfloat16)
    stream_float = stream_in.astype(jnp.float32)
    normed_in = rms_scale(stream_float, gain_post).astype(jnp.bfloat16)
    probs = jax.nn.softmax(route_logits[0], axis=-1).astype(jnp.bfloat16)
    alive = jnp.arange(rows_here, dtype=jnp.int32) < live_count[0, 0]
    expert_of = route_ids[0].reshape(-1)
    route_alive = jnp.repeat(alive, top_count)
    onehot = (
        (expert_of[:, None] == jnp.arange(expert_count, dtype=jnp.int32)[None, :])
        & route_alive[:, None]
    ).astype(jnp.int32)
    earlier = jnp.sum((jnp.cumsum(onehot, axis=0) - onehot) * onehot, axis=1)
    target = expert_of * capacity + earlier
    match = (target[:, None] == jnp.arange(slot_count, dtype=jnp.int32)[None, :]) & route_alive[
        :, None
    ]
    placed = match.reshape(rows_here, top_count, slot_count)
    gather_matrix = jnp.any(placed, axis=1).astype(jnp.bfloat16)
    send_rows = lax.dot_general(
        gather_matrix, normed_in, (((0,), (0,)), ((), ())), preferred_element_type=jnp.float32
    ).astype(jnp.bfloat16)
    send_flags = jnp.sum(gather_matrix.astype(jnp.float32), axis=0).astype(jnp.bfloat16)
    combine_matrix = jnp.sum(
        jnp.where(placed, probs.astype(jnp.float32)[:, :, None], jnp.float32(0.0)), axis=1
    ).astype(jnp.bfloat16)
    arrived_rows, arrived_flags = (
        lax.all_to_all(
            send_rows.reshape(expert_count, capacity, model_width),
            "expert",
            split_axis=0,
            concat_axis=0,
            tiled=True,
        ),
        lax.all_to_all(
            send_flags.reshape(expert_count, capacity),
            "expert",
            split_axis=0,
            concat_axis=0,
            tiled=True,
        ),
    )
    arrived = arrived_rows.reshape(slot_count, model_width)
    flags = arrived_flags.reshape(slot_count)
    gate_up_full, down_full = (
        lax.all_gather(w_gate_up, "dp", axis=1, tiled=True),
        lax.all_gather(w_down, "dp", axis=2, tiled=True),
    )
    live_slot = (flags > 0.5).astype(jnp.int32)
    order = jnp.argsort(1 - live_slot, stable=True)
    live_total = jnp.sum(live_slot)
    packed = arrived[order]
    block_len = math.gcd(slot_count, 128)
    block_total = (live_total + block_len - 1) // block_len

    def run_block(index, outputs):
        begin = index * block_len
        rows_in = lax.dynamic_slice_in_dim(packed, begin, block_len, 0)
        block_out = swiglu_rows(rows_in, gate_up_full[0], down_full[0], hidden_units)
        return lax.dynamic_update_slice_in_dim(outputs, block_out, begin, 0)

    packed_out = lax.fori_loop(
        0, block_total, run_block, jnp.zeros((slot_count, model_width), jnp.bfloat16)
    )
    position = (
        jnp.zeros((slot_count,), jnp.int32).at[order].set(jnp.arange(slot_count, dtype=jnp.int32))
    )
    results = packed_out[position]
    returned = lax.all_to_all(
        results.reshape(expert_count, capacity, model_width),
        "expert",
        split_axis=0,
        concat_axis=0,
        tiled=True,
    )
    returned = returned.reshape(slot_count, model_width)
    mixture = jnp.dot(combine_matrix, returned, preferred_element_type=jnp.float32)
    stream_out = (stream_float + mixture).astype(jnp.bfloat16)
    normed_out = rms_scale(stream_out.astype(jnp.float32), gain_final).astype(jnp.bfloat16)
    return (stream_out[None], normed_out[None])


MIB = 1024 * 1024
BF16, F32 = jnp.bfloat16, jnp.float32


def whole_vmem():
    return pl.BlockSpec(memory_space=pltpu.VMEM)


def whole_smem():
    return pl.BlockSpec(memory_space=pltpu.SMEM)


def fixed(*shape):
    return pl.BlockSpec(shape, lambda i: (0,) * len(shape))


def dot(a, b):
    return jnp.dot(a, b, preferred_element_type=F32)


def small_cost():
    return pl.CostEstimate(flops=1, bytes_accessed=1, transcendentals=0)


def kernel_params(mib):
    return pltpu.CompilerParams(vmem_limit_bytes=mib * MIB)


def seat():
    expert = lax.axis_index("expert")
    return expert, lax.shift_right_logical(expert, 2), expert & 3, lax.axis_index("dp")


def aligned(index, step):
    return pl.ds(pl.multiple_of(index * step, step), step)


def cut_kernel(resid, r0, r1, r23):
    expert, outer, inner, dp = seat()
    rows, lanes = r0.shape
    r0[...] = resid[:, aligned(outer, lanes)]
    r1[...] = resid[:, aligned(outer ^ 1, lanes)]
    for i in range(2):
        r23[i * rows : (i + 1) * rows, :] = resid[:, aligned(outer ^ (2 + i), lanes)]


def share_kernel(live, ids, logits, share_ref):
    expert, outer, inner, dp = seat()
    rows, top = ids.shape
    experts, lanes = share_ref.shape
    value = logits[...]
    value = jnp.exp(value - jnp.max(value, axis=1, keepdims=True))
    probs = (value / jnp.sum(value, axis=1, keepdims=True)).astype(BF16).astype(F32)
    probs = jnp.where(lax.broadcasted_iota(jnp.int32, (rows, top), 0) < live[0, 0], probs, 0.0)
    names = lax.broadcasted_iota(jnp.int32, (rows, experts), 1)
    table = jnp.zeros((rows, experts), F32)
    for k in range(top):
        table = table + jnp.where(ids[:, k : k + 1] == names, probs[:, k : k + 1], 0.0)
    spots = lax.broadcasted_iota(jnp.int32, (rows, lanes), 1) - outer * rows
    spots = (spots == lax.broadcasted_iota(jnp.int32, (rows, lanes), 0)).astype(F32).astype(BF16)
    share_ref[...] = lax.dot_general(
        table.astype(BF16), spots, (((0,), (0,)), ((), ())), preferred_element_type=F32
    ).astype(BF16)


def proj_kernel(a0, a1, a2, a3, w0, w1, w2, w3, keep_ref, send_ref, rows, part):
    expert, outer, inner, dp = seat()
    full = a0.shape[0]
    half = full // 2
    block = w0.shape[1]
    for s, a in enumerate((a0, a1, a2, a3)):
        rows[aligned(outer ^ s, full), :] = a[...]
    for j, w in enumerate((w0, w1, w2, w3)):
        part[:, aligned(inner ^ j, block)] = dot(rows[...], w[...]).astype(BF16)
    for spot in range(4):
        keep_ref[spot * half : (spot + 1) * half, :] = part[aligned(2 * spot + dp, half), :]
        send_ref[spot * half : (spot + 1) * half, :] = part[aligned(2 * spot + 1 - dp, half), :]


def stream_kernel(keep, arrived, r0, r13, r2, share, block_ref):
    expert, outer, inner, dp = seat()
    count = keep.shape[0]
    small = r0.shape[0]
    for s, r in enumerate((r0[...], r13[0:small, :], r2[0:small, :], r13[small:, :])):
        rows = aligned(outer ^ s, small)
        product = keep[rows, :].astype(F32) + arrived[rows, :].astype(F32)
        block_ref[rows, :] = (r.astype(F32) + product).astype(BF16)
    block_ref[count:, :] = share[...]


def piece_kernel(starts, weights, *refs):
    *outs, semaphores = refs
    copies = []
    at = 0
    for k, out in enumerate(outs):
        depth, width = out.shape[0], out.shape[1] // 2
        for i in range(2):
            copies.append(
                pltpu.make_async_copy(
                    weights.at[pl.ds(at, depth), pl.ds(starts[i], width)],
                    out.at[:, pl.ds(i * width, width)],
                    semaphores.at[i, k],
                )
            )
        at += depth
    for copy in copies:
        copy.start()
    for copy in copies:
        copy.wait()


def swiglu(gate, up, share):
    return (gate / (1.0 + jnp.exp(-gate)) * up * share).astype(BF16)


def norm_kernel(b0, b1, b2, b3, gain, group_ref, own_ref):
    expert, outer, inner, dp = seat()
    count = group_ref.shape[0]
    width = b0.shape[1]
    experts = b0.shape[0] - count
    small = own_ref.shape[0]
    square = jnp.zeros((count, 1), F32)
    share = jnp.zeros((experts, count), F32)
    for s, b in enumerate((b0, b1, b2, b3)):
        value = b[0:count, :]
        group_ref[:, aligned((outer + 4 - s) & 3, width)] = value
        value = value.astype(F32)
        square = square + jnp.sum(value * value, axis=1, keepdims=True)
        share = share + b[count : count + experts, 0:count].astype(F32)
    own_ref[...] = group_ref[aligned(outer, small), 0 : 4 * width]
    scale = lax.rsqrt(square / (4 * width) + 1e-06)
    for s in range(4):
        cols = slice(s * width, (s + 1) * width)
        value = group_ref[:, cols].astype(F32)
        group_ref[:, cols] = (value * scale * gain[:, cols]).astype(BF16)
    lanes = (experts, 128)
    spread = lax.broadcasted_iota(jnp.int32, lanes, 0) == lax.broadcasted_iota(jnp.int32, lanes, 1)
    group_ref[:, 4 * width :] = lax.dot_general(
        share.astype(BF16),
        spread.astype(F32).astype(BF16),
        (((0,), (0,)), ((), ())),
        preferred_element_type=F32,
    ).astype(BF16)


def first_gate_kernel(
    group_x, group_cx, group, group_c, own, early,
    first_ref, second_ref, part_ref, other_ref, share_ref, mine_ref,
):
    expert, outer, inner, dp = seat()
    count = group.shape[0]
    half = other_ref.shape[1]
    cut = first_ref.shape[1]
    for j, g in enumerate((group_x, group_cx, group, group_c)):
        rows = slice(j * count, (j + 1) * count)
        mine_ref[rows, :] = g[:, aligned(dp, half)]
        other_ref[rows, :] = g[:, aligned(1 - dp, half)]
        share = g[:, 2 * half : 2 * half + 128].astype(F32)
        picked = lax.broadcasted_iota(jnp.int32, share.shape, 1) == expert
        share = jnp.sum(jnp.where(picked, share, 0.0), axis=1, keepdims=True)
        share_ref[rows, :] = jnp.broadcast_to(share, (count, 128))
    mine, other = mine_ref[...], other_ref[...]
    gate = dot(mine, own[:, 0:cut]) + dot(other, early[:, 0:cut])
    up = dot(mine, own[:, 2 * cut : 3 * cut]) + dot(other, early[:, cut : 2 * cut])
    inner = swiglu(gate, up, share_ref[:, 0:1])
    first_ref[...] = inner[: 3 * count]
    second_ref[...] = inner[3 * count :]
    part_ref[:, 0:cut] = dot(mine, own[:, cut : 2 * cut])
    part_ref[:, cut : 2 * cut] = dot(mine, own[:, 3 * cut : 4 * cut])


def last_gate_kernel(second, part, other, share, *refs):
    *late, far_ref, rest_ref = refs
    count, cut = second.shape
    gate, up = part[:, 0:cut], part[:, cut : 2 * cut]
    at = 0
    for piece in late:
        rows = other[:, at : at + piece.shape[0]]
        gate = gate + dot(rows, piece[:, 0:cut])
        up = up + dot(rows, piece[:, cut : 2 * cut])
        at += piece.shape[0]
    value = swiglu(gate, up, share[:, 0:1])
    far_ref[...] = value[: 2 * count]
    rest_ref[0:count, :] = second[...]
    rest_ref[count:, :] = value[2 * count :]


def down_rows(pieces, wd, keep_ref, sends, rows):
    expert, outer, inner, dp = seat()
    core = inner & 1
    count, side = sends[0].shape
    small = count // 4
    for h, places in enumerate(pieces):
        cut = places[0][0].shape[1]
        cols = slice(h * cut, (h + 1) * cut)
        for i in range(2):
            for j in range(2):
                ref, start = places[j]
                kept = aligned(start // small + ((outer + 2 * core + i) & 3), small)
                at = (2 * i + j) * small
                rows[at : at + small, cols] = ref[kept, :]
                ref, start = places[1 - j]
                sent = aligned(start // small + ((outer + 2 - 2 * core + i) & 3), small)
                rows[count + at : count + at + small, cols] = ref[sent, :]
    for at in range(0, wd.shape[1], 256):
        value = dot(rows[...], wd[:, at : at + 256]).astype(BF16)
        keep_ref[:, at : at + 256] = value[:count]
        sends[at // side][:, at % side : at % side + 256] = value[count:]


def far_places(first, far):
    count = far.shape[0] // 2
    return ((first, 0), (first, count)), ((far, 0), (far, count))


def near_places(first, rest):
    count = rest.shape[0] // 3
    return ((first, 2 * count), (rest, 0)), ((rest, count), (rest, 2 * count))


def down_both_kernel(first, far, rest, wd, keep_far, *refs):
    *sends, keep_near, rows = refs
    half = len(sends) // 2
    down_rows(far_places(first, far), wd, keep_far, sends[:half], rows)
    down_rows(near_places(first, rest), wd, keep_near, sends[half:], rows)


def down_far_kernel(first, far, wd, keep_ref, *refs):
    *sends, rows = refs
    down_rows(far_places(first, far), wd, keep_ref, sends, rows)


def down_near_kernel(first, rest, wd, keep_ref, *refs):
    *sends, rows = refs
    down_rows(near_places(first, rest), wd, keep_ref, sends, rows)


def added(keep, cores, cols):
    side = cores[0].shape[1]
    return keep[:, cols].astype(F32) + cores[cols.start // side][:, cols.start % side : cols.start % side + 256].astype(F32)


def fold_kernel(keep, *refs):
    *cores, out = refs
    for at in range(0, keep.shape[1], 256):
        cols = slice(at, at + 256)
        out[:, cols] = added(keep, cores, cols).astype(BF16)


def pieces_kernel(far, keep, *refs):
    *cores, first, second = refs
    half = first.shape[0]
    for at in range(0, keep.shape[1], 256):
        cols = slice(at, at + 256)
        total = (added(keep, cores, cols) + far[:, cols].astype(F32)).astype(BF16)
        first[:, cols] = total[:half]
        second[:, cols] = total[half:]


def gather_kernel(own, a0, a1, b0, b1, keep_ref, send_ref):
    expert, outer, inner, dp = seat()
    small = own.shape[0] // 2
    start = jnp.where((inner & 1) == 0, own[...].astype(F32), a0[...].astype(F32))
    for i, total in enumerate((start + a1[...].astype(F32), b0[...].astype(F32) + b1[...].astype(F32))):
        rows = slice(i * small, (i + 1) * small)
        keep_ref[rows, :] = total[:small]
        send_ref[rows, :] = total[small:].astype(BF16)


def tail_kernel(own, keep, core, gain, stream_ref, normed_ref):
    expert, outer, inner, dp = seat()
    small, half = own.shape[0], keep.shape[1]
    for i, at in enumerate((dp, 1 - dp)):
        rows = slice(i * small, (i + 1) * small)
        cols = aligned(at, half)
        mixture = keep[rows, :] + core[rows, :].astype(F32)
        stream_ref[:, cols] = (own[:, cols].astype(F32) + mixture).astype(BF16)
    normed_ref[...] = rms_scale(stream_ref[...].astype(F32), gain[...]).astype(BF16)


def body_paired(
    attn,
    resid,
    w_out,
    gain_post,
    route_ids,
    route_logits,
    live_count,
    w_gate_up,
    w_down,
    gain_final,
):
    rows_here = resid.shape[1]
    model_width = resid.shape[2]
    expert_count = lax.axis_size("expert")
    hidden = w_down.shape[1]
    half_width = w_down.shape[2]
    quarter = model_width // 4
    vmem, smem = whole_vmem(), whole_smem()

    def shape_of(*shape, dtype=BF16):
        return jax.ShapeDtypeStruct(shape, dtype)

    def call(kernel, name, mib, outs, *args, scratch=(), first=vmem):
        return pl.pallas_call(
            kernel,
            out_shape=outs,
            in_specs=[first] + [vmem] * (len(args) - 1),
            out_specs=tuple(vmem for _ in outs),
            scratch_shapes=list(scratch),
            compiler_params=kernel_params(mib),
            cost_estimate=small_cost(),
            name=name,
        )(*args)

    def swap_dp(x):
        return lax.ppermute(x, "dp", [(0, 1), (1, 0)])

    def shift_outer(x, s):
        return lax.ppermute(
            x, "expert", [(i, (i + 4 * s) % expert_count) for i in range(expert_count)]
        )

    def send_outer(x, i, cross):
        pairs = []
        for at in range(2 * expert_count):
            d, e = divmod(at, expert_count)
            step = 2 * (e % 2) + i
            if step or cross:
                pairs.append((at, (d ^ cross) * expert_count + (e + 4 * step) % expert_count))
        return lax.ppermute(x, ("dp", "expert"), pairs)

    def swap_inner(x, j):
        return lax.ppermute(x, "expert", [(i, i ^ j) for i in range(expert_count)])

    def swap_outer(x, s):
        return lax.ppermute(x, "expert", [(i, i ^ (4 * s)) for i in range(expert_count)])

    def after(x, *results):
        return lax.optimization_barrier((x, *results))[0]

    def weight_piece(first, size, depths):
        return pl.pallas_call(
            functools.partial(piece_kernel, (first, hidden + first)),
            out_shape=tuple(shape_of(depth, 2 * size) for depth in depths),
            in_specs=[pl.BlockSpec(memory_space=pl.ANY)],
            out_specs=tuple(vmem for _ in depths),
            scratch_shapes=[pltpu.SemaphoreType.DMA((2, len(depths)))],
            compiler_params=kernel_params(8),
            cost_estimate=small_cost(),
            name="weight_piece",
        )(w_gate_up[0])

    piece = shape_of(rows_here, quarter)
    r_own, r_1, r_23 = call(
        cut_kernel, "cut_resid", 4, (piece, piece, shape_of(2 * rows_here, quarter)), resid[0]
    )
    (share,) = call(
        share_kernel,
        "share",
        4,
        (shape_of(expert_count, quarter),),
        live_count,
        route_ids[0],
        route_logits[0],
        first=smem,
    )
    cut_width = hidden // 2
    early_piece = weight_piece(0, cut_width, (half_width,))[0]
    late_pieces = weight_piece(cut_width, cut_width, (half_width * 640 // 1024, half_width * 384 // 1024))
    gate_up_early = swap_dp(early_piece)
    a = [attn[0], swap_outer(attn[0], 1), swap_outer(attn[0], 2)]
    w_x = swap_inner(w_out, 2)
    r_2 = swap_outer(r_23, 2)
    a.append(swap_outer(after(a[2], a[1], r_2), 1))
    w_c = swap_inner(after(w_out, w_x, share, *late_pieces), 1)
    w_cx = swap_inner(w_x, 1)
    r_13 = swap_outer(jnp.concatenate([r_1, r_2[rows_here:]], axis=0), 1)

    product = shape_of(4 * rows_here, quarter)
    keep, send = call(
        proj_kernel,
        "projection",
        8,
        (product, product),
        *a[:3],
        after(a[3], r_13),
        w_out,
        w_c,
        w_x,
        w_cx,
        scratch=(
            pltpu.VMEM((8 * rows_here, attn.shape[2]), BF16),
            pltpu.VMEM((8 * rows_here, quarter), BF16),
        ),
    )
    arrived = swap_dp(send)
    gate_up_late = [swap_dp(after(piece, send)) for piece in late_pieces]
    (block,) = call(
        stream_kernel,
        "stream",
        4,
        (shape_of(4 * rows_here + expert_count, quarter),),
        after(keep, gate_up_early),
        arrived,
        r_own,
        r_13,
        r_2,
        share,
    )

    def norm(b0, b1, b2, b3):
        outs = (shape_of(4 * rows_here, model_width + 128), shape_of(rows_here, model_width))
        return call(norm_kernel, "norm", 8, outs, b0, b1, b2, b3, gain_post[None])

    blocks = [block] + [shift_outer(block, s) for s in (1, 2, 3)]
    group, stream_own = norm(*blocks)
    blocks_x = [swap_inner(b, 2) for b in blocks]
    group_x, unused = norm(*blocks_x)
    group_c = swap_inner(group, 1)
    group_cx = swap_inner(group_x, 1)

    row_total = 16 * rows_here
    half_rows = row_total // 2
    inner_first, inner_second, part, other_rows, share_rows = call(
        first_gate_kernel,
        "first_gate_up",
        24,
        (
            shape_of(row_total * 3 // 4, cut_width),
            shape_of(row_total // 4, cut_width),
            shape_of(row_total, hidden, dtype=F32),
            shape_of(row_total, half_width),
            shape_of(row_total, 128, dtype=F32),
        ),
        group_x,
        group_cx,
        group,
        group_c,
        w_gate_up[0],
        gate_up_early,
        scratch=(pltpu.VMEM((row_total, half_width), BF16),),
    )
    inner_far, inner_rest = call(
        last_gate_kernel,
        "last_gate_up",
        16,
        (shape_of(half_rows, cut_width), shape_of(row_total * 3 // 4, cut_width)),
        inner_second,
        part,
        other_rows,
        share_rows,
        *gate_up_late,
    )
    first_other = swap_dp(inner_first)
    far_other = swap_dp(inner_far)
    rest_other = swap_dp(inner_rest)

    count = row_total // 4
    quarter_out = shape_of(count, half_width)

    def parts_of(many):
        return (shape_of(count, half_width // many),) * many

    scratch = (pltpu.VMEM((half_rows, hidden), BF16),)

    def down(kernel, rows, many):
        keep, *send = call(
            kernel, "down", 12, (quarter_out, *parts_of(many)), first_other, rows, w_down[0], scratch=scratch
        )
        return keep, send

    def swap_cores(halves):
        return [swap_inner(half, 1) for half in halves]

    def fold(keep, halves):
        return call(fold_kernel, "fold", 4, (quarter_out,), keep, *halves)[0]

    def pieces(far, keep, send):
        outs = (shape_of(2 * rows_here, half_width),) * 2
        return call(pieces_kernel, "pieces", 4, outs, far, keep, *swap_cores(send))

    outs = (quarter_out, *parts_of(2), *parts_of(2), quarter_out)
    keep_far, *send, keep_near = call(
        down_both_kernel, "down_both", 16, outs, inner_first, inner_far, inner_rest, w_down[0], scratch=scratch
    )
    far = swap_inner(fold(keep_far, swap_cores(send[:2])), 2)
    first_far = far
    own, second = pieces(far, keep_near, send[2:])
    mine = [send_outer(own, 0, False), send_outer(second, 1, False)]

    keep_far, send = down(down_far_kernel, far_other, 2)
    far = swap_inner(fold(after(keep_far, own), swap_cores(send)), 2)
    keep_near, send = down(down_near_kernel, rest_other, 2)
    cut = pieces(far, after(keep_near, *mine), send)
    others = [send_outer(cut[i], i, True) for i in range(2)]

    sums = shape_of(2 * rows_here, half_width)
    keep, send = call(
        gather_kernel,
        "gather",
        4,
        (shape_of(2 * rows_here, half_width, dtype=F32), sums),
        own,
        *mine,
        *others,
    )
    out = shape_of(rows_here, model_width)
    stream_out, normed_out = call(
        tail_kernel, "closing", 8, (out, out), stream_own, keep, swap_inner(send, 1), gain_final[None]
    )
    return (stream_out[None], normed_out[None])


def solution(mesh):
    placed = (
        P("expert", None, "dp"),
        P("expert", "dp", None),
        P("dp", "expert"),
        P(),
        P("expert", "dp", None),
        P("expert", "dp", None),
        P("expert", "dp"),
        P("expert", "dp", None),
        P("expert", None, "dp"),
        P(),
    )
    paired = mesh.shape["dp"] == 2 and mesh.shape["expert"] == 16
    return jax.shard_map(
        body_paired if paired else body_general,
        mesh=mesh,
        in_specs=placed,
        out_specs=(P("expert", "dp", None), P("expert", "dp", None)),
        check_vma=False,
    )
```

```python
import functools
import math

import jax
import jax.numpy as jnp
from jax import lax
from jax.experimental import pallas as pl
from jax.experimental.pallas import tpu as pltpu
from jax.sharding import PartitionSpec as P


def rms_scale(values, gain):
    return values * lax.rsqrt(jnp.mean(values * values, axis=-1, keepdims=True) + 1e-06) * gain


def swiglu_rows(rows_in, gate_up, down, hidden_units):
    both = jnp.dot(rows_in, gate_up, preferred_element_type=jnp.float32)
    inner = (jax.nn.silu(both[:, :hidden_units]) * both[:, hidden_units:]).astype(jnp.bfloat16)
    return jnp.dot(inner, down, preferred_element_type=jnp.float32).astype(jnp.bfloat16)


def body_general(
    attn,
    resid,
    w_out,
    gain_post,
    route_ids,
    route_logits,
    live_count,
    w_gate_up,
    w_down,
    gain_final,
):
    rows_here = resid.shape[1]
    model_width = resid.shape[2]
    top_count = route_ids.shape[2]
    dp_count = lax.axis_size("dp")
    expert_count = lax.axis_size("expert")
    hidden_units = w_down.shape[1]
    capacity = dp_count * max(1, 2 * rows_here * top_count // (expert_count * dp_count))
    slot_count = expert_count * capacity
    flat_attn = attn[0]
    partial_out = jnp.dot(
        flat_attn,
        lax.all_gather(w_out, "expert", axis=1, tiled=True),
        preferred_element_type=jnp.float32,
    )
    projected = lax.psum_scatter(
        partial_out.astype(jnp.bfloat16), "dp", scatter_dimension=0, tiled=True
    ).astype(jnp.float32)
    stream_in = (resid[0].astype(jnp.float32) + projected).astype(jnp.bfloat16)
    stream_float = stream_in.astype(jnp.float32)
    normed_in = rms_scale(stream_float, gain_post).astype(jnp.bfloat16)
    probs = jax.nn.softmax(route_logits[0], axis=-1).astype(jnp.bfloat16)
    alive = jnp.arange(rows_here, dtype=jnp.int32) < live_count[0, 0]
    expert_of = route_ids[0].reshape(-1)
    route_alive = jnp.repeat(alive, top_count)
    onehot = (
        (expert_of[:, None] == jnp.arange(expert_count, dtype=jnp.int32)[None, :])
        & route_alive[:, None]
    ).astype(jnp.int32)
    earlier = jnp.sum((jnp.cumsum(onehot, axis=0) - onehot) * onehot, axis=1)
    target = expert_of * capacity + earlier
    match = (target[:, None] == jnp.arange(slot_count, dtype=jnp.int32)[None, :]) & route_alive[
        :, None
    ]
    placed = match.reshape(rows_here, top_count, slot_count)
    gather_matrix = jnp.any(placed, axis=1).astype(jnp.bfloat16)
    send_rows = lax.dot_general(
        gather_matrix, normed_in, (((0,), (0,)), ((), ())), preferred_element_type=jnp.float32
    ).astype(jnp.bfloat16)
    send_flags = jnp.sum(gather_matrix.astype(jnp.float32), axis=0).astype(jnp.bfloat16)
    combine_matrix = jnp.sum(
        jnp.where(placed, probs.astype(jnp.float32)[:, :, None], jnp.float32(0.0)), axis=1
    ).astype(jnp.bfloat16)
    arrived_rows, arrived_flags = (
        lax.all_to_all(
            send_rows.reshape(expert_count, capacity, model_width),
            "expert",
            split_axis=0,
            concat_axis=0,
            tiled=True,
        ),
        lax.all_to_all(
            send_flags.reshape(expert_count, capacity),
            "expert",
            split_axis=0,
            concat_axis=0,
            tiled=True,
        ),
    )
    arrived = arrived_rows.reshape(slot_count, model_width)
    flags = arrived_flags.reshape(slot_count)
    gate_up_full, down_full = (
        lax.all_gather(w_gate_up, "dp", axis=1, tiled=True),
        lax.all_gather(w_down, "dp", axis=2, tiled=True),
    )
    live_slot = (flags > 0.5).astype(jnp.int32)
    order = jnp.argsort(1 - live_slot, stable=True)
    live_total = jnp.sum(live_slot)
    packed = arrived[order]
    block_len = math.gcd(slot_count, 128)
    block_total = (live_total + block_len - 1) // block_len

    def run_block(index, outputs):
        begin = index * block_len
        rows_in = lax.dynamic_slice_in_dim(packed, begin, block_len, 0)
        block_out = swiglu_rows(rows_in, gate_up_full[0], down_full[0], hidden_units)
        return lax.dynamic_update_slice_in_dim(outputs, block_out, begin, 0)

    packed_out = lax.fori_loop(
        0, block_total, run_block, jnp.zeros((slot_count, model_width), jnp.bfloat16)
    )
    position = (
        jnp.zeros((slot_count,), jnp.int32).at[order].set(jnp.arange(slot_count, dtype=jnp.int32))
    )
    results = packed_out[position]
    returned = lax.all_to_all(
        results.reshape(expert_count, capacity, model_width),
        "expert",
        split_axis=0,
        concat_axis=0,
        tiled=True,
    )
    returned = returned.reshape(slot_count, model_width)
    mixture = jnp.dot(combine_matrix, returned, preferred_element_type=jnp.float32)
    stream_out = (stream_float + mixture).astype(jnp.bfloat16)
    normed_out = rms_scale(stream_out.astype(jnp.float32), gain_final).astype(jnp.bfloat16)
    return (stream_out[None], normed_out[None])


MIB = 1024 * 1024
BF16, F32 = jnp.bfloat16, jnp.float32


def whole_vmem():
    return pl.BlockSpec(memory_space=pltpu.VMEM)


def whole_smem():
    return pl.BlockSpec(memory_space=pltpu.SMEM)


def fixed(*shape):
    return pl.BlockSpec(shape, lambda i: (0,) * len(shape))


def dot(a, b):
    return jnp.dot(a, b, preferred_element_type=F32)


def small_cost():
    return pl.CostEstimate(flops=1, bytes_accessed=1, transcendentals=0)


def kernel_params(mib):
    return pltpu.CompilerParams(vmem_limit_bytes=mib * MIB)


def seat():
    expert = lax.axis_index("expert")
    return expert, lax.shift_right_logical(expert, 2), expert & 3, lax.axis_index("dp")


def aligned(index, step):
    return pl.ds(pl.multiple_of(index * step, step), step)


def cut_kernel(resid, r0, r1, r23):
    expert, outer, inner, dp = seat()
    rows, lanes = r0.shape
    r0[...] = resid[:, aligned(outer, lanes)]
    r1[...] = resid[:, aligned(outer ^ 1, lanes)]
    for i in range(2):
        r23[i * rows : (i + 1) * rows, :] = resid[:, aligned(outer ^ (2 + i), lanes)]


def share_kernel(live, ids, logits, share_ref):
    expert, outer, inner, dp = seat()
    rows, top = ids.shape
    experts, lanes = share_ref.shape
    value = logits[...]
    value = jnp.exp(value - jnp.max(value, axis=1, keepdims=True))
    probs = (value / jnp.sum(value, axis=1, keepdims=True)).astype(BF16).astype(F32)
    probs = jnp.where(lax.broadcasted_iota(jnp.int32, (rows, top), 0) < live[0, 0], probs, 0.0)
    names = lax.broadcasted_iota(jnp.int32, (rows, experts), 1)
    table = jnp.zeros((rows, experts), F32)
    for k in range(top):
        table = table + jnp.where(ids[:, k : k + 1] == names, probs[:, k : k + 1], 0.0)
    spots = lax.broadcasted_iota(jnp.int32, (rows, lanes), 1) - outer * rows
    spots = (spots == lax.broadcasted_iota(jnp.int32, (rows, lanes), 0)).astype(F32).astype(BF16)
    share_ref[...] = lax.dot_general(
        table.astype(BF16), spots, (((0,), (0,)), ((), ())), preferred_element_type=F32
    ).astype(BF16)


def proj_kernel(a0, a1, a2, a3, w0, w1, w2, w3, keep_ref, send_ref, rows, part):
    expert, outer, inner, dp = seat()
    full = a0.shape[0]
    half = full // 2
    block = w0.shape[1]
    for s, a in enumerate((a0, a1, a2, a3)):
        rows[aligned(outer ^ s, full), :] = a[...]
    for j, w in enumerate((w0, w1, w2, w3)):
        part[:, aligned(inner ^ j, block)] = dot(rows[...], w[...]).astype(BF16)
    for spot in range(4):
        keep_ref[spot * half : (spot + 1) * half, :] = part[aligned(2 * spot + dp, half), :]
        send_ref[spot * half : (spot + 1) * half, :] = part[aligned(2 * spot + 1 - dp, half), :]


def stream_kernel(keep, arrived, r0, r13, r2, share, block_ref):
    expert, outer, inner, dp = seat()
    count = keep.shape[0]
    small = r0.shape[0]
    for s, r in enumerate((r0[...], r13[0:small, :], r2[0:small, :], r13[small:, :])):
        rows = aligned(outer ^ s, small)
        product = keep[rows, :].astype(F32) + arrived[rows, :].astype(F32)
        block_ref[rows, :] = (r.astype(F32) + product).astype(BF16)
    block_ref[count:, :] = share[...]


def piece_kernel(starts, weights, *refs):
    *outs, semaphores = refs
    copies = []
    at = 0
    for k, out in enumerate(outs):
        depth, width = out.shape[0], out.shape[1] // 2
        for i in range(2):
            copies.append(
                pltpu.make_async_copy(
                    weights.at[pl.ds(at, depth), pl.ds(starts[i], width)],
                    out.at[:, pl.ds(i * width, width)],
                    semaphores.at[i, k],
                )
            )
        at += depth
    for copy in copies:
        copy.start()
    for copy in copies:
        copy.wait()


def swiglu(gate, up, share):
    return (gate / (1.0 + jnp.exp(-gate)) * up * share).astype(BF16)


def norm_kernel(b0, b1, b2, b3, gain, group_ref, own_ref):
    expert, outer, inner, dp = seat()
    count = group_ref.shape[0]
    width = b0.shape[1]
    experts = b0.shape[0] - count
    small = own_ref.shape[0]
    square = jnp.zeros((count, 1), F32)
    share = jnp.zeros((experts, count), F32)
    for s, b in enumerate((b0, b1, b2, b3)):
        value = b[0:count, :]
        group_ref[:, aligned((outer + 4 - s) & 3, width)] = value
        value = value.astype(F32)
        square = square + jnp.sum(value * value, axis=1, keepdims=True)
        share = share + b[count : count + experts, 0:count].astype(F32)
    own_ref[...] = group_ref[aligned(outer, small), 0 : 4 * width]
    scale = lax.rsqrt(square / (4 * width) + 1e-06)
    for s in range(4):
        cols = slice(s * width, (s + 1) * width)
        value = group_ref[:, cols].astype(F32)
        group_ref[:, cols] = (value * scale * gain[:, cols]).astype(BF16)
    lanes = (experts, 128)
    spread = lax.broadcasted_iota(jnp.int32, lanes, 0) == lax.broadcasted_iota(jnp.int32, lanes, 1)
    group_ref[:, 4 * width :] = lax.dot_general(
        share.astype(BF16),
        spread.astype(F32).astype(BF16),
        (((0,), (0,)), ((), ())),
        preferred_element_type=F32,
    ).astype(BF16)


def first_gate_kernel(
    group_x, group_cx, group, group_c, own, early,
    first_ref, second_ref, part_ref, other_ref, share_ref, mine_ref,
):
    expert, outer, inner, dp = seat()
    count = group.shape[0]
    half = other_ref.shape[1]
    cut = first_ref.shape[1]
    for j, g in enumerate((group_x, group_cx, group, group_c)):
        rows = slice(j * count, (j + 1) * count)
        mine_ref[rows, :] = g[:, aligned(dp, half)]
        other_ref[rows, :] = g[:, aligned(1 - dp, half)]
        share = g[:, 2 * half : 2 * half + 128].astype(F32)
        picked = lax.broadcasted_iota(jnp.int32, share.shape, 1) == expert
        share = jnp.sum(jnp.where(picked, share, 0.0), axis=1, keepdims=True)
        share_ref[rows, :] = jnp.broadcast_to(share, (count, 128))
    mine, other = mine_ref[...], other_ref[...]
    gate = dot(mine, own[:, 0:cut]) + dot(other, early[:, 0:cut])
    up = dot(mine, own[:, 2 * cut : 3 * cut]) + dot(other, early[:, cut : 2 * cut])
    inner = swiglu(gate, up, share_ref[:, 0:1])
    first_ref[...] = inner[: 3 * count]
    second_ref[...] = inner[3 * count :]
    part_ref[:, 0:cut] = dot(mine, own[:, cut : 2 * cut])
    part_ref[:, cut : 2 * cut] = dot(mine, own[:, 3 * cut : 4 * cut])


def last_gate_kernel(second, part, other, share, *refs):
    *late, far_ref, rest_ref = refs
    count, cut = second.shape
    gate, up = part[:, 0:cut], part[:, cut : 2 * cut]
    at = 0
    for piece in late:
        rows = other[:, at : at + piece.shape[0]]
        gate = gate + dot(rows, piece[:, 0:cut])
        up = up + dot(rows, piece[:, cut : 2 * cut])
        at += piece.shape[0]
    value = swiglu(gate, up, share[:, 0:1])
    far_ref[...] = value[: 2 * count]
    rest_ref[0:count, :] = second[...]
    rest_ref[count:, :] = value[2 * count :]


def down_rows(pieces, wd, keep_ref, sends, rows):
    expert, outer, inner, dp = seat()
    core = inner & 1
    count, side = sends[0].shape
    small = count // 4
    for h, places in enumerate(pieces):
        cut = places[0][0].shape[1]
        cols = slice(h * cut, (h + 1) * cut)
        for i in range(2):
            for j in range(2):
                ref, start = places[j]
                kept = aligned(start // small + ((outer + 3 - core - 2 * i) & 3), small)
                at = (2 * i + j) * small
                rows[at : at + small, cols] = ref[kept, :]
                ref, start = places[1 - j]
                sent = aligned(start // small + ((outer + 2 + core - 2 * i) & 3), small)
                rows[count + at : count + at + small, cols] = ref[sent, :]
    for at in range(0, wd.shape[1], 256):
        value = dot(rows[...], wd[:, at : at + 256]).astype(BF16)
        keep_ref[:, at : at + 256] = value[:count]
        sends[at // side][:, at % side : at % side + 256] = value[count:]


def far_places(first, far):
    count = far.shape[0] // 2
    return ((first, 0), (first, count)), ((far, 0), (far, count))


def near_places(first, rest):
    count = rest.shape[0] // 3
    return ((first, 2 * count), (rest, 0)), ((rest, count), (rest, 2 * count))


def down_far_kernel(first, far, wd, keep_ref, *refs):
    *sends, rows = refs
    down_rows(far_places(first, far), wd, keep_ref, sends, rows)


def down_near_kernel(first, rest, wd, keep_ref, *refs):
    *sends, rows = refs
    down_rows(near_places(first, rest), wd, keep_ref, sends, rows)


def added(keep, cores, cols):
    side = cores[0].shape[1]
    return keep[:, cols].astype(F32) + cores[cols.start // side][:, cols.start % side : cols.start % side + 256].astype(F32)


def fold_kernel(keep, *refs):
    *cores, out = refs
    for at in range(0, keep.shape[1], 256):
        cols = slice(at, at + 256)
        out[:, cols] = added(keep, cores, cols).astype(BF16)


def pieces_kernel(far, keep, *refs):
    *cores, first, second = refs
    half = first.shape[0]
    for at in range(0, keep.shape[1], 256):
        cols = slice(at, at + 256)
        total = (added(keep, cores, cols) + far[:, cols].astype(F32)).astype(BF16)
        first[:, cols] = total[:half]
        second[:, cols] = total[half:]


def gather_kernel(own, a0, a1, b0, b1, keep_ref, send_ref):
    expert, outer, inner, dp = seat()
    small = own.shape[0] // 2
    last = jnp.where((inner & 1) == 1, own[...].astype(F32), a1[...].astype(F32))
    for i, total in enumerate((a0[...].astype(F32) + last, b0[...].astype(F32) + b1[...].astype(F32))):
        rows = slice(i * small, (i + 1) * small)
        keep_ref[rows, :] = total[:small]
        send_ref[rows, :] = total[small:].astype(BF16)


def tail_kernel(own, keep, core, gain, stream_ref, normed_ref):
    expert, outer, inner, dp = seat()
    small, half = own.shape[0], keep.shape[1]
    for i, at in enumerate((dp, 1 - dp)):
        rows = slice(i * small, (i + 1) * small)
        cols = aligned(at, half)
        mixture = keep[rows, :] + core[rows, :].astype(F32)
        stream_ref[:, cols] = (own[:, cols].astype(F32) + mixture).astype(BF16)
    normed_ref[...] = rms_scale(stream_ref[...].astype(F32), gain[...]).astype(BF16)


def body_paired(
    attn,
    resid,
    w_out,
    gain_post,
    route_ids,
    route_logits,
    live_count,
    w_gate_up,
    w_down,
    gain_final,
):
    rows_here = resid.shape[1]
    model_width = resid.shape[2]
    expert_count = lax.axis_size("expert")
    hidden = w_down.shape[1]
    half_width = w_down.shape[2]
    quarter = model_width // 4
    vmem, smem = whole_vmem(), whole_smem()

    def shape_of(*shape, dtype=BF16):
        return jax.ShapeDtypeStruct(shape, dtype)

    def call(kernel, name, mib, outs, *args, scratch=(), first=vmem):
        return pl.pallas_call(
            kernel,
            out_shape=outs,
            in_specs=[first] + [vmem] * (len(args) - 1),
            out_specs=tuple(vmem for _ in outs),
            scratch_shapes=list(scratch),
            compiler_params=kernel_params(mib),
            cost_estimate=small_cost(),
            name=name,
        )(*args)

    def swap_dp(x):
        return lax.ppermute(x, "dp", [(0, 1), (1, 0)])

    def shift_outer(x, s):
        return lax.ppermute(
            x, "expert", [(i, (i + 4 * s) % expert_count) for i in range(expert_count)]
        )

    def send_outer(x, i, cross):
        pairs = []
        for at in range(2 * expert_count):
            d, e = divmod(at, expert_count)
            step = 3 - e % 2 - 2 * i
            if step or cross:
                pairs.append((at, (d ^ cross) * expert_count + (e + 4 * step) % expert_count))
        return lax.ppermute(x, ("dp", "expert"), pairs)

    def swap_inner(x, j):
        return lax.ppermute(x, "expert", [(i, i ^ j) for i in range(expert_count)])

    def swap_outer(x, s):
        return lax.ppermute(x, "expert", [(i, i ^ (4 * s)) for i in range(expert_count)])

    def after(x, *results):
        return lax.optimization_barrier((x, *results))[0]

    def weight_piece(first, size, depths):
        return pl.pallas_call(
            functools.partial(piece_kernel, (first, hidden + first)),
            out_shape=tuple(shape_of(depth, 2 * size) for depth in depths),
            in_specs=[pl.BlockSpec(memory_space=pl.ANY)],
            out_specs=tuple(vmem for _ in depths),
            scratch_shapes=[pltpu.SemaphoreType.DMA((2, len(depths)))],
            compiler_params=kernel_params(8),
            cost_estimate=small_cost(),
            name="weight_piece",
        )(w_gate_up[0])

    piece = shape_of(rows_here, quarter)
    r_own, r_1, r_23 = call(
        cut_kernel, "cut_resid", 4, (piece, piece, shape_of(2 * rows_here, quarter)), resid[0]
    )
    (share,) = call(
        share_kernel,
        "share",
        4,
        (shape_of(expert_count, quarter),),
        live_count,
        route_ids[0],
        route_logits[0],
        first=smem,
    )
    cut_width = hidden // 2
    early_piece = weight_piece(0, cut_width, (half_width,))[0]
    late_pieces = weight_piece(cut_width, cut_width, (half_width * 640 // 1024, half_width * 384 // 1024))
    gate_up_early = swap_dp(early_piece)
    a = [attn[0], swap_outer(attn[0], 1), swap_outer(attn[0], 2)]
    w_x = swap_inner(w_out, 2)
    r_2 = swap_outer(r_23, 2)
    a.append(swap_outer(after(a[2], a[1], r_2), 1))
    w_c = swap_inner(after(w_out, w_x, share, *late_pieces), 1)
    w_cx = swap_inner(w_x, 1)
    r_13 = swap_outer(jnp.concatenate([r_1, r_2[rows_here:]], axis=0), 1)

    product = shape_of(4 * rows_here, quarter)
    keep, send = call(
        proj_kernel,
        "projection",
        8,
        (product, product),
        *a[:3],
        after(a[3], r_13),
        w_out,
        w_c,
        w_x,
        w_cx,
        scratch=(
            pltpu.VMEM((8 * rows_here, attn.shape[2]), BF16),
            pltpu.VMEM((8 * rows_here, quarter), BF16),
        ),
    )
    arrived = swap_dp(send)
    gate_up_late = [swap_dp(after(piece, send)) for piece in late_pieces]
    (block,) = call(
        stream_kernel,
        "stream",
        4,
        (shape_of(4 * rows_here + expert_count, quarter),),
        after(keep, gate_up_early),
        arrived,
        r_own,
        r_13,
        r_2,
        share,
    )

    def norm(b0, b1, b2, b3):
        outs = (shape_of(4 * rows_here, model_width + 128), shape_of(rows_here, model_width))
        return call(norm_kernel, "norm", 8, outs, b0, b1, b2, b3, gain_post[None])

    blocks = [block] + [shift_outer(block, s) for s in (1, 2, 3)]
    group, stream_own = norm(*blocks)
    blocks_x = [swap_inner(b, 2) for b in blocks]
    group_x, unused = norm(*blocks_x)
    group_c = swap_inner(group, 1)
    group_cx = swap_inner(group_x, 1)

    row_total = 16 * rows_here
    half_rows = row_total // 2
    inner_first, inner_second, part, other_rows, share_rows = call(
        first_gate_kernel,
        "first_gate_up",
        24,
        (
            shape_of(row_total * 3 // 4, cut_width),
            shape_of(row_total // 4, cut_width),
            shape_of(row_total, hidden, dtype=F32),
            shape_of(row_total, half_width),
            shape_of(row_total, 128, dtype=F32),
        ),
        group_x,
        group_cx,
        group,
        group_c,
        w_gate_up[0],
        gate_up_early,
        scratch=(pltpu.VMEM((row_total, half_width), BF16),),
    )
    inner_far, inner_rest = call(
        last_gate_kernel,
        "last_gate_up",
        16,
        (shape_of(half_rows, cut_width), shape_of(row_total * 3 // 4, cut_width)),
        inner_second,
        part,
        other_rows,
        share_rows,
        *gate_up_late,
    )
    first_other = swap_dp(inner_first)
    far_other = swap_dp(inner_far)
    rest_other = swap_dp(inner_rest)

    count = row_total // 4
    quarter_out = shape_of(count, half_width)

    def parts_of(many):
        return (shape_of(count, half_width // many),) * many

    scratch = (pltpu.VMEM((half_rows, hidden), BF16),)

    def down(kernel, first, rows, many):
        keep, *send = call(
            kernel, "down", 12, (quarter_out, *parts_of(many)), first, rows, w_down[0], scratch=scratch
        )
        return keep, send

    def swap_cores(halves):
        return [swap_inner(half, 1) for half in halves]

    def fold(keep, halves):
        return call(fold_kernel, "fold", 4, (quarter_out,), keep, *halves)[0]

    def pieces(far, keep, send):
        outs = (shape_of(2 * rows_here, half_width),) * 2
        return call(pieces_kernel, "pieces", 4, outs, far, keep, *swap_cores(send))

    keep_far, send = down(down_far_kernel, inner_first, inner_far, 2)
    far = swap_inner(fold(keep_far, swap_cores(send)), 2)
    keep_near, send = down(down_near_kernel, inner_first, inner_rest, 2)
    first, own = pieces(far, keep_near, send)
    mine = [send_outer(first, 0, False), send_outer(own, 1, False)]

    keep_far, send = down(down_far_kernel, first_other, far_other, 2)
    far = swap_inner(fold(after(keep_far, own), swap_cores(send)), 2)
    keep_near, send = down(down_near_kernel, first_other, rest_other, 2)
    cut = pieces(far, after(keep_near, *mine), send)
    others = [send_outer(cut[i], i, True) for i in range(2)]

    sums = shape_of(2 * rows_here, half_width)
    keep, send = call(
        gather_kernel,
        "gather",
        4,
        (shape_of(2 * rows_here, half_width, dtype=F32), sums),
        own,
        *mine,
        *others,
    )
    out = shape_of(rows_here, model_width)
    stream_out, normed_out = call(
        tail_kernel, "closing", 8, (out, out), stream_own, keep, swap_inner(send, 1), gain_final[None]
    )
    return (stream_out[None], normed_out[None])


def solution(mesh):
    placed = (
        P("expert", None, "dp"),
        P("expert", "dp", None),
        P("dp", "expert"),
        P(),
        P("expert", "dp", None),
        P("expert", "dp", None),
        P("expert", "dp"),
        P("expert", "dp", None),
        P("expert", None, "dp"),
        P(),
    )
    paired = mesh.shape["dp"] == 2 and mesh.shape["expert"] == 16
    return jax.shard_map(
        body_paired if paired else body_general,
        mesh=mesh,
        in_specs=placed,
        out_specs=(P("expert", "dp", None), P("expert", "dp", None)),
        check_vma=False,
    )
```

```python
import functools
import math

import jax
import jax.numpy as jnp
from jax import lax
from jax.experimental import pallas as pl
from jax.experimental.pallas import tpu as pltpu
from jax.sharding import PartitionSpec as P


def rms_scale(values, gain):
    return values * lax.rsqrt(jnp.mean(values * values, axis=-1, keepdims=True) + 1e-06) * gain


def swiglu_rows(rows_in, gate_up, down, hidden_units):
    both = jnp.dot(rows_in, gate_up, preferred_element_type=jnp.float32)
    inner = (jax.nn.silu(both[:, :hidden_units]) * both[:, hidden_units:]).astype(jnp.bfloat16)
    return jnp.dot(inner, down, preferred_element_type=jnp.float32).astype(jnp.bfloat16)


def body_general(
    attn,
    resid,
    w_out,
    gain_post,
    route_ids,
    route_logits,
    live_count,
    w_gate_up,
    w_down,
    gain_final,
):
    rows_here = resid.shape[1]
    model_width = resid.shape[2]
    top_count = route_ids.shape[2]
    dp_count = lax.axis_size("dp")
    expert_count = lax.axis_size("expert")
    hidden_units = w_down.shape[1]
    capacity = dp_count * max(1, 2 * rows_here * top_count // (expert_count * dp_count))
    slot_count = expert_count * capacity
    flat_attn = attn[0]
    partial_out = jnp.dot(
        flat_attn,
        lax.all_gather(w_out, "expert", axis=1, tiled=True),
        preferred_element_type=jnp.float32,
    )
    projected = lax.psum_scatter(
        partial_out.astype(jnp.bfloat16), "dp", scatter_dimension=0, tiled=True
    ).astype(jnp.float32)
    stream_in = (resid[0].astype(jnp.float32) + projected).astype(jnp.bfloat16)
    stream_float = stream_in.astype(jnp.float32)
    normed_in = rms_scale(stream_float, gain_post).astype(jnp.bfloat16)
    probs = jax.nn.softmax(route_logits[0], axis=-1).astype(jnp.bfloat16)
    alive = jnp.arange(rows_here, dtype=jnp.int32) < live_count[0, 0]
    expert_of = route_ids[0].reshape(-1)
    route_alive = jnp.repeat(alive, top_count)
    onehot = (
        (expert_of[:, None] == jnp.arange(expert_count, dtype=jnp.int32)[None, :])
        & route_alive[:, None]
    ).astype(jnp.int32)
    earlier = jnp.sum((jnp.cumsum(onehot, axis=0) - onehot) * onehot, axis=1)
    target = expert_of * capacity + earlier
    match = (target[:, None] == jnp.arange(slot_count, dtype=jnp.int32)[None, :]) & route_alive[
        :, None
    ]
    placed = match.reshape(rows_here, top_count, slot_count)
    gather_matrix = jnp.any(placed, axis=1).astype(jnp.bfloat16)
    send_rows = lax.dot_general(
        gather_matrix, normed_in, (((0,), (0,)), ((), ())), preferred_element_type=jnp.float32
    ).astype(jnp.bfloat16)
    send_flags = jnp.sum(gather_matrix.astype(jnp.float32), axis=0).astype(jnp.bfloat16)
    combine_matrix = jnp.sum(
        jnp.where(placed, probs.astype(jnp.float32)[:, :, None], jnp.float32(0.0)), axis=1
    ).astype(jnp.bfloat16)
    arrived_rows, arrived_flags = (
        lax.all_to_all(
            send_rows.reshape(expert_count, capacity, model_width),
            "expert",
            split_axis=0,
            concat_axis=0,
            tiled=True,
        ),
        lax.all_to_all(
            send_flags.reshape(expert_count, capacity),
            "expert",
            split_axis=0,
            concat_axis=0,
            tiled=True,
        ),
    )
    arrived = arrived_rows.reshape(slot_count, model_width)
    flags = arrived_flags.reshape(slot_count)
    gate_up_full, down_full = (
        lax.all_gather(w_gate_up, "dp", axis=1, tiled=True),
        lax.all_gather(w_down, "dp", axis=2, tiled=True),
    )
    live_slot = (flags > 0.5).astype(jnp.int32)
    order = jnp.argsort(1 - live_slot, stable=True)
    live_total = jnp.sum(live_slot)
    packed = arrived[order]
    block_len = math.gcd(slot_count, 128)
    block_total = (live_total + block_len - 1) // block_len

    def run_block(index, outputs):
        begin = index * block_len
        rows_in = lax.dynamic_slice_in_dim(packed, begin, block_len, 0)
        block_out = swiglu_rows(rows_in, gate_up_full[0], down_full[0], hidden_units)
        return lax.dynamic_update_slice_in_dim(outputs, block_out, begin, 0)

    packed_out = lax.fori_loop(
        0, block_total, run_block, jnp.zeros((slot_count, model_width), jnp.bfloat16)
    )
    position = (
        jnp.zeros((slot_count,), jnp.int32).at[order].set(jnp.arange(slot_count, dtype=jnp.int32))
    )
    results = packed_out[position]
    returned = lax.all_to_all(
        results.reshape(expert_count, capacity, model_width),
        "expert",
        split_axis=0,
        concat_axis=0,
        tiled=True,
    )
    returned = returned.reshape(slot_count, model_width)
    mixture = jnp.dot(combine_matrix, returned, preferred_element_type=jnp.float32)
    stream_out = (stream_float + mixture).astype(jnp.bfloat16)
    normed_out = rms_scale(stream_out.astype(jnp.float32), gain_final).astype(jnp.bfloat16)
    return (stream_out[None], normed_out[None])


MIB = 1024 * 1024
BF16, F32 = jnp.bfloat16, jnp.float32


def whole_vmem():
    return pl.BlockSpec(memory_space=pltpu.VMEM)


def whole_smem():
    return pl.BlockSpec(memory_space=pltpu.SMEM)


def fixed(*shape):
    return pl.BlockSpec(shape, lambda i: (0,) * len(shape))


def dot(a, b):
    return jnp.dot(a, b, preferred_element_type=F32)


def small_cost():
    return pl.CostEstimate(flops=1, bytes_accessed=1, transcendentals=0)


def kernel_params(mib):
    return pltpu.CompilerParams(vmem_limit_bytes=mib * MIB)


def seat():
    expert = lax.axis_index("expert")
    return expert, lax.shift_right_logical(expert, 2), expert & 3, lax.axis_index("dp")


def aligned(index, step):
    return pl.ds(pl.multiple_of(index * step, step), step)


def cut_kernel(resid, r0, r1, r23):
    expert, outer, inner, dp = seat()
    rows, lanes = r0.shape
    r0[...] = resid[:, aligned(outer, lanes)]
    r1[...] = resid[:, aligned(outer ^ 1, lanes)]
    for i in range(2):
        r23[i * rows : (i + 1) * rows, :] = resid[:, aligned(outer ^ (2 + i), lanes)]


def share_kernel(live, ids, logits, share_ref):
    expert, outer, inner, dp = seat()
    rows, top = ids.shape
    experts, lanes = share_ref.shape
    value = logits[...]
    value = jnp.exp(value - jnp.max(value, axis=1, keepdims=True))
    probs = (value / jnp.sum(value, axis=1, keepdims=True)).astype(BF16).astype(F32)
    probs = jnp.where(lax.broadcasted_iota(jnp.int32, (rows, top), 0) < live[0, 0], probs, 0.0)
    names = lax.broadcasted_iota(jnp.int32, (rows, experts), 1)
    table = jnp.zeros((rows, experts), F32)
    for k in range(top):
        table = table + jnp.where(ids[:, k : k + 1] == names, probs[:, k : k + 1], 0.0)
    spots = lax.broadcasted_iota(jnp.int32, (rows, lanes), 1) - outer * rows
    spots = (spots == lax.broadcasted_iota(jnp.int32, (rows, lanes), 0)).astype(F32).astype(BF16)
    share_ref[...] = lax.dot_general(
        table.astype(BF16), spots, (((0,), (0,)), ((), ())), preferred_element_type=F32
    ).astype(BF16)


def proj_kernel(a0, a1, a2, a3, w0, w1, w2, w3, keep_ref, send_ref, rows, part):
    expert, outer, inner, dp = seat()
    full = a0.shape[0]
    half = full // 2
    block = w0.shape[1]
    for s, a in enumerate((a0, a1, a2, a3)):
        rows[aligned(outer ^ s, full), :] = a[...]
    for j, w in enumerate((w0, w1, w2, w3)):
        part[:, aligned(inner ^ j, block)] = dot(rows[...], w[...]).astype(BF16)
    for spot in range(4):
        keep_ref[spot * half : (spot + 1) * half, :] = part[aligned(2 * spot + dp, half), :]
        send_ref[spot * half : (spot + 1) * half, :] = part[aligned(2 * spot + 1 - dp, half), :]


def stream_kernel(keep, arrived, r0, r13, r2, share, block_ref):
    expert, outer, inner, dp = seat()
    count = keep.shape[0]
    small = r0.shape[0]
    for s, r in enumerate((r0[...], r13[0:small, :], r2[0:small, :], r13[small:, :])):
        rows = aligned(outer ^ s, small)
        product = keep[rows, :].astype(F32) + arrived[rows, :].astype(F32)
        block_ref[rows, :] = (r.astype(F32) + product).astype(BF16)
    block_ref[count:, :] = share[...]


def piece_kernel(starts, weights, *refs):
    *outs, semaphores = refs
    copies = []
    at = 0
    for k, out in enumerate(outs):
        depth, width = out.shape[0], out.shape[1] // 2
        for i in range(2):
            copies.append(
                pltpu.make_async_copy(
                    weights.at[pl.ds(at, depth), pl.ds(starts[i], width)],
                    out.at[:, pl.ds(i * width, width)],
                    semaphores.at[i, k],
                )
            )
        at += depth
    for copy in copies:
        copy.start()
    for copy in copies:
        copy.wait()


def swiglu(gate, up, share):
    return (gate / (1.0 + jnp.exp(-gate)) * up * share).astype(BF16)


def norm_kernel(b0, b1, b2, b3, gain, group_ref, own_ref):
    expert, outer, inner, dp = seat()
    count = group_ref.shape[0]
    width = b0.shape[1]
    experts = b0.shape[0] - count
    small = own_ref.shape[0]
    square = jnp.zeros((count, 1), F32)
    share = jnp.zeros((experts, count), F32)
    for s, b in enumerate((b0, b1, b2, b3)):
        value = b[0:count, :]
        group_ref[:, aligned(outer ^ s, width)] = value
        value = value.astype(F32)
        square = square + jnp.sum(value * value, axis=1, keepdims=True)
        share = share + b[count : count + experts, 0:count].astype(F32)
    own_ref[...] = group_ref[aligned(outer, small), 0 : 4 * width]
    scale = lax.rsqrt(square / (4 * width) + 1e-06)
    for s in range(4):
        cols = slice(s * width, (s + 1) * width)
        value = group_ref[:, cols].astype(F32)
        group_ref[:, cols] = (value * scale * gain[:, cols]).astype(BF16)
    lanes = (experts, 128)
    spread = lax.broadcasted_iota(jnp.int32, lanes, 0) == lax.broadcasted_iota(jnp.int32, lanes, 1)
    group_ref[:, 4 * width :] = lax.dot_general(
        share.astype(BF16),
        spread.astype(F32).astype(BF16),
        (((0,), (0,)), ((), ())),
        preferred_element_type=F32,
    ).astype(BF16)


def first_gate_kernel(
    group_x, group_cx, group, group_c, own, early,
    first_ref, second_ref, part_ref, other_ref, share_ref, mine_ref,
):
    expert, outer, inner, dp = seat()
    count = group.shape[0]
    half = other_ref.shape[1]
    cut = first_ref.shape[1]
    for j, g in enumerate((group_x, group_cx, group, group_c)):
        rows = slice(j * count, (j + 1) * count)
        mine_ref[rows, :] = g[:, aligned(dp, half)]
        other_ref[rows, :] = g[:, aligned(1 - dp, half)]
        share = g[:, 2 * half : 2 * half + 128].astype(F32)
        picked = lax.broadcasted_iota(jnp.int32, share.shape, 1) == expert
        share = jnp.sum(jnp.where(picked, share, 0.0), axis=1, keepdims=True)
        share_ref[rows, :] = jnp.broadcast_to(share, (count, 128))
    mine, other = mine_ref[...], other_ref[...]
    gate = dot(mine, own[:, 0:cut]) + dot(other, early[:, 0:cut])
    up = dot(mine, own[:, 2 * cut : 3 * cut]) + dot(other, early[:, cut : 2 * cut])
    inner = swiglu(gate, up, share_ref[:, 0:1])
    first_ref[...] = inner[: 3 * count]
    second_ref[...] = inner[3 * count :]
    part_ref[:, 0:cut] = dot(mine, own[:, cut : 2 * cut])
    part_ref[:, cut : 2 * cut] = dot(mine, own[:, 3 * cut : 4 * cut])


def last_gate_kernel(second, part, other, share, *refs):
    *late, far_ref, rest_ref = refs
    count, cut = second.shape
    gate, up = part[:, 0:cut], part[:, cut : 2 * cut]
    at = 0
    for piece in late:
        rows = other[:, at : at + piece.shape[0]]
        gate = gate + dot(rows, piece[:, 0:cut])
        up = up + dot(rows, piece[:, cut : 2 * cut])
        at += piece.shape[0]
    value = swiglu(gate, up, share[:, 0:1])
    far_ref[...] = value[: 2 * count]
    rest_ref[0:count, :] = second[...]
    rest_ref[count:, :] = value[2 * count :]


def down_rows(pieces, wd, keep_ref, sends, rows):
    expert, outer, inner, dp = seat()
    core = inner & 1
    count, side = sends[0].shape
    small = count // 4
    for h, places in enumerate(pieces):
        cut = places[0][0].shape[1]
        cols = slice(h * cut, (h + 1) * cut)
        for i in range(2):
            for j in range(2):
                ref, start = places[j]
                kept = aligned(start // small + (outer ^ (2 * core + i)), small)
                at = (2 * i + j) * small
                rows[at : at + small, cols] = ref[kept, :]
                ref, start = places[1 - j]
                sent = aligned(start // small + (outer ^ (2 - 2 * core + i)), small)
                rows[count + at : count + at + small, cols] = ref[sent, :]
    for at in range(0, wd.shape[1], 256):
        value = dot(rows[...], wd[:, at : at + 256]).astype(BF16)
        keep_ref[:, at : at + 256] = value[:count]
        sends[at // side][:, at % side : at % side + 256] = value[count:]


def far_places(first, far):
    count = far.shape[0] // 2
    return ((first, 0), (first, count)), ((far, 0), (far, count))


def near_places(first, rest):
    count = rest.shape[0] // 3
    return ((first, 2 * count), (rest, 0)), ((rest, count), (rest, 2 * count))


def down_both_kernel(first, far, rest, wd, keep_far, *refs):
    *sends, keep_near, rows = refs
    half = len(sends) // 2
    down_rows(far_places(first, far), wd, keep_far, sends[:half], rows)
    down_rows(near_places(first, rest), wd, keep_near, sends[half:], rows)


def down_far_kernel(first, far, wd, keep_ref, *refs):
    *sends, rows = refs
    down_rows(far_places(first, far), wd, keep_ref, sends, rows)


def down_near_kernel(first, rest, wd, keep_ref, *refs):
    *sends, rows = refs
    down_rows(near_places(first, rest), wd, keep_ref, sends, rows)


def added(keep, cores, cols):
    side = cores[0].shape[1]
    return keep[:, cols].astype(F32) + cores[cols.start // side][:, cols.start % side : cols.start % side + 256].astype(F32)


def fold_kernel(keep, *refs):
    *cores, out = refs
    for at in range(0, keep.shape[1], 256):
        cols = slice(at, at + 256)
        out[:, cols] = added(keep, cores, cols).astype(BF16)


def pieces_kernel(far, keep, *refs):
    *cores, first, second = refs
    half = first.shape[0]
    for at in range(0, keep.shape[1], 256):
        cols = slice(at, at + 256)
        total = (added(keep, cores, cols) + far[:, cols].astype(F32)).astype(BF16)
        first[:, cols] = total[:half]
        second[:, cols] = total[half:]


def gather_kernel(own, a0, a1, b0, b1, keep_ref, send_ref):
    expert, outer, inner, dp = seat()
    small = own.shape[0] // 2
    start = jnp.where((inner & 1) == 0, own[...].astype(F32), a0[...].astype(F32))
    for i, total in enumerate((start + a1[...].astype(F32), b0[...].astype(F32) + b1[...].astype(F32))):
        rows = slice(i * small, (i + 1) * small)
        keep_ref[rows, :] = total[:small]
        send_ref[rows, :] = total[small:].astype(BF16)


def tail_kernel(own, keep, core, gain, stream_ref, normed_ref):
    expert, outer, inner, dp = seat()
    small, half = own.shape[0], keep.shape[1]
    for i, at in enumerate((dp, 1 - dp)):
        rows = slice(i * small, (i + 1) * small)
        cols = aligned(at, half)
        mixture = keep[rows, :] + core[rows, :].astype(F32)
        stream_ref[:, cols] = (own[:, cols].astype(F32) + mixture).astype(BF16)
    normed_ref[...] = rms_scale(stream_ref[...].astype(F32), gain[...]).astype(BF16)


def body_paired(
    attn,
    resid,
    w_out,
    gain_post,
    route_ids,
    route_logits,
    live_count,
    w_gate_up,
    w_down,
    gain_final,
):
    rows_here = resid.shape[1]
    model_width = resid.shape[2]
    expert_count = lax.axis_size("expert")
    hidden = w_down.shape[1]
    half_width = w_down.shape[2]
    quarter = model_width // 4
    vmem, smem = whole_vmem(), whole_smem()

    def shape_of(*shape, dtype=BF16):
        return jax.ShapeDtypeStruct(shape, dtype)

    def call(kernel, name, mib, outs, *args, scratch=(), first=vmem):
        return pl.pallas_call(
            kernel,
            out_shape=outs,
            in_specs=[first] + [vmem] * (len(args) - 1),
            out_specs=tuple(vmem for _ in outs),
            scratch_shapes=list(scratch),
            compiler_params=kernel_params(mib),
            cost_estimate=small_cost(),
            name=name,
        )(*args)

    def swap_dp(x):
        return lax.ppermute(x, "dp", [(0, 1), (1, 0)])

    def send_outer(x, i, cross):
        pairs = []
        for at in range(2 * expert_count):
            d, e = divmod(at, expert_count)
            step = 2 * (e % 2) + i
            if step or cross:
                pairs.append((at, (d ^ cross) * expert_count + (e ^ (4 * step))))
        return lax.ppermute(x, ("dp", "expert"), pairs)

    def swap_inner(x, j):
        return lax.ppermute(x, "expert", [(i, i ^ j) for i in range(expert_count)])

    def swap_outer(x, s):
        return lax.ppermute(x, "expert", [(i, i ^ (4 * s)) for i in range(expert_count)])

    def after(x, *results):
        return lax.optimization_barrier((x, *results))[0]

    def weight_piece(first, size, depths):
        return pl.pallas_call(
            functools.partial(piece_kernel, (first, hidden + first)),
            out_shape=tuple(shape_of(depth, 2 * size) for depth in depths),
            in_specs=[pl.BlockSpec(memory_space=pl.ANY)],
            out_specs=tuple(vmem for _ in depths),
            scratch_shapes=[pltpu.SemaphoreType.DMA((2, len(depths)))],
            compiler_params=kernel_params(8),
            cost_estimate=small_cost(),
            name="weight_piece",
        )(w_gate_up[0])

    piece = shape_of(rows_here, quarter)
    r_own, r_1, r_23 = call(
        cut_kernel, "cut_resid", 4, (piece, piece, shape_of(2 * rows_here, quarter)), resid[0]
    )
    (share,) = call(
        share_kernel,
        "share",
        4,
        (shape_of(expert_count, quarter),),
        live_count,
        route_ids[0],
        route_logits[0],
        first=smem,
    )
    cut_width = hidden // 2
    early_piece = weight_piece(0, cut_width, (half_width,))[0]
    late_pieces = weight_piece(cut_width, cut_width, (half_width * 640 // 1024, half_width * 384 // 1024))
    gate_up_early = swap_dp(early_piece)
    a = [attn[0], swap_outer(attn[0], 1), swap_outer(attn[0], 2)]
    w_x = swap_inner(w_out, 2)
    r_2 = swap_outer(r_23, 2)
    a.append(swap_outer(after(a[2], a[1], r_2), 1))
    w_c = swap_inner(after(w_out, w_x, share, *late_pieces), 1)
    w_cx = swap_inner(w_x, 1)
    r_13 = swap_outer(jnp.concatenate([r_1, r_2[rows_here:]], axis=0), 1)

    product = shape_of(4 * rows_here, quarter)
    keep, send = call(
        proj_kernel,
        "projection",
        8,
        (product, product),
        *a[:3],
        after(a[3], r_13),
        w_out,
        w_c,
        w_x,
        w_cx,
        scratch=(
            pltpu.VMEM((8 * rows_here, attn.shape[2]), BF16),
            pltpu.VMEM((8 * rows_here, quarter), BF16),
        ),
    )
    arrived = swap_dp(send)
    gate_up_late = [swap_dp(after(piece, send)) for piece in late_pieces]
    (block,) = call(
        stream_kernel,
        "stream",
        4,
        (shape_of(4 * rows_here + expert_count, quarter),),
        after(keep, gate_up_early),
        arrived,
        r_own,
        r_13,
        r_2,
        share,
    )

    def norm(b0, b1, b2, b3):
        outs = (shape_of(4 * rows_here, model_width + 128), shape_of(rows_here, model_width))
        return call(norm_kernel, "norm", 8, outs, b0, b1, b2, b3, gain_post[None])

    blocks = [block] + [swap_outer(block, s) for s in (1, 2, 3)]
    group, stream_own = norm(*blocks)
    blocks_x = [swap_inner(b, 2) for b in blocks]
    group_x, unused = norm(*blocks_x)
    group_c = swap_inner(group, 1)
    group_cx = swap_inner(group_x, 1)

    row_total = 16 * rows_here
    half_rows = row_total // 2
    inner_first, inner_second, part, other_rows, share_rows = call(
        first_gate_kernel,
        "first_gate_up",
        24,
        (
            shape_of(row_total * 3 // 4, cut_width),
            shape_of(row_total // 4, cut_width),
            shape_of(row_total, hidden, dtype=F32),
            shape_of(row_total, half_width),
            shape_of(row_total, 128, dtype=F32),
        ),
        group_x,
        group_cx,
        group,
        group_c,
        w_gate_up[0],
        gate_up_early,
        scratch=(pltpu.VMEM((row_total, half_width), BF16),),
    )
    inner_far, inner_rest = call(
        last_gate_kernel,
        "last_gate_up",
        16,
        (shape_of(half_rows, cut_width), shape_of(row_total * 3 // 4, cut_width)),
        inner_second,
        part,
        other_rows,
        share_rows,
        *gate_up_late,
    )
    first_other = swap_dp(inner_first)
    far_other = swap_dp(inner_far)
    rest_other = swap_dp(inner_rest)

    count = row_total // 4
    quarter_out = shape_of(count, half_width)

    def parts_of(many):
        return (shape_of(count, half_width // many),) * many

    scratch = (pltpu.VMEM((half_rows, hidden), BF16),)

    def down(kernel, rows, many):
        keep, *send = call(
            kernel, "down", 12, (quarter_out, *parts_of(many)), first_other, rows, w_down[0], scratch=scratch
        )
        return keep, send

    def swap_cores(halves):
        return [swap_inner(half, 1) for half in halves]

    def fold(keep, halves):
        return call(fold_kernel, "fold", 4, (quarter_out,), keep, *halves)[0]

    def pieces(far, keep, send):
        outs = (shape_of(2 * rows_here, half_width),) * 2
        return call(pieces_kernel, "pieces", 4, outs, far, keep, *swap_cores(send))

    outs = (quarter_out, *parts_of(2), *parts_of(2), quarter_out)
    keep_far, *send, keep_near = call(
        down_both_kernel, "down_both", 16, outs, inner_first, inner_far, inner_rest, w_down[0], scratch=scratch
    )
    far = swap_inner(fold(keep_far, swap_cores(send[:2])), 2)
    first_far = far
    own, second = pieces(far, keep_near, send[2:])
    mine = [send_outer(own, 0, False), send_outer(second, 1, False)]

    keep_far, send = down(down_far_kernel, far_other, 2)
    far = swap_inner(fold(after(keep_far, own), swap_cores(send)), 2)
    keep_near, send = down(down_near_kernel, rest_other, 2)
    cut = pieces(far, after(keep_near, *mine), send)
    others = [send_outer(cut[i], i, True) for i in range(2)]

    sums = shape_of(2 * rows_here, half_width)
    keep, send = call(
        gather_kernel,
        "gather",
        4,
        (shape_of(2 * rows_here, half_width, dtype=F32), sums),
        own,
        *mine,
        *others,
    )
    out = shape_of(rows_here, model_width)
    stream_out, normed_out = call(
        tail_kernel, "closing", 8, (out, out), stream_own, keep, swap_inner(send, 1), gain_final[None]
    )
    return (stream_out[None], normed_out[None])


def solution(mesh):
    placed = (
        P("expert", None, "dp"),
        P("expert", "dp", None),
        P("dp", "expert"),
        P(),
        P("expert", "dp", None),
        P("expert", "dp", None),
        P("expert", "dp"),
        P("expert", "dp", None),
        P("expert", None, "dp"),
        P(),
    )
    paired = mesh.shape["dp"] == 2 and mesh.shape["expert"] == 16
    return jax.shard_map(
        body_paired if paired else body_general,
        mesh=mesh,
        in_specs=placed,
        out_specs=(P("expert", "dp", None), P("expert", "dp", None)),
        check_vma=False,
    )
```

```python
import functools
import math

import jax
import jax.numpy as jnp
from jax import lax
from jax.experimental import pallas as pl
from jax.experimental.pallas import tpu as pltpu
from jax.sharding import PartitionSpec as P


def rms_scale(values, gain):
    return values * lax.rsqrt(jnp.mean(values * values, axis=-1, keepdims=True) + 1e-06) * gain


def swiglu_rows(rows_in, gate_up, down, hidden_units):
    both = jnp.dot(rows_in, gate_up, preferred_element_type=jnp.float32)
    inner = (jax.nn.silu(both[:, :hidden_units]) * both[:, hidden_units:]).astype(jnp.bfloat16)
    return jnp.dot(inner, down, preferred_element_type=jnp.float32).astype(jnp.bfloat16)


def body_general(
    attn,
    resid,
    w_out,
    gain_post,
    route_ids,
    route_logits,
    live_count,
    w_gate_up,
    w_down,
    gain_final,
):
    rows_here = resid.shape[1]
    model_width = resid.shape[2]
    top_count = route_ids.shape[2]
    dp_count = lax.axis_size("dp")
    expert_count = lax.axis_size("expert")
    hidden_units = w_down.shape[1]
    capacity = dp_count * max(1, 2 * rows_here * top_count // (expert_count * dp_count))
    slot_count = expert_count * capacity
    flat_attn = attn[0]
    partial_out = jnp.dot(
        flat_attn,
        lax.all_gather(w_out, "expert", axis=1, tiled=True),
        preferred_element_type=jnp.float32,
    )
    projected = lax.psum_scatter(
        partial_out.astype(jnp.bfloat16), "dp", scatter_dimension=0, tiled=True
    ).astype(jnp.float32)
    stream_in = (resid[0].astype(jnp.float32) + projected).astype(jnp.bfloat16)
    stream_float = stream_in.astype(jnp.float32)
    normed_in = rms_scale(stream_float, gain_post).astype(jnp.bfloat16)
    probs = jax.nn.softmax(route_logits[0], axis=-1).astype(jnp.bfloat16)
    alive = jnp.arange(rows_here, dtype=jnp.int32) < live_count[0, 0]
    expert_of = route_ids[0].reshape(-1)
    route_alive = jnp.repeat(alive, top_count)
    onehot = (
        (expert_of[:, None] == jnp.arange(expert_count, dtype=jnp.int32)[None, :])
        & route_alive[:, None]
    ).astype(jnp.int32)
    earlier = jnp.sum((jnp.cumsum(onehot, axis=0) - onehot) * onehot, axis=1)
    target = expert_of * capacity + earlier
    match = (target[:, None] == jnp.arange(slot_count, dtype=jnp.int32)[None, :]) & route_alive[
        :, None
    ]
    placed = match.reshape(rows_here, top_count, slot_count)
    gather_matrix = jnp.any(placed, axis=1).astype(jnp.bfloat16)
    send_rows = lax.dot_general(
        gather_matrix, normed_in, (((0,), (0,)), ((), ())), preferred_element_type=jnp.float32
    ).astype(jnp.bfloat16)
    send_flags = jnp.sum(gather_matrix.astype(jnp.float32), axis=0).astype(jnp.bfloat16)
    combine_matrix = jnp.sum(
        jnp.where(placed, probs.astype(jnp.float32)[:, :, None], jnp.float32(0.0)), axis=1
    ).astype(jnp.bfloat16)
    arrived_rows, arrived_flags = (
        lax.all_to_all(
            send_rows.reshape(expert_count, capacity, model_width),
            "expert",
            split_axis=0,
            concat_axis=0,
            tiled=True,
        ),
        lax.all_to_all(
            send_flags.reshape(expert_count, capacity),
            "expert",
            split_axis=0,
            concat_axis=0,
            tiled=True,
        ),
    )
    arrived = arrived_rows.reshape(slot_count, model_width)
    flags = arrived_flags.reshape(slot_count)
    gate_up_full, down_full = (
        lax.all_gather(w_gate_up, "dp", axis=1, tiled=True),
        lax.all_gather(w_down, "dp", axis=2, tiled=True),
    )
    live_slot = (flags > 0.5).astype(jnp.int32)
    order = jnp.argsort(1 - live_slot, stable=True)
    live_total = jnp.sum(live_slot)
    packed = arrived[order]
    block_len = math.gcd(slot_count, 128)
    block_total = (live_total + block_len - 1) // block_len

    def run_block(index, outputs):
        begin = index * block_len
        rows_in = lax.dynamic_slice_in_dim(packed, begin, block_len, 0)
        block_out = swiglu_rows(rows_in, gate_up_full[0], down_full[0], hidden_units)
        return lax.dynamic_update_slice_in_dim(outputs, block_out, begin, 0)

    packed_out = lax.fori_loop(
        0, block_total, run_block, jnp.zeros((slot_count, model_width), jnp.bfloat16)
    )
    position = (
        jnp.zeros((slot_count,), jnp.int32).at[order].set(jnp.arange(slot_count, dtype=jnp.int32))
    )
    results = packed_out[position]
    returned = lax.all_to_all(
        results.reshape(expert_count, capacity, model_width),
        "expert",
        split_axis=0,
        concat_axis=0,
        tiled=True,
    )
    returned = returned.reshape(slot_count, model_width)
    mixture = jnp.dot(combine_matrix, returned, preferred_element_type=jnp.float32)
    stream_out = (stream_float + mixture).astype(jnp.bfloat16)
    normed_out = rms_scale(stream_out.astype(jnp.float32), gain_final).astype(jnp.bfloat16)
    return (stream_out[None], normed_out[None])


MIB = 1024 * 1024
BF16, F32 = jnp.bfloat16, jnp.float32


def whole_vmem():
    return pl.BlockSpec(memory_space=pltpu.VMEM)


def whole_smem():
    return pl.BlockSpec(memory_space=pltpu.SMEM)


def fixed(*shape):
    return pl.BlockSpec(shape, lambda i: (0,) * len(shape))


def dot(a, b):
    return jnp.dot(a, b, preferred_element_type=F32)


def small_cost():
    return pl.CostEstimate(flops=1, bytes_accessed=1, transcendentals=0)


def kernel_params(mib):
    return pltpu.CompilerParams(vmem_limit_bytes=mib * MIB)


def seat():
    expert = lax.axis_index("expert")
    return expert, lax.shift_right_logical(expert, 2), expert & 3, lax.axis_index("dp")


def aligned(index, step):
    return pl.ds(pl.multiple_of(index * step, step), step)


def cut_kernel(resid, r0, r1, r23):
    expert, outer, inner, dp = seat()
    rows, lanes = r0.shape
    r0[...] = resid[:, aligned(outer, lanes)]
    r1[...] = resid[:, aligned(outer ^ 1, lanes)]
    for i in range(2):
        r23[i * rows : (i + 1) * rows, :] = resid[:, aligned(outer ^ (2 + i), lanes)]


def share_kernel(live, ids, logits, share_ref):
    expert, outer, inner, dp = seat()
    rows, top = ids.shape
    experts, lanes = share_ref.shape
    value = logits[...]
    value = jnp.exp(value - jnp.max(value, axis=1, keepdims=True))
    probs = (value / jnp.sum(value, axis=1, keepdims=True)).astype(BF16).astype(F32)
    probs = jnp.where(lax.broadcasted_iota(jnp.int32, (rows, top), 0) < live[0, 0], probs, 0.0)
    names = lax.broadcasted_iota(jnp.int32, (rows, experts), 1)
    table = jnp.zeros((rows, experts), F32)
    for k in range(top):
        table = table + jnp.where(ids[:, k : k + 1] == names, probs[:, k : k + 1], 0.0)
    spots = lax.broadcasted_iota(jnp.int32, (rows, lanes), 1) - outer * rows
    spots = (spots == lax.broadcasted_iota(jnp.int32, (rows, lanes), 0)).astype(F32).astype(BF16)
    share_ref[...] = lax.dot_general(
        table.astype(BF16), spots, (((0,), (0,)), ((), ())), preferred_element_type=F32
    ).astype(BF16)


def proj_kernel(a0, a1, a2, a3, w0, w1, w2, w3, keep_ref, send_ref, rows, part):
    expert, outer, inner, dp = seat()
    full = a0.shape[0]
    half = full // 2
    block = w0.shape[1]
    for s, a in enumerate((a0, a1, a2, a3)):
        rows[aligned(outer ^ s, full), :] = a[...]
    for j, w in enumerate((w0, w1, w2, w3)):
        part[:, aligned(inner ^ j, block)] = dot(rows[...], w[...]).astype(BF16)
    for spot in range(4):
        keep_ref[spot * half : (spot + 1) * half, :] = part[aligned(2 * spot + dp, half), :]
        send_ref[spot * half : (spot + 1) * half, :] = part[aligned(2 * spot + 1 - dp, half), :]


def stream_kernel(keep, arrived, r0, r13, r2, share, block_ref):
    expert, outer, inner, dp = seat()
    count = keep.shape[0]
    small = r0.shape[0]
    for s, r in enumerate((r0[...], r13[0:small, :], r2[0:small, :], r13[small:, :])):
        rows = aligned(outer ^ s, small)
        product = keep[rows, :].astype(F32) + arrived[rows, :].astype(F32)
        block_ref[rows, :] = (r.astype(F32) + product).astype(BF16)
    block_ref[count:, :] = share[...]


def piece_kernel(starts, weights, *refs):
    *outs, semaphores = refs
    copies = []
    at = 0
    for k, out in enumerate(outs):
        depth, width = out.shape[0], out.shape[1] // 2
        for i in range(2):
            copies.append(
                pltpu.make_async_copy(
                    weights.at[pl.ds(at, depth), pl.ds(starts[i], width)],
                    out.at[:, pl.ds(i * width, width)],
                    semaphores.at[i, k],
                )
            )
        at += depth
    for copy in copies:
        copy.start()
    for copy in copies:
        copy.wait()


def swiglu(gate, up, share):
    return (gate / (1.0 + jnp.exp(-gate)) * up * share).astype(BF16)


def norm_kernel(b0, b1, b2, b3, gain, group_ref, own_ref):
    expert, outer, inner, dp = seat()
    count = group_ref.shape[0]
    width = b0.shape[1]
    experts = b0.shape[0] - count
    small = own_ref.shape[0]
    square = jnp.zeros((count, 1), F32)
    share = jnp.zeros((experts, count), F32)
    for s, b in enumerate((b0, b1, b2, b3)):
        value = b[0:count, :]
        group_ref[:, aligned(outer ^ s, width)] = value
        value = value.astype(F32)
        square = square + jnp.sum(value * value, axis=1, keepdims=True)
        share = share + b[count : count + experts, 0:count].astype(F32)
    own_ref[...] = group_ref[aligned(outer, small), 0 : 4 * width]
    scale = lax.rsqrt(square / (4 * width) + 1e-06)
    for s in range(4):
        cols = slice(s * width, (s + 1) * width)
        value = group_ref[:, cols].astype(F32)
        group_ref[:, cols] = (value * scale * gain[:, cols]).astype(BF16)
    lanes = (experts, 128)
    spread = lax.broadcasted_iota(jnp.int32, lanes, 0) == lax.broadcasted_iota(jnp.int32, lanes, 1)
    group_ref[:, 4 * width :] = lax.dot_general(
        share.astype(BF16),
        spread.astype(F32).astype(BF16),
        (((0,), (0,)), ((), ())),
        preferred_element_type=F32,
    ).astype(BF16)


def first_gate_kernel(
    group_x, group_cx, group, group_c, own, early,
    first_ref, second_ref, part_ref, other_ref, share_ref, mine_ref,
):
    expert, outer, inner, dp = seat()
    count = group.shape[0]
    half = other_ref.shape[1]
    cut = first_ref.shape[1]
    for j, g in enumerate((group_x, group_cx, group, group_c)):
        rows = slice(j * count, (j + 1) * count)
        mine_ref[rows, :] = g[:, aligned(dp, half)]
        other_ref[rows, :] = g[:, aligned(1 - dp, half)]
        share = g[:, 2 * half : 2 * half + 128].astype(F32)
        picked = lax.broadcasted_iota(jnp.int32, share.shape, 1) == expert
        share = jnp.sum(jnp.where(picked, share, 0.0), axis=1, keepdims=True)
        share_ref[rows, :] = jnp.broadcast_to(share, (count, 128))
    mine, other = mine_ref[...], other_ref[...]
    gate = dot(mine, own[:, 0:cut]) + dot(other, early[:, 0:cut])
    up = dot(mine, own[:, 2 * cut : 3 * cut]) + dot(other, early[:, cut : 2 * cut])
    inner = swiglu(gate, up, share_ref[:, 0:1])
    first_ref[...] = inner[: 3 * count]
    second_ref[...] = inner[3 * count :]
    part_ref[:, 0:cut] = dot(mine, own[:, cut : 2 * cut])
    part_ref[:, cut : 2 * cut] = dot(mine, own[:, 3 * cut : 4 * cut])


def last_gate_kernel(second, part, other, share, *refs):
    *late, far_ref, rest_ref = refs
    count, cut = second.shape
    gate, up = part[:, 0:cut], part[:, cut : 2 * cut]
    at = 0
    for piece in late:
        rows = other[:, at : at + piece.shape[0]]
        gate = gate + dot(rows, piece[:, 0:cut])
        up = up + dot(rows, piece[:, cut : 2 * cut])
        at += piece.shape[0]
    value = swiglu(gate, up, share[:, 0:1])
    far_ref[...] = value[: 2 * count]
    rest_ref[0:count, :] = second[...]
    rest_ref[count:, :] = value[2 * count :]


def down_rows(pieces, wd, keep_ref, sends, rows):
    expert, outer, inner, dp = seat()
    core = inner & 1
    count, side = sends[0].shape
    small = count // 4
    for h, places in enumerate(pieces):
        cut = places[0][0].shape[1]
        cols = slice(h * cut, (h + 1) * cut)
        for i in range(2):
            for j in range(2):
                ref, start = places[j]
                kept = aligned(start // small + (outer ^ (core if i else 3 - core)), small)
                at = (2 * i + j) * small
                rows[at : at + small, cols] = ref[kept, :]
                ref, start = places[1 - j]
                sent = aligned(start // small + (outer ^ (1 - core if i else 2 + core)), small)
                rows[count + at : count + at + small, cols] = ref[sent, :]
    for at in range(0, wd.shape[1], 256):
        value = dot(rows[...], wd[:, at : at + 256]).astype(BF16)
        keep_ref[:, at : at + 256] = value[:count]
        sends[at // side][:, at % side : at % side + 256] = value[count:]


def far_places(first, far):
    count = far.shape[0] // 2
    return ((first, 0), (first, count)), ((far, 0), (far, count))


def near_places(first, rest):
    count = rest.shape[0] // 3
    return ((first, 2 * count), (rest, 0)), ((rest, count), (rest, 2 * count))


def down_both_kernel(first, far, rest, wd, keep_far, *refs):
    *sends, keep_near, rows = refs
    half = len(sends) // 2
    down_rows(far_places(first, far), wd, keep_far, sends[:half], rows)
    down_rows(near_places(first, rest), wd, keep_near, sends[half:], rows)


def down_far_kernel(first, far, wd, keep_ref, *refs):
    *sends, rows = refs
    down_rows(far_places(first, far), wd, keep_ref, sends, rows)


def down_near_kernel(first, rest, wd, keep_ref, *refs):
    *sends, rows = refs
    down_rows(near_places(first, rest), wd, keep_ref, sends, rows)


def added(keep, cores, cols):
    side = cores[0].shape[1]
    return keep[:, cols].astype(F32) + cores[cols.start // side][:, cols.start % side : cols.start % side + 256].astype(F32)


def fold_kernel(keep, *refs):
    *cores, out = refs
    for at in range(0, keep.shape[1], 256):
        cols = slice(at, at + 256)
        out[:, cols] = added(keep, cores, cols).astype(BF16)


def pieces_kernel(far, keep, *refs):
    *cores, first, second = refs
    half = first.shape[0]
    for at in range(0, keep.shape[1], 256):
        cols = slice(at, at + 256)
        total = (added(keep, cores, cols) + far[:, cols].astype(F32)).astype(BF16)
        first[:, cols] = total[:half]
        second[:, cols] = total[half:]


def gather_kernel(own, a0, a1, b0, b1, keep_ref, send_ref):
    expert, outer, inner, dp = seat()
    small = own.shape[0] // 2
    last = jnp.where((inner & 1) == 0, own[...].astype(F32), a1[...].astype(F32))
    for i, total in enumerate((a0[...].astype(F32) + last, b0[...].astype(F32) + b1[...].astype(F32))):
        rows = slice(i * small, (i + 1) * small)
        keep_ref[rows, :] = total[:small]
        send_ref[rows, :] = total[small:].astype(BF16)


def tail_kernel(own, keep, core, gain, stream_ref, normed_ref):
    expert, outer, inner, dp = seat()
    small, half = own.shape[0], keep.shape[1]
    for i, at in enumerate((dp, 1 - dp)):
        rows = slice(i * small, (i + 1) * small)
        cols = aligned(at, half)
        mixture = keep[rows, :] + core[rows, :].astype(F32)
        stream_ref[:, cols] = (own[:, cols].astype(F32) + mixture).astype(BF16)
    normed_ref[...] = rms_scale(stream_ref[...].astype(F32), gain[...]).astype(BF16)


def body_paired(
    attn,
    resid,
    w_out,
    gain_post,
    route_ids,
    route_logits,
    live_count,
    w_gate_up,
    w_down,
    gain_final,
):
    rows_here = resid.shape[1]
    model_width = resid.shape[2]
    expert_count = lax.axis_size("expert")
    hidden = w_down.shape[1]
    half_width = w_down.shape[2]
    quarter = model_width // 4
    vmem, smem = whole_vmem(), whole_smem()

    def shape_of(*shape, dtype=BF16):
        return jax.ShapeDtypeStruct(shape, dtype)

    def call(kernel, name, mib, outs, *args, scratch=(), first=vmem):
        return pl.pallas_call(
            kernel,
            out_shape=outs,
            in_specs=[first] + [vmem] * (len(args) - 1),
            out_specs=tuple(vmem for _ in outs),
            scratch_shapes=list(scratch),
            compiler_params=kernel_params(mib),
            cost_estimate=small_cost(),
            name=name,
        )(*args)

    def swap_dp(x):
        return lax.ppermute(x, "dp", [(0, 1), (1, 0)])

    def send_outer(x, i, cross):
        pairs = []
        for at in range(2 * expert_count):
            d, e = divmod(at, expert_count)
            step = e % 2 if i else 3 - e % 2
            if step or cross:
                pairs.append((at, (d ^ cross) * expert_count + (e ^ (4 * step))))
        return lax.ppermute(x, ("dp", "expert"), pairs)

    def swap_inner(x, j):
        return lax.ppermute(x, "expert", [(i, i ^ j) for i in range(expert_count)])

    def swap_outer(x, s):
        return lax.ppermute(x, "expert", [(i, i ^ (4 * s)) for i in range(expert_count)])

    def after(x, *results):
        return lax.optimization_barrier((x, *results))[0]

    def weight_piece(first, size, depths):
        return pl.pallas_call(
            functools.partial(piece_kernel, (first, hidden + first)),
            out_shape=tuple(shape_of(depth, 2 * size) for depth in depths),
            in_specs=[pl.BlockSpec(memory_space=pl.ANY)],
            out_specs=tuple(vmem for _ in depths),
            scratch_shapes=[pltpu.SemaphoreType.DMA((2, len(depths)))],
            compiler_params=kernel_params(8),
            cost_estimate=small_cost(),
            name="weight_piece",
        )(w_gate_up[0])

    piece = shape_of(rows_here, quarter)
    r_own, r_1, r_23 = call(
        cut_kernel, "cut_resid", 4, (piece, piece, shape_of(2 * rows_here, quarter)), resid[0]
    )
    (share,) = call(
        share_kernel,
        "share",
        4,
        (shape_of(expert_count, quarter),),
        live_count,
        route_ids[0],
        route_logits[0],
        first=smem,
    )
    cut_width = hidden // 2
    early_piece = weight_piece(0, cut_width, (half_width,))[0]
    late_pieces = weight_piece(cut_width, cut_width, (half_width * 640 // 1024, half_width * 384 // 1024))
    gate_up_early = swap_dp(early_piece)
    a = [attn[0], swap_outer(attn[0], 1), swap_outer(attn[0], 2)]
    w_x = swap_inner(w_out, 2)
    r_2 = swap_outer(r_23, 2)
    a.append(swap_outer(after(a[2], a[1], r_2), 1))
    w_c = swap_inner(after(w_out, w_x, share, *late_pieces), 1)
    w_cx = swap_inner(w_x, 1)
    r_13 = swap_outer(jnp.concatenate([r_1, r_2[rows_here:]], axis=0), 1)

    product = shape_of(4 * rows_here, quarter)
    keep, send = call(
        proj_kernel,
        "projection",
        8,
        (product, product),
        *a[:3],
        after(a[3], r_13),
        w_out,
        w_c,
        w_x,
        w_cx,
        scratch=(
            pltpu.VMEM((8 * rows_here, attn.shape[2]), BF16),
            pltpu.VMEM((8 * rows_here, quarter), BF16),
        ),
    )
    arrived = swap_dp(send)
    gate_up_late = [swap_dp(after(piece, send)) for piece in late_pieces]
    (block,) = call(
        stream_kernel,
        "stream",
        4,
        (shape_of(4 * rows_here + expert_count, quarter),),
        after(keep, gate_up_early),
        arrived,
        r_own,
        r_13,
        r_2,
        share,
    )

    def norm(b0, b1, b2, b3):
        outs = (shape_of(4 * rows_here, model_width + 128), shape_of(rows_here, model_width))
        return call(norm_kernel, "norm", 8, outs, b0, b1, b2, b3, gain_post[None])

    blocks = [block] + [swap_outer(block, s) for s in (1, 2, 3)]
    group, stream_own = norm(*blocks)
    blocks_x = [swap_inner(b, 2) for b in blocks]
    group_x, unused = norm(*blocks_x)
    group_c = swap_inner(group, 1)
    group_cx = swap_inner(group_x, 1)

    row_total = 16 * rows_here
    half_rows = row_total // 2
    inner_first, inner_second, part, other_rows, share_rows = call(
        first_gate_kernel,
        "first_gate_up",
        24,
        (
            shape_of(row_total * 3 // 4, cut_width),
            shape_of(row_total // 4, cut_width),
            shape_of(row_total, hidden, dtype=F32),
            shape_of(row_total, half_width),
            shape_of(row_total, 128, dtype=F32),
        ),
        group_x,
        group_cx,
        group,
        group_c,
        w_gate_up[0],
        gate_up_early,
        scratch=(pltpu.VMEM((row_total, half_width), BF16),),
    )
    inner_far, inner_rest = call(
        last_gate_kernel,
        "last_gate_up",
        16,
        (shape_of(half_rows, cut_width), shape_of(row_total * 3 // 4, cut_width)),
        inner_second,
        part,
        other_rows,
        share_rows,
        *gate_up_late,
    )
    first_other = swap_dp(inner_first)
    far_other = swap_dp(inner_far)
    rest_other = swap_dp(inner_rest)

    count = row_total // 4
    quarter_out = shape_of(count, half_width)

    def parts_of(many):
        return (shape_of(count, half_width // many),) * many

    scratch = (pltpu.VMEM((half_rows, hidden), BF16),)

    def down(kernel, rows, many):
        keep, *send = call(
            kernel, "down", 12, (quarter_out, *parts_of(many)), first_other, rows, w_down[0], scratch=scratch
        )
        return keep, send

    def swap_cores(halves):
        return [swap_inner(half, 1) for half in halves]

    def fold(keep, halves):
        return call(fold_kernel, "fold", 4, (quarter_out,), keep, *halves)[0]

    def pieces(far, keep, send):
        outs = (shape_of(2 * rows_here, half_width),) * 2
        return call(pieces_kernel, "pieces", 4, outs, far, keep, *swap_cores(send))

    outs = (quarter_out, *parts_of(2), *parts_of(2), quarter_out)
    keep_far, *send, keep_near = call(
        down_both_kernel, "down_both", 16, outs, inner_first, inner_far, inner_rest, w_down[0], scratch=scratch
    )
    far = swap_inner(fold(keep_far, swap_cores(send[:2])), 2)
    first_far = far
    first, own = pieces(far, keep_near, send[2:])
    mine = [send_outer(first, 0, False), send_outer(own, 1, False)]

    keep_far, send = down(down_far_kernel, far_other, 2)
    far = swap_inner(fold(after(keep_far, own), swap_cores(send)), 2)
    keep_near, send = down(down_near_kernel, rest_other, 2)
    cut = pieces(far, after(keep_near, *mine), send)
    others = [send_outer(cut[i], i, True) for i in range(2)]

    sums = shape_of(2 * rows_here, half_width)
    keep, send = call(
        gather_kernel,
        "gather",
        4,
        (shape_of(2 * rows_here, half_width, dtype=F32), sums),
        own,
        *mine,
        *others,
    )
    out = shape_of(rows_here, model_width)
    stream_out, normed_out = call(
        tail_kernel, "closing", 8, (out, out), stream_own, keep, swap_inner(send, 1), gain_final[None]
    )
    return (stream_out[None], normed_out[None])


def solution(mesh):
    placed = (
        P("expert", None, "dp"),
        P("expert", "dp", None),
        P("dp", "expert"),
        P(),
        P("expert", "dp", None),
        P("expert", "dp", None),
        P("expert", "dp"),
        P("expert", "dp", None),
        P("expert", None, "dp"),
        P(),
    )
    paired = mesh.shape["dp"] == 2 and mesh.shape["expert"] == 16
    return jax.shard_map(
        body_paired if paired else body_general,
        mesh=mesh,
        in_specs=placed,
        out_specs=(P("expert", "dp", None), P("expert", "dp", None)),
        check_vma=False,
    )
```

```python
import functools
import math

import jax
import jax.numpy as jnp
from jax import lax
from jax.experimental import pallas as pl
from jax.experimental.pallas import tpu as pltpu
from jax.sharding import PartitionSpec as P


def rms_scale(values, gain):
    return values * lax.rsqrt(jnp.mean(values * values, axis=-1, keepdims=True) + 1e-06) * gain


def swiglu_rows(rows_in, gate_up, down, hidden_units):
    both = jnp.dot(rows_in, gate_up, preferred_element_type=jnp.float32)
    inner = (jax.nn.silu(both[:, :hidden_units]) * both[:, hidden_units:]).astype(jnp.bfloat16)
    return jnp.dot(inner, down, preferred_element_type=jnp.float32).astype(jnp.bfloat16)


def body_general(
    attn,
    resid,
    w_out,
    gain_post,
    route_ids,
    route_logits,
    live_count,
    w_gate_up,
    w_down,
    gain_final,
):
    rows_here = resid.shape[1]
    model_width = resid.shape[2]
    top_count = route_ids.shape[2]
    dp_count = lax.axis_size("dp")
    expert_count = lax.axis_size("expert")
    hidden_units = w_down.shape[1]
    capacity = dp_count * max(1, 2 * rows_here * top_count // (expert_count * dp_count))
    slot_count = expert_count * capacity
    flat_attn = attn[0]
    partial_out = jnp.dot(
        flat_attn,
        lax.all_gather(w_out, "expert", axis=1, tiled=True),
        preferred_element_type=jnp.float32,
    )
    projected = lax.psum_scatter(
        partial_out.astype(jnp.bfloat16), "dp", scatter_dimension=0, tiled=True
    ).astype(jnp.float32)
    stream_in = (resid[0].astype(jnp.float32) + projected).astype(jnp.bfloat16)
    stream_float = stream_in.astype(jnp.float32)
    normed_in = rms_scale(stream_float, gain_post).astype(jnp.bfloat16)
    probs = jax.nn.softmax(route_logits[0], axis=-1).astype(jnp.bfloat16)
    alive = jnp.arange(rows_here, dtype=jnp.int32) < live_count[0, 0]
    expert_of = route_ids[0].reshape(-1)
    route_alive = jnp.repeat(alive, top_count)
    onehot = (
        (expert_of[:, None] == jnp.arange(expert_count, dtype=jnp.int32)[None, :])
        & route_alive[:, None]
    ).astype(jnp.int32)
    earlier = jnp.sum((jnp.cumsum(onehot, axis=0) - onehot) * onehot, axis=1)
    target = expert_of * capacity + earlier
    match = (target[:, None] == jnp.arange(slot_count, dtype=jnp.int32)[None, :]) & route_alive[
        :, None
    ]
    placed = match.reshape(rows_here, top_count, slot_count)
    gather_matrix = jnp.any(placed, axis=1).astype(jnp.bfloat16)
    send_rows = lax.dot_general(
        gather_matrix, normed_in, (((0,), (0,)), ((), ())), preferred_element_type=jnp.float32
    ).astype(jnp.bfloat16)
    send_flags = jnp.sum(gather_matrix.astype(jnp.float32), axis=0).astype(jnp.bfloat16)
    combine_matrix = jnp.sum(
        jnp.where(placed, probs.astype(jnp.float32)[:, :, None], jnp.float32(0.0)), axis=1
    ).astype(jnp.bfloat16)
    arrived_rows, arrived_flags = (
        lax.all_to_all(
            send_rows.reshape(expert_count, capacity, model_width),
            "expert",
            split_axis=0,
            concat_axis=0,
            tiled=True,
        ),
        lax.all_to_all(
            send_flags.reshape(expert_count, capacity),
            "expert",
            split_axis=0,
            concat_axis=0,
            tiled=True,
        ),
    )
    arrived = arrived_rows.reshape(slot_count, model_width)
    flags = arrived_flags.reshape(slot_count)
    gate_up_full, down_full = (
        lax.all_gather(w_gate_up, "dp", axis=1, tiled=True),
        lax.all_gather(w_down, "dp", axis=2, tiled=True),
    )
    live_slot = (flags > 0.5).astype(jnp.int32)
    order = jnp.argsort(1 - live_slot, stable=True)
    live_total = jnp.sum(live_slot)
    packed = arrived[order]
    block_len = math.gcd(slot_count, 128)
    block_total = (live_total + block_len - 1) // block_len

    def run_block(index, outputs):
        begin = index * block_len
        rows_in = lax.dynamic_slice_in_dim(packed, begin, block_len, 0)
        block_out = swiglu_rows(rows_in, gate_up_full[0], down_full[0], hidden_units)
        return lax.dynamic_update_slice_in_dim(outputs, block_out, begin, 0)

    packed_out = lax.fori_loop(
        0, block_total, run_block, jnp.zeros((slot_count, model_width), jnp.bfloat16)
    )
    position = (
        jnp.zeros((slot_count,), jnp.int32).at[order].set(jnp.arange(slot_count, dtype=jnp.int32))
    )
    results = packed_out[position]
    returned = lax.all_to_all(
        results.reshape(expert_count, capacity, model_width),
        "expert",
        split_axis=0,
        concat_axis=0,
        tiled=True,
    )
    returned = returned.reshape(slot_count, model_width)
    mixture = jnp.dot(combine_matrix, returned, preferred_element_type=jnp.float32)
    stream_out = (stream_float + mixture).astype(jnp.bfloat16)
    normed_out = rms_scale(stream_out.astype(jnp.float32), gain_final).astype(jnp.bfloat16)
    return (stream_out[None], normed_out[None])


MIB = 1024 * 1024
BF16, F32 = jnp.bfloat16, jnp.float32


def whole_vmem():
    return pl.BlockSpec(memory_space=pltpu.VMEM)


def whole_smem():
    return pl.BlockSpec(memory_space=pltpu.SMEM)


def fixed(*shape):
    return pl.BlockSpec(shape, lambda i: (0,) * len(shape))


def dot(a, b):
    return jnp.dot(a, b, preferred_element_type=F32)


def small_cost():
    return pl.CostEstimate(flops=1, bytes_accessed=1, transcendentals=0)


def kernel_params(mib):
    return pltpu.CompilerParams(vmem_limit_bytes=mib * MIB)


def seat():
    expert = lax.axis_index("expert")
    return expert, lax.shift_right_logical(expert, 2), expert & 3, lax.axis_index("dp")


def aligned(index, step):
    return pl.ds(pl.multiple_of(index * step, step), step)


def cut_kernel(resid, r0, r1, r23):
    expert, outer, inner, dp = seat()
    rows, lanes = r0.shape
    r0[...] = resid[:, aligned(outer, lanes)]
    r1[...] = resid[:, aligned(outer ^ 1, lanes)]
    for i in range(2):
        r23[i * rows : (i + 1) * rows, :] = resid[:, aligned(outer ^ (2 + i), lanes)]


def share_kernel(live, ids, logits, share_ref):
    expert, outer, inner, dp = seat()
    rows, top = ids.shape
    experts, lanes = share_ref.shape
    value = logits[...]
    value = jnp.exp(value - jnp.max(value, axis=1, keepdims=True))
    probs = (value / jnp.sum(value, axis=1, keepdims=True)).astype(BF16).astype(F32)
    probs = jnp.where(lax.broadcasted_iota(jnp.int32, (rows, top), 0) < live[0, 0], probs, 0.0)
    names = lax.broadcasted_iota(jnp.int32, (rows, experts), 1)
    table = jnp.zeros((rows, experts), F32)
    for k in range(top):
        table = table + jnp.where(ids[:, k : k + 1] == names, probs[:, k : k + 1], 0.0)
    spots = lax.broadcasted_iota(jnp.int32, (rows, lanes), 1) - outer * rows
    spots = (spots == lax.broadcasted_iota(jnp.int32, (rows, lanes), 0)).astype(F32).astype(BF16)
    share_ref[...] = lax.dot_general(
        table.astype(BF16), spots, (((0,), (0,)), ((), ())), preferred_element_type=F32
    ).astype(BF16)


def proj_kernel(a0, a1, a2, a3, w0, w1, w2, w3, keep_ref, send_ref, rows, part):
    expert, outer, inner, dp = seat()
    full = a0.shape[0]
    half = full // 2
    block = w0.shape[1]
    for s, a in enumerate((a0, a1, a2, a3)):
        rows[aligned(outer ^ s, full), :] = a[...]
    for j, w in enumerate((w0, w1, w2, w3)):
        part[:, aligned(inner ^ j, block)] = dot(rows[...], w[...]).astype(BF16)
    for spot in range(4):
        keep_ref[spot * half : (spot + 1) * half, :] = part[aligned(2 * spot + dp, half), :]
        send_ref[spot * half : (spot + 1) * half, :] = part[aligned(2 * spot + 1 - dp, half), :]


def stream_kernel(keep, arrived, r0, r13, r2, share, block_ref):
    expert, outer, inner, dp = seat()
    count = keep.shape[0]
    small = r0.shape[0]
    for s, r in enumerate((r0[...], r13[0:small, :], r2[0:small, :], r13[small:, :])):
        rows = aligned(outer ^ s, small)
        product = keep[rows, :].astype(F32) + arrived[rows, :].astype(F32)
        block_ref[rows, :] = (r.astype(F32) + product).astype(BF16)
    block_ref[count:, :] = share[...]


def piece_kernel(starts, weights, *refs):
    *outs, semaphores = refs
    copies = []
    at = 0
    for k, out in enumerate(outs):
        depth, width = out.shape[0], out.shape[1] // 2
        for i in range(2):
            copies.append(
                pltpu.make_async_copy(
                    weights.at[pl.ds(at, depth), pl.ds(starts[i], width)],
                    out.at[:, pl.ds(i * width, width)],
                    semaphores.at[i, k],
                )
            )
        at += depth
    for copy in copies:
        copy.start()
    for copy in copies:
        copy.wait()


def swiglu(gate, up, share):
    return (gate / (1.0 + jnp.exp(-gate)) * up * share).astype(BF16)


def norm_kernel(b0, b1, b2, b3, gain, group_ref, own_ref):
    expert, outer, inner, dp = seat()
    count = group_ref.shape[0]
    width = b0.shape[1]
    experts = b0.shape[0] - count
    small = own_ref.shape[0]
    square = jnp.zeros((count, 1), F32)
    share = jnp.zeros((experts, count), F32)
    for s, b in enumerate((b0, b1, b2, b3)):
        value = b[0:count, :]
        group_ref[:, aligned((outer + 4 - s) & 3, width)] = value
        value = value.astype(F32)
        square = square + jnp.sum(value * value, axis=1, keepdims=True)
        share = share + b[count : count + experts, 0:count].astype(F32)
    own_ref[...] = group_ref[aligned(outer, small), 0 : 4 * width]
    scale = lax.rsqrt(square / (4 * width) + 1e-06)
    for s in range(4):
        cols = slice(s * width, (s + 1) * width)
        value = group_ref[:, cols].astype(F32)
        group_ref[:, cols] = (value * scale * gain[:, cols]).astype(BF16)
    lanes = (experts, 128)
    spread = lax.broadcasted_iota(jnp.int32, lanes, 0) == lax.broadcasted_iota(jnp.int32, lanes, 1)
    group_ref[:, 4 * width :] = lax.dot_general(
        share.astype(BF16),
        spread.astype(F32).astype(BF16),
        (((0,), (0,)), ((), ())),
        preferred_element_type=F32,
    ).astype(BF16)


def first_gate_kernel(
    group_x, group_cx, group, group_c, own, early,
    first_ref, second_ref, part_ref, other_ref, share_ref, mine_ref,
):
    expert, outer, inner, dp = seat()
    count = group.shape[0]
    half = other_ref.shape[1]
    cut = first_ref.shape[1]
    for j, g in enumerate((group_x, group_cx, group, group_c)):
        rows = slice(j * count, (j + 1) * count)
        mine_ref[rows, :] = g[:, aligned(dp, half)]
        other_ref[rows, :] = g[:, aligned(1 - dp, half)]
        share = g[:, 2 * half : 2 * half + 128].astype(F32)
        picked = lax.broadcasted_iota(jnp.int32, share.shape, 1) == expert
        share = jnp.sum(jnp.where(picked, share, 0.0), axis=1, keepdims=True)
        share_ref[rows, :] = jnp.broadcast_to(share, (count, 128))
    mine, other = mine_ref[...], other_ref[...]
    gate = dot(mine, own[:, 0:cut]) + dot(other, early[:, 0:cut])
    up = dot(mine, own[:, 2 * cut : 3 * cut]) + dot(other, early[:, cut : 2 * cut])
    inner = swiglu(gate, up, share_ref[:, 0:1])
    first_ref[...] = inner[: 3 * count]
    second_ref[...] = inner[3 * count :]
    part_ref[:, 0:cut] = dot(mine, own[:, cut : 2 * cut])
    part_ref[:, cut : 2 * cut] = dot(mine, own[:, 3 * cut : 4 * cut])


def last_gate_kernel(second, part, other, share, *refs):
    *late, far_ref, rest_ref = refs
    count, cut = second.shape
    gate, up = part[:, 0:cut], part[:, cut : 2 * cut]
    at = 0
    for piece in late:
        rows = other[:, at : at + piece.shape[0]]
        gate = gate + dot(rows, piece[:, 0:cut])
        up = up + dot(rows, piece[:, cut : 2 * cut])
        at += piece.shape[0]
    value = swiglu(gate, up, share[:, 0:1])
    far_ref[...] = value[: 2 * count]
    rest_ref[0:count, :] = second[...]
    rest_ref[count:, :] = value[2 * count :]


def down_rows(pieces, wd, keep_ref, sends, rows):
    expert, outer, inner, dp = seat()
    core = inner & 1
    count, side = sends[0].shape
    small = count // 4
    for h, places in enumerate(pieces):
        cut = places[0][0].shape[1]
        cols = slice(h * cut, (h + 1) * cut)
        for i in range(2):
            for j in range(2):
                ref, start = places[j]
                kept = aligned(start // small + ((outer + 2 * core + 1 - i) & 3), small)
                at = (2 * i + j) * small
                rows[at : at + small, cols] = ref[kept, :]
                ref, start = places[1 - j]
                sent = aligned(start // small + ((outer + 3 - 2 * core - i) & 3), small)
                rows[count + at : count + at + small, cols] = ref[sent, :]
    for at in range(0, wd.shape[1], 256):
        value = dot(rows[...], wd[:, at : at + 256]).astype(BF16)
        keep_ref[:, at : at + 256] = value[:count]
        sends[at // side][:, at % side : at % side + 256] = value[count:]


def far_places(first, far):
    count = far.shape[0] // 2
    return ((first, 0), (first, count)), ((far, 0), (far, count))


def near_places(first, rest):
    count = rest.shape[0] // 3
    return ((first, 2 * count), (rest, 0)), ((rest, count), (rest, 2 * count))


def down_both_kernel(first, far, rest, wd, keep_far, *refs):
    *sends, keep_near, rows = refs
    half = len(sends) // 2
    down_rows(far_places(first, far), wd, keep_far, sends[:half], rows)
    down_rows(near_places(first, rest), wd, keep_near, sends[half:], rows)


def down_far_kernel(first, far, wd, keep_ref, *refs):
    *sends, rows = refs
    down_rows(far_places(first, far), wd, keep_ref, sends, rows)


def down_near_kernel(first, rest, wd, keep_ref, *refs):
    *sends, rows = refs
    down_rows(near_places(first, rest), wd, keep_ref, sends, rows)


def added(keep, cores, cols):
    side = cores[0].shape[1]
    return keep[:, cols].astype(F32) + cores[cols.start // side][:, cols.start % side : cols.start % side + 256].astype(F32)


def fold_kernel(keep, *refs):
    *cores, out = refs
    for at in range(0, keep.shape[1], 256):
        cols = slice(at, at + 256)
        out[:, cols] = added(keep, cores, cols).astype(BF16)


def pieces_kernel(far, keep, *refs):
    *cores, first, second = refs
    half = first.shape[0]
    for at in range(0, keep.shape[1], 256):
        cols = slice(at, at + 256)
        total = (added(keep, cores, cols) + far[:, cols].astype(F32)).astype(BF16)
        first[:, cols] = total[:half]
        second[:, cols] = total[half:]


def gather_kernel(own, a0, a1, b0, b1, keep_ref, send_ref):
    expert, outer, inner, dp = seat()
    small = own.shape[0] // 2
    last = jnp.where((inner & 1) == 0, own[...].astype(F32), a1[...].astype(F32))
    for i, total in enumerate((a0[...].astype(F32) + last, b0[...].astype(F32) + b1[...].astype(F32))):
        rows = slice(i * small, (i + 1) * small)
        keep_ref[rows, :] = total[:small]
        send_ref[rows, :] = total[small:].astype(BF16)


def tail_kernel(own, keep, core, gain, stream_ref, normed_ref):
    expert, outer, inner, dp = seat()
    small, half = own.shape[0], keep.shape[1]
    for i, at in enumerate((dp, 1 - dp)):
        rows = slice(i * small, (i + 1) * small)
        cols = aligned(at, half)
        mixture = keep[rows, :] + core[rows, :].astype(F32)
        stream_ref[:, cols] = (own[:, cols].astype(F32) + mixture).astype(BF16)
    normed_ref[...] = rms_scale(stream_ref[...].astype(F32), gain[...]).astype(BF16)


def body_paired(
    attn,
    resid,
    w_out,
    gain_post,
    route_ids,
    route_logits,
    live_count,
    w_gate_up,
    w_down,
    gain_final,
):
    rows_here = resid.shape[1]
    model_width = resid.shape[2]
    expert_count = lax.axis_size("expert")
    hidden = w_down.shape[1]
    half_width = w_down.shape[2]
    quarter = model_width // 4
    vmem, smem = whole_vmem(), whole_smem()

    def shape_of(*shape, dtype=BF16):
        return jax.ShapeDtypeStruct(shape, dtype)

    def call(kernel, name, mib, outs, *args, scratch=(), first=vmem):
        return pl.pallas_call(
            kernel,
            out_shape=outs,
            in_specs=[first] + [vmem] * (len(args) - 1),
            out_specs=tuple(vmem for _ in outs),
            scratch_shapes=list(scratch),
            compiler_params=kernel_params(mib),
            cost_estimate=small_cost(),
            name=name,
        )(*args)

    def swap_dp(x):
        return lax.ppermute(x, "dp", [(0, 1), (1, 0)])

    def shift_outer(x, s):
        return lax.ppermute(
            x, "expert", [(i, (i + 4 * s) % expert_count) for i in range(expert_count)]
        )

    def send_outer(x, i, cross):
        pairs = []
        for at in range(2 * expert_count):
            d, e = divmod(at, expert_count)
            step = 2 * (e % 2) + 1 - i
            if step or cross:
                pairs.append((at, (d ^ cross) * expert_count + (e + 4 * step) % expert_count))
        return lax.ppermute(x, ("dp", "expert"), pairs)

    def swap_inner(x, j):
        return lax.ppermute(x, "expert", [(i, i ^ j) for i in range(expert_count)])

    def swap_outer(x, s):
        return lax.ppermute(x, "expert", [(i, i ^ (4 * s)) for i in range(expert_count)])

    def after(x, *results):
        return lax.optimization_barrier((x, *results))[0]

    def weight_piece(first, size, depths):
        return pl.pallas_call(
            functools.partial(piece_kernel, (first, hidden + first)),
            out_shape=tuple(shape_of(depth, 2 * size) for depth in depths),
            in_specs=[pl.BlockSpec(memory_space=pl.ANY)],
            out_specs=tuple(vmem for _ in depths),
            scratch_shapes=[pltpu.SemaphoreType.DMA((2, len(depths)))],
            compiler_params=kernel_params(8),
            cost_estimate=small_cost(),
            name="weight_piece",
        )(w_gate_up[0])

    piece = shape_of(rows_here, quarter)
    r_own, r_1, r_23 = call(
        cut_kernel, "cut_resid", 4, (piece, piece, shape_of(2 * rows_here, quarter)), resid[0]
    )
    (share,) = call(
        share_kernel,
        "share",
        4,
        (shape_of(expert_count, quarter),),
        live_count,
        route_ids[0],
        route_logits[0],
        first=smem,
    )
    cut_width = hidden // 2
    early_piece = weight_piece(0, cut_width, (half_width,))[0]
    late_pieces = weight_piece(cut_width, cut_width, (half_width * 640 // 1024, half_width * 384 // 1024))
    gate_up_early = swap_dp(early_piece)
    a = [attn[0], swap_outer(attn[0], 1), swap_outer(attn[0], 2)]
    w_x = swap_inner(w_out, 2)
    r_2 = swap_outer(r_23, 2)
    a.append(swap_outer(after(a[2], a[1], r_2), 1))
    w_c = swap_inner(after(w_out, w_x, share, *late_pieces), 1)
    w_cx = swap_inner(w_x, 1)
    r_13 = swap_outer(jnp.concatenate([r_1, r_2[rows_here:]], axis=0), 1)

    product = shape_of(4 * rows_here, quarter)
    keep, send = call(
        proj_kernel,
        "projection",
        8,
        (product, product),
        *a[:3],
        after(a[3], r_13),
        w_out,
        w_c,
        w_x,
        w_cx,
        scratch=(
            pltpu.VMEM((8 * rows_here, attn.shape[2]), BF16),
            pltpu.VMEM((8 * rows_here, quarter), BF16),
        ),
    )
    arrived = swap_dp(send)
    gate_up_late = [swap_dp(after(piece, send)) for piece in late_pieces]
    (block,) = call(
        stream_kernel,
        "stream",
        4,
        (shape_of(4 * rows_here + expert_count, quarter),),
        after(keep, gate_up_early),
        arrived,
        r_own,
        r_13,
        r_2,
        share,
    )

    def norm(b0, b1, b2, b3):
        outs = (shape_of(4 * rows_here, model_width + 128), shape_of(rows_here, model_width))
        return call(norm_kernel, "norm", 8, outs, b0, b1, b2, b3, gain_post[None])

    blocks = [block] + [shift_outer(block, s) for s in (1, 2, 3)]
    group, stream_own = norm(*blocks)
    blocks_x = [swap_inner(b, 2) for b in blocks]
    group_x, unused = norm(*blocks_x)
    group_c = swap_inner(group, 1)
    group_cx = swap_inner(group_x, 1)

    row_total = 16 * rows_here
    half_rows = row_total // 2
    inner_first, inner_second, part, other_rows, share_rows = call(
        first_gate_kernel,
        "first_gate_up",
        24,
        (
            shape_of(row_total * 3 // 4, cut_width),
            shape_of(row_total // 4, cut_width),
            shape_of(row_total, hidden, dtype=F32),
            shape_of(row_total, half_width),
            shape_of(row_total, 128, dtype=F32),
        ),
        group_x,
        group_cx,
        group,
        group_c,
        w_gate_up[0],
        gate_up_early,
        scratch=(pltpu.VMEM((row_total, half_width), BF16),),
    )
    inner_far, inner_rest = call(
        last_gate_kernel,
        "last_gate_up",
        16,
        (shape_of(half_rows, cut_width), shape_of(row_total * 3 // 4, cut_width)),
        inner_second,
        part,
        other_rows,
        share_rows,
        *gate_up_late,
    )
    first_other = swap_dp(inner_first)
    far_other = swap_dp(inner_far)
    rest_other = swap_dp(inner_rest)

    count = row_total // 4
    quarter_out = shape_of(count, half_width)

    def parts_of(many):
        return (shape_of(count, half_width // many),) * many

    scratch = (pltpu.VMEM((half_rows, hidden), BF16),)

    def down(kernel, rows, many):
        keep, *send = call(
            kernel, "down", 12, (quarter_out, *parts_of(many)), first_other, rows, w_down[0], scratch=scratch
        )
        return keep, send

    def swap_cores(halves):
        return [swap_inner(half, 1) for half in halves]

    def fold(keep, halves):
        return call(fold_kernel, "fold", 4, (quarter_out,), keep, *halves)[0]

    def pieces(far, keep, send):
        outs = (shape_of(2 * rows_here, half_width),) * 2
        return call(pieces_kernel, "pieces", 4, outs, far, keep, *swap_cores(send))

    outs = (quarter_out, *parts_of(2), *parts_of(2), quarter_out)
    keep_far, *send, keep_near = call(
        down_both_kernel, "down_both", 16, outs, inner_first, inner_far, inner_rest, w_down[0], scratch=scratch
    )
    far = swap_inner(fold(keep_far, swap_cores(send[:2])), 2)
    first_far = far
    first, own = pieces(far, keep_near, send[2:])
    mine = [send_outer(first, 0, False), send_outer(own, 1, False)]

    keep_far, send = down(down_far_kernel, far_other, 2)
    far = swap_inner(fold(after(keep_far, own), swap_cores(send)), 2)
    keep_near, send = down(down_near_kernel, rest_other, 2)
    cut = pieces(far, after(keep_near, *mine), send)
    others = [send_outer(cut[i], i, True) for i in range(2)]

    sums = shape_of(2 * rows_here, half_width)
    keep, send = call(
        gather_kernel,
        "gather",
        4,
        (shape_of(2 * rows_here, half_width, dtype=F32), sums),
        own,
        *mine,
        *others,
    )
    out = shape_of(rows_here, model_width)
    stream_out, normed_out = call(
        tail_kernel, "closing", 8, (out, out), stream_own, keep, swap_inner(send, 1), gain_final[None]
    )
    return (stream_out[None], normed_out[None])


def solution(mesh):
    placed = (
        P("expert", None, "dp"),
        P("expert", "dp", None),
        P("dp", "expert"),
        P(),
        P("expert", "dp", None),
        P("expert", "dp", None),
        P("expert", "dp"),
        P("expert", "dp", None),
        P("expert", None, "dp"),
        P(),
    )
    paired = mesh.shape["dp"] == 2 and mesh.shape["expert"] == 16
    return jax.shard_map(
        body_paired if paired else body_general,
        mesh=mesh,
        in_specs=placed,
        out_specs=(P("expert", "dp", None), P("expert", "dp", None)),
        check_vma=False,
    )
```

```python
import functools
import math

import jax
import jax.numpy as jnp
from jax import lax
from jax.experimental import pallas as pl
from jax.experimental.pallas import tpu as pltpu
from jax.sharding import PartitionSpec as P


def rms_scale(values, gain):
    return values * lax.rsqrt(jnp.mean(values * values, axis=-1, keepdims=True) + 1e-06) * gain


def swiglu_rows(rows_in, gate_up, down, hidden_units):
    both = jnp.dot(rows_in, gate_up, preferred_element_type=jnp.float32)
    inner = (jax.nn.silu(both[:, :hidden_units]) * both[:, hidden_units:]).astype(jnp.bfloat16)
    return jnp.dot(inner, down, preferred_element_type=jnp.float32).astype(jnp.bfloat16)


def body_general(
    attn,
    resid,
    w_out,
    gain_post,
    route_ids,
    route_logits,
    live_count,
    w_gate_up,
    w_down,
    gain_final,
):
    rows_here = resid.shape[1]
    model_width = resid.shape[2]
    top_count = route_ids.shape[2]
    dp_count = lax.axis_size("dp")
    expert_count = lax.axis_size("expert")
    hidden_units = w_down.shape[1]
    capacity = dp_count * max(1, 2 * rows_here * top_count // (expert_count * dp_count))
    slot_count = expert_count * capacity
    flat_attn = attn[0]
    partial_out = jnp.dot(
        flat_attn,
        lax.all_gather(w_out, "expert", axis=1, tiled=True),
        preferred_element_type=jnp.float32,
    )
    projected = lax.psum_scatter(
        partial_out.astype(jnp.bfloat16), "dp", scatter_dimension=0, tiled=True
    ).astype(jnp.float32)
    stream_in = (resid[0].astype(jnp.float32) + projected).astype(jnp.bfloat16)
    stream_float = stream_in.astype(jnp.float32)
    normed_in = rms_scale(stream_float, gain_post).astype(jnp.bfloat16)
    probs = jax.nn.softmax(route_logits[0], axis=-1).astype(jnp.bfloat16)
    alive = jnp.arange(rows_here, dtype=jnp.int32) < live_count[0, 0]
    expert_of = route_ids[0].reshape(-1)
    route_alive = jnp.repeat(alive, top_count)
    onehot = (
        (expert_of[:, None] == jnp.arange(expert_count, dtype=jnp.int32)[None, :])
        & route_alive[:, None]
    ).astype(jnp.int32)
    earlier = jnp.sum((jnp.cumsum(onehot, axis=0) - onehot) * onehot, axis=1)
    target = expert_of * capacity + earlier
    match = (target[:, None] == jnp.arange(slot_count, dtype=jnp.int32)[None, :]) & route_alive[
        :, None
    ]
    placed = match.reshape(rows_here, top_count, slot_count)
    gather_matrix = jnp.any(placed, axis=1).astype(jnp.bfloat16)
    send_rows = lax.dot_general(
        gather_matrix, normed_in, (((0,), (0,)), ((), ())), preferred_element_type=jnp.float32
    ).astype(jnp.bfloat16)
    send_flags = jnp.sum(gather_matrix.astype(jnp.float32), axis=0).astype(jnp.bfloat16)
    combine_matrix = jnp.sum(
        jnp.where(placed, probs.astype(jnp.float32)[:, :, None], jnp.float32(0.0)), axis=1
    ).astype(jnp.bfloat16)
    arrived_rows, arrived_flags = (
        lax.all_to_all(
            send_rows.reshape(expert_count, capacity, model_width),
            "expert",
            split_axis=0,
            concat_axis=0,
            tiled=True,
        ),
        lax.all_to_all(
            send_flags.reshape(expert_count, capacity),
            "expert",
            split_axis=0,
            concat_axis=0,
            tiled=True,
        ),
    )
    arrived = arrived_rows.reshape(slot_count, model_width)
    flags = arrived_flags.reshape(slot_count)
    gate_up_full, down_full = (
        lax.all_gather(w_gate_up, "dp", axis=1, tiled=True),
        lax.all_gather(w_down, "dp", axis=2, tiled=True),
    )
    live_slot = (flags > 0.5).astype(jnp.int32)
    order = jnp.argsort(1 - live_slot, stable=True)
    live_total = jnp.sum(live_slot)
    packed = arrived[order]
    block_len = math.gcd(slot_count, 128)
    block_total = (live_total + block_len - 1) // block_len

    def run_block(index, outputs):
        begin = index * block_len
        rows_in = lax.dynamic_slice_in_dim(packed, begin, block_len, 0)
        block_out = swiglu_rows(rows_in, gate_up_full[0], down_full[0], hidden_units)
        return lax.dynamic_update_slice_in_dim(outputs, block_out, begin, 0)

    packed_out = lax.fori_loop(
        0, block_total, run_block, jnp.zeros((slot_count, model_width), jnp.bfloat16)
    )
    position = (
        jnp.zeros((slot_count,), jnp.int32).at[order].set(jnp.arange(slot_count, dtype=jnp.int32))
    )
    results = packed_out[position]
    returned = lax.all_to_all(
        results.reshape(expert_count, capacity, model_width),
        "expert",
        split_axis=0,
        concat_axis=0,
        tiled=True,
    )
    returned = returned.reshape(slot_count, model_width)
    mixture = jnp.dot(combine_matrix, returned, preferred_element_type=jnp.float32)
    stream_out = (stream_float + mixture).astype(jnp.bfloat16)
    normed_out = rms_scale(stream_out.astype(jnp.float32), gain_final).astype(jnp.bfloat16)
    return (stream_out[None], normed_out[None])


MIB = 1024 * 1024
BF16, F32 = jnp.bfloat16, jnp.float32


def whole_vmem():
    return pl.BlockSpec(memory_space=pltpu.VMEM)


def whole_smem():
    return pl.BlockSpec(memory_space=pltpu.SMEM)


def fixed(*shape):
    return pl.BlockSpec(shape, lambda i: (0,) * len(shape))


def dot(a, b):
    return jnp.dot(a, b, preferred_element_type=F32)


def small_cost():
    return pl.CostEstimate(flops=1, bytes_accessed=1, transcendentals=0)


def kernel_params(mib):
    return pltpu.CompilerParams(vmem_limit_bytes=mib * MIB)


def seat():
    expert = lax.axis_index("expert")
    return expert, lax.shift_right_logical(expert, 2), expert & 3, lax.axis_index("dp")


def aligned(index, step):
    return pl.ds(pl.multiple_of(index * step, step), step)


def cut_kernel(resid, r0, r1, r23):
    expert, outer, inner, dp = seat()
    rows, lanes = r0.shape
    r0[...] = resid[:, aligned(outer, lanes)]
    r1[...] = resid[:, aligned(outer ^ 1, lanes)]
    for i in range(2):
        r23[i * rows : (i + 1) * rows, :] = resid[:, aligned(outer ^ (2 + i), lanes)]


def share_kernel(live, ids, logits, share_ref):
    expert, outer, inner, dp = seat()
    rows, top = ids.shape
    experts, lanes = share_ref.shape
    value = logits[...]
    value = jnp.exp(value - jnp.max(value, axis=1, keepdims=True))
    probs = (value / jnp.sum(value, axis=1, keepdims=True)).astype(BF16).astype(F32)
    probs = jnp.where(lax.broadcasted_iota(jnp.int32, (rows, top), 0) < live[0, 0], probs, 0.0)
    names = lax.broadcasted_iota(jnp.int32, (rows, experts), 1)
    table = jnp.zeros((rows, experts), F32)
    for k in range(top):
        table = table + jnp.where(ids[:, k : k + 1] == names, probs[:, k : k + 1], 0.0)
    spots = lax.broadcasted_iota(jnp.int32, (rows, lanes), 1) - outer * rows
    spots = (spots == lax.broadcasted_iota(jnp.int32, (rows, lanes), 0)).astype(F32).astype(BF16)
    share_ref[...] = lax.dot_general(
        table.astype(BF16), spots, (((0,), (0,)), ((), ())), preferred_element_type=F32
    ).astype(BF16)


def proj_kernel(a0, a1, a2, a3, w0, w1, w2, w3, keep_ref, send_ref, rows, part):
    expert, outer, inner, dp = seat()
    full = a0.shape[0]
    half = full // 2
    block = w0.shape[1]
    for s, a in enumerate((a0, a1, a2, a3)):
        rows[aligned(outer ^ s, full), :] = a[...]
    for j, w in enumerate((w0, w1, w2, w3)):
        part[:, aligned(inner ^ j, block)] = dot(rows[...], w[...]).astype(BF16)
    for spot in range(4):
        keep_ref[spot * half : (spot + 1) * half, :] = part[aligned(2 * spot + dp, half), :]
        send_ref[spot * half : (spot + 1) * half, :] = part[aligned(2 * spot + 1 - dp, half), :]


def stream_kernel(keep, arrived, r0, r13, r2, share, block_ref):
    expert, outer, inner, dp = seat()
    count = keep.shape[0]
    small = r0.shape[0]
    for s, r in enumerate((r0[...], r13[0:small, :], r2[0:small, :], r13[small:, :])):
        rows = aligned(outer ^ s, small)
        product = keep[rows, :].astype(F32) + arrived[rows, :].astype(F32)
        block_ref[rows, :] = (r.astype(F32) + product).astype(BF16)
    block_ref[count:, :] = share[...]


def piece_kernel(starts, weights, *refs):
    *outs, semaphores = refs
    copies = []
    at = 0
    for k, out in enumerate(outs):
        depth, width = out.shape[0], out.shape[1] // 2
        for i in range(2):
            copies.append(
                pltpu.make_async_copy(
                    weights.at[pl.ds(at, depth), pl.ds(starts[i], width)],
                    out.at[:, pl.ds(i * width, width)],
                    semaphores.at[i, k],
                )
            )
        at += depth
    for copy in copies:
        copy.start()
    for copy in copies:
        copy.wait()


def swiglu(gate, up, share):
    return (gate / (1.0 + jnp.exp(-gate)) * up * share).astype(BF16)


def norm_kernel(b0, b1, b2, b3, gain, group_ref, own_ref):
    expert, outer, inner, dp = seat()
    count = group_ref.shape[0]
    width = b0.shape[1]
    experts = b0.shape[0] - count
    small = own_ref.shape[0]
    square = jnp.zeros((count, 1), F32)
    share = jnp.zeros((experts, count), F32)
    for s, b in enumerate((b0, b1, b2, b3)):
        value = b[0:count, :]
        group_ref[:, aligned((outer + 4 - s) & 3, width)] = value
        value = value.astype(F32)
        square = square + jnp.sum(value * value, axis=1, keepdims=True)
        share = share + b[count : count + experts, 0:count].astype(F32)
    own_ref[...] = group_ref[aligned(outer, small), 0 : 4 * width]
    scale = lax.rsqrt(square / (4 * width) + 1e-06)
    for s in range(4):
        cols = slice(s * width, (s + 1) * width)
        value = group_ref[:, cols].astype(F32)
        group_ref[:, cols] = (value * scale * gain[:, cols]).astype(BF16)
    lanes = (experts, 128)
    spread = lax.broadcasted_iota(jnp.int32, lanes, 0) == lax.broadcasted_iota(jnp.int32, lanes, 1)
    group_ref[:, 4 * width :] = lax.dot_general(
        share.astype(BF16),
        spread.astype(F32).astype(BF16),
        (((0,), (0,)), ((), ())),
        preferred_element_type=F32,
    ).astype(BF16)


def first_gate_kernel(
    group_x, group_cx, group, group_c, own, early,
    first_ref, second_ref, part_ref, other_ref, share_ref, mine_ref,
):
    expert, outer, inner, dp = seat()
    count = group.shape[0]
    half = other_ref.shape[1]
    cut = first_ref.shape[1]
    for j, g in enumerate((group_x, group_cx, group, group_c)):
        rows = slice(j * count, (j + 1) * count)
        mine_ref[rows, :] = g[:, aligned(dp, half)]
        other_ref[rows, :] = g[:, aligned(1 - dp, half)]
        share = g[:, 2 * half : 2 * half + 128].astype(F32)
        picked = lax.broadcasted_iota(jnp.int32, share.shape, 1) == expert
        share = jnp.sum(jnp.where(picked, share, 0.0), axis=1, keepdims=True)
        share_ref[rows, :] = jnp.broadcast_to(share, (count, 128))
    mine, other = mine_ref[...], other_ref[...]
    gate = dot(mine, own[:, 0:cut]) + dot(other, early[:, 0:cut])
    up = dot(mine, own[:, 2 * cut : 3 * cut]) + dot(other, early[:, cut : 2 * cut])
    inner = swiglu(gate, up, share_ref[:, 0:1])
    first_ref[...] = inner[: 3 * count]
    second_ref[...] = inner[3 * count :]
    part_ref[:, 0:cut] = dot(mine, own[:, cut : 2 * cut])
    part_ref[:, cut : 2 * cut] = dot(mine, own[:, 3 * cut : 4 * cut])


def last_gate_kernel(second, part, other, share, *refs):
    *late, far_ref, rest_ref = refs
    count, cut = second.shape
    gate, up = part[:, 0:cut], part[:, cut : 2 * cut]
    at = 0
    for piece in late:
        rows = other[:, at : at + piece.shape[0]]
        gate = gate + dot(rows, piece[:, 0:cut])
        up = up + dot(rows, piece[:, cut : 2 * cut])
        at += piece.shape[0]
    value = swiglu(gate, up, share[:, 0:1])
    far_ref[...] = value[: 2 * count]
    rest_ref[0:count, :] = second[...]
    rest_ref[count:, :] = value[2 * count :]


def down_rows(pieces, wd, keep_ref, sends, rows):
    expert, outer, inner, dp = seat()
    core = inner & 1
    count, side = sends[0].shape
    small = count // 4
    for h, places in enumerate(pieces):
        cut = places[0][0].shape[1]
        cols = slice(h * cut, (h + 1) * cut)
        for i in range(2):
            for j in range(2):
                ref, start = places[j]
                kept = aligned(start // small + ((outer + 2 * core + i) & 3), small)
                at = (2 * i + j) * small
                rows[at : at + small, cols] = ref[kept, :]
                ref, start = places[1 - j]
                sent = aligned(start // small + ((outer + 2 - 2 * core + i) & 3), small)
                rows[count + at : count + at + small, cols] = ref[sent, :]
    for at in range(0, wd.shape[1], 256):
        value = dot(rows[...], wd[:, at : at + 256]).astype(BF16)
        keep_ref[:, at : at + 256] = value[:count]
        sends[at // side][:, at % side : at % side + 256] = value[count:]


def far_places(first, far):
    count = far.shape[0] // 2
    return ((first, 0), (first, count)), ((far, 0), (far, count))


def near_places(first, rest):
    count = rest.shape[0] // 3
    return ((first, 2 * count), (rest, 0)), ((rest, count), (rest, 2 * count))


def down_both_kernel(first, far, rest, wd, keep_far, *refs):
    *sends, keep_near, rows = refs
    half = len(sends) // 2
    down_rows(far_places(first, far), wd, keep_far, sends[:half], rows)
    down_rows(near_places(first, rest), wd, keep_near, sends[half:], rows)


def down_far_kernel(first, far, wd, keep_ref, *refs):
    *sends, rows = refs
    down_rows(far_places(first, far), wd, keep_ref, sends, rows)


def down_near_kernel(first, rest, wd, keep_ref, *refs):
    *sends, rows = refs
    down_rows(near_places(first, rest), wd, keep_ref, sends, rows)


def added(keep, cores, cols):
    side = cores[0].shape[1]
    return keep[:, cols].astype(F32) + cores[cols.start // side][:, cols.start % side : cols.start % side + 256].astype(F32)


def fold_kernel(keep, *refs):
    *cores, out = refs
    for at in range(0, keep.shape[1], 256):
        cols = slice(at, at + 256)
        out[:, cols] = added(keep, cores, cols).astype(BF16)


def pieces_kernel(far, keep, *refs):
    *cores, first, second = refs
    half = first.shape[0]
    for at in range(0, keep.shape[1], 256):
        cols = slice(at, at + 256)
        total = (added(keep, cores, cols) + far[:, cols].astype(F32)).astype(BF16)
        first[:, cols] = total[:half]
        second[:, cols] = total[half:]


def messages_kernel(keep_far, keep_near, *refs):
    *cores, first, second = refs
    half = first.shape[0] // 2
    parts = len(cores) // 2
    for h, (keep, core) in enumerate(((keep_far, cores[:parts]), (keep_near, cores[parts:]))):
        for at in range(0, keep.shape[1], 256):
            cols = slice(at, at + 256)
            total = added(keep, core, cols).astype(BF16)
            first[h * half : (h + 1) * half, cols] = total[:half]
            second[h * half : (h + 1) * half, cols] = total[half:]


def outer_sum_kernel(own, a0, a1, far_ref, near_ref):
    expert, outer, inner, dp = seat()
    half = far_ref.shape[0]
    total = jnp.where((inner & 1) == 0, own[...].astype(F32), a0[...].astype(F32)) + a1[...].astype(F32)
    far_ref[...] = total[:half].astype(BF16)
    near_ref[...] = total[half:]


def gather_kernel(near, far, b0, b1, keep_ref, send_ref):
    small = near.shape[0] // 2
    for i, total in enumerate(
        (near[...] + far[...].astype(F32), b0[...].astype(F32) + b1[...].astype(F32))
    ):
        rows = slice(i * small, (i + 1) * small)
        keep_ref[rows, :] = total[:small]
        send_ref[rows, :] = total[small:].astype(BF16)


def tail_kernel(own, keep, core, gain, stream_ref, normed_ref):
    expert, outer, inner, dp = seat()
    small, half = own.shape[0], keep.shape[1]
    for i, at in enumerate((dp, 1 - dp)):
        rows = slice(i * small, (i + 1) * small)
        cols = aligned(at, half)
        mixture = keep[rows, :] + core[rows, :].astype(F32)
        stream_ref[:, cols] = (own[:, cols].astype(F32) + mixture).astype(BF16)
    normed_ref[...] = rms_scale(stream_ref[...].astype(F32), gain[...]).astype(BF16)


def body_paired(
    attn,
    resid,
    w_out,
    gain_post,
    route_ids,
    route_logits,
    live_count,
    w_gate_up,
    w_down,
    gain_final,
):
    rows_here = resid.shape[1]
    model_width = resid.shape[2]
    expert_count = lax.axis_size("expert")
    hidden = w_down.shape[1]
    half_width = w_down.shape[2]
    quarter = model_width // 4
    vmem, smem = whole_vmem(), whole_smem()

    def shape_of(*shape, dtype=BF16):
        return jax.ShapeDtypeStruct(shape, dtype)

    def call(kernel, name, mib, outs, *args, scratch=(), first=vmem):
        return pl.pallas_call(
            kernel,
            out_shape=outs,
            in_specs=[first] + [vmem] * (len(args) - 1),
            out_specs=tuple(vmem for _ in outs),
            scratch_shapes=list(scratch),
            compiler_params=kernel_params(mib),
            cost_estimate=small_cost(),
            name=name,
        )(*args)

    def swap_dp(x):
        return lax.ppermute(x, "dp", [(0, 1), (1, 0)])

    def shift_outer(x, s):
        return lax.ppermute(
            x, "expert", [(i, (i + 4 * s) % expert_count) for i in range(expert_count)]
        )

    def send_outer(x, i, cross):
        pairs = []
        for at in range(2 * expert_count):
            d, e = divmod(at, expert_count)
            step = 2 * (e % 2) + i
            if step or cross:
                pairs.append((at, (d ^ cross) * expert_count + (e + 4 * step) % expert_count))
        return lax.ppermute(x, ("dp", "expert"), pairs)

    def swap_inner(x, j):
        return lax.ppermute(x, "expert", [(i, i ^ j) for i in range(expert_count)])

    def swap_outer(x, s):
        return lax.ppermute(x, "expert", [(i, i ^ (4 * s)) for i in range(expert_count)])

    def after(x, *results):
        return lax.optimization_barrier((x, *results))[0]

    def weight_piece(first, size, depths):
        return pl.pallas_call(
            functools.partial(piece_kernel, (first, hidden + first)),
            out_shape=tuple(shape_of(depth, 2 * size) for depth in depths),
            in_specs=[pl.BlockSpec(memory_space=pl.ANY)],
            out_specs=tuple(vmem for _ in depths),
            scratch_shapes=[pltpu.SemaphoreType.DMA((2, len(depths)))],
            compiler_params=kernel_params(8),
            cost_estimate=small_cost(),
            name="weight_piece",
        )(w_gate_up[0])

    piece = shape_of(rows_here, quarter)
    r_own, r_1, r_23 = call(
        cut_kernel, "cut_resid", 4, (piece, piece, shape_of(2 * rows_here, quarter)), resid[0]
    )
    (share,) = call(
        share_kernel,
        "share",
        4,
        (shape_of(expert_count, quarter),),
        live_count,
        route_ids[0],
        route_logits[0],
        first=smem,
    )
    cut_width = hidden // 2
    early_piece = weight_piece(0, cut_width, (half_width,))[0]
    late_pieces = weight_piece(cut_width, cut_width, (half_width * 640 // 1024, half_width * 384 // 1024))
    gate_up_early = swap_dp(early_piece)
    a = [attn[0], swap_outer(attn[0], 1), swap_outer(attn[0], 2)]
    w_x = swap_inner(w_out, 2)
    r_2 = swap_outer(r_23, 2)
    a.append(swap_outer(after(a[2], a[1], r_2), 1))
    w_c = swap_inner(after(w_out, w_x, share, *late_pieces), 1)
    w_cx = swap_inner(w_x, 1)
    r_13 = swap_outer(jnp.concatenate([r_1, r_2[rows_here:]], axis=0), 1)

    product = shape_of(4 * rows_here, quarter)
    keep, send = call(
        proj_kernel,
        "projection",
        8,
        (product, product),
        *a[:3],
        after(a[3], r_13),
        w_out,
        w_c,
        w_x,
        w_cx,
        scratch=(
            pltpu.VMEM((8 * rows_here, attn.shape[2]), BF16),
            pltpu.VMEM((8 * rows_here, quarter), BF16),
        ),
    )
    arrived = swap_dp(send)
    gate_up_late = [swap_dp(after(piece, send)) for piece in late_pieces]
    (block,) = call(
        stream_kernel,
        "stream",
        4,
        (shape_of(4 * rows_here + expert_count, quarter),),
        after(keep, gate_up_early),
        arrived,
        r_own,
        r_13,
        r_2,
        share,
    )

    def norm(b0, b1, b2, b3):
        outs = (shape_of(4 * rows_here, model_width + 128), shape_of(rows_here, model_width))
        return call(norm_kernel, "norm", 8, outs, b0, b1, b2, b3, gain_post[None])

    blocks = [block] + [shift_outer(block, s) for s in (1, 2, 3)]
    group, stream_own = norm(*blocks)
    blocks_x = [swap_inner(b, 2) for b in blocks]
    group_x, unused = norm(*blocks_x)
    group_c = swap_inner(group, 1)
    group_cx = swap_inner(group_x, 1)

    row_total = 16 * rows_here
    half_rows = row_total // 2
    inner_first, inner_second, part, other_rows, share_rows = call(
        first_gate_kernel,
        "first_gate_up",
        24,
        (
            shape_of(row_total * 3 // 4, cut_width),
            shape_of(row_total // 4, cut_width),
            shape_of(row_total, hidden, dtype=F32),
            shape_of(row_total, half_width),
            shape_of(row_total, 128, dtype=F32),
        ),
        group_x,
        group_cx,
        group,
        group_c,
        w_gate_up[0],
        gate_up_early,
        scratch=(pltpu.VMEM((row_total, half_width), BF16),),
    )
    inner_far, inner_rest = call(
        last_gate_kernel,
        "last_gate_up",
        16,
        (shape_of(half_rows, cut_width), shape_of(row_total * 3 // 4, cut_width)),
        inner_second,
        part,
        other_rows,
        share_rows,
        *gate_up_late,
    )
    first_other = swap_dp(inner_first)
    far_other = swap_dp(inner_far)
    rest_other = swap_dp(inner_rest)

    count = row_total // 4
    quarter_out = shape_of(count, half_width)

    def parts_of(many):
        return (shape_of(count, half_width // many),) * many

    scratch = (pltpu.VMEM((half_rows, hidden), BF16),)

    def down(kernel, rows, many):
        keep, *send = call(
            kernel, "down", 12, (quarter_out, *parts_of(many)), first_other, rows, w_down[0], scratch=scratch
        )
        return keep, send

    def swap_cores(halves):
        return [swap_inner(half, 1) for half in halves]

    def fold(keep, halves):
        return call(fold_kernel, "fold", 4, (quarter_out,), keep, *halves)[0]

    def pieces(far, keep, send):
        outs = (shape_of(2 * rows_here, half_width),) * 2
        return call(pieces_kernel, "pieces", 4, outs, far, keep, *swap_cores(send))

    outs = (quarter_out, *parts_of(2), *parts_of(2), quarter_out)
    keep_far, *send, keep_near = call(
        down_both_kernel, "down_both", 16, outs, inner_first, inner_far, inner_rest, w_down[0], scratch=scratch
    )
    message = shape_of(4 * rows_here, half_width)
    own, second = call(
        messages_kernel, "messages", 4, (message, message), keep_far, keep_near, *swap_cores(send)
    )
    half_message = shape_of(2 * rows_here, half_width)
    mine_far, mine_near = call(
        outer_sum_kernel,
        "outer_sum",
        4,
        (half_message, shape_of(2 * rows_here, half_width, dtype=F32)),
        own,
        send_outer(own, 0, False),
        send_outer(second, 1, False),
    )
    mine_far = swap_inner(mine_far, 2)

    keep_far, send = down(down_far_kernel, far_other, 2)
    far = swap_inner(fold(keep_far, swap_cores(send)), 2)
    keep_near, send = down(down_near_kernel, after(rest_other, mine_near), 2)
    cut = pieces(far, keep_near, send)
    others = [send_outer(cut[i], i, True) for i in range(2)]

    sums = shape_of(2 * rows_here, half_width)
    keep, send = call(
        gather_kernel,
        "gather",
        4,
        (shape_of(2 * rows_here, half_width, dtype=F32), sums),
        mine_near,
        mine_far,
        *others,
    )
    out = shape_of(rows_here, model_width)
    stream_out, normed_out = call(
        tail_kernel, "closing", 8, (out, out), stream_own, keep, swap_inner(send, 1), gain_final[None]
    )
    return (stream_out[None], normed_out[None])


def solution(mesh):
    placed = (
        P("expert", None, "dp"),
        P("expert", "dp", None),
        P("dp", "expert"),
        P(),
        P("expert", "dp", None),
        P("expert", "dp", None),
        P("expert", "dp"),
        P("expert", "dp", None),
        P("expert", None, "dp"),
        P(),
    )
    paired = mesh.shape["dp"] == 2 and mesh.shape["expert"] == 16
    return jax.shard_map(
        body_paired if paired else body_general,
        mesh=mesh,
        in_specs=placed,
        out_specs=(P("expert", "dp", None), P("expert", "dp", None)),
        check_vma=False,
    )
```

```python
import functools
import math

import jax
import jax.numpy as jnp
from jax import lax
from jax.experimental import pallas as pl
from jax.experimental.pallas import tpu as pltpu
from jax.sharding import PartitionSpec as P


def rms_scale(values, gain):
    return values * lax.rsqrt(jnp.mean(values * values, axis=-1, keepdims=True) + 1e-06) * gain


def swiglu_rows(rows_in, gate_up, down, hidden_units):
    both = jnp.dot(rows_in, gate_up, preferred_element_type=jnp.float32)
    inner = (jax.nn.silu(both[:, :hidden_units]) * both[:, hidden_units:]).astype(jnp.bfloat16)
    return jnp.dot(inner, down, preferred_element_type=jnp.float32).astype(jnp.bfloat16)


def body_general(
    attn,
    resid,
    w_out,
    gain_post,
    route_ids,
    route_logits,
    live_count,
    w_gate_up,
    w_down,
    gain_final,
):
    rows_here = resid.shape[1]
    model_width = resid.shape[2]
    top_count = route_ids.shape[2]
    dp_count = lax.axis_size("dp")
    expert_count = lax.axis_size("expert")
    hidden_units = w_down.shape[1]
    capacity = dp_count * max(1, 2 * rows_here * top_count // (expert_count * dp_count))
    slot_count = expert_count * capacity
    flat_attn = attn[0]
    partial_out = jnp.dot(
        flat_attn,
        lax.all_gather(w_out, "expert", axis=1, tiled=True),
        preferred_element_type=jnp.float32,
    )
    projected = lax.psum_scatter(
        partial_out.astype(jnp.bfloat16), "dp", scatter_dimension=0, tiled=True
    ).astype(jnp.float32)
    stream_in = (resid[0].astype(jnp.float32) + projected).astype(jnp.bfloat16)
    stream_float = stream_in.astype(jnp.float32)
    normed_in = rms_scale(stream_float, gain_post).astype(jnp.bfloat16)
    probs = jax.nn.softmax(route_logits[0], axis=-1).astype(jnp.bfloat16)
    alive = jnp.arange(rows_here, dtype=jnp.int32) < live_count[0, 0]
    expert_of = route_ids[0].reshape(-1)
    route_alive = jnp.repeat(alive, top_count)
    onehot = (
        (expert_of[:, None] == jnp.arange(expert_count, dtype=jnp.int32)[None, :])
        & route_alive[:, None]
    ).astype(jnp.int32)
    earlier = jnp.sum((jnp.cumsum(onehot, axis=0) - onehot) * onehot, axis=1)
    target = expert_of * capacity + earlier
    match = (target[:, None] == jnp.arange(slot_count, dtype=jnp.int32)[None, :]) & route_alive[
        :, None
    ]
    placed = match.reshape(rows_here, top_count, slot_count)
    gather_matrix = jnp.any(placed, axis=1).astype(jnp.bfloat16)
    send_rows = lax.dot_general(
        gather_matrix, normed_in, (((0,), (0,)), ((), ())), preferred_element_type=jnp.float32
    ).astype(jnp.bfloat16)
    send_flags = jnp.sum(gather_matrix.astype(jnp.float32), axis=0).astype(jnp.bfloat16)
    combine_matrix = jnp.sum(
        jnp.where(placed, probs.astype(jnp.float32)[:, :, None], jnp.float32(0.0)), axis=1
    ).astype(jnp.bfloat16)
    arrived_rows, arrived_flags = (
        lax.all_to_all(
            send_rows.reshape(expert_count, capacity, model_width),
            "expert",
            split_axis=0,
            concat_axis=0,
            tiled=True,
        ),
        lax.all_to_all(
            send_flags.reshape(expert_count, capacity),
            "expert",
            split_axis=0,
            concat_axis=0,
            tiled=True,
        ),
    )
    arrived = arrived_rows.reshape(slot_count, model_width)
    flags = arrived_flags.reshape(slot_count)
    gate_up_full, down_full = (
        lax.all_gather(w_gate_up, "dp", axis=1, tiled=True),
        lax.all_gather(w_down, "dp", axis=2, tiled=True),
    )
    live_slot = (flags > 0.5).astype(jnp.int32)
    order = jnp.argsort(1 - live_slot, stable=True)
    live_total = jnp.sum(live_slot)
    packed = arrived[order]
    block_len = math.gcd(slot_count, 128)
    block_total = (live_total + block_len - 1) // block_len

    def run_block(index, outputs):
        begin = index * block_len
        rows_in = lax.dynamic_slice_in_dim(packed, begin, block_len, 0)
        block_out = swiglu_rows(rows_in, gate_up_full[0], down_full[0], hidden_units)
        return lax.dynamic_update_slice_in_dim(outputs, block_out, begin, 0)

    packed_out = lax.fori_loop(
        0, block_total, run_block, jnp.zeros((slot_count, model_width), jnp.bfloat16)
    )
    position = (
        jnp.zeros((slot_count,), jnp.int32).at[order].set(jnp.arange(slot_count, dtype=jnp.int32))
    )
    results = packed_out[position]
    returned = lax.all_to_all(
        results.reshape(expert_count, capacity, model_width),
        "expert",
        split_axis=0,
        concat_axis=0,
        tiled=True,
    )
    returned = returned.reshape(slot_count, model_width)
    mixture = jnp.dot(combine_matrix, returned, preferred_element_type=jnp.float32)
    stream_out = (stream_float + mixture).astype(jnp.bfloat16)
    normed_out = rms_scale(stream_out.astype(jnp.float32), gain_final).astype(jnp.bfloat16)
    return (stream_out[None], normed_out[None])


MIB = 1024 * 1024
BF16, F32 = jnp.bfloat16, jnp.float32


def whole_vmem():
    return pl.BlockSpec(memory_space=pltpu.VMEM)


def whole_smem():
    return pl.BlockSpec(memory_space=pltpu.SMEM)


def fixed(*shape):
    return pl.BlockSpec(shape, lambda i: (0,) * len(shape))


def dot(a, b):
    return jnp.dot(a, b, preferred_element_type=F32)


def small_cost():
    return pl.CostEstimate(flops=1, bytes_accessed=1, transcendentals=0)


def kernel_params(mib):
    return pltpu.CompilerParams(vmem_limit_bytes=mib * MIB)


def seat():
    expert = lax.axis_index("expert")
    return expert, lax.shift_right_logical(expert, 2), expert & 3, lax.axis_index("dp")


def aligned(index, step):
    return pl.ds(pl.multiple_of(index * step, step), step)


def cut_kernel(resid, r0, r1, r23):
    expert, outer, inner, dp = seat()
    rows, lanes = r0.shape
    r0[...] = resid[:, aligned(outer, lanes)]
    r1[...] = resid[:, aligned(outer ^ 1, lanes)]
    for i in range(2):
        r23[i * rows : (i + 1) * rows, :] = resid[:, aligned(outer ^ (2 + i), lanes)]


def share_kernel(live, ids, logits, share_ref):
    expert, outer, inner, dp = seat()
    rows, top = ids.shape
    experts, lanes = share_ref.shape
    value = logits[...]
    value = jnp.exp(value - jnp.max(value, axis=1, keepdims=True))
    probs = (value / jnp.sum(value, axis=1, keepdims=True)).astype(BF16).astype(F32)
    probs = jnp.where(lax.broadcasted_iota(jnp.int32, (rows, top), 0) < live[0, 0], probs, 0.0)
    names = lax.broadcasted_iota(jnp.int32, (rows, experts), 1)
    table = jnp.zeros((rows, experts), F32)
    for k in range(top):
        table = table + jnp.where(ids[:, k : k + 1] == names, probs[:, k : k + 1], 0.0)
    spots = lax.broadcasted_iota(jnp.int32, (rows, lanes), 1) - outer * rows
    spots = (spots == lax.broadcasted_iota(jnp.int32, (rows, lanes), 0)).astype(F32).astype(BF16)
    share_ref[...] = lax.dot_general(
        table.astype(BF16), spots, (((0,), (0,)), ((), ())), preferred_element_type=F32
    ).astype(BF16)


def proj_kernel(a0, a1, a2, a3, w0, w1, w2, w3, keep_ref, send_ref, rows, part):
    expert, outer, inner, dp = seat()
    full = a0.shape[0]
    half = full // 2
    block = w0.shape[1]
    for s, a in enumerate((a0, a1, a2, a3)):
        rows[aligned(outer ^ s, full), :] = a[...]
    for j, w in enumerate((w0, w1, w2, w3)):
        part[:, aligned(inner ^ j, block)] = dot(rows[...], w[...]).astype(BF16)
    for spot in range(4):
        keep_ref[spot * half : (spot + 1) * half, :] = part[aligned(2 * spot + dp, half), :]
        send_ref[spot * half : (spot + 1) * half, :] = part[aligned(2 * spot + 1 - dp, half), :]


def stream_kernel(keep, arrived, r0, r13, r2, share, block_ref):
    expert, outer, inner, dp = seat()
    count = keep.shape[0]
    small = r0.shape[0]
    for s, r in enumerate((r0[...], r13[0:small, :], r2[0:small, :], r13[small:, :])):
        rows = aligned(outer ^ s, small)
        product = keep[rows, :].astype(F32) + arrived[rows, :].astype(F32)
        block_ref[rows, :] = (r.astype(F32) + product).astype(BF16)
    block_ref[count:, :] = share[...]


def piece_kernel(starts, weights, *refs):
    *outs, semaphores = refs
    copies = []
    at = 0
    for k, out in enumerate(outs):
        depth, width = out.shape[0], out.shape[1] // 2
        for i in range(2):
            copies.append(
                pltpu.make_async_copy(
                    weights.at[pl.ds(at, depth), pl.ds(starts[i], width)],
                    out.at[:, pl.ds(i * width, width)],
                    semaphores.at[i, k],
                )
            )
        at += depth
    for copy in copies:
        copy.start()
    for copy in copies:
        copy.wait()


def swiglu(gate, up, share):
    return (gate / (1.0 + jnp.exp(-gate)) * up * share).astype(BF16)


def norm_kernel(b0, b1, b2, b3, gain, group_ref, own_ref):
    expert, outer, inner, dp = seat()
    count = group_ref.shape[0]
    width = b0.shape[1]
    experts = b0.shape[0] - count
    small = own_ref.shape[0]
    square = jnp.zeros((count, 1), F32)
    share = jnp.zeros((experts, count), F32)
    for s, b in enumerate((b0, b1, b2, b3)):
        value = b[0:count, :]
        group_ref[:, aligned((outer + 4 - s) & 3, width)] = value
        value = value.astype(F32)
        square = square + jnp.sum(value * value, axis=1, keepdims=True)
        share = share + b[count : count + experts, 0:count].astype(F32)
    own_ref[...] = group_ref[aligned(outer, small), 0 : 4 * width]
    scale = lax.rsqrt(square / (4 * width) + 1e-06)
    for s in range(4):
        cols = slice(s * width, (s + 1) * width)
        value = group_ref[:, cols].astype(F32)
        group_ref[:, cols] = (value * scale * gain[:, cols]).astype(BF16)
    lanes = (experts, 128)
    spread = lax.broadcasted_iota(jnp.int32, lanes, 0) == lax.broadcasted_iota(jnp.int32, lanes, 1)
    group_ref[:, 4 * width :] = lax.dot_general(
        share.astype(BF16),
        spread.astype(F32).astype(BF16),
        (((0,), (0,)), ((), ())),
        preferred_element_type=F32,
    ).astype(BF16)


def first_gate_kernel(
    group_x, group_cx, group, group_c, own, early,
    first_ref, second_ref, part_ref, other_ref, share_ref, mine_ref,
):
    expert, outer, inner, dp = seat()
    count = group.shape[0]
    half = other_ref.shape[1]
    cut = first_ref.shape[1]
    for j, g in enumerate((group_x, group_cx, group, group_c)):
        rows = slice(j * count, (j + 1) * count)
        mine_ref[rows, :] = g[:, aligned(dp, half)]
        other_ref[rows, :] = g[:, aligned(1 - dp, half)]
        share = g[:, 2 * half : 2 * half + 128].astype(F32)
        picked = lax.broadcasted_iota(jnp.int32, share.shape, 1) == expert
        share = jnp.sum(jnp.where(picked, share, 0.0), axis=1, keepdims=True)
        share_ref[rows, :] = jnp.broadcast_to(share, (count, 128))
    mine, other = mine_ref[...], other_ref[...]
    gate = dot(mine, own[:, 0:cut]) + dot(other, early[:, 0:cut])
    up = dot(mine, own[:, 2 * cut : 3 * cut]) + dot(other, early[:, cut : 2 * cut])
    inner = swiglu(gate, up, share_ref[:, 0:1])
    first_ref[...] = inner[: 3 * count]
    second_ref[...] = inner[3 * count :]
    part_ref[:, 0:cut] = dot(mine, own[:, cut : 2 * cut])
    part_ref[:, cut : 2 * cut] = dot(mine, own[:, 3 * cut : 4 * cut])


def last_gate_kernel(second, part, other, share, *refs):
    *late, far_ref, rest_ref = refs
    count, cut = second.shape
    gate, up = part[:, 0:cut], part[:, cut : 2 * cut]
    at = 0
    for piece in late:
        rows = other[:, at : at + piece.shape[0]]
        gate = gate + dot(rows, piece[:, 0:cut])
        up = up + dot(rows, piece[:, cut : 2 * cut])
        at += piece.shape[0]
    value = swiglu(gate, up, share[:, 0:1])
    far_ref[...] = value[: 2 * count]
    rest_ref[0:count, :] = second[...]
    rest_ref[count:, :] = value[2 * count :]


def down_rows(pieces, wd, keep_ref, sends, rows):
    expert, outer, inner, dp = seat()
    core = inner & 1
    count, side = sends[0].shape
    small = count // 4
    for h, places in enumerate(pieces):
        cut = places[0][0].shape[1]
        cols = slice(h * cut, (h + 1) * cut)
        for i in range(2):
            for j in range(2):
                ref, start = places[j]
                kept = aligned(start // small + ((outer + 2 * core + i) & 3), small)
                at = (2 * i + j) * small
                rows[at : at + small, cols] = ref[kept, :]
                ref, start = places[1 - j]
                sent = aligned(start // small + ((outer + 2 - 2 * core + i) & 3), small)
                rows[count + at : count + at + small, cols] = ref[sent, :]
    for at in range(0, wd.shape[1], 256):
        value = dot(rows[...], wd[:, at : at + 256]).astype(BF16)
        keep_ref[:, at : at + 256] = value[:count]
        sends[at // side][:, at % side : at % side + 256] = value[count:]


def far_places(first, far):
    count = far.shape[0] // 2
    return ((first, 0), (first, count)), ((far, 0), (far, count))


def near_places(first, rest):
    count = rest.shape[0] // 3
    return ((first, 2 * count), (rest, 0)), ((rest, count), (rest, 2 * count))


def down_both_kernel(first, far, rest, wd, keep_far, *refs):
    *sends, keep_near, rows = refs
    half = len(sends) // 2
    down_rows(far_places(first, far), wd, keep_far, sends[:half], rows)
    down_rows(near_places(first, rest), wd, keep_near, sends[half:], rows)


def down_far_kernel(first, far, wd, keep_ref, *refs):
    *sends, rows = refs
    down_rows(far_places(first, far), wd, keep_ref, sends, rows)


def down_near_kernel(first, rest, wd, keep_ref, *refs):
    *sends, rows = refs
    down_rows(near_places(first, rest), wd, keep_ref, sends, rows)


def added(keep, cores, cols):
    side = cores[0].shape[1]
    return keep[:, cols].astype(F32) + cores[cols.start // side][:, cols.start % side : cols.start % side + 256].astype(F32)


def fold_kernel(keep, *refs):
    *cores, out = refs
    for at in range(0, keep.shape[1], 256):
        cols = slice(at, at + 256)
        out[:, cols] = added(keep, cores, cols).astype(BF16)


def pieces_kernel(far, keep, *refs):
    *cores, first, second = refs
    half = first.shape[0]
    for at in range(0, keep.shape[1], 256):
        cols = slice(at, at + 256)
        total = (added(keep, cores, cols) + far[:, cols].astype(F32)).astype(BF16)
        first[:, cols] = total[:half]
        second[:, cols] = total[half:]


def messages_kernel(keep_far, keep_near, *refs):
    *cores, first, second = refs
    half = first.shape[0] // 2
    parts = len(cores) // 2
    for h, (keep, core) in enumerate(((keep_far, cores[:parts]), (keep_near, cores[parts:]))):
        for at in range(0, keep.shape[1], 256):
            cols = slice(at, at + 256)
            total = added(keep, core, cols).astype(BF16)
            first[h * half : (h + 1) * half, cols] = total[:half]
            second[h * half : (h + 1) * half, cols] = total[half:]


def outer_sum_kernel(own, a0, a1, far_ref, near_ref):
    expert, outer, inner, dp = seat()
    half = far_ref.shape[0]
    total = jnp.where((inner & 1) == 0, own[...].astype(F32), a0[...].astype(F32)) + a1[...].astype(F32)
    far_ref[...] = total[:half].astype(BF16)
    near_ref[...] = total[half:]


def gather_kernel(near, far, b0, b1, keep_ref, send_ref):
    small = near.shape[0] // 2
    for i, total in enumerate(
        (near[...] + far[...].astype(F32), b0[...].astype(F32) + b1[...].astype(F32))
    ):
        rows = slice(i * small, (i + 1) * small)
        keep_ref[rows, :] = total[:small]
        send_ref[rows, :] = total[small:].astype(BF16)


def tail_kernel(own, keep, core, gain, stream_ref, normed_ref):
    expert, outer, inner, dp = seat()
    small, half = own.shape[0], keep.shape[1]
    for i, at in enumerate((dp, 1 - dp)):
        rows = slice(i * small, (i + 1) * small)
        cols = aligned(at, half)
        mixture = keep[rows, :] + core[rows, :].astype(F32)
        stream_ref[:, cols] = (own[:, cols].astype(F32) + mixture).astype(BF16)
    normed_ref[...] = rms_scale(stream_ref[...].astype(F32), gain[...]).astype(BF16)


def body_paired(
    attn,
    resid,
    w_out,
    gain_post,
    route_ids,
    route_logits,
    live_count,
    w_gate_up,
    w_down,
    gain_final,
):
    rows_here = resid.shape[1]
    model_width = resid.shape[2]
    expert_count = lax.axis_size("expert")
    hidden = w_down.shape[1]
    half_width = w_down.shape[2]
    quarter = model_width // 4
    vmem, smem = whole_vmem(), whole_smem()

    def shape_of(*shape, dtype=BF16):
        return jax.ShapeDtypeStruct(shape, dtype)

    def call(kernel, name, mib, outs, *args, scratch=(), first=vmem):
        return pl.pallas_call(
            kernel,
            out_shape=outs,
            in_specs=[first] + [vmem] * (len(args) - 1),
            out_specs=tuple(vmem for _ in outs),
            scratch_shapes=list(scratch),
            compiler_params=kernel_params(mib),
            cost_estimate=small_cost(),
            name=name,
        )(*args)

    def swap_dp(x):
        return lax.ppermute(x, "dp", [(0, 1), (1, 0)])

    def shift_outer(x, s):
        return lax.ppermute(
            x, "expert", [(i, (i + 4 * s) % expert_count) for i in range(expert_count)]
        )

    def send_outer(x, i, cross):
        pairs = []
        for at in range(2 * expert_count):
            d, e = divmod(at, expert_count)
            step = 2 * (e % 2) + i
            if step or cross:
                pairs.append((at, (d ^ cross) * expert_count + (e + 4 * step) % expert_count))
        return lax.ppermute(x, ("dp", "expert"), pairs)

    def swap_inner(x, j):
        return lax.ppermute(x, "expert", [(i, i ^ j) for i in range(expert_count)])

    def swap_outer(x, s):
        return lax.ppermute(x, "expert", [(i, i ^ (4 * s)) for i in range(expert_count)])

    def after(x, *results):
        return lax.optimization_barrier((x, *results))[0]

    def weight_piece(first, size, depths):
        return pl.pallas_call(
            functools.partial(piece_kernel, (first, hidden + first)),
            out_shape=tuple(shape_of(depth, 2 * size) for depth in depths),
            in_specs=[pl.BlockSpec(memory_space=pl.ANY)],
            out_specs=tuple(vmem for _ in depths),
            scratch_shapes=[pltpu.SemaphoreType.DMA((2, len(depths)))],
            compiler_params=kernel_params(8),
            cost_estimate=small_cost(),
            name="weight_piece",
        )(w_gate_up[0])

    piece = shape_of(rows_here, quarter)
    r_own, r_1, r_23 = call(
        cut_kernel, "cut_resid", 4, (piece, piece, shape_of(2 * rows_here, quarter)), resid[0]
    )
    (share,) = call(
        share_kernel,
        "share",
        4,
        (shape_of(expert_count, quarter),),
        live_count,
        route_ids[0],
        route_logits[0],
        first=smem,
    )
    cut_width = hidden // 2
    early_piece = weight_piece(0, cut_width, (half_width,))[0]
    late_pieces = weight_piece(cut_width, cut_width, (half_width * 640 // 1024, half_width * 384 // 1024))
    gate_up_early = swap_dp(early_piece)
    a = [attn[0], swap_outer(attn[0], 1), swap_outer(attn[0], 2)]
    w_x = swap_inner(w_out, 2)
    r_2 = swap_outer(r_23, 2)
    a.append(swap_outer(after(a[2], a[1], r_2), 1))
    w_c = swap_inner(after(w_out, w_x, share, *late_pieces), 1)
    w_cx = swap_inner(w_x, 1)
    r_13 = swap_outer(jnp.concatenate([r_1, r_2[rows_here:]], axis=0), 1)

    product = shape_of(4 * rows_here, quarter)
    keep, send = call(
        proj_kernel,
        "projection",
        8,
        (product, product),
        *a[:3],
        after(a[3], r_13),
        w_out,
        w_c,
        w_x,
        w_cx,
        scratch=(
            pltpu.VMEM((8 * rows_here, attn.shape[2]), BF16),
            pltpu.VMEM((8 * rows_here, quarter), BF16),
        ),
    )
    arrived = swap_dp(send)
    gate_up_late = [swap_dp(after(piece, send)) for piece in late_pieces]
    (block,) = call(
        stream_kernel,
        "stream",
        4,
        (shape_of(4 * rows_here + expert_count, quarter),),
        after(keep, gate_up_early),
        arrived,
        r_own,
        r_13,
        r_2,
        share,
    )

    def norm(b0, b1, b2, b3):
        outs = (shape_of(4 * rows_here, model_width + 128), shape_of(rows_here, model_width))
        return call(norm_kernel, "norm", 8, outs, b0, b1, b2, b3, gain_post[None])

    blocks = [block] + [shift_outer(block, s) for s in (1, 2, 3)]
    group, stream_own = norm(*blocks)
    blocks_x = [swap_inner(b, 2) for b in blocks]
    group_x, unused = norm(*blocks_x)
    group_c = swap_inner(group, 1)
    group_cx = swap_inner(group_x, 1)

    row_total = 16 * rows_here
    half_rows = row_total // 2
    inner_first, inner_second, part, other_rows, share_rows = call(
        first_gate_kernel,
        "first_gate_up",
        24,
        (
            shape_of(row_total * 3 // 4, cut_width),
            shape_of(row_total // 4, cut_width),
            shape_of(row_total, hidden, dtype=F32),
            shape_of(row_total, half_width),
            shape_of(row_total, 128, dtype=F32),
        ),
        group_x,
        group_cx,
        group,
        group_c,
        w_gate_up[0],
        gate_up_early,
        scratch=(pltpu.VMEM((row_total, half_width), BF16),),
    )
    inner_far, inner_rest = call(
        last_gate_kernel,
        "last_gate_up",
        16,
        (shape_of(half_rows, cut_width), shape_of(row_total * 3 // 4, cut_width)),
        inner_second,
        part,
        other_rows,
        share_rows,
        *gate_up_late,
    )
    first_other = swap_dp(inner_first)
    far_other = swap_dp(inner_far)
    rest_other = swap_dp(inner_rest)

    count = row_total // 4
    quarter_out = shape_of(count, half_width)

    def parts_of(many):
        return (shape_of(count, half_width // many),) * many

    scratch = (pltpu.VMEM((half_rows, hidden), BF16),)

    def down(kernel, rows, many):
        keep, *send = call(
            kernel, "down", 12, (quarter_out, *parts_of(many)), first_other, rows, w_down[0], scratch=scratch
        )
        return keep, send

    def swap_cores(halves):
        return [swap_inner(half, 1) for half in halves]

    def fold(keep, halves):
        return call(fold_kernel, "fold", 4, (quarter_out,), keep, *halves)[0]

    def pieces(far, keep, send):
        outs = (shape_of(2 * rows_here, half_width),) * 2
        return call(pieces_kernel, "pieces", 4, outs, far, keep, *swap_cores(send))

    outs = (quarter_out, *parts_of(2), *parts_of(2), quarter_out)
    keep_far, *send, keep_near = call(
        down_both_kernel, "down_both", 16, outs, inner_first, inner_far, inner_rest, w_down[0], scratch=scratch
    )
    message = shape_of(4 * rows_here, half_width)
    own, second = call(
        messages_kernel, "messages", 4, (message, message), keep_far, keep_near, *swap_cores(send)
    )
    half_message = shape_of(2 * rows_here, half_width)
    mine_far, mine_near = call(
        outer_sum_kernel,
        "outer_sum",
        4,
        (half_message, shape_of(2 * rows_here, half_width, dtype=F32)),
        own,
        send_outer(own, 0, False),
        send_outer(second, 1, False),
    )
    mine_far = swap_inner(mine_far, 2)

    keep_far, send = down(down_far_kernel, far_other, 2)
    far = swap_inner(fold(keep_far, swap_cores(send)), 2)
    keep_near, send = down(down_near_kernel, rest_other, 2)
    cut = pieces(far, keep_near, [send[0], after(send[1], mine_near)])
    others = [send_outer(cut[i], i, True) for i in range(2)]

    sums = shape_of(2 * rows_here, half_width)
    keep, send = call(
        gather_kernel,
        "gather",
        4,
        (shape_of(2 * rows_here, half_width, dtype=F32), sums),
        mine_near,
        mine_far,
        *others,
    )
    out = shape_of(rows_here, model_width)
    stream_out, normed_out = call(
        tail_kernel, "closing", 8, (out, out), stream_own, keep, swap_inner(send, 1), gain_final[None]
    )
    return (stream_out[None], normed_out[None])


def solution(mesh):
    placed = (
        P("expert", None, "dp"),
        P("expert", "dp", None),
        P("dp", "expert"),
        P(),
        P("expert", "dp", None),
        P("expert", "dp", None),
        P("expert", "dp"),
        P("expert", "dp", None),
        P("expert", None, "dp"),
        P(),
    )
    paired = mesh.shape["dp"] == 2 and mesh.shape["expert"] == 16
    return jax.shard_map(
        body_paired if paired else body_general,
        mesh=mesh,
        in_specs=placed,
        out_specs=(P("expert", "dp", None), P("expert", "dp", None)),
        check_vma=False,
    )
```

```python
import functools
import math

import jax
import jax.numpy as jnp
from jax import lax
from jax.experimental import pallas as pl
from jax.experimental.pallas import tpu as pltpu
from jax.sharding import PartitionSpec as P


def rms_scale(values, gain):
    return values * lax.rsqrt(jnp.mean(values * values, axis=-1, keepdims=True) + 1e-06) * gain


def swiglu_rows(rows_in, gate_up, down, hidden_units):
    both = jnp.dot(rows_in, gate_up, preferred_element_type=jnp.float32)
    inner = (jax.nn.silu(both[:, :hidden_units]) * both[:, hidden_units:]).astype(jnp.bfloat16)
    return jnp.dot(inner, down, preferred_element_type=jnp.float32).astype(jnp.bfloat16)


def body_general(
    attn,
    resid,
    w_out,
    gain_post,
    route_ids,
    route_logits,
    live_count,
    w_gate_up,
    w_down,
    gain_final,
):
    rows_here = resid.shape[1]
    model_width = resid.shape[2]
    top_count = route_ids.shape[2]
    dp_count = lax.axis_size("dp")
    expert_count = lax.axis_size("expert")
    hidden_units = w_down.shape[1]
    capacity = dp_count * max(1, 2 * rows_here * top_count // (expert_count * dp_count))
    slot_count = expert_count * capacity
    flat_attn = attn[0]
    partial_out = jnp.dot(
        flat_attn,
        lax.all_gather(w_out, "expert", axis=1, tiled=True),
        preferred_element_type=jnp.float32,
    )
    projected = lax.psum_scatter(
        partial_out.astype(jnp.bfloat16), "dp", scatter_dimension=0, tiled=True
    ).astype(jnp.float32)
    stream_in = (resid[0].astype(jnp.float32) + projected).astype(jnp.bfloat16)
    stream_float = stream_in.astype(jnp.float32)
    normed_in = rms_scale(stream_float, gain_post).astype(jnp.bfloat16)
    probs = jax.nn.softmax(route_logits[0], axis=-1).astype(jnp.bfloat16)
    alive = jnp.arange(rows_here, dtype=jnp.int32) < live_count[0, 0]
    expert_of = route_ids[0].reshape(-1)
    route_alive = jnp.repeat(alive, top_count)
    onehot = (
        (expert_of[:, None] == jnp.arange(expert_count, dtype=jnp.int32)[None, :])
        & route_alive[:, None]
    ).astype(jnp.int32)
    earlier = jnp.sum((jnp.cumsum(onehot, axis=0) - onehot) * onehot, axis=1)
    target = expert_of * capacity + earlier
    match = (target[:, None] == jnp.arange(slot_count, dtype=jnp.int32)[None, :]) & route_alive[
        :, None
    ]
    placed = match.reshape(rows_here, top_count, slot_count)
    gather_matrix = jnp.any(placed, axis=1).astype(jnp.bfloat16)
    send_rows = lax.dot_general(
        gather_matrix, normed_in, (((0,), (0,)), ((), ())), preferred_element_type=jnp.float32
    ).astype(jnp.bfloat16)
    send_flags = jnp.sum(gather_matrix.astype(jnp.float32), axis=0).astype(jnp.bfloat16)
    combine_matrix = jnp.sum(
        jnp.where(placed, probs.astype(jnp.float32)[:, :, None], jnp.float32(0.0)), axis=1
    ).astype(jnp.bfloat16)
    arrived_rows, arrived_flags = (
        lax.all_to_all(
            send_rows.reshape(expert_count, capacity, model_width),
            "expert",
            split_axis=0,
            concat_axis=0,
            tiled=True,
        ),
        lax.all_to_all(
            send_flags.reshape(expert_count, capacity),
            "expert",
            split_axis=0,
            concat_axis=0,
            tiled=True,
        ),
    )
    arrived = arrived_rows.reshape(slot_count, model_width)
    flags = arrived_flags.reshape(slot_count)
    gate_up_full, down_full = (
        lax.all_gather(w_gate_up, "dp", axis=1, tiled=True),
        lax.all_gather(w_down, "dp", axis=2, tiled=True),
    )
    live_slot = (flags > 0.5).astype(jnp.int32)
    order = jnp.argsort(1 - live_slot, stable=True)
    live_total = jnp.sum(live_slot)
    packed = arrived[order]
    block_len = math.gcd(slot_count, 128)
    block_total = (live_total + block_len - 1) // block_len

    def run_block(index, outputs):
        begin = index * block_len
        rows_in = lax.dynamic_slice_in_dim(packed, begin, block_len, 0)
        block_out = swiglu_rows(rows_in, gate_up_full[0], down_full[0], hidden_units)
        return lax.dynamic_update_slice_in_dim(outputs, block_out, begin, 0)

    packed_out = lax.fori_loop(
        0, block_total, run_block, jnp.zeros((slot_count, model_width), jnp.bfloat16)
    )
    position = (
        jnp.zeros((slot_count,), jnp.int32).at[order].set(jnp.arange(slot_count, dtype=jnp.int32))
    )
    results = packed_out[position]
    returned = lax.all_to_all(
        results.reshape(expert_count, capacity, model_width),
        "expert",
        split_axis=0,
        concat_axis=0,
        tiled=True,
    )
    returned = returned.reshape(slot_count, model_width)
    mixture = jnp.dot(combine_matrix, returned, preferred_element_type=jnp.float32)
    stream_out = (stream_float + mixture).astype(jnp.bfloat16)
    normed_out = rms_scale(stream_out.astype(jnp.float32), gain_final).astype(jnp.bfloat16)
    return (stream_out[None], normed_out[None])


MIB = 1024 * 1024
BF16, F32 = jnp.bfloat16, jnp.float32


def whole_vmem():
    return pl.BlockSpec(memory_space=pltpu.VMEM)


def whole_smem():
    return pl.BlockSpec(memory_space=pltpu.SMEM)


def fixed(*shape):
    return pl.BlockSpec(shape, lambda i: (0,) * len(shape))


def dot(a, b):
    return jnp.dot(a, b, preferred_element_type=F32)


def small_cost():
    return pl.CostEstimate(flops=1, bytes_accessed=1, transcendentals=0)


def kernel_params(mib):
    return pltpu.CompilerParams(vmem_limit_bytes=mib * MIB)


def seat():
    expert = lax.axis_index("expert")
    return expert, lax.shift_right_logical(expert, 2), expert & 3, lax.axis_index("dp")


def aligned(index, step):
    return pl.ds(pl.multiple_of(index * step, step), step)


def cut_kernel(resid, r0, r1, r23):
    expert, outer, inner, dp = seat()
    rows, lanes = r0.shape
    r0[...] = resid[:, aligned(outer, lanes)]
    r1[...] = resid[:, aligned(outer ^ 1, lanes)]
    for i in range(2):
        r23[i * rows : (i + 1) * rows, :] = resid[:, aligned(outer ^ (2 + i), lanes)]


def share_kernel(live, ids, logits, share_ref):
    expert, outer, inner, dp = seat()
    rows, top = ids.shape
    experts, lanes = share_ref.shape
    value = logits[...]
    value = jnp.exp(value - jnp.max(value, axis=1, keepdims=True))
    probs = (value / jnp.sum(value, axis=1, keepdims=True)).astype(BF16).astype(F32)
    probs = jnp.where(lax.broadcasted_iota(jnp.int32, (rows, top), 0) < live[0, 0], probs, 0.0)
    names = lax.broadcasted_iota(jnp.int32, (rows, experts), 1)
    table = jnp.zeros((rows, experts), F32)
    for k in range(top):
        table = table + jnp.where(ids[:, k : k + 1] == names, probs[:, k : k + 1], 0.0)
    spots = lax.broadcasted_iota(jnp.int32, (rows, lanes), 1) - outer * rows
    spots = (spots == lax.broadcasted_iota(jnp.int32, (rows, lanes), 0)).astype(F32).astype(BF16)
    share_ref[...] = lax.dot_general(
        table.astype(BF16), spots, (((0,), (0,)), ((), ())), preferred_element_type=F32
    ).astype(BF16)


def proj_kernel(a0, a1, a2, a3, w0, w1, w2, w3, keep_ref, send_ref, rows, part):
    expert, outer, inner, dp = seat()
    full = a0.shape[0]
    half = full // 2
    block = w0.shape[1]
    for s, a in enumerate((a0, a1, a2, a3)):
        rows[aligned(outer ^ s, full), :] = a[...]
    for j, w in enumerate((w0, w1, w2, w3)):
        part[:, aligned(inner ^ j, block)] = dot(rows[...], w[...]).astype(BF16)
    for spot in range(4):
        keep_ref[spot * half : (spot + 1) * half, :] = part[aligned(2 * spot + dp, half), :]
        send_ref[spot * half : (spot + 1) * half, :] = part[aligned(2 * spot + 1 - dp, half), :]


def stream_kernel(keep, arrived, r0, r13, r2, share, block_ref):
    expert, outer, inner, dp = seat()
    count = keep.shape[0]
    small = r0.shape[0]
    for s, r in enumerate((r0[...], r13[0:small, :], r2[0:small, :], r13[small:, :])):
        rows = aligned(outer ^ s, small)
        product = keep[rows, :].astype(F32) + arrived[rows, :].astype(F32)
        block_ref[rows, :] = (r.astype(F32) + product).astype(BF16)
    block_ref[count:, :] = share[...]


def piece_kernel(starts, weights, *refs):
    *outs, semaphores = refs
    copies = []
    at = 0
    for k, out in enumerate(outs):
        depth, width = out.shape[0], out.shape[1] // 2
        for i in range(2):
            copies.append(
                pltpu.make_async_copy(
                    weights.at[pl.ds(at, depth), pl.ds(starts[i], width)],
                    out.at[:, pl.ds(i * width, width)],
                    semaphores.at[i, k],
                )
            )
        at += depth
    for copy in copies:
        copy.start()
    for copy in copies:
        copy.wait()


def swiglu(gate, up, share):
    return (gate / (1.0 + jnp.exp(-gate)) * up * share).astype(BF16)


def norm_kernel(b0, b1, b2, b3, gain, group_ref, own_ref):
    expert, outer, inner, dp = seat()
    count = group_ref.shape[0]
    width = b0.shape[1]
    experts = b0.shape[0] - count
    small = own_ref.shape[0]
    square = jnp.zeros((count, 1), F32)
    share = jnp.zeros((experts, count), F32)
    for s, b in enumerate((b0, b1, b2, b3)):
        value = b[0:count, :]
        group_ref[:, aligned((outer + 4 - s) & 3, width)] = value
        value = value.astype(F32)
        square = square + jnp.sum(value * value, axis=1, keepdims=True)
        share = share + b[count : count + experts, 0:count].astype(F32)
    own_ref[...] = group_ref[aligned(outer, small), 0 : 4 * width]
    scale = lax.rsqrt(square / (4 * width) + 1e-06)
    for s in range(4):
        cols = slice(s * width, (s + 1) * width)
        value = group_ref[:, cols].astype(F32)
        group_ref[:, cols] = (value * scale * gain[:, cols]).astype(BF16)
    lanes = (experts, 128)
    spread = lax.broadcasted_iota(jnp.int32, lanes, 0) == lax.broadcasted_iota(jnp.int32, lanes, 1)
    group_ref[:, 4 * width :] = lax.dot_general(
        share.astype(BF16),
        spread.astype(F32).astype(BF16),
        (((0,), (0,)), ((), ())),
        preferred_element_type=F32,
    ).astype(BF16)


def first_gate_kernel(
    group_x, group_cx, group, group_c, own, early,
    first_ref, second_ref, part_ref, other_ref, share_ref, mine_ref,
):
    expert, outer, inner, dp = seat()
    count = group.shape[0]
    half = other_ref.shape[1]
    cut = first_ref.shape[1]
    for j, g in enumerate((group_x, group_cx, group, group_c)):
        rows = slice(j * count, (j + 1) * count)
        mine_ref[rows, :] = g[:, aligned(dp, half)]
        other_ref[rows, :] = g[:, aligned(1 - dp, half)]
        share = g[:, 2 * half : 2 * half + 128].astype(F32)
        picked = lax.broadcasted_iota(jnp.int32, share.shape, 1) == expert
        share = jnp.sum(jnp.where(picked, share, 0.0), axis=1, keepdims=True)
        share_ref[rows, :] = jnp.broadcast_to(share, (count, 128))
    mine, other = mine_ref[...], other_ref[...]
    gate = dot(mine, own[:, 0:cut]) + dot(other, early[:, 0:cut])
    up = dot(mine, own[:, 2 * cut : 3 * cut]) + dot(other, early[:, cut : 2 * cut])
    inner = swiglu(gate, up, share_ref[:, 0:1])
    first_ref[...] = inner[: 3 * count]
    second_ref[...] = inner[3 * count :]
    part_ref[:, 0:cut] = dot(mine, own[:, cut : 2 * cut])
    part_ref[:, cut : 2 * cut] = dot(mine, own[:, 3 * cut : 4 * cut])


def last_gate_kernel(second, part, other, share, *refs):
    *late, far_ref, rest_ref = refs
    count, cut = second.shape
    gate, up = part[:, 0:cut], part[:, cut : 2 * cut]
    at = 0
    for piece in late:
        rows = other[:, at : at + piece.shape[0]]
        gate = gate + dot(rows, piece[:, 0:cut])
        up = up + dot(rows, piece[:, cut : 2 * cut])
        at += piece.shape[0]
    value = swiglu(gate, up, share[:, 0:1])
    far_ref[...] = value[: 2 * count]
    rest_ref[0:count, :] = second[...]
    rest_ref[count:, :] = value[2 * count :]


def down_rows(pieces, wd, keep_ref, sends, rows):
    expert, outer, inner, dp = seat()
    core = inner & 1
    count, side = sends[0].shape
    small = count // 4
    for h, places in enumerate(pieces):
        cut = places[0][0].shape[1]
        cols = slice(h * cut, (h + 1) * cut)
        for i in range(2):
            for j in range(2):
                ref, start = places[j]
                kept = aligned(start // small + ((outer + 2 * core + i) & 3), small)
                at = (2 * i + j) * small
                rows[at : at + small, cols] = ref[kept, :]
                ref, start = places[1 - j]
                sent = aligned(start // small + ((outer + 2 - 2 * core + i) & 3), small)
                rows[count + at : count + at + small, cols] = ref[sent, :]
    for at in range(0, wd.shape[1], 256):
        value = dot(rows[...], wd[:, at : at + 256]).astype(BF16)
        keep_ref[:, at : at + 256] = value[:count]
        sends[at // side][:, at % side : at % side + 256] = value[count:]


def far_places(first, far):
    count = far.shape[0] // 2
    return ((first, 0), (first, count)), ((far, 0), (far, count))


def near_places(first, rest):
    count = rest.shape[0] // 3
    return ((first, 2 * count), (rest, 0)), ((rest, count), (rest, 2 * count))


def down_both_kernel(first, far, rest, wd, keep_far, *refs):
    *sends, keep_near, rows = refs
    half = len(sends) // 2
    down_rows(far_places(first, far), wd, keep_far, sends[:half], rows)
    down_rows(near_places(first, rest), wd, keep_near, sends[half:], rows)


def down_far_kernel(first, far, wd, keep_ref, *refs):
    *sends, rows = refs
    down_rows(far_places(first, far), wd, keep_ref, sends, rows)


def down_near_kernel(first, rest, wd, keep_ref, *refs):
    *sends, rows = refs
    down_rows(near_places(first, rest), wd, keep_ref, sends, rows)


def added(keep, cores, cols):
    side = cores[0].shape[1]
    return keep[:, cols].astype(F32) + cores[cols.start // side][:, cols.start % side : cols.start % side + 256].astype(F32)


def fold_kernel(keep, *refs):
    *cores, out = refs
    for at in range(0, keep.shape[1], 256):
        cols = slice(at, at + 256)
        out[:, cols] = added(keep, cores, cols).astype(BF16)


def pieces_kernel(far, keep, *refs):
    *cores, first, second = refs
    half = first.shape[0]
    for at in range(0, keep.shape[1], 256):
        cols = slice(at, at + 256)
        total = (added(keep, cores, cols) + far[:, cols].astype(F32)).astype(BF16)
        first[:, cols] = total[:half]
        second[:, cols] = total[half:]


def messages_kernel(keep_far, keep_near, *refs):
    *cores, first, second = refs
    half = first.shape[0] // 2
    parts = len(cores) // 2
    for h, (keep, core) in enumerate(((keep_far, cores[:parts]), (keep_near, cores[parts:]))):
        for at in range(0, keep.shape[1], 256):
            cols = slice(at, at + 256)
            total = added(keep, core, cols).astype(BF16)
            first[h * half : (h + 1) * half, cols] = total[:half]
            second[h * half : (h + 1) * half, cols] = total[half:]


def outer_sum_kernel(own, a0, a1, far_a, far_b, near_ref):
    expert, outer, inner, dp = seat()
    half, side = far_a.shape
    total = jnp.where((inner & 1) == 0, own[...].astype(F32), a0[...].astype(F32)) + a1[...].astype(F32)
    far_a[...] = total[:half, :side].astype(BF16)
    far_b[...] = total[:half, side:].astype(BF16)
    near_ref[...] = total[half:]


def gather_kernel(near, far_a, far_b, b0, b1, keep_ref, send_ref):
    small = near.shape[0] // 2
    for i, total in enumerate(
        (near[...] + jnp.concatenate([far_a[...], far_b[...]], axis=1).astype(F32), b0[...].astype(F32) + b1[...].astype(F32))
    ):
        rows = slice(i * small, (i + 1) * small)
        keep_ref[rows, :] = total[:small]
        send_ref[rows, :] = total[small:].astype(BF16)


def tail_kernel(own, keep, core, gain, stream_ref, normed_ref):
    expert, outer, inner, dp = seat()
    small, half = own.shape[0], keep.shape[1]
    for i, at in enumerate((dp, 1 - dp)):
        rows = slice(i * small, (i + 1) * small)
        cols = aligned(at, half)
        mixture = keep[rows, :] + core[rows, :].astype(F32)
        stream_ref[:, cols] = (own[:, cols].astype(F32) + mixture).astype(BF16)
    normed_ref[...] = rms_scale(stream_ref[...].astype(F32), gain[...]).astype(BF16)


def body_paired(
    attn,
    resid,
    w_out,
    gain_post,
    route_ids,
    route_logits,
    live_count,
    w_gate_up,
    w_down,
    gain_final,
):
    rows_here = resid.shape[1]
    model_width = resid.shape[2]
    expert_count = lax.axis_size("expert")
    hidden = w_down.shape[1]
    half_width = w_down.shape[2]
    quarter = model_width // 4
    vmem, smem = whole_vmem(), whole_smem()

    def shape_of(*shape, dtype=BF16):
        return jax.ShapeDtypeStruct(shape, dtype)

    def call(kernel, name, mib, outs, *args, scratch=(), first=vmem):
        return pl.pallas_call(
            kernel,
            out_shape=outs,
            in_specs=[first] + [vmem] * (len(args) - 1),
            out_specs=tuple(vmem for _ in outs),
            scratch_shapes=list(scratch),
            compiler_params=kernel_params(mib),
            cost_estimate=small_cost(),
            name=name,
        )(*args)

    def swap_dp(x):
        return lax.ppermute(x, "dp", [(0, 1), (1, 0)])

    def shift_outer(x, s):
        return lax.ppermute(
            x, "expert", [(i, (i + 4 * s) % expert_count) for i in range(expert_count)]
        )

    def send_outer(x, i, cross):
        pairs = []
        for at in range(2 * expert_count):
            d, e = divmod(at, expert_count)
            step = 2 * (e % 2) + i
            if step or cross:
                pairs.append((at, (d ^ cross) * expert_count + (e + 4 * step) % expert_count))
        return lax.ppermute(x, ("dp", "expert"), pairs)

    def swap_inner(x, j):
        return lax.ppermute(x, "expert", [(i, i ^ j) for i in range(expert_count)])

    def swap_outer(x, s):
        return lax.ppermute(x, "expert", [(i, i ^ (4 * s)) for i in range(expert_count)])

    def after(x, *results):
        return lax.optimization_barrier((x, *results))[0]

    def weight_piece(first, size, depths):
        return pl.pallas_call(
            functools.partial(piece_kernel, (first, hidden + first)),
            out_shape=tuple(shape_of(depth, 2 * size) for depth in depths),
            in_specs=[pl.BlockSpec(memory_space=pl.ANY)],
            out_specs=tuple(vmem for _ in depths),
            scratch_shapes=[pltpu.SemaphoreType.DMA((2, len(depths)))],
            compiler_params=kernel_params(8),
            cost_estimate=small_cost(),
            name="weight_piece",
        )(w_gate_up[0])

    piece = shape_of(rows_here, quarter)
    r_own, r_1, r_23 = call(
        cut_kernel, "cut_resid", 4, (piece, piece, shape_of(2 * rows_here, quarter)), resid[0]
    )
    (share,) = call(
        share_kernel,
        "share",
        4,
        (shape_of(expert_count, quarter),),
        live_count,
        route_ids[0],
        route_logits[0],
        first=smem,
    )
    cut_width = hidden // 2
    early_piece = weight_piece(0, cut_width, (half_width,))[0]
    late_pieces = weight_piece(cut_width, cut_width, (half_width * 640 // 1024, half_width * 384 // 1024))
    gate_up_early = swap_dp(early_piece)
    a = [attn[0], swap_outer(attn[0], 1), swap_outer(attn[0], 2)]
    w_x = swap_inner(w_out, 2)
    r_2 = swap_outer(r_23, 2)
    a.append(swap_outer(after(a[2], a[1], r_2), 1))
    w_c = swap_inner(after(w_out, w_x, share, *late_pieces), 1)
    w_cx = swap_inner(w_x, 1)
    r_13 = swap_outer(jnp.concatenate([r_1, r_2[rows_here:]], axis=0), 1)

    product = shape_of(4 * rows_here, quarter)
    keep, send = call(
        proj_kernel,
        "projection",
        8,
        (product, product),
        *a[:3],
        after(a[3], r_13),
        w_out,
        w_c,
        w_x,
        w_cx,
        scratch=(
            pltpu.VMEM((8 * rows_here, attn.shape[2]), BF16),
            pltpu.VMEM((8 * rows_here, quarter), BF16),
        ),
    )
    arrived = swap_dp(send)
    gate_up_late = [swap_dp(after(piece, send)) for piece in late_pieces]
    (block,) = call(
        stream_kernel,
        "stream",
        4,
        (shape_of(4 * rows_here + expert_count, quarter),),
        after(keep, gate_up_early),
        arrived,
        r_own,
        r_13,
        r_2,
        share,
    )

    def norm(b0, b1, b2, b3):
        outs = (shape_of(4 * rows_here, model_width + 128), shape_of(rows_here, model_width))
        return call(norm_kernel, "norm", 8, outs, b0, b1, b2, b3, gain_post[None])

    blocks = [block] + [shift_outer(block, s) for s in (1, 2, 3)]
    group, stream_own = norm(*blocks)
    blocks_x = [swap_inner(b, 2) for b in blocks]
    group_x, unused = norm(*blocks_x)
    group_c = swap_inner(group, 1)
    group_cx = swap_inner(group_x, 1)

    row_total = 16 * rows_here
    half_rows = row_total // 2
    inner_first, inner_second, part, other_rows, share_rows = call(
        first_gate_kernel,
        "first_gate_up",
        24,
        (
            shape_of(row_total * 3 // 4, cut_width),
            shape_of(row_total // 4, cut_width),
            shape_of(row_total, hidden, dtype=F32),
            shape_of(row_total, half_width),
            shape_of(row_total, 128, dtype=F32),
        ),
        group_x,
        group_cx,
        group,
        group_c,
        w_gate_up[0],
        gate_up_early,
        scratch=(pltpu.VMEM((row_total, half_width), BF16),),
    )
    inner_far, inner_rest = call(
        last_gate_kernel,
        "last_gate_up",
        16,
        (shape_of(half_rows, cut_width), shape_of(row_total * 3 // 4, cut_width)),
        inner_second,
        part,
        other_rows,
        share_rows,
        *gate_up_late,
    )
    first_other = swap_dp(inner_first)
    far_other = swap_dp(inner_far)
    rest_other = swap_dp(inner_rest)

    count = row_total // 4
    quarter_out = shape_of(count, half_width)

    def parts_of(many):
        return (shape_of(count, half_width // many),) * many

    scratch = (pltpu.VMEM((half_rows, hidden), BF16),)

    def down(kernel, rows, many):
        keep, *send = call(
            kernel, "down", 12, (quarter_out, *parts_of(many)), first_other, rows, w_down[0], scratch=scratch
        )
        return keep, send

    def swap_cores(halves):
        return [swap_inner(half, 1) for half in halves]

    def fold(keep, halves):
        return call(fold_kernel, "fold", 4, (quarter_out,), keep, *halves)[0]

    def pieces(far, keep, send):
        outs = (shape_of(2 * rows_here, half_width),) * 2
        return call(pieces_kernel, "pieces", 4, outs, far, keep, *swap_cores(send))

    outs = (quarter_out, *parts_of(2), *parts_of(2), quarter_out)
    keep_far, *send, keep_near = call(
        down_both_kernel, "down_both", 16, outs, inner_first, inner_far, inner_rest, w_down[0], scratch=scratch
    )
    message = shape_of(4 * rows_here, half_width)
    own, second = call(
        messages_kernel, "messages", 4, (message, message), keep_far, keep_near, *swap_cores(send)
    )
    half_message = shape_of(2 * rows_here, half_width // 2)
    *mine_far, mine_near = call(
        outer_sum_kernel,
        "outer_sum",
        4,
        (half_message, half_message, shape_of(2 * rows_here, half_width, dtype=F32)),
        own,
        send_outer(own, 0, False),
        send_outer(second, 1, False),
    )
    mine_far = [swap_inner(half, 2) for half in mine_far]

    keep_far, send = down(down_far_kernel, far_other, 2)
    far = swap_inner(fold(keep_far, swap_cores(send)), 2)
    keep_near, send = down(down_near_kernel, rest_other, 2)
    cut = pieces(far, keep_near, [send[0], after(send[1], mine_near)])
    others = [send_outer(cut[i], i, True) for i in range(2)]

    sums = shape_of(2 * rows_here, half_width)
    keep, send = call(
        gather_kernel,
        "gather",
        4,
        (shape_of(2 * rows_here, half_width, dtype=F32), sums),
        mine_near,
        *mine_far,
        *others,
    )
    out = shape_of(rows_here, model_width)
    stream_out, normed_out = call(
        tail_kernel, "closing", 8, (out, out), stream_own, keep, swap_inner(send, 1), gain_final[None]
    )
    return (stream_out[None], normed_out[None])


def solution(mesh):
    placed = (
        P("expert", None, "dp"),
        P("expert", "dp", None),
        P("dp", "expert"),
        P(),
        P("expert", "dp", None),
        P("expert", "dp", None),
        P("expert", "dp"),
        P("expert", "dp", None),
        P("expert", None, "dp"),
        P(),
    )
    paired = mesh.shape["dp"] == 2 and mesh.shape["expert"] == 16
    return jax.shard_map(
        body_paired if paired else body_general,
        mesh=mesh,
        in_specs=placed,
        out_specs=(P("expert", "dp", None), P("expert", "dp", None)),
        check_vma=False,
    )
```

```python
import functools
import math

import jax
import jax.numpy as jnp
from jax import lax
from jax.experimental import pallas as pl
from jax.experimental.pallas import tpu as pltpu
from jax.sharding import PartitionSpec as P


def rms_scale(values, gain):
    return values * lax.rsqrt(jnp.mean(values * values, axis=-1, keepdims=True) + 1e-06) * gain


def swiglu_rows(rows_in, gate_up, down, hidden_units):
    both = jnp.dot(rows_in, gate_up, preferred_element_type=jnp.float32)
    inner = (jax.nn.silu(both[:, :hidden_units]) * both[:, hidden_units:]).astype(jnp.bfloat16)
    return jnp.dot(inner, down, preferred_element_type=jnp.float32).astype(jnp.bfloat16)


def body_general(
    attn,
    resid,
    w_out,
    gain_post,
    route_ids,
    route_logits,
    live_count,
    w_gate_up,
    w_down,
    gain_final,
):
    rows_here = resid.shape[1]
    model_width = resid.shape[2]
    top_count = route_ids.shape[2]
    dp_count = lax.axis_size("dp")
    expert_count = lax.axis_size("expert")
    hidden_units = w_down.shape[1]
    capacity = dp_count * max(1, 2 * rows_here * top_count // (expert_count * dp_count))
    slot_count = expert_count * capacity
    flat_attn = attn[0]
    partial_out = jnp.dot(
        flat_attn,
        lax.all_gather(w_out, "expert", axis=1, tiled=True),
        preferred_element_type=jnp.float32,
    )
    projected = lax.psum_scatter(
        partial_out.astype(jnp.bfloat16), "dp", scatter_dimension=0, tiled=True
    ).astype(jnp.float32)
    stream_in = (resid[0].astype(jnp.float32) + projected).astype(jnp.bfloat16)
    stream_float = stream_in.astype(jnp.float32)
    normed_in = rms_scale(stream_float, gain_post).astype(jnp.bfloat16)
    probs = jax.nn.softmax(route_logits[0], axis=-1).astype(jnp.bfloat16)
    alive = jnp.arange(rows_here, dtype=jnp.int32) < live_count[0, 0]
    expert_of = route_ids[0].reshape(-1)
    route_alive = jnp.repeat(alive, top_count)
    onehot = (
        (expert_of[:, None] == jnp.arange(expert_count, dtype=jnp.int32)[None, :])
        & route_alive[:, None]
    ).astype(jnp.int32)
    earlier = jnp.sum((jnp.cumsum(onehot, axis=0) - onehot) * onehot, axis=1)
    target = expert_of * capacity + earlier
    match = (target[:, None] == jnp.arange(slot_count, dtype=jnp.int32)[None, :]) & route_alive[
        :, None
    ]
    placed = match.reshape(rows_here, top_count, slot_count)
    gather_matrix = jnp.any(placed, axis=1).astype(jnp.bfloat16)
    send_rows = lax.dot_general(
        gather_matrix, normed_in, (((0,), (0,)), ((), ())), preferred_element_type=jnp.float32
    ).astype(jnp.bfloat16)
    send_flags = jnp.sum(gather_matrix.astype(jnp.float32), axis=0).astype(jnp.bfloat16)
    combine_matrix = jnp.sum(
        jnp.where(placed, probs.astype(jnp.float32)[:, :, None], jnp.float32(0.0)), axis=1
    ).astype(jnp.bfloat16)
    arrived_rows, arrived_flags = (
        lax.all_to_all(
            send_rows.reshape(expert_count, capacity, model_width),
            "expert",
            split_axis=0,
            concat_axis=0,
            tiled=True,
        ),
        lax.all_to_all(
            send_flags.reshape(expert_count, capacity),
            "expert",
            split_axis=0,
            concat_axis=0,
            tiled=True,
        ),
    )
    arrived = arrived_rows.reshape(slot_count, model_width)
    flags = arrived_flags.reshape(slot_count)
    gate_up_full, down_full = (
        lax.all_gather(w_gate_up, "dp", axis=1, tiled=True),
        lax.all_gather(w_down, "dp", axis=2, tiled=True),
    )
    live_slot = (flags > 0.5).astype(jnp.int32)
    order = jnp.argsort(1 - live_slot, stable=True)
    live_total = jnp.sum(live_slot)
    packed = arrived[order]
    block_len = math.gcd(slot_count, 128)
    block_total = (live_total + block_len - 1) // block_len

    def run_block(index, outputs):
        begin = index * block_len
        rows_in = lax.dynamic_slice_in_dim(packed, begin, block_len, 0)
        block_out = swiglu_rows(rows_in, gate_up_full[0], down_full[0], hidden_units)
        return lax.dynamic_update_slice_in_dim(outputs, block_out, begin, 0)

    packed_out = lax.fori_loop(
        0, block_total, run_block, jnp.zeros((slot_count, model_width), jnp.bfloat16)
    )
    position = (
        jnp.zeros((slot_count,), jnp.int32).at[order].set(jnp.arange(slot_count, dtype=jnp.int32))
    )
    results = packed_out[position]
    returned = lax.all_to_all(
        results.reshape(expert_count, capacity, model_width),
        "expert",
        split_axis=0,
        concat_axis=0,
        tiled=True,
    )
    returned = returned.reshape(slot_count, model_width)
    mixture = jnp.dot(combine_matrix, returned, preferred_element_type=jnp.float32)
    stream_out = (stream_float + mixture).astype(jnp.bfloat16)
    normed_out = rms_scale(stream_out.astype(jnp.float32), gain_final).astype(jnp.bfloat16)
    return (stream_out[None], normed_out[None])


MIB = 1024 * 1024
BF16, F32 = jnp.bfloat16, jnp.float32


def whole_vmem():
    return pl.BlockSpec(memory_space=pltpu.VMEM)


def whole_smem():
    return pl.BlockSpec(memory_space=pltpu.SMEM)


def fixed(*shape):
    return pl.BlockSpec(shape, lambda i: (0,) * len(shape))


def dot(a, b):
    return jnp.dot(a, b, preferred_element_type=F32)


def small_cost():
    return pl.CostEstimate(flops=1, bytes_accessed=1, transcendentals=0)


def kernel_params(mib):
    return pltpu.CompilerParams(vmem_limit_bytes=mib * MIB)


def seat():
    expert = lax.axis_index("expert")
    return expert, lax.shift_right_logical(expert, 2), expert & 3, lax.axis_index("dp")


def aligned(index, step):
    return pl.ds(pl.multiple_of(index * step, step), step)


def cut_kernel(resid, r0, r1, r23):
    expert, outer, inner, dp = seat()
    rows, lanes = r0.shape
    r0[...] = resid[:, aligned(outer, lanes)]
    r1[...] = resid[:, aligned(outer ^ 1, lanes)]
    for i in range(2):
        r23[i * rows : (i + 1) * rows, :] = resid[:, aligned(outer ^ (2 + i), lanes)]


def share_kernel(live, ids, logits, share_ref):
    expert, outer, inner, dp = seat()
    rows, top = ids.shape
    experts, lanes = share_ref.shape
    value = logits[...]
    value = jnp.exp(value - jnp.max(value, axis=1, keepdims=True))
    probs = (value / jnp.sum(value, axis=1, keepdims=True)).astype(BF16).astype(F32)
    probs = jnp.where(lax.broadcasted_iota(jnp.int32, (rows, top), 0) < live[0, 0], probs, 0.0)
    names = lax.broadcasted_iota(jnp.int32, (rows, experts), 1)
    table = jnp.zeros((rows, experts), F32)
    for k in range(top):
        table = table + jnp.where(ids[:, k : k + 1] == names, probs[:, k : k + 1], 0.0)
    spots = lax.broadcasted_iota(jnp.int32, (rows, lanes), 1) - outer * rows
    spots = (spots == lax.broadcasted_iota(jnp.int32, (rows, lanes), 0)).astype(F32).astype(BF16)
    share_ref[...] = lax.dot_general(
        table.astype(BF16), spots, (((0,), (0,)), ((), ())), preferred_element_type=F32
    ).astype(BF16)


def proj_kernel(a0, a1, a2, a3, w0, w1, w2, w3, keep_ref, send_ref, rows, part):
    expert, outer, inner, dp = seat()
    full = a0.shape[0]
    half = full // 2
    block = w0.shape[1]
    for s, a in enumerate((a0, a1, a2, a3)):
        rows[aligned(outer ^ s, full), :] = a[...]
    for j, w in enumerate((w0, w1, w2, w3)):
        part[:, aligned(inner ^ j, block)] = dot(rows[...], w[...]).astype(BF16)
    for spot in range(4):
        keep_ref[spot * half : (spot + 1) * half, :] = part[aligned(2 * spot + dp, half), :]
        send_ref[spot * half : (spot + 1) * half, :] = part[aligned(2 * spot + 1 - dp, half), :]


def stream_kernel(keep, arrived, r0, r13, r2, share, block_ref):
    expert, outer, inner, dp = seat()
    count = keep.shape[0]
    small = r0.shape[0]
    for s, r in enumerate((r0[...], r13[0:small, :], r2[0:small, :], r13[small:, :])):
        rows = aligned(outer ^ s, small)
        product = keep[rows, :].astype(F32) + arrived[rows, :].astype(F32)
        block_ref[rows, :] = (r.astype(F32) + product).astype(BF16)
    block_ref[count:, :] = share[...]


def piece_kernel(starts, weights, *refs):
    *outs, semaphores = refs
    copies = []
    at = 0
    for k, out in enumerate(outs):
        depth, width = out.shape[0], out.shape[1] // 2
        for i in range(2):
            copies.append(
                pltpu.make_async_copy(
                    weights.at[pl.ds(at, depth), pl.ds(starts[i], width)],
                    out.at[:, pl.ds(i * width, width)],
                    semaphores.at[i, k],
                )
            )
        at += depth
    for copy in copies:
        copy.start()
    for copy in copies:
        copy.wait()


def swiglu(gate, up, share):
    return (gate / (1.0 + jnp.exp(-gate)) * up * share).astype(BF16)


def norm_kernel(b0, b1, b2, b3, gain, group_ref, own_ref):
    expert, outer, inner, dp = seat()
    count = group_ref.shape[0]
    width = b0.shape[1]
    experts = b0.shape[0] - count
    small = own_ref.shape[0]
    square = jnp.zeros((count, 1), F32)
    share = jnp.zeros((experts, count), F32)
    for s, b in enumerate((b0, b1, b2, b3)):
        value = b[0:count, :]
        group_ref[:, aligned((outer + 4 - s) & 3, width)] = value
        value = value.astype(F32)
        square = square + jnp.sum(value * value, axis=1, keepdims=True)
        share = share + b[count : count + experts, 0:count].astype(F32)
    own_ref[...] = group_ref[aligned(outer, small), 0 : 4 * width]
    scale = lax.rsqrt(square / (4 * width) + 1e-06)
    for s in range(4):
        cols = slice(s * width, (s + 1) * width)
        value = group_ref[:, cols].astype(F32)
        group_ref[:, cols] = (value * scale * gain[:, cols]).astype(BF16)
    lanes = (experts, 128)
    spread = lax.broadcasted_iota(jnp.int32, lanes, 0) == lax.broadcasted_iota(jnp.int32, lanes, 1)
    group_ref[:, 4 * width :] = lax.dot_general(
        share.astype(BF16),
        spread.astype(F32).astype(BF16),
        (((0,), (0,)), ((), ())),
        preferred_element_type=F32,
    ).astype(BF16)


def first_gate_kernel(
    group_x, group_cx, group, group_c, own, early,
    first_ref, second_ref, part_ref, other_ref, share_ref, mine_ref,
):
    expert, outer, inner, dp = seat()
    count = group.shape[0]
    half = other_ref.shape[1]
    cut = first_ref.shape[1]
    for j, g in enumerate((group_x, group_cx, group, group_c)):
        rows = slice(j * count, (j + 1) * count)
        mine_ref[rows, :] = g[:, aligned(dp, half)]
        other_ref[rows, :] = g[:, aligned(1 - dp, half)]
        share = g[:, 2 * half : 2 * half + 128].astype(F32)
        picked = lax.broadcasted_iota(jnp.int32, share.shape, 1) == expert
        share = jnp.sum(jnp.where(picked, share, 0.0), axis=1, keepdims=True)
        share_ref[rows, :] = jnp.broadcast_to(share, (count, 128))
    mine, other = mine_ref[...], other_ref[...]
    gate = dot(mine, own[:, 0:cut]) + dot(other, early[:, 0:cut])
    up = dot(mine, own[:, 2 * cut : 3 * cut]) + dot(other, early[:, cut : 2 * cut])
    inner = swiglu(gate, up, share_ref[:, 0:1])
    first_ref[...] = inner[: 3 * count]
    second_ref[...] = inner[3 * count :]
    part_ref[:, 0:cut] = dot(mine, own[:, cut : 2 * cut])
    part_ref[:, cut : 2 * cut] = dot(mine, own[:, 3 * cut : 4 * cut])


def last_gate_kernel(second, part, other, share, *refs):
    *late, far_ref, rest_ref = refs
    count, cut = second.shape
    gate, up = part[:, 0:cut], part[:, cut : 2 * cut]
    at = 0
    for piece in late:
        rows = other[:, at : at + piece.shape[0]]
        gate = gate + dot(rows, piece[:, 0:cut])
        up = up + dot(rows, piece[:, cut : 2 * cut])
        at += piece.shape[0]
    value = swiglu(gate, up, share[:, 0:1])
    far_ref[...] = value[: 2 * count]
    rest_ref[0:count, :] = second[...]
    rest_ref[count:, :] = value[2 * count :]


def down_rows(pieces, wd, keep_ref, sends, rows):
    expert, outer, inner, dp = seat()
    core = inner & 1
    count, side = sends[0].shape
    small = count // 4
    for h, places in enumerate(pieces):
        cut = places[0][0].shape[1]
        cols = slice(h * cut, (h + 1) * cut)
        for i in range(2):
            for j in range(2):
                ref, start = places[j]
                kept = aligned(start // small + ((outer + 2 * core + i) & 3), small)
                at = (2 * i + j) * small
                rows[at : at + small, cols] = ref[kept, :]
                ref, start = places[1 - j]
                sent = aligned(start // small + ((outer + 2 - 2 * core + i) & 3), small)
                rows[count + at : count + at + small, cols] = ref[sent, :]
    for at in range(0, wd.shape[1], 256):
        value = dot(rows[...], wd[:, at : at + 256]).astype(BF16)
        keep_ref[:, at : at + 256] = value[:count]
        sends[at // side][:, at % side : at % side + 256] = value[count:]


def far_places(first, far):
    count = far.shape[0] // 2
    return ((first, 0), (first, count)), ((far, 0), (far, count))


def near_places(first, rest):
    count = rest.shape[0] // 3
    return ((first, 2 * count), (rest, 0)), ((rest, count), (rest, 2 * count))


def down_both_kernel(first, far, rest, wd, keep_far, *refs):
    *sends, keep_near, rows = refs
    half = len(sends) // 2
    down_rows(far_places(first, far), wd, keep_far, sends[:half], rows)
    down_rows(near_places(first, rest), wd, keep_near, sends[half:], rows)


def down_far_kernel(first, far, wd, keep_ref, *refs):
    *sends, rows = refs
    down_rows(far_places(first, far), wd, keep_ref, sends, rows)


def down_near_kernel(first, rest, wd, keep_ref, *refs):
    *sends, rows = refs
    down_rows(near_places(first, rest), wd, keep_ref, sends, rows)


def added(keep, cores, cols):
    side = cores[0].shape[1]
    return keep[:, cols].astype(F32) + cores[cols.start // side][:, cols.start % side : cols.start % side + 256].astype(F32)


def fold_kernel(keep, *refs):
    *cores, out = refs
    for at in range(0, keep.shape[1], 256):
        cols = slice(at, at + 256)
        out[:, cols] = added(keep, cores, cols).astype(BF16)


def pieces_kernel(far, keep, *refs):
    *cores, first, second = refs
    half = first.shape[0]
    for at in range(0, keep.shape[1], 256):
        cols = slice(at, at + 256)
        total = (added(keep, cores, cols) + far[:, cols].astype(F32)).astype(BF16)
        first[:, cols] = total[:half]
        second[:, cols] = total[half:]


def messages_kernel(keep_far, keep_near, *refs):
    *cores, first, second = refs
    half = first.shape[0] // 2
    parts = len(cores) // 2
    for h, (keep, core) in enumerate(((keep_far, cores[:parts]), (keep_near, cores[parts:]))):
        for at in range(0, keep.shape[1], 256):
            cols = slice(at, at + 256)
            total = added(keep, core, cols).astype(BF16)
            first[h * half : (h + 1) * half, cols] = total[:half]
            second[h * half : (h + 1) * half, cols] = total[half:]


def outer_sum_kernel(own, a0, a1, far_ref, near_ref):
    expert, outer, inner, dp = seat()
    half = far_ref.shape[0]
    total = jnp.where((inner & 1) == 0, own[...].astype(F32), a0[...].astype(F32)) + a1[...].astype(F32)
    far_ref[...] = total[:half].astype(BF16)
    near_ref[...] = total[half:]


def gather_kernel(near, far, b0, b1, keep_ref, send_ref):
    small = near.shape[0] // 2
    for i, total in enumerate(
        (near[...] + far[...].astype(F32), b0[...].astype(F32) + b1[...].astype(F32))
    ):
        rows = slice(i * small, (i + 1) * small)
        keep_ref[rows, :] = total[:small]
        send_ref[rows, :] = total[small:].astype(BF16)


def tail_kernel(own, keep, core, gain, stream_ref, normed_ref):
    expert, outer, inner, dp = seat()
    small, half = own.shape[0], keep.shape[1]
    for i, at in enumerate((dp, 1 - dp)):
        rows = slice(i * small, (i + 1) * small)
        cols = aligned(at, half)
        mixture = keep[rows, :] + core[rows, :].astype(F32)
        stream_ref[:, cols] = (own[:, cols].astype(F32) + mixture).astype(BF16)
    normed_ref[...] = rms_scale(stream_ref[...].astype(F32), gain[...]).astype(BF16)


def body_paired(
    attn,
    resid,
    w_out,
    gain_post,
    route_ids,
    route_logits,
    live_count,
    w_gate_up,
    w_down,
    gain_final,
):
    rows_here = resid.shape[1]
    model_width = resid.shape[2]
    expert_count = lax.axis_size("expert")
    hidden = w_down.shape[1]
    half_width = w_down.shape[2]
    quarter = model_width // 4
    vmem, smem = whole_vmem(), whole_smem()

    def shape_of(*shape, dtype=BF16):
        return jax.ShapeDtypeStruct(shape, dtype)

    def call(kernel, name, mib, outs, *args, scratch=(), first=vmem):
        return pl.pallas_call(
            kernel,
            out_shape=outs,
            in_specs=[first] + [vmem] * (len(args) - 1),
            out_specs=tuple(vmem for _ in outs),
            scratch_shapes=list(scratch),
            compiler_params=kernel_params(mib),
            cost_estimate=small_cost(),
            name=name,
        )(*args)

    def swap_dp(x):
        return lax.ppermute(x, "dp", [(0, 1), (1, 0)])

    def shift_outer(x, s):
        return lax.ppermute(
            x, "expert", [(i, (i + 4 * s) % expert_count) for i in range(expert_count)]
        )

    def send_outer(x, i, cross):
        pairs = []
        for at in range(2 * expert_count):
            d, e = divmod(at, expert_count)
            step = 2 * (e % 2) + i
            if step or cross:
                pairs.append((at, (d ^ cross) * expert_count + (e + 4 * step) % expert_count))
        return lax.ppermute(x, ("dp", "expert"), pairs)

    def swap_inner(x, j):
        return lax.ppermute(x, "expert", [(i, i ^ j) for i in range(expert_count)])

    def swap_outer(x, s):
        return lax.ppermute(x, "expert", [(i, i ^ (4 * s)) for i in range(expert_count)])

    def after(x, *results):
        return lax.optimization_barrier((x, *results))[0]

    def weight_piece(first, size, depths):
        return pl.pallas_call(
            functools.partial(piece_kernel, (first, hidden + first)),
            out_shape=tuple(shape_of(depth, 2 * size) for depth in depths),
            in_specs=[pl.BlockSpec(memory_space=pl.ANY)],
            out_specs=tuple(vmem for _ in depths),
            scratch_shapes=[pltpu.SemaphoreType.DMA((2, len(depths)))],
            compiler_params=kernel_params(8),
            cost_estimate=small_cost(),
            name="weight_piece",
        )(w_gate_up[0])

    piece = shape_of(rows_here, quarter)
    r_own, r_1, r_23 = call(
        cut_kernel, "cut_resid", 4, (piece, piece, shape_of(2 * rows_here, quarter)), resid[0]
    )
    (share,) = call(
        share_kernel,
        "share",
        4,
        (shape_of(expert_count, quarter),),
        live_count,
        route_ids[0],
        route_logits[0],
        first=smem,
    )
    cut_width = hidden // 2
    early_piece = weight_piece(0, cut_width, (half_width,))[0]
    late_pieces = weight_piece(cut_width, cut_width, (half_width * 640 // 1024, half_width * 384 // 1024))
    gate_up_early = swap_dp(early_piece)
    a = [attn[0], swap_outer(attn[0], 1), swap_outer(attn[0], 2)]
    w_x = swap_inner(w_out, 2)
    r_2 = swap_outer(r_23, 2)
    a.append(swap_outer(after(a[2], a[1], r_2), 1))
    w_c = swap_inner(after(w_out, w_x, share, *late_pieces), 1)
    w_cx = swap_inner(w_x, 1)
    r_13 = swap_outer(jnp.concatenate([r_1, r_2[rows_here:]], axis=0), 1)

    product = shape_of(4 * rows_here, quarter)
    keep, send = call(
        proj_kernel,
        "projection",
        8,
        (product, product),
        *a[:3],
        after(a[3], r_13),
        w_out,
        w_c,
        w_x,
        w_cx,
        scratch=(
            pltpu.VMEM((8 * rows_here, attn.shape[2]), BF16),
            pltpu.VMEM((8 * rows_here, quarter), BF16),
        ),
    )
    arrived = swap_dp(send)
    gate_up_late = [swap_dp(after(piece, send)) for piece in late_pieces]
    (block,) = call(
        stream_kernel,
        "stream",
        4,
        (shape_of(4 * rows_here + expert_count, quarter),),
        after(keep, gate_up_early),
        arrived,
        r_own,
        r_13,
        r_2,
        share,
    )

    def norm(b0, b1, b2, b3):
        outs = (shape_of(4 * rows_here, model_width + 128), shape_of(rows_here, model_width))
        return call(norm_kernel, "norm", 8, outs, b0, b1, b2, b3, gain_post[None])

    blocks = [block] + [shift_outer(block, s) for s in (1, 2, 3)]
    group, stream_own = norm(*blocks)
    blocks_x = [swap_inner(b, 2) for b in blocks]
    group_x, unused = norm(*blocks_x)
    group_c = swap_inner(group, 1)
    group_cx = swap_inner(group_x, 1)

    row_total = 16 * rows_here
    half_rows = row_total // 2
    inner_first, inner_second, part, other_rows, share_rows = call(
        first_gate_kernel,
        "first_gate_up",
        24,
        (
            shape_of(row_total * 3 // 4, cut_width),
            shape_of(row_total // 4, cut_width),
            shape_of(row_total, hidden, dtype=F32),
            shape_of(row_total, half_width),
            shape_of(row_total, 128, dtype=F32),
        ),
        group_x,
        group_cx,
        group,
        group_c,
        w_gate_up[0],
        gate_up_early,
        scratch=(pltpu.VMEM((row_total, half_width), BF16),),
    )
    inner_far, inner_rest = call(
        last_gate_kernel,
        "last_gate_up",
        16,
        (shape_of(half_rows, cut_width), shape_of(row_total * 3 // 4, cut_width)),
        inner_second,
        part,
        other_rows,
        share_rows,
        *gate_up_late,
    )
    first_other = swap_dp(inner_first)
    far_other = swap_dp(inner_far)
    rest_other = swap_dp(inner_rest)

    count = row_total // 4
    quarter_out = shape_of(count, half_width)

    def parts_of(many):
        return (shape_of(count, half_width // many),) * many

    scratch = (pltpu.VMEM((half_rows, hidden), BF16),)

    def down(kernel, rows, many):
        keep, *send = call(
            kernel, "down", 12, (quarter_out, *parts_of(many)), first_other, rows, w_down[0], scratch=scratch
        )
        return keep, send

    def swap_cores(halves):
        return [swap_inner(half, 1) for half in halves]

    def fold(keep, halves):
        return call(fold_kernel, "fold", 4, (quarter_out,), keep, *halves)[0]

    def pieces(far, keep, send):
        outs = (shape_of(2 * rows_here, half_width),) * 2
        return call(pieces_kernel, "pieces", 4, outs, far, keep, *swap_cores(send))

    outs = (quarter_out, *parts_of(1), *parts_of(1), quarter_out)
    keep_far, *send, keep_near = call(
        down_both_kernel, "down_both", 16, outs, inner_first, inner_far, inner_rest, w_down[0], scratch=scratch
    )
    message = shape_of(4 * rows_here, half_width)
    own, second = call(
        messages_kernel, "messages", 4, (message, message), keep_far, keep_near, *swap_cores(send)
    )
    half_message = shape_of(2 * rows_here, half_width)
    mine_far, mine_near = call(
        outer_sum_kernel,
        "outer_sum",
        4,
        (half_message, shape_of(2 * rows_here, half_width, dtype=F32)),
        own,
        send_outer(own, 0, False),
        send_outer(second, 1, False),
    )
    mine_far = swap_inner(mine_far, 2)

    keep_far, send = down(down_far_kernel, far_other, 2)
    far = swap_inner(fold(keep_far, swap_cores(send)), 2)
    keep_near, send = down(down_near_kernel, rest_other, 2)
    cut = pieces(far, keep_near, [send[0], after(send[1], mine_near)])
    others = [send_outer(cut[i], i, True) for i in range(2)]

    sums = shape_of(2 * rows_here, half_width)
    keep, send = call(
        gather_kernel,
        "gather",
        4,
        (shape_of(2 * rows_here, half_width, dtype=F32), sums),
        mine_near,
        mine_far,
        *others,
    )
    out = shape_of(rows_here, model_width)
    stream_out, normed_out = call(
        tail_kernel, "closing", 8, (out, out), stream_own, keep, swap_inner(send, 1), gain_final[None]
    )
    return (stream_out[None], normed_out[None])


def solution(mesh):
    placed = (
        P("expert", None, "dp"),
        P("expert", "dp", None),
        P("dp", "expert"),
        P(),
        P("expert", "dp", None),
        P("expert", "dp", None),
        P("expert", "dp"),
        P("expert", "dp", None),
        P("expert", None, "dp"),
        P(),
    )
    paired = mesh.shape["dp"] == 2 and mesh.shape["expert"] == 16
    return jax.shard_map(
        body_paired if paired else body_general,
        mesh=mesh,
        in_specs=placed,
        out_specs=(P("expert", "dp", None), P("expert", "dp", None)),
        check_vma=False,
    )
```
